32 devices in a mesh: row: 4 (over z), col: 8 (over y, x, core).
Axes of the slice: x: 2, y: 2, z: 4, core: 2. Of those that a mesh axis runs over, the one named last changes fastest.
Arguments:
- current_block: float32 [48, 65536], P(None, ('row', 'col')), may hold values from -12 to 12, as said below
- previous_block: float32 [48, 65536], P(None, ('row', 'col')), may hold values from -12 to 12
- previous_coupling: float32 [48, 48], replicated, may hold values from -0.875 to 0.875
- stored_blocks: float32 [8, 48, 65536], P(None, None, ('row', 'col')), may hold values from -12 to 12
- stiffness_diag: float32 [65536], P(('row', 'col')), may hold values from 1 to 10
- lumped_mass: float32 [65536], P(('row', 'col')), may hold values from 0.25 to 24
- tile_values: bfloat16 [16384, 128, 128], P(('row', 'col')), may hold values from -0.14941406 to 0.14941406
- tile_rows: int32 [16384], P(('row', 'col')), may hold values from 0 to 63, as said below
- tile_cols: int32 [16384], P(('row', 'col')), may hold values from 0 to 127
- tile_counts: int32 [32], P(('row', 'col')), may hold values from 128 to 512, as said below
Outputs:
- residual_block: float32 [48, 65536], P(None, ('row', 'col'))
- coefficients: float32 [9, 48, 48], replicated
- gram: float32 [48, 48], replicated
The draws below stay inside these ranges and needn't reach their ends.
Inputs may be any that keep to these rules, and one draw needn't show every extreme that they name: `current_block`: each entry shares a part with the same entry of the other Lanczos blocks. `tile_rows`: some local output tile rows hold far more tiles than others. `tile_counts`: exactly one device has all 512 slots occupied.
All inputs are finite; a program needn't handle non-finite values.
Results may differ from the reference program's by a relative error of at most 0.0044.
Values may be sent and summed in bfloat16 or wider, within the bound.
No kernel may reach another device: no remote copies, remote signals or barrier semaphores. Data moves between devices by JAX's collectives and lax.ppermute only.
A program may use at most 128 MiB of HBM per device.

```python
import math
import jax
import jax.numpy as jnp
from jax import lax

BLOCK = 48
STORED = 8
TILE = 128
TPS = 16
TMAX = 512
SLAB = 2048
NRT = 64
NCT = 128
NTOT = 65536
N_ROW = 4
N_COL = 8
DEVICES = 32


def shared_vectors(key, which, shape, weight_plain):
    own_key = jax.random.fold_in(key, which)
    common = jax.random.normal(jax.random.fold_in(key, 77), (BLOCK, NTOT), jnp.float32)
    common = jnp.clip(common, -6.0, 6.0)
    own = jnp.clip(jax.random.normal(own_key, shape, jnp.float32), -6.0, 6.0)
    return own + weight_plain * common


def draw_current_block(key, part):
    return shared_vectors(key, 11, (BLOCK, NTOT), 0.6)


def draw_previous_block(key, part):
    return shared_vectors(key, 12, (BLOCK, NTOT), 0.3)


def draw_stored_blocks(key, part):
    return shared_vectors(key, 13, (STORED, BLOCK, NTOT), 0.5)


def draw_lumped_mass(key, part):
    level = jax.random.uniform(jax.random.fold_in(key, 21), (NTOT,), jnp.float32, jnp.log(0.25), jnp.log(4.0))
    position = jnp.arange(NTOT, dtype=jnp.float32) / NTOT
    return jnp.exp(level) * (1.0 + 2.0 * position)


def draw_tile_rows(key, part):
    heavy = jax.random.randint(jax.random.fold_in(key, 31), (4,), 0, NRT)
    picker = jax.random.randint(jax.random.fold_in(key, 32), (DEVICES * TMAX,), 0, 4)
    choose = jax.random.randint(jax.random.fold_in(key, 33), (DEVICES * TMAX,), 0, 2)
    spread = jax.random.randint(jax.random.fold_in(key, 34), (DEVICES * TMAX,), 0, NRT)
    return jnp.where(choose == 0, heavy[picker], spread).astype(jnp.int32)


def draw_tile_counts(key, part):
    base = jax.random.randint(jax.random.fold_in(key, 41), (DEVICES,), TMAX // 4, TMAX // 2 + 1)
    busiest = jax.random.randint(jax.random.fold_in(key, 42), (), 0, DEVICES)
    return jnp.where(jnp.arange(DEVICES, dtype=jnp.int32) == busiest, TMAX, base).astype(jnp.int32)


def touch_ends(array, key, smallest, top_value):
    longest = array.shape.index(max(array.shape))
    spots = []
    for shift in (0, 1):
        where = [jax.random.randint(jax.random.fold_in(key, axis), (), 0, length) for axis, length in enumerate(array.shape)]
        where[longest] = (where[longest] + shift) % array.shape[longest]
        spots.append(tuple(where))
    return array.at[spots[0]].set(smallest).at[spots[1]].set(top_value)


def level_of(rng, extent, pieces, smallest, top_value):
    factor_of = 1.0
    for dim, shards_of in pieces:
        draws = jax.random.uniform(jax.random.fold_in(jax.random.fold_in(rng, 6), dim), (shards_of,), jnp.float32, smallest / len(pieces), top_value / len(pieces))
        factor_of = factor_of * jnp.repeat(jnp.exp(draws), extent[dim] // shards_of).reshape((-1,) + (1,) * (len(extent) - 1 - dim))
    return factor_of


def gaussian(rng, extent, scale, most, split=(), kind=jnp.bfloat16):
    array = jax.random.normal(rng, extent, jnp.float32) * scale
    if len(split) > 0:
        array = level_of(rng, extent, split, -0.22, 0.18) * array
    return jnp.clip(array, min=-most, max=most).astype(kind)


def setup_inputs(seed: int = 0) -> dict:
    streams_of = jax.random.split(jax.random.key(seed), 11)
    current_block = draw_current_block(jax.random.fold_in(streams_of[10], 71), 0)
    previous_block = draw_previous_block(jax.random.fold_in(streams_of[10], 71), 0)
    previous_coupling = gaussian(streams_of[2], (BLOCK, BLOCK), BLOCK ** -0.5, 0.875, (), jnp.float32)
    stored_blocks = draw_stored_blocks(jax.random.fold_in(streams_of[10], 71), 0)
    stiffness_diag = jnp.clip(jnp.exp(math.log(10.0) - 2.3025851 * jax.random.uniform(streams_of[4], (NTOT,), jnp.float32) ** level_of(streams_of[4], (NTOT,), ((0, 32),), -0.2, 0.2)), 1.0, 10.0)
    lumped_mass = draw_lumped_mass(jax.random.fold_in(streams_of[10], 71), 0)
    tile_values = gaussian(streams_of[6], (DEVICES * TMAX, TILE, TILE), 0.025, 0.14941406, ((0, 32),))
    tile_rows = draw_tile_rows(jax.random.fold_in(streams_of[10], 71), 0)
    tile_cols = touch_ends(jax.random.randint(streams_of[8], (DEVICES * TMAX,), 0, NCT), jax.random.fold_in(streams_of[8], 1), 0, NCT - 1).astype(jnp.int32)
    tile_counts = draw_tile_counts(jax.random.fold_in(streams_of[10], 71), 0)
    return {"current_block": current_block, "previous_block": previous_block, "previous_coupling": previous_coupling, "stored_blocks": stored_blocks, "stiffness_diag": stiffness_diag, "lumped_mass": lumped_mass, "tile_values": tile_values, "tile_rows": tile_rows, "tile_cols": tile_cols, "tile_counts": tile_counts}


def reference(current_block, previous_block, previous_coupling, stored_blocks, stiffness_diag, lumped_mass, tile_values, tile_rows, tile_cols, tile_counts):
    device_total = N_ROW * N_COL
    rounded = current_block.astype(jnp.bfloat16)
    groups = rounded.reshape(BLOCK, N_ROW, NCT, TILE)
    values = tile_values.reshape(device_total, TMAX, TILE, TILE)
    row_lists = tile_rows.reshape(device_total, TMAX)
    col_lists = tile_cols.reshape(device_total, TMAX)
    slot_ids = jnp.arange(TMAX, dtype=jnp.int32)
    targets = jnp.arange(NRT, dtype=jnp.int32)

    def one_device(running, device):
        row_index = device // N_COL
        col_index = device % N_COL
        panels = lax.dynamic_index_in_dim(groups, row_index, axis=1, keepdims=False)
        picked = jnp.take(panels, col_lists[device], axis=1).astype(jnp.float32)
        products = jnp.einsum("btj,tij->tbi", picked, values[device].astype(jnp.float32))
        occupied = slot_ids < tile_counts[device]
        selector = ((row_lists[device][None, :] == targets[:, None]) & occupied[None, :]).astype(jnp.float32)
        contrib = jnp.einsum("at,tbi->abi", selector, products, precision=lax.Precision.HIGHEST)
        contrib = contrib.reshape(N_ROW, TPS, BLOCK, TILE).transpose(0, 2, 1, 3).reshape(N_ROW, BLOCK, SLAB)
        running = running.at[:, col_index].add(contrib)
        return running, None

    start_acc = jnp.zeros((N_ROW, N_COL, BLOCK, SLAB), jnp.float32)
    accum, _ = lax.scan(one_device, start_acc, jnp.arange(device_total, dtype=jnp.int32))
    product = accum.transpose(2, 0, 1, 3).reshape(BLOCK, NTOT)
    product = product + stiffness_diag[None, :] * current_block
    recurrence = product - jnp.dot(previous_coupling, previous_block, precision=lax.Precision.HIGHEST, preferred_element_type=jnp.float32)
    basis = jnp.concatenate([current_block[None], stored_blocks], axis=0)
    weighted = recurrence * lumped_mass[None, :] / NTOT
    coefficients = jnp.einsum("kpi,qi->kpq", basis, weighted, precision=lax.Precision.HIGHEST)
    residual_block = recurrence - jnp.einsum("kpq,kpi->qi", coefficients, basis, precision=lax.Precision.HIGHEST)
    gram = jnp.einsum("qi,pi->qp", residual_block * lumped_mass[None, :] / NTOT, residual_block, precision=lax.Precision.HIGHEST)
    return residual_block, coefficients, gram
```

```python
import functools

import jax
import jax.numpy as jnp
from jax import lax
from jax.experimental import pallas as pl
from jax.experimental.pallas import tpu as pltpu
from jax.sharding import PartitionSpec as P

LANES = 128
CHUNK = 32
UNROLL = 8
NT = (((1,), (1,)), ((), ()))
MIB = 1 << 20


def swap(value, axis, mask):
    count = lax.axis_size(axis)
    return lax.ppermute(value, axis, [(i, i ^ mask) for i in range(count)])


def tree_sum(values):
    while len(values) > 1:
        values = [values[i] + values[i + 1] for i in range(0, len(values), 2)]
    return values[0]


def split(value):
    high = value.astype(jnp.bfloat16)
    low = (value - high.astype(jnp.float32)).astype(jnp.bfloat16)
    return high, low


def mm(a, b, dims=(((1,), (0,)), ((), ()))):
    return lax.dot_general(a, b, dims, preferred_element_type=jnp.float32)


def dot_split(a, b, dims=(((1,), (0,)), ((), ()))):
    rows = a.shape[0]
    a_high, a_low = split(a)
    b_high, b_low = split(b)
    both = mm(jnp.concatenate([a_high, a_low], axis=0), b_high, dims)
    return both[:rows] + both[rows:] + mm(a_high, b_low, dims)


def start_kernel(current, previous, coupling, diag, out):
    out[...] = diag[...] * current[...] - jnp.dot(
        coupling[...],
        previous[...],
        precision=lax.Precision.HIGHEST,
        preferred_element_type=jnp.float32,
    )


def tiles_kernel(row_devs, col_devs, place, rows, cols, counts, *refs):
    panels = refs[:col_devs]
    tiles = refs[col_devs]
    own = refs[col_devs + 1]
    sends = refs[col_devs + 2 : col_devs + 1 + row_devs]
    panel_buf, tile_buf, acc, panel_sem, tile_sem = refs[col_devs + 1 + row_devs :]
    slab_tiles = own.shape[1] // LANES
    targets = row_devs * slab_tiles
    row, col, count = place[0], place[1], counts[0]
    chunks = (count + CHUNK - 1) // CHUNK

    def tile_copy(k):
        window = pl.ds(k * CHUNK, CHUNK)
        return pltpu.make_async_copy(tiles.at[window], tile_buf.at[window], tile_sem.at[k])

    panel_copies = [
        pltpu.make_async_copy(panels[m], panel_buf.at[m], panel_sem.at[m]) for m in range(col_devs)
    ]
    for copy in panel_copies:
        copy.start()

    @pl.loop(0, chunks)
    def _(k):
        tile_copy(k).start()

    acc[...] = jnp.zeros_like(acc)
    for copy in panel_copies:
        copy.wait()

    @pl.loop(0, chunks)
    def _(k):
        tile_copy(k).wait()
        groups = jnp.minimum(CHUNK // UNROLL, (count - k * CHUNK + UNROLL - 1) // UNROLL)

        @pl.loop(0, groups)
        def _(g):
            first = k * CHUNK + g * UNROLL
            parts = []
            for u in range(UNROLL):
                b = cols[first + u]
                source = (b // slab_tiles) ^ col
                where = pl.multiple_of((b % slab_tiles) * LANES, LANES)
                parts.append(mm(panel_buf[source, :, pl.ds(where, LANES)], tile_buf[first + u], NT))
            for u in range(UNROLL):
                a = jnp.where(first + u < count, rows[first + u], targets)
                acc[a] += parts[u]

    for s in range(slab_tiles):
        window = pl.ds(s * LANES, LANES)
        own[:, window] = acc[row * slab_tiles + s]
        for m in range(1, row_devs):
            sends[m - 1][:, window] = acc[(row ^ m) * slab_tiles + s].astype(jnp.bfloat16)


def coefficient_kernel(cells, pieces, *refs):
    base, own = refs[0], refs[1]
    received = refs[2 : 1 + pieces]
    mass, current, stored, recurrence, out = refs[1 + pieces :]
    total = base[...] + own[...]
    for ref in received:
        total = total + ref[...].astype(jnp.float32)
    recurrence[...] = total
    weighted = total * (mass[...] * (1.0 / cells))
    basis = jnp.concatenate([current[...], stored[...]], axis=0)
    coef = dot_split(weighted, basis, NT)
    width = coef.shape[0]
    groups = out.shape[0] // width
    coef = jnp.concatenate(
        [coef, jnp.zeros((width, groups * LANES - coef.shape[1]), jnp.float32)], axis=1
    )
    for g in range(groups):
        out[g * width : (g + 1) * width, :] = coef[:, g * LANES : (g + 1) * LANES]


def residual_kernel(cells, col_devs, place, *refs):
    pieces = refs[:col_devs]
    recurrence, mass, current, stored, residual, coef_out, gram, gathered, packed = refs[col_devs:]
    col = place[1]
    rows = pieces[0].shape[0]
    for m in range(col_devs):
        gathered[m] = pieces[m][...]
    for p in range(col_devs):
        packed[p * rows : (p + 1) * rows, :] = gathered[p ^ col]
    width = recurrence.shape[0]
    groups = packed.shape[0] // width
    coef = jnp.concatenate(
        [packed[g * width : (g + 1) * width, :] for g in range(groups)], axis=1
    )
    basis = jnp.concatenate([current[...], stored[...]], axis=0)
    coef = coef[:, : basis.shape[0]]
    coef_out[...] = coef
    value = recurrence[...] - dot_split(coef, basis)
    residual[...] = value
    local = dot_split(value * (mass[...] * (1.0 / cells)), value, NT)
    half = width // 2
    gram[...] = jnp.zeros_like(gram)
    gram[:, :width] = local[:half]
    gram[:, LANES // 2 : LANES // 2 + width] = local[half:]


def vmem(count):
    return [pl.BlockSpec(memory_space=pltpu.VMEM)] * count


def smem(count):
    return [pl.BlockSpec(memory_space=pltpu.SMEM)] * count


def local(
    current_block,
    previous_block,
    previous_coupling,
    stored_blocks,
    stiffness_diag,
    lumped_mass,
    tile_values,
    tile_rows,
    tile_cols,
    tile_counts,
):
    row_devs = lax.axis_size("row")
    col_devs = lax.axis_size("col")
    width, slab_len = current_block.shape
    stored_count = stored_blocks.shape[0]
    slots, tile_len, _ = tile_values.shape
    slab_tiles = slab_len // tile_len
    cells = slab_len * row_devs * col_devs
    f32, bf16 = jnp.float32, jnp.bfloat16
    place = jnp.stack([lax.axis_index("row"), lax.axis_index("col")]).astype(jnp.int32)
    stored = stored_blocks.reshape(stored_count * width, slab_len)
    mass = lumped_mass.reshape(1, slab_len)
    diag = stiffness_diag.reshape(1, slab_len)
    slab = jax.ShapeDtypeStruct((width, slab_len), f32)

    with jax.named_scope("gather"):
        rounded = current_block.astype(bf16)
        panels = [rounded] + [None] * (col_devs - 1)
        for m in range(2, col_devs, 2):
            panels[m] = swap(rounded, "col", m)
        for m in range(0, col_devs, 2):
            panels[m + 1] = swap(panels[m], "col", 1)

    with jax.named_scope("start"):
        base = pl.pallas_call(
            start_kernel,
            out_shape=slab,
            in_specs=vmem(4),
            out_specs=vmem(1)[0],
            cost_estimate=pl.CostEstimate(
                flops=12 * width * width * slab_len, bytes_accessed=12 * width * slab_len, transcendentals=0
            ),
        )(current_block, previous_block, previous_coupling, diag)

    with jax.named_scope("tiles"):
        outs = pl.pallas_call(
            functools.partial(tiles_kernel, row_devs, col_devs),
            out_shape=[slab] + [jax.ShapeDtypeStruct((width, slab_len), bf16)] * (row_devs - 1),
            in_specs=smem(4) + [pl.BlockSpec(memory_space=pl.ANY)] * (col_devs + 1),
            out_specs=vmem(row_devs),
            scratch_shapes=[
                pltpu.VMEM((col_devs, width, slab_len), bf16),
                pltpu.VMEM((slots, tile_len, tile_len), bf16),
                pltpu.VMEM((row_devs * slab_tiles + 1, width, tile_len), f32),
                pltpu.SemaphoreType.DMA((col_devs,)),
                pltpu.SemaphoreType.DMA((slots // CHUNK,)),
            ],
            compiler_params=pltpu.CompilerParams(vmem_limit_bytes=40 * MIB),
            cost_estimate=pl.CostEstimate(
                flops=2 * slots * width * tile_len * tile_len,
                bytes_accessed=2 * slots * tile_len * tile_len,
                transcendentals=0,
            ),
        )(place, tile_rows, tile_cols, tile_counts, *panels, tile_values)

    with jax.named_scope("scatter"):
        received = [swap(outs[m], "row", m) for m in range(1, row_devs)]

    pad_groups = -(-(stored_count + 1) * width // LANES)
    with jax.named_scope("coefficients"):
        recurrence, partial = pl.pallas_call(
            functools.partial(coefficient_kernel, cells, row_devs),
            out_shape=[slab, jax.ShapeDtypeStruct((pad_groups * width, LANES), f32)],
            in_specs=vmem(row_devs + 4),
            out_specs=vmem(2),
            compiler_params=pltpu.CompilerParams(vmem_limit_bytes=40 * MIB),
        )(base, outs[0], *received, mass, current_block, stored)
        pieces = partial.reshape(col_devs, pad_groups * width // col_devs, LANES)
        pieces = lax.all_to_all(pieces, "col", 0, 0)
        piece = jnp.sum(pieces, axis=0)
        piece = tree_sum([piece] + [swap(piece, "row", m) for m in range(1, row_devs)])
        pieces = [piece] + [swap(piece, "col", m) for m in range(1, col_devs)]

    with jax.named_scope("residual"):
        basis_rows = (stored_count + 1) * width
        residual_block, coef, gram = pl.pallas_call(
            functools.partial(residual_kernel, cells, col_devs),
            out_shape=[
                slab,
                jax.ShapeDtypeStruct((width, basis_rows), f32),
                jax.ShapeDtypeStruct((width // 2, LANES), f32),
            ],
            in_specs=smem(1) + vmem(col_devs + 4),
            out_specs=vmem(3),
            scratch_shapes=[
                pltpu.VMEM((col_devs, pad_groups * width // col_devs, LANES), f32),
                pltpu.VMEM((pad_groups * width, LANES), f32),
            ],
            compiler_params=pltpu.CompilerParams(vmem_limit_bytes=40 * MIB),
        )(place, *pieces, recurrence, mass, current_block, stored)
        coefficients = coef.T.reshape(stored_count + 1, width, width)

    with jax.named_scope("gram"):
        gram = tree_sum([gram] + [swap(gram, "col", m) for m in range(1, col_devs)])
        gram = tree_sum([gram] + [swap(gram, "row", m) for m in range(1, row_devs)])
        gram = jnp.concatenate(
            [gram[:, :width], gram[:, LANES // 2 : LANES // 2 + width]], axis=0
        )
    return (residual_block, coefficients, gram)


def solution(mesh):
    return jax.shard_map(
        local,
        mesh=mesh,
        in_specs=(
            P(None, ("row", "col")),
            P(None, ("row", "col")),
            P(),
            P(None, None, ("row", "col")),
            P(("row", "col")),
            P(("row", "col")),
            P(("row", "col"), None, None),
            P(("row", "col")),
            P(("row", "col")),
            P(("row", "col")),
        ),
        out_specs=(P(None, ("row", "col")), P(), P()),
        check_vma=False,
    )
```

```python
import functools

import jax
import jax.numpy as jnp
from jax import lax
from jax.experimental import pallas as pl
from jax.experimental.pallas import tpu as pltpu
from jax.sharding import PartitionSpec as P

LANES = 128
UNROLL = 8
NT = (((1,), (1,)), ((), ()))
MIB = 1 << 20


def swap(value, axis, mask):
    count = lax.axis_size(axis)
    return lax.ppermute(value, axis, [(i, i ^ mask) for i in range(count)])


def split(value):
    high = value.astype(jnp.bfloat16)
    low = (value - high.astype(jnp.float32)).astype(jnp.bfloat16)
    return high, low


def mm(a, b, dims=(((1,), (0,)), ((), ()))):
    return lax.dot_general(a, b, dims, preferred_element_type=jnp.float32)


def dot_split(a, b, dims=(((1,), (0,)), ((), ()))):
    rows = a.shape[0]
    a_high, a_low = split(a)
    b_high, b_low = split(b)
    both = mm(jnp.concatenate([a_high, a_low], axis=0), b_high, dims)
    return both[:rows] + both[rows:] + mm(a_high, b_low, dims)


def blocks(shape):
    return [(q, k) for q in range(0, shape[0], 8) for k in range(0, shape[1], LANES)]


def start_kernel(current, previous, coupling, diag, out):
    out[...] = diag[...] * current[...] - jnp.dot(
        coupling[...],
        previous[...],
        precision=lax.Precision.HIGHEST,
        preferred_element_type=jnp.float32,
    )


def plan_kernel(row_devs, col_devs, slab_tiles, place, counts, rows, cols, out):
    f32, bf16, i32 = jnp.float32, jnp.bfloat16, jnp.int32
    slots, places = rows.shape[1], out.shape[1]
    targets = row_devs * slab_tiles

    def iota(shape, dim):
        return lax.broadcasted_iota(i32, shape, dim)

    slot = iota((1, slots), 1)
    occupied = slot < counts[0]
    row = jnp.where(occupied, rows[...], -1)
    member = (iota((targets, slots), 0) == row).astype(f32)
    member_bf = member.astype(bf16)
    earlier = (iota((slots, slots), 0) < iota((slots, slots), 1)).astype(f32).astype(bf16)
    rank = jnp.sum(member * mm(member_bf, earlier), axis=0, keepdims=True)
    sizes = mm(jnp.ones((8, slots), bf16), member_bf, NT)[:1]
    sizes = 2.0 * jnp.floor(0.5 * (sizes + 1.0))
    before = (iota((targets, targets), 1) < iota((targets, targets), 0)).astype(f32)
    begin = jnp.sum(before * sizes, axis=1, keepdims=True)
    total = jnp.sum(sizes, axis=1, keepdims=True)
    position = jnp.sum(member * begin, axis=0, keepdims=True) + rank
    position = jnp.where(occupied, position.astype(i32), -1)
    chosen = (iota((places, slots), 0) == position).astype(f32).astype(bf16)
    slot_f = slot.astype(f32)
    slot_high = jnp.floor(slot_f * (1.0 / 16.0))
    facts = [slot_high, slot_f - 16.0 * slot_high, cols[...].astype(f32), row.astype(f32), jnp.ones((1, slots), f32)]
    facts = jnp.concatenate(facts + [jnp.zeros((3, slots), f32)], axis=0).astype(bf16)
    found = mm(facts, chosen, NT)
    valid = found[4:5] > 0.5
    source = jnp.floor(found[2:3] * (1.0 / slab_tiles))
    tile = found[2:3] - slab_tiles * source
    out[0:1] = (16.0 * found[0:1] + found[1:2]).astype(i32)
    out[1:2] = jnp.where(valid, source.astype(i32) ^ place[1], col_devs)
    out[2:3] = tile.astype(i32)
    out[3:4] = jnp.where(valid, found[3:4].astype(i32), targets)
    out[4:8] = jnp.broadcast_to(total.astype(i32), (4, places))


def tiles_kernel(row_devs, col_devs, place, plan, *refs):
    panels = refs[:col_devs]
    tiles = refs[col_devs]
    own = refs[col_devs + 1]
    sends = refs[col_devs + 2 : col_devs + 1 + row_devs]
    panel_buf, acc, panel_sem = refs[col_devs + 1 + row_devs :]
    slab_tiles = own.shape[1] // LANES
    row = place[0]

    panel_copies = [
        pltpu.make_async_copy(panels[m], panel_buf.at[m], panel_sem.at[m]) for m in range(col_devs)
    ]
    for copy in panel_copies:
        copy.start()
    panel_buf[col_devs, :, :LANES] = jnp.zeros((own.shape[0], LANES), jnp.bfloat16)
    acc[...] = jnp.zeros_like(acc)
    for copy in panel_copies:
        copy.wait()

    def panel(p):
        where = pl.multiple_of(plan[2, p] * LANES, LANES)
        return panel_buf[plan[1, p], :, pl.ds(where, LANES)]

    @pl.loop(0, (plan[4, 0] + 2 * UNROLL - 1) // (2 * UNROLL))
    def _(g):
        first = g * 2 * UNROLL
        parts = []
        for u in range(UNROLL):
            p = first + 2 * u
            left = jnp.concatenate([panel(p), panel(p + 1)], axis=1)
            right = jnp.concatenate([tiles[plan[0, p]], tiles[plan[0, p + 1]]], axis=1)
            parts.append(mm(left, right, NT))
        for u in range(UNROLL):
            acc[plan[3, first + 2 * u]] += parts[u]

    for s in range(slab_tiles):
        window = pl.ds(s * LANES, LANES)
        own[:, window] = acc[row * slab_tiles + s]
        for m in range(1, row_devs):
            sends[m - 1][:, window] = acc[(row ^ m) * slab_tiles + s].astype(jnp.bfloat16)


def coefficient_kernel(cells, pieces, *refs):
    base, own = refs[0], refs[1]
    received = refs[2 : 1 + pieces]
    mass, current, stored, recurrence, out = refs[1 + pieces :]
    total = base[...] + own[...]
    for ref in received:
        total = total + ref[...].astype(jnp.float32)
    recurrence[...] = total
    weighted = total * (mass[...] * (1.0 / cells))
    basis = jnp.concatenate([current[...], stored[...]], axis=0)
    coef = dot_split(weighted, basis, NT)
    width = coef.shape[0]
    groups = out.shape[0] // width
    spare = -coef.shape[1] % LANES
    coef = jnp.concatenate([coef, jnp.zeros((coef.shape[0], spare), jnp.float32)], axis=1)
    out[...] = jnp.zeros_like(out)
    for p, (q, k) in enumerate(blocks(coef.shape)):
        out[p] = coef[q : q + 8, k : k + LANES]


def residual_kernel(cells, pieces, recurrence, mass, current, stored, residual, coef_out, gram, packed):
    width = recurrence.shape[0]
    for p, (q, k) in enumerate(blocks(packed.shape)):
        packed[q : q + 8, k : k + LANES] = pieces[p]
    coef = packed[...]
    basis = jnp.concatenate([current[...], stored[...]], axis=0)
    coef = coef[:, : basis.shape[0]]
    coef_out[...] = coef
    value = recurrence[...] - dot_split(coef, basis)
    residual[...] = value
    local = dot_split(value * (mass[...] * (1.0 / cells)), value, NT)
    half = width // 2
    gram[...] = jnp.zeros_like(gram)
    gram[:, :width] = local[:half]
    gram[:, LANES // 2 : LANES // 2 + width] = local[half:]


def vmem(count):
    return [pl.BlockSpec(memory_space=pltpu.VMEM)] * count


def smem(count):
    return [pl.BlockSpec(memory_space=pltpu.SMEM)] * count


def local(
    current_block,
    previous_block,
    previous_coupling,
    stored_blocks,
    stiffness_diag,
    lumped_mass,
    tile_values,
    tile_rows,
    tile_cols,
    tile_counts,
):
    row_devs = lax.axis_size("row")
    col_devs = lax.axis_size("col")
    width, slab_len = current_block.shape
    stored_count = stored_blocks.shape[0]
    slots, tile_len, _ = tile_values.shape
    slab_tiles = slab_len // tile_len
    cells = slab_len * row_devs * col_devs
    f32, bf16 = jnp.float32, jnp.bfloat16
    place = jnp.stack([lax.axis_index("row"), lax.axis_index("col")]).astype(jnp.int32)
    stored = stored_blocks.reshape(stored_count * width, slab_len)
    mass = lumped_mass.reshape(1, slab_len)
    diag = stiffness_diag.reshape(1, slab_len)
    slab = jax.ShapeDtypeStruct((width, slab_len), f32)

    with jax.named_scope("gather"):
        rounded = current_block.astype(bf16)
        panels = [rounded] + [None] * (col_devs - 1)
        for m in range(2, col_devs, 2):
            panels[m] = swap(rounded, "col", m)
        for m in range(0, col_devs, 2):
            panels[m + 1] = swap(panels[m], "col", 1)

    with jax.named_scope("start"):
        base = pl.pallas_call(
            start_kernel,
            out_shape=slab,
            in_specs=vmem(4),
            out_specs=vmem(1)[0],
            cost_estimate=pl.CostEstimate(
                flops=12 * width * width * slab_len, bytes_accessed=12 * width * slab_len, transcendentals=0
            ),
        )(current_block, previous_block, previous_coupling, diag)

    with jax.named_scope("plan"):
        targets = row_devs * slab_tiles
        places = -(-(slots + targets) // LANES) * LANES
        plan = pl.pallas_call(
            functools.partial(plan_kernel, row_devs, col_devs, slab_tiles),
            out_shape=jax.ShapeDtypeStruct((8, places), jnp.int32),
            in_specs=smem(2) + vmem(2),
            out_specs=vmem(1)[0],
            cost_estimate=pl.CostEstimate(flops=4 * slots * slots * targets, bytes_accessed=8192, transcendentals=0),
        )(place, tile_counts, tile_rows.reshape(1, slots), tile_cols.reshape(1, slots))

    with jax.named_scope("tiles"):
        outs = pl.pallas_call(
            functools.partial(tiles_kernel, row_devs, col_devs),
            out_shape=[slab] + [jax.ShapeDtypeStruct((width, slab_len), bf16)] * (row_devs - 1),
            in_specs=smem(2) + [pl.BlockSpec(memory_space=pl.ANY)] * col_devs + vmem(1),
            out_specs=vmem(row_devs),
            scratch_shapes=[
                pltpu.VMEM((col_devs + 1, width, slab_len), bf16),
                pltpu.VMEM((targets + 1, width, tile_len), f32),
                pltpu.SemaphoreType.DMA((col_devs,)),
            ],
            compiler_params=pltpu.CompilerParams(vmem_limit_bytes=32 * MIB),
            cost_estimate=pl.CostEstimate(
                flops=2 * slots * width * tile_len * tile_len,
                bytes_accessed=2 * slots * tile_len * tile_len,
                transcendentals=0,
            ),
        )(place, plan, *panels, tile_values)

    with jax.named_scope("scatter"):
        received = [swap(outs[m], "row", m) for m in range(1, row_devs)]

    devices = row_devs * col_devs
    both = ("row", "col")
    basis_rows = (stored_count + 1) * width
    padded = (width, -(-basis_rows // LANES) * LANES)
    with jax.named_scope("coefficients"):
        recurrence, partial = pl.pallas_call(
            functools.partial(coefficient_kernel, cells, row_devs),
            out_shape=[slab, jax.ShapeDtypeStruct((devices, 8, LANES), f32)],
            in_specs=vmem(row_devs + 4),
            out_specs=vmem(2),
            compiler_params=pltpu.CompilerParams(vmem_limit_bytes=24 * MIB),
        )(base, outs[0], *received, mass, current_block, stored)
        piece = jnp.sum(lax.all_to_all(partial, both, 0, 0), axis=0)
        pieces = lax.all_to_all(jnp.broadcast_to(piece, partial.shape), both, 0, 0)

    with jax.named_scope("residual"):
        residual_block, coef, gram = pl.pallas_call(
            functools.partial(residual_kernel, cells),
            out_shape=[
                slab,
                jax.ShapeDtypeStruct((width, basis_rows), f32),
                jax.ShapeDtypeStruct((width // 2, LANES), f32),
            ],
            in_specs=vmem(5),
            out_specs=vmem(3),
            scratch_shapes=[pltpu.VMEM(padded, f32)],
            compiler_params=pltpu.CompilerParams(vmem_limit_bytes=24 * MIB),
        )(pieces, recurrence, mass, current_block, stored)
        coefficients = coef.T.reshape(stored_count + 1, width, width)

    with jax.named_scope("gram"):
        grams = jnp.broadcast_to(gram, (devices,) + gram.shape)
        gram = jnp.sum(lax.all_to_all(grams, both, 0, 0), axis=0)
        gram = jnp.concatenate(
            [gram[:, :width], gram[:, LANES // 2 : LANES // 2 + width]], axis=0
        )
    return (residual_block, coefficients, gram)


def solution(mesh):
    return jax.shard_map(
        local,
        mesh=mesh,
        in_specs=(
            P(None, ("row", "col")),
            P(None, ("row", "col")),
            P(),
            P(None, None, ("row", "col")),
            P(("row", "col")),
            P(("row", "col")),
            P(("row", "col"), None, None),
            P(("row", "col")),
            P(("row", "col")),
            P(("row", "col")),
        ),
        out_specs=(P(None, ("row", "col")), P(), P()),
        check_vma=False,
    )
```

```python
import functools

import jax
import jax.numpy as jnp
from jax import lax
from jax.experimental import pallas as pl
from jax.experimental.pallas import tpu as pltpu
from jax.sharding import PartitionSpec as P

LANES = 128
CHUNK = 32
UNROLL = 8
NT = (((1,), (1,)), ((), ()))
MIB = 1 << 20


def swap(value, axis, mask):
    count = lax.axis_size(axis)
    return lax.ppermute(value, axis, [(i, i ^ mask) for i in range(count)])


def spread(value, axis):
    copies = jnp.broadcast_to(value, (lax.axis_size(axis),) + value.shape)
    return lax.all_to_all(copies, axis, 0, 0)


def total(value, axis):
    return jnp.sum(spread(value, axis), axis=0)


def split(value):
    high = value.astype(jnp.bfloat16)
    low = (value - high.astype(jnp.float32)).astype(jnp.bfloat16)
    return high, low


def mm(a, b, dims=(((1,), (0,)), ((), ()))):
    return lax.dot_general(a, b, dims, preferred_element_type=jnp.float32)


def dot_split(a, b, dims=(((1,), (0,)), ((), ()))):
    rows = a.shape[0]
    a_high, a_low = split(a)
    b_high, b_low = split(b)
    both = mm(jnp.concatenate([a_high, a_low], axis=0), b_high, dims)
    return both[:rows] + both[rows:] + mm(a_high, b_low, dims)


def blocks(shape):
    return [(q, k) for q in range(0, shape[0], 8) for k in range(0, shape[1], LANES)]


def start_kernel(current, previous, coupling, diag, out):
    out[...] = diag[...] * current[...] - jnp.dot(
        coupling[...],
        previous[...],
        precision=lax.Precision.HIGHEST,
        preferred_element_type=jnp.float32,
    )


def plan_kernel(row_devs, col_devs, slab_tiles, place, counts, rows, cols, tiles, out, held, sem):
    chunks = (counts[0] + CHUNK - 1) // CHUNK

    def tile_copy(k):
        window = pl.ds(k * CHUNK, CHUNK)
        return pltpu.make_async_copy(tiles.at[window], held.at[window], sem.at[k])

    @pl.loop(0, chunks)
    def _(k):
        tile_copy(k).start()

    f32, bf16, i32 = jnp.float32, jnp.bfloat16, jnp.int32
    slots, places = rows.shape[1], out.shape[1]
    targets = row_devs * slab_tiles

    def iota(shape, dim):
        return lax.broadcasted_iota(i32, shape, dim)

    slot = iota((1, slots), 1)
    occupied = slot < counts[0]
    row = jnp.where(occupied, rows[...], -1)
    member = (iota((targets, slots), 0) == row).astype(f32)
    member_bf = member.astype(bf16)
    earlier = (iota((slots, slots), 0) < iota((slots, slots), 1)).astype(f32).astype(bf16)
    rank = jnp.sum(member * mm(member_bf, earlier), axis=0, keepdims=True)
    sizes = mm(jnp.ones((8, slots), bf16), member_bf, NT)[:1]
    sizes = 2.0 * jnp.floor(0.5 * (sizes + 1.0))
    before = (iota((targets, targets), 1) < iota((targets, targets), 0)).astype(f32)
    begin = jnp.sum(before * sizes, axis=1, keepdims=True)
    total = jnp.sum(sizes, axis=1, keepdims=True)
    position = jnp.sum(member * begin, axis=0, keepdims=True) + rank
    position = jnp.where(occupied, position.astype(i32), -1)
    chosen = (iota((places, slots), 0) == position).astype(f32).astype(bf16)
    slot_f = slot.astype(f32)
    slot_high = jnp.floor(slot_f * (1.0 / 16.0))
    facts = [slot_high, slot_f - 16.0 * slot_high, cols[...].astype(f32), row.astype(f32), jnp.ones((1, slots), f32)]
    facts = jnp.concatenate(facts + [jnp.zeros((3, slots), f32)], axis=0).astype(bf16)
    found = mm(facts, chosen, NT)
    valid = found[4:5] > 0.5
    source = jnp.floor(found[2:3] * (1.0 / slab_tiles))
    tile = found[2:3] - slab_tiles * source
    out[0:1] = (16.0 * found[0:1] + found[1:2]).astype(i32)
    out[1:2] = jnp.where(valid, source.astype(i32) ^ place[1], col_devs)
    out[2:3] = tile.astype(i32)
    out[3:4] = jnp.where(valid, found[3:4].astype(i32), targets)
    out[4:8] = jnp.broadcast_to(total.astype(i32), (4, places))

    @pl.loop(0, chunks)
    def _(k):
        tile_copy(k).wait()


def tiles_kernel(row_devs, col_devs, place, plan, *refs):
    panels = refs[:col_devs]
    tiles = refs[col_devs]
    own = refs[col_devs + 1]
    sends = refs[col_devs + 2 : col_devs + 1 + row_devs]
    panel_buf, acc, panel_sem = refs[col_devs + 1 + row_devs :]
    slab_tiles = own.shape[1] // LANES
    row = place[0]

    panel_copies = [
        pltpu.make_async_copy(panels[m], panel_buf.at[m], panel_sem.at[m]) for m in range(col_devs)
    ]
    for copy in panel_copies:
        copy.start()
    panel_buf[col_devs, :, :LANES] = jnp.zeros((own.shape[0], LANES), jnp.bfloat16)
    acc[...] = jnp.zeros_like(acc)
    for copy in panel_copies:
        copy.wait()

    def panel(p):
        where = pl.multiple_of(plan[2, p] * LANES, LANES)
        return panel_buf[plan[1, p], :, pl.ds(where, LANES)]

    @pl.loop(0, (plan[4, 0] + 2 * UNROLL - 1) // (2 * UNROLL))
    def _(g):
        for u in range(UNROLL):
            p = g * 2 * UNROLL + 2 * u
            left = jnp.concatenate([tiles[plan[0, p]], tiles[plan[0, p + 1]]], axis=1)
            right = jnp.concatenate([panel(p), panel(p + 1)], axis=1)
            acc[plan[3, p]] += mm(left, right, NT)

    def turned(t):
        value = acc[t]
        width = value.shape[1]
        spare = jnp.zeros((value.shape[0], LANES - width), jnp.float32)
        return jnp.concatenate([value, spare], axis=1).T[:width]

    for s in range(slab_tiles):
        window = pl.ds(s * LANES, LANES)
        own[:, window] = turned(row * slab_tiles + s)
        for m in range(1, row_devs):
            sends[m - 1][:, window] = turned((row ^ m) * slab_tiles + s).astype(jnp.bfloat16)


def coefficient_kernel(cells, pieces, *refs):
    base, own = refs[0], refs[1]
    received = refs[2 : 1 + pieces]
    mass, current, stored, recurrence, out = refs[1 + pieces :]
    total = base[...] + own[...]
    for ref in received:
        total = total + ref[...].astype(jnp.float32)
    recurrence[...] = total
    weighted = total * (mass[...] * (1.0 / cells))
    basis = jnp.concatenate([current[...], stored[...]], axis=0)
    coef = dot_split(weighted, basis, NT)
    width = coef.shape[0]
    groups = out.shape[0] // width
    spare = -coef.shape[1] % LANES
    coef = jnp.concatenate([coef, jnp.zeros((coef.shape[0], spare), jnp.float32)], axis=1)
    out[...] = jnp.zeros_like(out)
    for p, (q, k) in enumerate(blocks(coef.shape)):
        out[p // out.shape[1], p % out.shape[1]] = coef[q : q + 8, k : k + LANES]


def residual_kernel(cells, pieces, recurrence, mass, current, stored, residual, coef_out, gram, packed):
    width = recurrence.shape[0]
    for p, (q, k) in enumerate(blocks(packed.shape)):
        packed[q : q + 8, k : k + LANES] = pieces[p]
    coef = packed[...]
    basis = jnp.concatenate([current[...], stored[...]], axis=0)
    coef = coef[:, : basis.shape[0]]
    coef_out[...] = coef
    value = recurrence[...] - dot_split(coef, basis)
    residual[...] = value
    local = dot_split(value * (mass[...] * (1.0 / cells)), value, NT)
    half = width // 2
    gram[...] = jnp.zeros_like(gram)
    gram[:, :width] = local[:half]
    gram[:, LANES // 2 : LANES // 2 + width] = local[half:]


def after_kernel(value, earlier, out):
    pass


def after(value, earlier):
    anywhere = pl.BlockSpec(memory_space=pl.ANY)
    return pl.pallas_call(
        after_kernel,
        out_shape=jax.ShapeDtypeStruct(value.shape, value.dtype),
        in_specs=[anywhere, anywhere],
        out_specs=anywhere,
        input_output_aliases={0: 0},
    )(value, earlier)


def vmem(count):
    return [pl.BlockSpec(memory_space=pltpu.VMEM)] * count


def smem(count):
    return [pl.BlockSpec(memory_space=pltpu.SMEM)] * count


def local(
    current_block,
    previous_block,
    previous_coupling,
    stored_blocks,
    stiffness_diag,
    lumped_mass,
    tile_values,
    tile_rows,
    tile_cols,
    tile_counts,
):
    row_devs = lax.axis_size("row")
    col_devs = lax.axis_size("col")
    width, slab_len = current_block.shape
    stored_count = stored_blocks.shape[0]
    slots, tile_len, _ = tile_values.shape
    slab_tiles = slab_len // tile_len
    cells = slab_len * row_devs * col_devs
    f32, bf16 = jnp.float32, jnp.bfloat16
    place = jnp.stack([lax.axis_index("row"), lax.axis_index("col")]).astype(jnp.int32)
    stored = stored_blocks.reshape(stored_count * width, slab_len)
    mass = lumped_mass.reshape(1, slab_len)
    diag = stiffness_diag.reshape(1, slab_len)
    slab = jax.ShapeDtypeStruct((width, slab_len), f32)

    with jax.named_scope("gather"):
        rounded = current_block.astype(bf16)
        panels = [rounded] + [None] * (col_devs - 1)
        for m in range(col_devs - 2, 0, -2):
            panels[m] = swap(rounded, "col", m)

    with jax.named_scope("plan"):
        targets = row_devs * slab_tiles
        places = -(-(slots + targets) // LANES) * LANES
        plan, held = pl.pallas_call(
            functools.partial(plan_kernel, row_devs, col_devs, slab_tiles),
            out_shape=[jax.ShapeDtypeStruct((8, places), jnp.int32), pltpu.VMEM(tile_values.shape, bf16)],
            in_specs=smem(2) + vmem(2) + [pl.BlockSpec(memory_space=pltpu.HBM)],
            out_specs=vmem(2),
            scratch_shapes=[pltpu.SemaphoreType.DMA((slots // CHUNK,))],
            compiler_params=pltpu.CompilerParams(vmem_limit_bytes=8 * MIB),
            cost_estimate=pl.CostEstimate(flops=4 * slots * slots * targets, bytes_accessed=8192, transcendentals=0),
        )(place, tile_counts, tile_rows.reshape(1, slots), tile_cols.reshape(1, slots), pltpu.with_memory_space_constraint(tile_values, pltpu.HBM))

    with jax.named_scope("gather"):
        panels[col_devs - 2] = after(panels[col_devs - 2], plan)
        for m in range(col_devs - 2, -2, -2):
            panels[m + 1] = swap(panels[m], "col", 1)

    with jax.named_scope("start"):
        base = pl.pallas_call(
            start_kernel,
            out_shape=slab,
            in_specs=vmem(4),
            out_specs=vmem(1)[0],
            cost_estimate=pl.CostEstimate(
                flops=12 * width * width * slab_len, bytes_accessed=12 * width * slab_len, transcendentals=0
            ),
        )(current_block, previous_block, previous_coupling, diag)

    with jax.named_scope("tiles"):
        outs = pl.pallas_call(
            functools.partial(tiles_kernel, row_devs, col_devs),
            out_shape=[slab] + [jax.ShapeDtypeStruct((width, slab_len), bf16)] * (row_devs - 1),
            in_specs=smem(2) + [pl.BlockSpec(memory_space=pl.ANY)] * col_devs + vmem(1),
            out_specs=vmem(row_devs),
            scratch_shapes=[
                pltpu.VMEM((col_devs + 1, width, slab_len), bf16),
                pltpu.VMEM((targets + 1, tile_len, width), f32),
                pltpu.SemaphoreType.DMA((col_devs,)),
            ],
            compiler_params=pltpu.CompilerParams(vmem_limit_bytes=12 * MIB),
            cost_estimate=pl.CostEstimate(
                flops=2 * slots * width * tile_len * tile_len,
                bytes_accessed=2 * slots * tile_len * tile_len,
                transcendentals=0,
            ),
        )(place, plan, *panels, held)

    with jax.named_scope("scatter"):
        received = [swap(outs[m], "row", m) for m in range(1, row_devs)]

    basis_rows = (stored_count + 1) * width
    padded = (width, -(-basis_rows // LANES) * LANES)
    share = -(-len(blocks(padded)) // col_devs)
    with jax.named_scope("coefficients"):
        recurrence, partial = pl.pallas_call(
            functools.partial(coefficient_kernel, cells, row_devs),
            out_shape=[slab, jax.ShapeDtypeStruct((col_devs, share, 8, LANES), f32)],
            in_specs=vmem(row_devs + 4),
            out_specs=vmem(2),
            compiler_params=pltpu.CompilerParams(vmem_limit_bytes=24 * MIB),
        )(base, outs[0], *received, mass, current_block, stored)
        piece = jnp.sum(lax.all_to_all(partial, "col", 0, 0), axis=0)
        piece = total(piece, "row")
        pieces = spread(piece, "col").reshape(-1, 8, LANES)

    with jax.named_scope("residual"):
        residual_block, coef, gram = pl.pallas_call(
            functools.partial(residual_kernel, cells),
            out_shape=[
                slab,
                jax.ShapeDtypeStruct((width, basis_rows), f32),
                jax.ShapeDtypeStruct((width // 2, LANES), f32),
            ],
            in_specs=vmem(5),
            out_specs=vmem(3),
            scratch_shapes=[pltpu.VMEM(padded, f32)],
            compiler_params=pltpu.CompilerParams(vmem_limit_bytes=24 * MIB),
        )(pieces, recurrence, mass, current_block, stored)
        coefficients = coef.T.reshape(stored_count + 1, width, width)

    with jax.named_scope("gram"):
        gram = total(total(gram, "col"), "row")
        gram = jnp.concatenate(
            [gram[:, :width], gram[:, LANES // 2 : LANES // 2 + width]], axis=0
        )
    return (residual_block, coefficients, gram)


def solution(mesh):
    return jax.shard_map(
        local,
        mesh=mesh,
        in_specs=(
            P(None, ("row", "col")),
            P(None, ("row", "col")),
            P(),
            P(None, None, ("row", "col")),
            P(("row", "col")),
            P(("row", "col")),
            P(("row", "col"), None, None),
            P(("row", "col")),
            P(("row", "col")),
            P(("row", "col")),
        ),
        out_specs=(P(None, ("row", "col")), P(), P()),
        check_vma=False,
    )
```

```python
import functools

import jax
import jax.numpy as jnp
from jax import lax
from jax.experimental import pallas as pl
from jax.experimental.pallas import tpu as pltpu
from jax.sharding import PartitionSpec as P

LANES = 128
CHUNK = 32
UNROLL = 4
NT = (((1,), (1,)), ((), ()))
MIB = 1 << 20


def swap(value, axis, mask):
    count = lax.axis_size(axis)
    return lax.ppermute(value, axis, [(i, i ^ mask) for i in range(count)])


def bits(axis):
    return [1 << i for i in range(lax.axis_size(axis).bit_length() - 1)]


def total(value, axis, masks):
    for m in masks:
        value = value + swap(value, axis, m)
    return value


def split(value):
    high = value.astype(jnp.bfloat16)
    low = (value - high.astype(jnp.float32)).astype(jnp.bfloat16)
    return high, low


def mm(a, b, dims=(((1,), (0,)), ((), ()))):
    return lax.dot_general(a, b, dims, preferred_element_type=jnp.float32)


def dot_split(a, b, dims=(((1,), (0,)), ((), ()))):
    rows = a.shape[0]
    a_high, a_low = split(a)
    b_high, b_low = split(b)
    both = mm(jnp.concatenate([a_high, a_low], axis=0), b_high, dims)
    return both[:rows] + both[rows:] + mm(a_high, b_low, dims)


def blocks(shape):
    return [(q, k) for q in range(0, shape[0], 8) for k in range(0, shape[1], LANES)]


def plan_kernel(row_devs, col_devs, slab_tiles, place, counts, rows, cols, tiles, out, held, sem):
    chunks = (counts[0] + CHUNK - 1) // CHUNK

    def tile_copy(k):
        window = pl.ds(k * CHUNK, CHUNK)
        return pltpu.make_async_copy(tiles.at[window], held.at[window], sem.at[k])

    @pl.loop(0, chunks)
    def _(k):
        tile_copy(k).start()

    f32, bf16, i32 = jnp.float32, jnp.bfloat16, jnp.int32
    slots, places = rows.shape[1], out.shape[1]
    targets = row_devs * slab_tiles
    bins = 2 * targets

    def iota(shape, dim):
        return lax.broadcasted_iota(i32, shape, dim)

    slot = iota((1, slots), 1)
    occupied = slot < counts[0]
    row = rows[...]
    row_owner = jnp.floor(row.astype(f32) * (1.0 / slab_tiles)).astype(i32)
    col_f = cols[...].astype(f32)
    source_f = jnp.floor(col_f * (1.0 / slab_tiles))
    source = source_f.astype(i32) ^ place[1]
    tile_f = col_f - slab_tiles * source_f
    far = row_devs - 1 - (row_owner ^ place[0])
    late_bin = targets + far * slab_tiles + row - row_owner * slab_tiles
    bin_of = jnp.where(occupied, jnp.where(source < 2, row, late_bin), -1)
    member = (iota((bins, slots), 0) == bin_of).astype(f32)
    member_bf = member.astype(bf16)
    earlier = (iota((slots, slots), 0) < iota((slots, slots), 1)).astype(f32).astype(bf16)
    rank = jnp.sum(member * mm(member_bf, earlier), axis=0, keepdims=True)
    sizes = mm(jnp.ones((8, slots), bf16), member_bf, NT)[:1]
    sizes = 2.0 * jnp.floor(0.5 * (sizes + 1.0))
    before = (iota((bins, bins), 1) < iota((bins, bins), 0)).astype(f32)
    begin = jnp.sum(before * sizes, axis=1, keepdims=True)
    position = jnp.sum(member * begin, axis=0, keepdims=True) + rank
    position = jnp.where(occupied, position.astype(i32), -1)
    chosen = (iota((places, slots), 0) == position).astype(f32).astype(bf16)
    slot_f = slot.astype(f32)
    slot_high = jnp.floor(slot_f * (1.0 / 16.0))
    facts = [slot_high, slot_f - 16.0 * slot_high, source.astype(f32), tile_f, row.astype(f32), jnp.ones((1, slots), f32)]
    facts = jnp.concatenate(facts + [jnp.zeros((2, slots), f32)], axis=0).astype(bf16)
    found = mm(facts, chosen, NT)
    valid = found[5:6] > 0.5
    out[0:1] = (16.0 * found[0:1] + found[1:2]).astype(i32)
    out[1:2] = jnp.where(valid, found[2:3].astype(i32), col_devs)
    out[2:3] = found[3:4].astype(i32)
    out[3:4] = found[4:5].astype(i32)
    out[4:8] = jnp.zeros((4, places), i32)
    phases = out.shape[0] - 8
    phase = iota((phases, bins), 0)
    edge = jnp.where(phase > 0, targets + (phase - 1) * slab_tiles, 0)
    edges = jnp.sum((iota((phases, bins), 1) < edge).astype(f32) * sizes, axis=1, keepdims=True)
    out[8:] = jnp.broadcast_to(edges.astype(i32), (phases, places))

    @pl.loop(0, chunks)
    def _(k):
        tile_copy(k).wait()


def add_products(plan, phase, first_row, spare_row, tiles, panel_buf, acc):
    begin, end = plan[8 + phase, 0], plan[9 + phase, 0]

    def panel(p):
        where = pl.multiple_of(plan[2, p] * LANES, LANES)
        return panel_buf[plan[1, p], :, pl.ds(where, LANES)]

    @pl.loop(0, (end - begin + 2 * UNROLL - 1) // (2 * UNROLL))
    def _(g):
        first = begin + g * 2 * UNROLL
        parts = []
        for u in range(UNROLL):
            p = first + 2 * u
            left = jnp.concatenate([panel(p), panel(p + 1)], axis=1)
            right = jnp.concatenate([tiles[plan[0, p]], tiles[plan[0, p + 1]]], axis=1)
            parts.append(mm(left, right, NT))
        for u in range(UNROLL):
            p = first + 2 * u
            a = jnp.where(p < end, plan[3, p] - first_row, spare_row)
            acc[a] += parts[u]


def load_panels(panels, panel_buf, sem):
    copies = [pltpu.make_async_copy(ref, panel_buf.at[m], sem.at[m]) for m, ref in enumerate(panels)]
    for copy in copies:
        copy.start()
    zero = panel_buf.shape[0] - 1
    panel_buf[zero, :, :LANES] = jnp.zeros((panel_buf.shape[1], LANES), jnp.bfloat16)
    return copies


def early_kernel(plan, own_panel, near_panel, tiles, acc, panel_buf, sem):
    copies = load_panels((own_panel, near_panel), panel_buf, sem)
    acc[...] = jnp.zeros_like(acc)
    for copy in copies:
        copy.wait()
    add_products(plan, 0, 0, acc.shape[0] - 1, tiles, panel_buf, acc)


def first_late_kernel(mask, phase, place, plan, *refs):
    panels = refs[:-6]
    tiles, early, send, panel_buf, acc, sem = refs[-6:]
    copies = load_panels(panels, panel_buf, sem)
    late_part(mask, phase, place, plan, tiles, early, panel_buf, acc, copies)
    put(send, acc)


def late_kernel(masks, place, plan, panel_buf, tiles, early, *refs):
    acc = refs[-1]
    for phase, (mask, send) in enumerate(zip(masks, refs), 2):
        late_part(mask, phase, place, plan, tiles, early, panel_buf, acc, ())
        put(send, acc)


def own_kernel(phase, place, plan, panel_buf, tiles, early, received, current, previous, coupling, diag, base, acc):
    late_part(0, phase, place, plan, tiles, early, panel_buf, acc, ())
    put(base, acc)
    base[...] += received[...].astype(jnp.float32) + diag[...] * current[...] - jnp.dot(
        coupling[...],
        previous[...],
        precision=lax.Precision.HIGHEST,
        preferred_element_type=jnp.float32,
    )


def late_part(mask, phase, place, plan, tiles, early, panel_buf, acc, copies):
    slab_tiles = acc.shape[0] - 1
    first_row = (place[0] ^ mask) * slab_tiles
    for s in range(slab_tiles):
        acc[s] = early[first_row + s]
    for copy in copies:
        copy.wait()
    add_products(plan, phase, first_row, slab_tiles, tiles, panel_buf, acc)


def put(out, acc):
    for s in range(acc.shape[0] - 1):
        out[:, s * LANES : (s + 1) * LANES] = acc[s].astype(out.dtype)


def coefficient_kernel(cells, received_count, place, base, *refs):
    received = refs[:received_count]
    mass, current, stored, recurrence, keep, give, halves = refs[received_count:]
    total = base[...]
    for ref in received:
        total = total + ref[...].astype(jnp.float32)
    recurrence[...] = total
    weighted = total * (mass[...] * (1.0 / cells))
    basis = jnp.concatenate([current[...], stored[...]], axis=0)
    coef = dot_split(weighted, basis, NT)
    spare = -coef.shape[1] % LANES
    coef = jnp.concatenate([coef, jnp.zeros((coef.shape[0], spare), jnp.float32)], axis=1)
    halves[...] = jnp.zeros_like(halves)
    for p, (q, k) in enumerate(blocks(coef.shape)):
        halves[p // halves.shape[1], p % halves.shape[1]] = coef[q : q + 8, k : k + LANES]
    core = place[1] & 1
    keep[...] = halves[core]
    give[...] = halves[1 - core]


def residual_kernel(
    cells, place, mine, other, recurrence, mass, current, stored, residual, coef_out, gram, halves, packed
):
    width = recurrence.shape[0]
    core = place[1] & 1
    halves[core] = mine[...]
    halves[1 - core] = other[...]
    for p, (q, k) in enumerate(blocks(packed.shape)):
        packed[q : q + 8, k : k + LANES] = halves[p // halves.shape[1], p % halves.shape[1]]
    coef = packed[...]
    basis = jnp.concatenate([current[...], stored[...]], axis=0)
    coef = coef[:, : basis.shape[0]]
    coef_out[...] = coef
    value = recurrence[...] - dot_split(coef, basis)
    residual[...] = value
    local = dot_split(value * (mass[...] * (1.0 / cells)), value, NT)
    half = width // 2
    gram[...] = jnp.zeros_like(gram)
    gram[:, :width] = local[:half]
    gram[:, LANES // 2 : LANES // 2 + width] = local[half:]


def after_kernel(value, earlier, out):
    pass


def after(value, earlier):
    anywhere = pl.BlockSpec(memory_space=pl.ANY)
    return pl.pallas_call(
        after_kernel,
        out_shape=jax.ShapeDtypeStruct(value.shape, value.dtype),
        in_specs=[anywhere, anywhere],
        out_specs=anywhere,
        input_output_aliases={0: 0},
        compiler_params=limit(1),
    )(value, earlier)


def limit(mib):
    return pltpu.CompilerParams(vmem_limit_bytes=mib * MIB)


def vmem(count):
    return [pl.BlockSpec(memory_space=pltpu.VMEM)] * count


def smem(count):
    return [pl.BlockSpec(memory_space=pltpu.SMEM)] * count


def local(
    current_block,
    previous_block,
    previous_coupling,
    stored_blocks,
    stiffness_diag,
    lumped_mass,
    tile_values,
    tile_rows,
    tile_cols,
    tile_counts,
):
    row_devs = lax.axis_size("row")
    col_devs = lax.axis_size("col")
    width, slab_len = current_block.shape
    stored_count = stored_blocks.shape[0]
    slots, tile_len, _ = tile_values.shape
    slab_tiles = slab_len // tile_len
    cells = slab_len * row_devs * col_devs
    f32, bf16 = jnp.float32, jnp.bfloat16
    place = jnp.stack([lax.axis_index("row"), lax.axis_index("col")]).astype(jnp.int32)
    stored = stored_blocks.reshape(stored_count * width, slab_len)
    mass = lumped_mass.reshape(1, slab_len)
    diag = stiffness_diag.reshape(1, slab_len)
    slab = jax.ShapeDtypeStruct((width, slab_len), f32)

    targets = row_devs * slab_tiles
    anywhere = [pl.BlockSpec(memory_space=pl.ANY)]
    panel_shape = (col_devs + 1, width, slab_len)
    early_shape = (targets + 1, width, tile_len)
    part_acc = pltpu.VMEM((slab_tiles + 1, width, tile_len), f32)

    def cost(flops):
        return pl.CostEstimate(flops=flops, bytes_accessed=flops // width, transcendentals=0)

    with jax.named_scope("gather"):
        rounded = current_block.astype(bf16)
        panels = [rounded] + [None] * (col_devs - 1)
        for m in range(col_devs - 2, 0, -2):
            panels[m] = swap(rounded, "col", m)
        panels[1] = swap(rounded, "col", 1)

    with jax.named_scope("plan"):
        places = -(-(slots + 2 * targets + 2 * UNROLL) // LANES) * LANES
        plan_rows = 8 + -(-(row_devs + 2) // 8) * 8
        plan, held = pl.pallas_call(
            functools.partial(plan_kernel, row_devs, col_devs, slab_tiles),
            out_shape=[jax.ShapeDtypeStruct((plan_rows, places), jnp.int32), pltpu.VMEM(tile_values.shape, bf16)],
            in_specs=smem(2) + vmem(2) + [pl.BlockSpec(memory_space=pltpu.HBM)],
            out_specs=vmem(2),
            scratch_shapes=[pltpu.SemaphoreType.DMA((slots // CHUNK,))],
            compiler_params=limit(8),
            cost_estimate=cost(2 * slots * width * tile_len * tile_len),
        )(
            place,
            tile_counts,
            tile_rows.reshape(1, slots),
            tile_cols.reshape(1, slots),
            pltpu.with_memory_space_constraint(tile_values, pltpu.HBM),
        )

    with jax.named_scope("early"):
        early = pl.pallas_call(
            early_kernel,
            out_shape=pltpu.VMEM(early_shape, f32),
            in_specs=smem(1) + anywhere * 2 + vmem(1),
            out_specs=vmem(1)[0],
            scratch_shapes=[pltpu.VMEM(panel_shape, bf16), pltpu.SemaphoreType.DMA((2,))],
            compiler_params=limit(8),
            cost_estimate=cost(slots * width * tile_len * tile_len // 2),
        )(plan, panels[0], panels[1], held)

    with jax.named_scope("gather"):
        for m in range(col_devs - 2, 0, -2):
            panels[m] = after(panels[m], early)
            panels[m + 1] = swap(panels[m], "col", 1)

    with jax.named_scope("late"):
        masks = list(range(row_devs - 1, 0, -1))
        part = jax.ShapeDtypeStruct((width, slab_len), bf16)
        first, gathered = pl.pallas_call(
            functools.partial(first_late_kernel, masks[0], 1),
            out_shape=[part, pltpu.VMEM(panel_shape, bf16)],
            in_specs=smem(2) + anywhere * col_devs + vmem(2),
            out_specs=vmem(2),
            scratch_shapes=[part_acc, pltpu.SemaphoreType.DMA((col_devs,))],
            compiler_params=limit(8),
            cost_estimate=cost(width),
        )(place, plan, *panels, held, early)
        first = swap(first, "row", masks[0])
        others = pl.pallas_call(
            functools.partial(late_kernel, masks[1:]),
            out_shape=[part] * len(masks[1:]),
            in_specs=smem(2) + vmem(3),
            out_specs=vmem(len(masks[1:])),
            scratch_shapes=[part_acc],
            compiler_params=limit(8),
            cost_estimate=cost(width),
        )(place, plan, gathered, held, early)
        received = [swap(other, "row", m) for m, other in zip(masks[1:], others)]
        base = pl.pallas_call(
            functools.partial(own_kernel, row_devs),
            out_shape=slab,
            in_specs=smem(2) + vmem(8),
            out_specs=vmem(1)[0],
            scratch_shapes=[part_acc],
            compiler_params=limit(8),
            cost_estimate=cost(width),
        )(place, plan, gathered, held, early, first, current_block, previous_block, previous_coupling, diag)

    basis_rows = (stored_count + 1) * width
    padded = (width, -(-basis_rows // LANES) * LANES)
    half = (-(-len(blocks(padded)) // 2), 8, LANES)
    with jax.named_scope("coefficients"):
        recurrence, keep, give = pl.pallas_call(
            functools.partial(coefficient_kernel, cells, len(received)),
            out_shape=[slab] + [jax.ShapeDtypeStruct(half, f32)] * 2,
            in_specs=smem(1) + vmem(len(received) + 4),
            out_specs=vmem(3),
            scratch_shapes=[pltpu.VMEM((2,) + half, f32)],
            compiler_params=limit(24),
        )(place, base, *received, mass, current_block, stored)
        mine = keep + swap(give, "col", 1)
        mine = total(total(mine, "col", bits("col")[1:]), "row", bits("row"))
        other = swap(mine, "col", 1)

    with jax.named_scope("residual"):
        residual_block, coef, gram = pl.pallas_call(
            functools.partial(residual_kernel, cells),
            out_shape=[
                slab,
                jax.ShapeDtypeStruct((width, basis_rows), f32),
                jax.ShapeDtypeStruct((width // 2, LANES), f32),
            ],
            in_specs=smem(1) + vmem(6),
            out_specs=vmem(3),
            scratch_shapes=[pltpu.VMEM((2,) + half, f32), pltpu.VMEM(padded, f32)],
            compiler_params=limit(24),
        )(place, mine, other, recurrence, mass, current_block, stored)
        coefficients = coef.T.reshape(stored_count + 1, width, width)

    with jax.named_scope("gram"):
        gram = total(total(gram, "col", bits("col")), "row", bits("row"))
        gram = jnp.concatenate(
            [gram[:, :width], gram[:, LANES // 2 : LANES // 2 + width]], axis=0
        )
    return (residual_block, coefficients, gram)


def solution(mesh):
    return jax.shard_map(
        local,
        mesh=mesh,
        in_specs=(
            P(None, ("row", "col")),
            P(None, ("row", "col")),
            P(),
            P(None, None, ("row", "col")),
            P(("row", "col")),
            P(("row", "col")),
            P(("row", "col"), None, None),
            P(("row", "col")),
            P(("row", "col")),
            P(("row", "col")),
        ),
        out_specs=(P(None, ("row", "col")), P(), P()),
        check_vma=False,
    )
```

```python
import functools

import jax
import jax.numpy as jnp
from jax import lax
from jax.experimental import pallas as pl
from jax.experimental.pallas import tpu as pltpu
from jax.sharding import PartitionSpec as P

LANES = 128
CHUNK = 32
GROUP = 4
UNROLL = 4
TILE_BIT, SOURCE_BIT, ROW_BIT = 10, 15, 20
NT = (((1,), (1,)), ((), ()))
MIB = 1 << 20


def swap(value, axis, mask):
    count = lax.axis_size(axis)
    return lax.ppermute(value, axis, [(i, i ^ mask) for i in range(count)])


def total(value, axis, step):
    values = [value] + [swap(value, axis, m) for m in range(step, lax.axis_size(axis), step)]
    while len(values) > 1:
        values = [values[i] + values[i + 1] for i in range(0, len(values), 2)]
    return values[0]


def split(value):
    high = value.astype(jnp.bfloat16)
    low = (value - high.astype(jnp.float32)).astype(jnp.bfloat16)
    return high, low


def mm(a, b, dims=(((1,), (0,)), ((), ()))):
    return lax.dot_general(a, b, dims, preferred_element_type=jnp.float32)


def dot_split(a, b, dims=(((1,), (0,)), ((), ()))):
    rows = a.shape[0]
    a_high, a_low = split(a)
    b_high, b_low = split(b)
    both = mm(jnp.concatenate([a_high, a_low], axis=0), b_high, dims)
    return both[:rows] + both[rows:] + mm(a_high, b_low, dims)


def blocks(shape):
    return [(q, k) for q in range(0, shape[0], 8) for k in range(0, shape[1], LANES)]


def plan_kernel(
    row_devs, col_devs, slab_tiles, place, counts, rows_hbm, cols_hbm, tiles, out, held, rows, cols, sem, list_sem
):
    chunks = (counts[0] + CHUNK - 1) // CHUNK
    row_copy = pltpu.make_async_copy(rows_hbm, rows, list_sem.at[0])
    col_copy = pltpu.make_async_copy(cols_hbm, cols, list_sem.at[1])
    row_copy.start()
    col_copy.start()

    def tile_copy(k):
        window = pl.ds(k * CHUNK, CHUNK)
        return pltpu.make_async_copy(tiles.at[window], held.at[window], sem.at[k])

    @pl.loop(0, chunks)
    def _(k):
        tile_copy(k).start()

    f32, bf16, i32 = jnp.float32, jnp.bfloat16, jnp.int32
    slots, places = rows.shape[1], out.shape[1] - LANES
    targets = row_devs * slab_tiles
    bins = 2 * targets

    def iota(shape, dim):
        return lax.broadcasted_iota(i32, shape, dim)

    slot = iota((1, slots), 1)
    occupied = slot < counts[0]
    earlier = (iota((slots, slots), 0) < iota((slots, slots), 1)).astype(f32).astype(bf16)
    row_copy.wait()
    col_copy.wait()
    row = rows[...]
    row_owner = jnp.floor(row.astype(f32) * (1.0 / slab_tiles)).astype(i32)
    col_f = cols[...].astype(f32)
    source_f = jnp.floor(col_f * (1.0 / slab_tiles))
    source = source_f.astype(i32) ^ place[1]
    tile_f = col_f - slab_tiles * source_f
    far = row_devs - 1 - (row_owner ^ place[0])
    late_bin = targets + far * slab_tiles + row - row_owner * slab_tiles
    bin_of = jnp.where(occupied, jnp.where(source < 2, row, late_bin), -1)
    member = (iota((bins, slots), 0) == bin_of).astype(f32)
    member_bf = member.astype(bf16)
    rank = jnp.sum(member * mm(member_bf, earlier), axis=0, keepdims=True)
    sizes = mm(jnp.ones((8, slots), bf16), member_bf, NT)
    sizes = GROUP * jnp.floor((sizes + (GROUP - 1.0)) * (1.0 / GROUP))
    before = (iota((bins, bins), 1) < iota((bins, bins), 0)).astype(f32)
    begin = jnp.sum(before * sizes[:1], axis=1, keepdims=True)
    position = jnp.sum(member * begin, axis=0, keepdims=True) + rank
    position = jnp.where(occupied, position.astype(i32), -1)
    chosen = (iota((places, slots), 0) == position).astype(f32).astype(bf16)
    slot_f = slot.astype(f32)
    slot_high = jnp.floor(slot_f * (1.0 / 16.0))
    facts = [slot_high, slot_f - 16.0 * slot_high, source.astype(f32), tile_f, row.astype(f32), jnp.ones((1, slots), f32)]
    facts = jnp.concatenate(facts + [jnp.zeros((2, slots), f32)], axis=0).astype(bf16)
    found = mm(facts, chosen, NT).astype(i32)
    source = jnp.where(found[5:6] > 0, found[2:3], col_devs)
    words = (found[4:5] << ROW_BIT) + (source << SOURCE_BIT) + (found[3:4] << TILE_BIT)
    out[:, :places] = words + (found[0:1] << 4) + found[1:2]
    phase = iota((bins, LANES), 1)
    edge = jnp.where(phase > 0, targets + (phase - 1) * slab_tiles, 0)
    inside = (iota((bins, LANES), 0) < edge).astype(f32).astype(bf16)
    out[:, places:] = mm(sizes.astype(bf16), inside)[:1].astype(i32)

    @pl.loop(0, chunks)
    def _(k):
        tile_copy(k).wait()


def field(word, low, high):
    return (word >> low) & ((1 << (high - low)) - 1)


def add_products(plan, phase, first_row, spare_row, tiles, panel_buf, acc):
    phases = plan.shape[1] - LANES
    begin, end = plan[0, phases + phase], plan[0, phases + phase + 1]

    def panel(word):
        where = pl.multiple_of(field(word, TILE_BIT, SOURCE_BIT) * LANES, LANES)
        return panel_buf[field(word, SOURCE_BIT, ROW_BIT), :, pl.ds(where, LANES)]

    @pl.loop(0, (end - begin + GROUP * UNROLL - 1) // (GROUP * UNROLL))
    def _(g):
        first = begin + g * GROUP * UNROLL
        parts = []
        for u in range(UNROLL):
            words = [plan[0, first + GROUP * u + i] for i in range(GROUP)]
            left = jnp.concatenate([panel(word) for word in words], axis=1)
            right = jnp.concatenate([tiles[field(word, 0, TILE_BIT)] for word in words], axis=1)
            parts.append(mm(left, right, NT))
        for u in range(UNROLL):
            p = first + GROUP * u
            a = jnp.where(p < end, (plan[0, p] >> ROW_BIT) - first_row, spare_row)
            acc[a] += parts[u]


def load_panels(panels, panel_buf, sem):
    copies = [pltpu.make_async_copy(ref, panel_buf.at[m], sem.at[m]) for m, ref in enumerate(panels)]
    for copy in copies:
        copy.start()
    zero = panel_buf.shape[0] - 1
    panel_buf[zero, :, :LANES] = jnp.zeros((panel_buf.shape[1], LANES), jnp.bfloat16)
    return copies


def early_kernel(plan, own_panel, near_panel, tiles, acc, panel_buf, sem):
    copies = load_panels((own_panel, near_panel), panel_buf, sem)
    acc[...] = jnp.zeros_like(acc)
    for copy in copies:
        copy.wait()
    add_products(plan, 0, 0, acc.shape[0] - 1, tiles, panel_buf, acc)


def first_late_kernel(mask, phase, place, plan, *refs):
    panels = refs[:-6]
    tiles, early, send, panel_buf, acc, sem = refs[-6:]
    copies = load_panels(panels, panel_buf, sem)
    late_part(mask, phase, place, plan, tiles, early, panel_buf, acc, copies)
    put(send, acc)


def late_kernel(masks, place, plan, panel_buf, tiles, early, *refs):
    acc = refs[-1]
    for phase, (mask, send) in enumerate(zip(masks, refs), 2):
        late_part(mask, phase, place, plan, tiles, early, panel_buf, acc, ())
        put(send, acc)


def own_kernel(phase, place, plan, panel_buf, tiles, early, received, current, previous, coupling, diag, base, acc):
    late_part(0, phase, place, plan, tiles, early, panel_buf, acc, ())
    put(base, acc)
    base[...] += received[...].astype(jnp.float32) + diag[...] * current[...] - jnp.dot(
        coupling[...],
        previous[...],
        precision=lax.Precision.HIGHEST,
        preferred_element_type=jnp.float32,
    )


def late_part(mask, phase, place, plan, tiles, early, panel_buf, acc, copies):
    slab_tiles = acc.shape[0] - 1
    first_row = (place[0] ^ mask) * slab_tiles
    for s in range(slab_tiles):
        acc[s] = early[first_row + s]
    for copy in copies:
        copy.wait()
    add_products(plan, phase, first_row, slab_tiles, tiles, panel_buf, acc)


def put(out, acc):
    for s in range(acc.shape[0] - 1):
        out[:, s * LANES : (s + 1) * LANES] = acc[s].astype(out.dtype)


def coefficient_kernel(cells, received_count, place, base, *refs):
    received = refs[:received_count]
    mass, current, stored, recurrence, keep, give, halves = refs[received_count:]
    total = base[...]
    for ref in received:
        total = total + ref[...].astype(jnp.float32)
    recurrence[...] = total
    weighted = total * (mass[...] * (1.0 / cells))
    basis = jnp.concatenate([current[...], stored[...]], axis=0)
    coef = dot_split(weighted, basis, NT)
    spare = -coef.shape[1] % LANES
    coef = jnp.concatenate([coef, jnp.zeros((coef.shape[0], spare), jnp.float32)], axis=1)
    halves[...] = jnp.zeros_like(halves)
    for p, (q, k) in enumerate(blocks(coef.shape)):
        halves[p // halves.shape[1], p % halves.shape[1]] = coef[q : q + 8, k : k + LANES]
    core = place[1] & 1
    keep[...] = halves[core]
    give[...] = halves[1 - core]


def residual_kernel(
    cells, place, mine, other, recurrence, mass, current, stored, residual, coef_out, gram, halves, packed
):
    width = recurrence.shape[0]
    core = place[1] & 1
    halves[core] = mine[...]
    halves[1 - core] = other[...]
    for p, (q, k) in enumerate(blocks(packed.shape)):
        packed[q : q + 8, k : k + LANES] = halves[p // halves.shape[1], p % halves.shape[1]]
    coef = packed[...]
    basis = jnp.concatenate([current[...], stored[...]], axis=0)
    coef = coef[:, : basis.shape[0]]
    coef_out[...] = coef
    value = recurrence[...] - dot_split(coef, basis)
    residual[...] = value
    local = dot_split(value * (mass[...] * (1.0 / cells)), value, NT)
    half = width // 2
    gram[...] = jnp.zeros_like(gram)
    gram[:, :width] = local[:half]
    gram[:, LANES // 2 : LANES // 2 + width] = local[half:]


def after_kernel(value, earlier, out):
    pass


def after(value, earlier):
    anywhere = pl.BlockSpec(memory_space=pl.ANY)
    return pl.pallas_call(
        after_kernel,
        out_shape=jax.ShapeDtypeStruct(value.shape, value.dtype),
        in_specs=[anywhere, anywhere],
        out_specs=anywhere,
        input_output_aliases={0: 0},
        compiler_params=limit(1),
    )(value, earlier)


def in_hbm(value):
    return pltpu.with_memory_space_constraint(value, pltpu.HBM)


def limit(mib):
    return pltpu.CompilerParams(vmem_limit_bytes=mib * MIB)


def vmem(count):
    return [pl.BlockSpec(memory_space=pltpu.VMEM)] * count


def smem(count):
    return [pl.BlockSpec(memory_space=pltpu.SMEM)] * count


def local(
    current_block,
    previous_block,
    previous_coupling,
    stored_blocks,
    stiffness_diag,
    lumped_mass,
    tile_values,
    tile_rows,
    tile_cols,
    tile_counts,
):
    row_devs = lax.axis_size("row")
    col_devs = lax.axis_size("col")
    width, slab_len = current_block.shape
    stored_count = stored_blocks.shape[0]
    slots, tile_len, _ = tile_values.shape
    slab_tiles = slab_len // tile_len
    cells = slab_len * row_devs * col_devs
    f32, bf16 = jnp.float32, jnp.bfloat16
    place = jnp.stack([lax.axis_index("row"), lax.axis_index("col")]).astype(jnp.int32)
    stored = stored_blocks.reshape(stored_count * width, slab_len)
    mass = lumped_mass.reshape(1, slab_len)
    diag = stiffness_diag.reshape(1, slab_len)
    slab = jax.ShapeDtypeStruct((width, slab_len), f32)

    targets = row_devs * slab_tiles
    anywhere = [pl.BlockSpec(memory_space=pl.ANY)]
    panel_shape = (col_devs + 1, width, slab_len)
    early_shape = (targets + 1, width, tile_len)
    part_acc = pltpu.VMEM((slab_tiles + 1, width, tile_len), f32)

    def cost(flops):
        return pl.CostEstimate(flops=flops, bytes_accessed=flops // width, transcendentals=0)

    with jax.named_scope("gather"):
        rounded = current_block.astype(bf16)
        panels = [rounded] + [None] * (col_devs - 1)
        for m in range(col_devs - 2, 0, -2):
            panels[m] = swap(rounded, "col", m)
        panels[1] = swap(rounded, "col", 1)

    with jax.named_scope("plan"):
        places = -(-(slots + (GROUP - 1) * 2 * targets + GROUP * UNROLL) // LANES) * LANES
        plan, held = pl.pallas_call(
            functools.partial(plan_kernel, row_devs, col_devs, slab_tiles),
            out_shape=[jax.ShapeDtypeStruct((1, places + LANES), jnp.int32), pltpu.VMEM(tile_values.shape, bf16)],
            in_specs=smem(2) + [pl.BlockSpec(memory_space=pltpu.HBM)] * 3,
            out_specs=vmem(2),
            scratch_shapes=[pltpu.VMEM((1, slots), jnp.int32)] * 2
            + [pltpu.SemaphoreType.DMA((slots // CHUNK,)), pltpu.SemaphoreType.DMA((2,))],
            compiler_params=limit(8),
            cost_estimate=cost(2 * slots * width * tile_len * tile_len),
        )(place, tile_counts, in_hbm(tile_rows.reshape(1, slots)), in_hbm(tile_cols.reshape(1, slots)), in_hbm(tile_values))

    with jax.named_scope("early"):
        early = pl.pallas_call(
            early_kernel,
            out_shape=pltpu.VMEM(early_shape, f32),
            in_specs=smem(1) + anywhere * 2 + vmem(1),
            out_specs=vmem(1)[0],
            scratch_shapes=[pltpu.VMEM(panel_shape, bf16), pltpu.SemaphoreType.DMA((2,))],
            compiler_params=limit(8),
            cost_estimate=cost(slots * width * tile_len * tile_len // 2),
        )(plan, panels[0], panels[1], held)

    with jax.named_scope("gather"):
        for m in range(col_devs - 2, 0, -2):
            panels[m] = after(panels[m], early)
            panels[m + 1] = swap(panels[m], "col", 1)

    with jax.named_scope("late"):
        masks = list(range(row_devs - 1, 0, -1))
        part = jax.ShapeDtypeStruct((width, slab_len), bf16)
        first, gathered = pl.pallas_call(
            functools.partial(first_late_kernel, masks[0], 1),
            out_shape=[part, pltpu.VMEM(panel_shape, bf16)],
            in_specs=smem(2) + anywhere * col_devs + vmem(2),
            out_specs=vmem(2),
            scratch_shapes=[part_acc, pltpu.SemaphoreType.DMA((col_devs,))],
            compiler_params=limit(8),
            cost_estimate=cost(width),
        )(place, plan, *panels, held, early)
        first = swap(first, "row", masks[0])
        others = pl.pallas_call(
            functools.partial(late_kernel, masks[1:]),
            out_shape=[part] * len(masks[1:]),
            in_specs=smem(2) + vmem(3),
            out_specs=vmem(len(masks[1:])),
            scratch_shapes=[part_acc],
            compiler_params=limit(8),
            cost_estimate=cost(width),
        )(place, plan, gathered, held, early)
        received = [swap(other, "row", m) for m, other in zip(masks[1:], others)]
        base = pl.pallas_call(
            functools.partial(own_kernel, row_devs),
            out_shape=slab,
            in_specs=smem(2) + vmem(8),
            out_specs=vmem(1)[0],
            scratch_shapes=[part_acc],
            compiler_params=limit(8),
            cost_estimate=cost(width),
        )(place, plan, gathered, held, early, first, current_block, previous_block, previous_coupling, diag)

    basis_rows = (stored_count + 1) * width
    padded = (width, -(-basis_rows // LANES) * LANES)
    half = (-(-len(blocks(padded)) // 2), 8, LANES)
    with jax.named_scope("coefficients"):
        recurrence, keep, give = pl.pallas_call(
            functools.partial(coefficient_kernel, cells, len(received)),
            out_shape=[slab] + [jax.ShapeDtypeStruct(half, f32)] * 2,
            in_specs=smem(1) + vmem(len(received) + 4),
            out_specs=vmem(3),
            scratch_shapes=[pltpu.VMEM((2,) + half, f32)],
            compiler_params=limit(24),
        )(place, base, *received, mass, current_block, stored)
        mine = keep + swap(give, "col", 1)
        mine = total(total(mine, "col", 2), "row", 1)
        other = swap(mine, "col", 1)

    with jax.named_scope("residual"):
        residual_block, coef, gram = pl.pallas_call(
            functools.partial(residual_kernel, cells),
            out_shape=[
                slab,
                jax.ShapeDtypeStruct((width, basis_rows), f32),
                jax.ShapeDtypeStruct((width // 2, LANES), f32),
            ],
            in_specs=smem(1) + vmem(6),
            out_specs=vmem(3),
            scratch_shapes=[pltpu.VMEM((2,) + half, f32), pltpu.VMEM(padded, f32)],
            compiler_params=limit(24),
        )(place, mine, other, recurrence, mass, current_block, stored)
        coefficients = coef.T.reshape(stored_count + 1, width, width)

    with jax.named_scope("gram"):
        gram = gram + swap(gram, "col", 1)
        gram = total(total(gram, "col", 2), "row", 1)
        gram = jnp.concatenate(
            [gram[:, :width], gram[:, LANES // 2 : LANES // 2 + width]], axis=0
        )
    return (residual_block, coefficients, gram)


def solution(mesh):
    return jax.shard_map(
        local,
        mesh=mesh,
        in_specs=(
            P(None, ("row", "col")),
            P(None, ("row", "col")),
            P(),
            P(None, None, ("row", "col")),
            P(("row", "col")),
            P(("row", "col")),
            P(("row", "col"), None, None),
            P(("row", "col")),
            P(("row", "col")),
            P(("row", "col")),
        ),
        out_specs=(P(None, ("row", "col")), P(), P()),
        check_vma=False,
    )
```

```python
import functools

import jax
import jax.numpy as jnp
from jax import lax
from jax.experimental import pallas as pl
from jax.experimental.pallas import tpu as pltpu
from jax.sharding import PartitionSpec as P

LANES = 128
CHUNK = 32
GROUP = 2
UNROLL = 4
TILE_BIT, SOURCE_BIT, ROW_BIT = 10, 15, 20
NT = (((1,), (1,)), ((), ()))
MIB = 1 << 20


def swap(value, axis, mask):
    count = lax.axis_size(axis)
    return lax.ppermute(value, axis, [(i, i ^ mask) for i in range(count)])


def total(value, axis, step):
    values = [value] + [swap(value, axis, m) for m in range(step, lax.axis_size(axis), step)]
    while len(values) > 1:
        values = [values[i] + values[i + 1] for i in range(0, len(values), 2)]
    return values[0]


def split(value):
    high = value.astype(jnp.bfloat16)
    low = (value - high.astype(jnp.float32)).astype(jnp.bfloat16)
    return high, low


def mm(a, b, dims=(((1,), (0,)), ((), ()))):
    return lax.dot_general(a, b, dims, preferred_element_type=jnp.float32)


def dot_split(a, b, dims=(((1,), (0,)), ((), ()))):
    rows = a.shape[0]
    a_high, a_low = split(a)
    b_high, b_low = split(b)
    both = mm(jnp.concatenate([a_high, a_low], axis=0), b_high, dims)
    return both[:rows] + both[rows:] + mm(a_high, b_low, dims)


def blocks(shape):
    return [(q, k) for q in range(0, shape[0], 8) for k in range(0, shape[1], LANES)]


def early_kernel(
    row_devs,
    col_devs,
    slab_tiles,
    place,
    counts,
    rows_hbm,
    cols_hbm,
    tiles,
    own_panel,
    near_panel,
    out,
    held,
    acc,
    rows,
    cols,
    plan,
    panel_buf,
    tile_sem,
    list_sem,
    panel_sem,
):
    chunks = (counts[0] + CHUNK - 1) // CHUNK
    row_copy = pltpu.make_async_copy(rows_hbm, rows, list_sem.at[0])
    col_copy = pltpu.make_async_copy(cols_hbm, cols, list_sem.at[1])
    row_copy.start()
    col_copy.start()

    def tile_copy(k):
        window = pl.ds(k * CHUNK, CHUNK)
        return pltpu.make_async_copy(tiles.at[window], held.at[window], tile_sem.at[k])

    @pl.loop(0, chunks)
    def _(k):
        tile_copy(k).start()

    copies = load_panels((own_panel, near_panel), panel_buf, panel_sem)
    f32, bf16, i32 = jnp.float32, jnp.bfloat16, jnp.int32
    slots, places = rows.shape[1], out.shape[1] - LANES
    targets = row_devs * slab_tiles
    bins = 2 * targets

    def iota(shape, dim):
        return lax.broadcasted_iota(i32, shape, dim)

    slot = iota((1, slots), 1)
    occupied = slot < counts[0]
    earlier = (iota((slots, slots), 0) < iota((slots, slots), 1)).astype(f32).astype(bf16)
    row_copy.wait()
    col_copy.wait()
    row = rows[...]
    row_owner = jnp.floor(row.astype(f32) * (1.0 / slab_tiles)).astype(i32)
    col_f = cols[...].astype(f32)
    source_f = jnp.floor(col_f * (1.0 / slab_tiles))
    source = source_f.astype(i32) ^ place[1]
    tile_f = col_f - slab_tiles * source_f
    far = row_devs - 1 - (row_owner ^ place[0])
    late_bin = targets + far * slab_tiles + row - row_owner * slab_tiles
    bin_of = jnp.where(occupied, jnp.where(source < 2, row, late_bin), -1)
    member = (iota((bins, slots), 0) == bin_of).astype(f32)
    member_bf = member.astype(bf16)
    rank = jnp.sum(member * mm(member_bf, earlier), axis=0, keepdims=True)
    sizes = mm(jnp.ones((8, slots), bf16), member_bf, NT)
    sizes = GROUP * jnp.floor((sizes + (GROUP - 1.0)) * (1.0 / GROUP))
    before = (iota((bins, bins), 1) < iota((bins, bins), 0)).astype(f32)
    begin = jnp.sum(before * sizes[:1], axis=1, keepdims=True)
    position = jnp.sum(member * begin, axis=0, keepdims=True) + rank
    position = jnp.where(occupied, position.astype(i32), -1)
    chosen = (iota((places, slots), 0) == position).astype(f32).astype(bf16)
    slot_f = slot.astype(f32)
    slot_high = jnp.floor(slot_f * (1.0 / 16.0))
    facts = [slot_high, slot_f - 16.0 * slot_high, source.astype(f32), tile_f, row.astype(f32), jnp.ones((1, slots), f32)]
    facts = jnp.concatenate(facts + [jnp.zeros((2, slots), f32)], axis=0).astype(bf16)
    found = mm(facts, chosen, NT).astype(i32)
    source = jnp.where(found[5:6] > 0, found[2:3], col_devs)
    words = (found[4:5] << ROW_BIT) + (source << SOURCE_BIT) + (found[3:4] << TILE_BIT)
    out[:, :places] = words + (found[0:1] << 4) + found[1:2]
    phase = iota((bins, LANES), 1)
    edge = jnp.where(phase > 0, targets + (phase - 1) * slab_tiles, 0)
    inside = (iota((bins, LANES), 0) < edge).astype(f32).astype(bf16)
    out[:, places:] = mm(sizes.astype(bf16), inside)[:1].astype(i32)
    plan_copy = pltpu.make_async_copy(out, plan, list_sem.at[2])
    plan_copy.start()
    acc[...] = jnp.zeros_like(acc)
    for copy in copies + [plan_copy]:
        copy.wait()

    @pl.loop(0, chunks)
    def _(k):
        tile_copy(k).wait()

    add_products(plan, 0, 0, targets, held, panel_buf, acc)


def field(word, low, high):
    return (word >> low) & ((1 << (high - low)) - 1)


def add_products(plan, phase, first_row, spare_row, tiles, panel_buf, acc):
    phases = plan.shape[1] - LANES
    begin, end = plan[0, phases + phase], plan[0, phases + phase + 1]

    def panel(word):
        where = pl.multiple_of(field(word, TILE_BIT, SOURCE_BIT) * LANES, LANES)
        return panel_buf[field(word, SOURCE_BIT, ROW_BIT), :, pl.ds(where, LANES)]

    @pl.loop(0, (end - begin + GROUP * UNROLL - 1) // (GROUP * UNROLL))
    def _(g):
        first = begin + g * GROUP * UNROLL
        parts = []
        for u in range(UNROLL):
            words = [plan[0, first + GROUP * u + i] for i in range(GROUP)]
            left = jnp.concatenate([panel(word) for word in words], axis=1)
            right = jnp.concatenate([tiles[field(word, 0, TILE_BIT)] for word in words], axis=1)
            parts.append(mm(left, right, NT))
        for u in range(UNROLL):
            p = first + GROUP * u
            a = jnp.where(p < end, (plan[0, p] >> ROW_BIT) - first_row, spare_row)
            acc[a] += parts[u]


def load_panels(panels, panel_buf, sem):
    copies = [pltpu.make_async_copy(ref, panel_buf.at[m], sem.at[m]) for m, ref in enumerate(panels)]
    for copy in copies:
        copy.start()
    zero = panel_buf.shape[0] - 1
    panel_buf[zero, :, :LANES] = jnp.zeros((panel_buf.shape[1], LANES), jnp.bfloat16)
    return copies


def first_late_kernel(mask, place, plan, *refs):
    panels = refs[:-6]
    tiles, early, send, panel_buf, acc, sem = refs[-6:]
    copies = load_panels(panels, panel_buf, sem)
    late_part(mask, place, plan, tiles, early, panel_buf, acc, copies)
    put(send, acc)


def late_kernel(masks, place, plan, panel_buf, tiles, early, *refs):
    acc = refs[-1]
    if masks is None:
        inner = (place[0] == 1) | (place[0] == 2)
        masks = (jnp.where(inner, 1, 2), jnp.where(inner, 2, 1))
    for mask, send in zip(masks, refs):
        late_part(mask, place, plan, tiles, early, panel_buf, acc, ())
        put(send, acc)


def own_kernel(place, plan, panel_buf, tiles, early, current, previous, coupling, diag, base, acc):
    late_part(0, place, plan, tiles, early, panel_buf, acc, ())
    put(base, acc)
    base[...] += diag[...] * current[...] - jnp.dot(
        coupling[...],
        previous[...],
        precision=lax.Precision.HIGHEST,
        preferred_element_type=jnp.float32,
    )


def late_part(mask, place, plan, tiles, early, panel_buf, acc, copies):
    slab_tiles = acc.shape[0] - 1
    row_devs = (early.shape[0] - 1) // slab_tiles
    first_row = (place[0] ^ mask) * slab_tiles
    for s in range(slab_tiles):
        acc[s] = early[first_row + s]
    for copy in copies:
        copy.wait()
    add_products(plan, row_devs - mask, first_row, slab_tiles, tiles, panel_buf, acc)


def put(out, acc):
    for s in range(acc.shape[0] - 1):
        out[:, s * LANES : (s + 1) * LANES] = acc[s].astype(out.dtype)


def coefficient_kernel(cells, received_count, place, base, *refs):
    received = refs[:received_count]
    mass, current, stored, recurrence, keep, give, halves = refs[received_count:]
    total = base[...]
    for ref in received:
        total = total + ref[...].astype(jnp.float32)
    recurrence[...] = total
    weighted = total * (mass[...] * (1.0 / cells))
    basis = jnp.concatenate([current[...], stored[...]], axis=0)
    coef = dot_split(weighted, basis, NT)
    spare = -coef.shape[1] % LANES
    coef = jnp.concatenate([coef, jnp.zeros((coef.shape[0], spare), jnp.float32)], axis=1)
    halves[...] = jnp.zeros_like(halves)
    for p, (q, k) in enumerate(blocks(coef.shape)):
        halves[p // halves.shape[1], p % halves.shape[1]] = coef[q : q + 8, k : k + LANES]
    core = place[1] & 1
    keep[...] = halves[core]
    give[...] = halves[1 - core]


def residual_kernel(
    cells, place, mine, other, recurrence, mass, current, stored, residual, coef_out, gram, halves, packed
):
    width = recurrence.shape[0]
    core = place[1] & 1
    halves[core] = mine[...]
    halves[1 - core] = other[...]
    for p, (q, k) in enumerate(blocks(packed.shape)):
        packed[q : q + 8, k : k + LANES] = halves[p // halves.shape[1], p % halves.shape[1]]
    coef = packed[...]
    basis = jnp.concatenate([current[...], stored[...]], axis=0)
    coef = coef[:, : basis.shape[0]]
    coef_out[...] = coef
    value = recurrence[...] - dot_split(coef, basis)
    residual[...] = value
    local = dot_split(value * (mass[...] * (1.0 / cells)), value, NT)
    half = width // 2
    gram[...] = jnp.zeros_like(gram)
    gram[:, :width] = local[:half]
    gram[:, LANES // 2 : LANES // 2 + width] = local[half:]


def after_kernel(value, earlier, out):
    pass


def after(value, earlier):
    anywhere = pl.BlockSpec(memory_space=pl.ANY)
    return pl.pallas_call(
        after_kernel,
        out_shape=jax.ShapeDtypeStruct(value.shape, value.dtype),
        in_specs=[anywhere, anywhere],
        out_specs=anywhere,
        input_output_aliases={0: 0},
        compiler_params=limit(1),
    )(value, earlier)


def in_hbm(value):
    return pltpu.with_memory_space_constraint(value, pltpu.HBM)


def limit(mib):
    return pltpu.CompilerParams(vmem_limit_bytes=mib * MIB)


def vmem(count):
    return [pl.BlockSpec(memory_space=pltpu.VMEM)] * count


def smem(count):
    return [pl.BlockSpec(memory_space=pltpu.SMEM)] * count


def local(
    current_block,
    previous_block,
    previous_coupling,
    stored_blocks,
    stiffness_diag,
    lumped_mass,
    tile_values,
    tile_rows,
    tile_cols,
    tile_counts,
):
    row_devs = lax.axis_size("row")
    col_devs = lax.axis_size("col")
    width, slab_len = current_block.shape
    stored_count = stored_blocks.shape[0]
    slots, tile_len, _ = tile_values.shape
    slab_tiles = slab_len // tile_len
    cells = slab_len * row_devs * col_devs
    f32, bf16 = jnp.float32, jnp.bfloat16
    place = jnp.stack([lax.axis_index("row"), lax.axis_index("col")]).astype(jnp.int32)
    stored = stored_blocks.reshape(stored_count * width, slab_len)
    mass = lumped_mass.reshape(1, slab_len)
    diag = stiffness_diag.reshape(1, slab_len)
    slab = jax.ShapeDtypeStruct((width, slab_len), f32)

    targets = row_devs * slab_tiles
    anywhere = [pl.BlockSpec(memory_space=pl.ANY)]
    panel_shape = (col_devs + 1, width, slab_len)
    early_shape = (targets + 1, width, tile_len)
    part_acc = pltpu.VMEM((slab_tiles + 1, width, tile_len), f32)

    def cost(flops):
        return pl.CostEstimate(flops=flops, bytes_accessed=flops // width, transcendentals=0)

    with jax.named_scope("gather"):
        rounded = current_block.astype(bf16)
        panels = [rounded] + [None] * (col_devs - 1)
        for m in range(col_devs - 2, 0, -2):
            panels[m] = swap(rounded, "col", m)
        panels[1] = swap(rounded, "col", 1)

    with jax.named_scope("early"):
        places = -(-(slots + (GROUP - 1) * 2 * targets + GROUP * UNROLL) // LANES) * LANES
        plan_shape = (1, places + LANES)
        plan, held, early = pl.pallas_call(
            functools.partial(early_kernel, row_devs, col_devs, slab_tiles),
            out_shape=[
                jax.ShapeDtypeStruct(plan_shape, jnp.int32),
                pltpu.VMEM(tile_values.shape, bf16),
                pltpu.VMEM(early_shape, f32),
            ],
            in_specs=smem(2) + [pl.BlockSpec(memory_space=pltpu.HBM)] * 3 + anywhere * 2,
            out_specs=vmem(3),
            scratch_shapes=[
                pltpu.VMEM((1, slots), jnp.int32),
                pltpu.VMEM((1, slots), jnp.int32),
                pltpu.SMEM(plan_shape, jnp.int32),
                pltpu.VMEM(panel_shape, bf16),
                pltpu.SemaphoreType.DMA((slots // CHUNK,)),
                pltpu.SemaphoreType.DMA((3,)),
                pltpu.SemaphoreType.DMA((2,)),
            ],
            compiler_params=limit(12),
            cost_estimate=cost(2 * slots * width * tile_len * tile_len),
        )(
            place,
            tile_counts,
            in_hbm(tile_rows.reshape(1, slots)),
            in_hbm(tile_cols.reshape(1, slots)),
            in_hbm(tile_values),
            panels[0],
            panels[1],
        )

    with jax.named_scope("gather"):
        for m in range(col_devs - 2, 0, -2):
            panels[m] = after(panels[m], early)
            panels[m + 1] = swap(panels[m], "col", 1)

    with jax.named_scope("late"):
        part = jax.ShapeDtypeStruct((width, slab_len), bf16)
        first, gathered = pl.pallas_call(
            functools.partial(first_late_kernel, row_devs - 1),
            out_shape=[part, pltpu.VMEM(panel_shape, bf16)],
            in_specs=smem(2) + anywhere * col_devs + vmem(2),
            out_specs=vmem(2),
            scratch_shapes=[part_acc, pltpu.SemaphoreType.DMA((col_devs,))],
            compiler_params=limit(8),
            cost_estimate=cost(width),
        )(place, plan, *panels, held, early)
        relay = row_devs == 4
        masks = None if relay else list(range(row_devs - 2, 0, -1))
        parts = [part, slab] if relay else [part] * (row_devs - 2)
        others = pl.pallas_call(
            functools.partial(late_kernel, masks),
            out_shape=parts,
            in_specs=smem(2) + vmem(3),
            out_specs=vmem(len(parts)),
            scratch_shapes=[part_acc],
            compiler_params=limit(8),
            cost_estimate=cost(width),
        )(place, plan, gathered, held, early)
        if relay:
            passing = lax.ppermute(first, "row", [(0, 1), (3, 2)])
            received = [lax.ppermute(first, "row", [(1, 2), (2, 1)])]
            received.append(lax.ppermute(others[0], "row", [(0, 2), (3, 1), (1, 0), (2, 3)]))
            joined = (others[1] + passing.astype(f32)).astype(bf16)
            received.append(lax.ppermute(joined, "row", [(0, 1), (1, 3), (3, 2), (2, 0)]))
        else:
            received = [swap(first, "row", row_devs - 1)]
            received += [swap(other, "row", m) for m, other in zip(masks, others)]
        base = pl.pallas_call(
            own_kernel,
            out_shape=slab,
            in_specs=smem(2) + vmem(7),
            out_specs=vmem(1)[0],
            scratch_shapes=[part_acc],
            compiler_params=limit(8),
            cost_estimate=cost(width),
        )(place, plan, gathered, held, early, current_block, previous_block, previous_coupling, diag)

    basis_rows = (stored_count + 1) * width
    padded = (width, -(-basis_rows // LANES) * LANES)
    half = (-(-len(blocks(padded)) // 2), 8, LANES)
    with jax.named_scope("coefficients"):
        recurrence, keep, give = pl.pallas_call(
            functools.partial(coefficient_kernel, cells, len(received)),
            out_shape=[slab] + [jax.ShapeDtypeStruct(half, f32)] * 2,
            in_specs=smem(1) + vmem(len(received) + 4),
            out_specs=vmem(3),
            scratch_shapes=[pltpu.VMEM((2,) + half, f32)],
            compiler_params=limit(24),
        )(place, base, *received, mass, current_block, stored)
        mine = keep + swap(give, "col", 1)
        mine = total(total(mine, "col", 2), "row", 1)
        other = swap(mine, "col", 1)

    with jax.named_scope("residual"):
        residual_block, coef, gram = pl.pallas_call(
            functools.partial(residual_kernel, cells),
            out_shape=[
                slab,
                jax.ShapeDtypeStruct((width, basis_rows), f32),
                jax.ShapeDtypeStruct((width // 2, LANES), f32),
            ],
            in_specs=smem(1) + vmem(6),
            out_specs=vmem(3),
            scratch_shapes=[pltpu.VMEM((2,) + half, f32), pltpu.VMEM(padded, f32)],
            compiler_params=limit(24),
        )(place, mine, other, recurrence, mass, current_block, stored)
        coefficients = coef.T.reshape(stored_count + 1, width, width)

    with jax.named_scope("gram"):
        gram = gram + swap(gram, "col", 1)
        gram = lax.psum(total(gram, "col", 2), "row")
        gram = jnp.concatenate(
            [gram[:, :width], gram[:, LANES // 2 : LANES // 2 + width]], axis=0
        )
    return (residual_block, coefficients, gram)


def solution(mesh):
    return jax.shard_map(
        local,
        mesh=mesh,
        in_specs=(
            P(None, ("row", "col")),
            P(None, ("row", "col")),
            P(),
            P(None, None, ("row", "col")),
            P(("row", "col")),
            P(("row", "col")),
            P(("row", "col"), None, None),
            P(("row", "col")),
            P(("row", "col")),
            P(("row", "col")),
        ),
        out_specs=(P(None, ("row", "col")), P(), P()),
        check_vma=False,
    )
```

```python
import functools

import jax
import jax.numpy as jnp
from jax import lax
from jax.experimental import pallas as pl
from jax.experimental.pallas import tpu as pltpu
from jax.sharding import PartitionSpec as P

LANES = 128
CHUNK = 32
GROUP = 2
UNROLL = 8
TILE_BIT, SOURCE_BIT, ROW_BIT = 10, 15, 20
NT = (((1,), (1,)), ((), ()))
MIB = 1 << 20


def swap(value, axis, mask):
    count = lax.axis_size(axis)
    return lax.ppermute(value, axis, [(i, i ^ mask) for i in range(count)])


def total(value, axis, step):
    values = [value] + [swap(value, axis, m) for m in range(step, lax.axis_size(axis), step)]
    while len(values) > 1:
        values = [values[i] + values[i + 1] for i in range(0, len(values), 2)]
    return values[0]


def split(value):
    high = value.astype(jnp.bfloat16)
    low = (value - high.astype(jnp.float32)).astype(jnp.bfloat16)
    return high, low


def mm(a, b, dims=(((1,), (0,)), ((), ()))):
    return lax.dot_general(a, b, dims, preferred_element_type=jnp.float32)


def dot_split(a, b, dims=(((1,), (0,)), ((), ()))):
    rows = a.shape[0]
    a_high, a_low = split(a)
    b_high, b_low = split(b)
    both = mm(jnp.concatenate([a_high, a_low], axis=0), b_high, dims)
    return both[:rows] + both[rows:] + mm(a_high, b_low, dims)


def blocks(shape):
    return [(q, k) for q in range(0, shape[0], 8) for k in range(0, shape[1], LANES)]


def early_kernel(
    row_devs,
    col_devs,
    slab_tiles,
    place,
    counts,
    rows_hbm,
    cols_hbm,
    tiles,
    own_panel,
    near_panel,
    out,
    held,
    acc,
    rows,
    cols,
    plan,
    panel_buf,
    tile_sem,
    list_sem,
    panel_sem,
):
    chunks = (counts[0] + CHUNK - 1) // CHUNK
    row_copy = pltpu.make_async_copy(rows_hbm, rows, list_sem.at[0])
    col_copy = pltpu.make_async_copy(cols_hbm, cols, list_sem.at[1])
    row_copy.start()
    col_copy.start()

    def tile_copy(k):
        window = pl.ds(k * CHUNK, CHUNK)
        return pltpu.make_async_copy(tiles.at[window], held.at[window], tile_sem.at[k])

    @pl.loop(0, chunks)
    def _(k):
        tile_copy(k).start()

    copies = load_panels((own_panel, near_panel), panel_buf, panel_sem)
    f32, bf16, i32 = jnp.float32, jnp.bfloat16, jnp.int32
    slots, places = rows.shape[1], out.shape[1] - LANES
    targets = row_devs * slab_tiles
    bins = 2 * targets

    def iota(shape, dim):
        return lax.broadcasted_iota(i32, shape, dim)

    slot = iota((1, slots), 1)
    occupied = slot < counts[0]
    earlier = (iota((slots, slots), 0) < iota((slots, slots), 1)).astype(f32).astype(bf16)
    row_copy.wait()
    col_copy.wait()
    row = rows[...]
    row_owner = jnp.floor(row.astype(f32) * (1.0 / slab_tiles)).astype(i32)
    col_f = cols[...].astype(f32)
    source_f = jnp.floor(col_f * (1.0 / slab_tiles))
    source = source_f.astype(i32) ^ place[1]
    tile_f = col_f - slab_tiles * source_f
    far = row_devs - 1 - (row_owner ^ place[0])
    late_bin = targets + far * slab_tiles + row - row_owner * slab_tiles
    bin_of = jnp.where(occupied, jnp.where(source < 2, row, late_bin), -1)
    member = (iota((bins, slots), 0) == bin_of).astype(f32)
    member_bf = member.astype(bf16)
    rank = jnp.sum(member * mm(member_bf, earlier), axis=0, keepdims=True)
    sizes = mm(jnp.ones((8, slots), bf16), member_bf, NT)
    sizes = GROUP * jnp.floor((sizes + (GROUP - 1.0)) * (1.0 / GROUP))
    before = (iota((bins, bins), 1) < iota((bins, bins), 0)).astype(f32)
    begin = jnp.sum(before * sizes[:1], axis=1, keepdims=True)
    position = jnp.sum(member * begin, axis=0, keepdims=True) + rank
    position = jnp.where(occupied, position.astype(i32), -1)
    chosen = (iota((places, slots), 0) == position).astype(f32).astype(bf16)
    slot_f = slot.astype(f32)
    slot_high = jnp.floor(slot_f * (1.0 / 16.0))
    facts = [slot_high, slot_f - 16.0 * slot_high, source.astype(f32), tile_f, row.astype(f32), jnp.ones((1, slots), f32)]
    facts = jnp.concatenate(facts + [jnp.zeros((2, slots), f32)], axis=0).astype(bf16)
    found = mm(facts, chosen, NT).astype(i32)
    source = jnp.where(found[5:6] > 0, found[2:3], col_devs)
    words = (found[4:5] << ROW_BIT) + (source << SOURCE_BIT) + (found[3:4] << TILE_BIT)
    out[:, :places] = words + (found[0:1] << 4) + found[1:2]
    phase = iota((bins, LANES), 1)
    edge = jnp.where(phase > 0, targets + (phase - 1) * slab_tiles, 0)
    inside = (iota((bins, LANES), 0) < edge).astype(f32).astype(bf16)
    out[:, places:] = mm(sizes.astype(bf16), inside)[:1].astype(i32)
    plan_copy = pltpu.make_async_copy(out, plan, list_sem.at[2])
    plan_copy.start()
    acc[...] = jnp.zeros_like(acc)
    for copy in copies + [plan_copy]:
        copy.wait()

    @pl.loop(0, chunks)
    def _(k):
        tile_copy(k).wait()

    add_products(plan, 0, 0, targets, held, panel_buf, acc)


def field(word, low, high):
    return (word >> low) & ((1 << (high - low)) - 1)


def add_products(plan, phase, first_row, spare_row, tiles, panel_buf, acc):
    phases = plan.shape[1] - LANES
    begin, end = plan[0, phases + phase], plan[0, phases + phase + 1]

    def panel(word):
        where = pl.multiple_of(field(word, TILE_BIT, SOURCE_BIT) * LANES, LANES)
        return panel_buf[field(word, SOURCE_BIT, ROW_BIT), :, pl.ds(where, LANES)]

    @pl.loop(0, (end - begin + GROUP * UNROLL - 1) // (GROUP * UNROLL))
    def _(g):
        first = begin + g * GROUP * UNROLL
        parts = []
        for u in range(UNROLL):
            words = [plan[0, first + GROUP * u + i] for i in range(GROUP)]
            left = jnp.concatenate([panel(word) for word in words], axis=1)
            right = jnp.concatenate([tiles[field(word, 0, TILE_BIT)] for word in words], axis=1)
            parts.append(mm(left, right, NT))
        for u in range(UNROLL):
            p = first + GROUP * u
            a = jnp.where(p < end, (plan[0, p] >> ROW_BIT) - first_row, spare_row)
            acc[a] += parts[u]


def load_panels(panels, panel_buf, sem):
    copies = [pltpu.make_async_copy(ref, panel_buf.at[m], sem.at[m]) for m, ref in enumerate(panels)]
    for copy in copies:
        copy.start()
    zero = panel_buf.shape[0] - 1
    panel_buf[zero, :, :LANES] = jnp.zeros((panel_buf.shape[1], LANES), jnp.bfloat16)
    return copies


def first_late_kernel(mask, place, plan, *refs):
    panels = refs[:-6]
    tiles, early, send, panel_buf, acc, sem = refs[-6:]
    copies = load_panels(panels, panel_buf, sem)
    late_part(mask, place, plan, tiles, early, panel_buf, acc, copies)
    put(send, acc)


def late_kernel(masks, place, plan, panel_buf, tiles, early, *refs):
    acc = refs[-1]
    for mask, send in zip(masks, refs):
        late_part(mask, place, plan, tiles, early, panel_buf, acc, ())
        put(send, acc)


def own_kernel(place, plan, panel_buf, tiles, early, received, current, previous, coupling, diag, base, acc):
    late_part(0, place, plan, tiles, early, panel_buf, acc, ())
    put(base, acc)
    base[...] += received[...].astype(jnp.float32) + diag[...] * current[...] - jnp.dot(
        coupling[...],
        previous[...],
        precision=lax.Precision.HIGHEST,
        preferred_element_type=jnp.float32,
    )


def late_part(mask, place, plan, tiles, early, panel_buf, acc, copies):
    slab_tiles = acc.shape[0] - 1
    row_devs = (early.shape[0] - 1) // slab_tiles
    first_row = (place[0] ^ mask) * slab_tiles
    for s in range(slab_tiles):
        acc[s] = early[first_row + s]
    for copy in copies:
        copy.wait()
    add_products(plan, row_devs - mask, first_row, slab_tiles, tiles, panel_buf, acc)


def put(out, acc):
    for s in range(acc.shape[0] - 1):
        out[:, s * LANES : (s + 1) * LANES] = acc[s].astype(out.dtype)


def coefficient_kernel(cells, received_count, place, base, *refs):
    received = refs[:received_count]
    mass, current, stored, recurrence, keep, give, halves = refs[received_count:]
    total = base[...]
    for ref in received:
        total = total + ref[...].astype(jnp.float32)
    recurrence[...] = total
    weighted = total * (mass[...] * (1.0 / cells))
    basis = jnp.concatenate([current[...], stored[...]], axis=0)
    coef = dot_split(weighted, basis, NT)
    spare = -coef.shape[1] % LANES
    coef = jnp.concatenate([coef, jnp.zeros((coef.shape[0], spare), jnp.float32)], axis=1)
    halves[...] = jnp.zeros_like(halves)
    for p, (q, k) in enumerate(blocks(coef.shape)):
        halves[p // halves.shape[1], p % halves.shape[1]] = coef[q : q + 8, k : k + LANES]
    core = place[1] & 1
    keep[...] = halves[core]
    give[...] = halves[1 - core]


def residual_kernel(
    cells, place, mine, other, recurrence, mass, current, stored, residual, coef_out, gram, halves, packed
):
    width = recurrence.shape[0]
    core = place[1] & 1
    halves[core] = mine[...]
    halves[1 - core] = other[...]
    for p, (q, k) in enumerate(blocks(packed.shape)):
        packed[q : q + 8, k : k + LANES] = halves[p // halves.shape[1], p % halves.shape[1]]
    coef = packed[...]
    basis = jnp.concatenate([current[...], stored[...]], axis=0)
    coef = coef[:, : basis.shape[0]]
    coef_out[...] = coef
    value = recurrence[...] - dot_split(coef, basis)
    residual[...] = value
    local = dot_split(value * (mass[...] * (1.0 / cells)), value, NT)
    half = width // 2
    gram[...] = jnp.zeros_like(gram)
    gram[:, :width] = local[:half]
    gram[:, LANES // 2 : LANES // 2 + width] = local[half:]


def after_kernel(value, earlier, out):
    pass


def after(value, earlier):
    anywhere = pl.BlockSpec(memory_space=pl.ANY)
    return pl.pallas_call(
        after_kernel,
        out_shape=jax.ShapeDtypeStruct(value.shape, value.dtype),
        in_specs=[anywhere, anywhere],
        out_specs=anywhere,
        input_output_aliases={0: 0},
        compiler_params=limit(1),
    )(value, earlier)


def in_hbm(value):
    return pltpu.with_memory_space_constraint(value, pltpu.HBM)


def limit(mib):
    return pltpu.CompilerParams(vmem_limit_bytes=mib * MIB)


def vmem(count):
    return [pl.BlockSpec(memory_space=pltpu.VMEM)] * count


def smem(count):
    return [pl.BlockSpec(memory_space=pltpu.SMEM)] * count


def local(
    current_block,
    previous_block,
    previous_coupling,
    stored_blocks,
    stiffness_diag,
    lumped_mass,
    tile_values,
    tile_rows,
    tile_cols,
    tile_counts,
):
    row_devs = lax.axis_size("row")
    col_devs = lax.axis_size("col")
    width, slab_len = current_block.shape
    stored_count = stored_blocks.shape[0]
    slots, tile_len, _ = tile_values.shape
    slab_tiles = slab_len // tile_len
    cells = slab_len * row_devs * col_devs
    f32, bf16 = jnp.float32, jnp.bfloat16
    place = jnp.stack([lax.axis_index("row"), lax.axis_index("col")]).astype(jnp.int32)
    stored = stored_blocks.reshape(stored_count * width, slab_len)
    mass = lumped_mass.reshape(1, slab_len)
    diag = stiffness_diag.reshape(1, slab_len)
    slab = jax.ShapeDtypeStruct((width, slab_len), f32)

    targets = row_devs * slab_tiles
    anywhere = [pl.BlockSpec(memory_space=pl.ANY)]
    panel_shape = (col_devs + 1, width, slab_len)
    early_shape = (targets + 1, width, tile_len)
    part_acc = pltpu.VMEM((slab_tiles + 1, width, tile_len), f32)

    def cost(flops):
        return pl.CostEstimate(flops=flops, bytes_accessed=flops // width, transcendentals=0)

    with jax.named_scope("gather"):
        rounded = current_block.astype(bf16)
        panels = [rounded] + [None] * (col_devs - 1)
        for m in range(col_devs - 2, 0, -2):
            panels[m] = swap(rounded, "col", m)
        panels[1] = swap(rounded, "col", 1)

    with jax.named_scope("early"):
        places = -(-(slots + (GROUP - 1) * 2 * targets + GROUP * UNROLL) // LANES) * LANES
        plan_shape = (1, places + LANES)
        plan, held, early = pl.pallas_call(
            functools.partial(early_kernel, row_devs, col_devs, slab_tiles),
            out_shape=[
                jax.ShapeDtypeStruct(plan_shape, jnp.int32),
                pltpu.VMEM(tile_values.shape, bf16),
                pltpu.VMEM(early_shape, f32),
            ],
            in_specs=smem(2) + [pl.BlockSpec(memory_space=pltpu.HBM)] * 3 + anywhere * 2,
            out_specs=vmem(3),
            scratch_shapes=[
                pltpu.VMEM((1, slots), jnp.int32),
                pltpu.VMEM((1, slots), jnp.int32),
                pltpu.SMEM(plan_shape, jnp.int32),
                pltpu.VMEM(panel_shape, bf16),
                pltpu.SemaphoreType.DMA((slots // CHUNK,)),
                pltpu.SemaphoreType.DMA((3,)),
                pltpu.SemaphoreType.DMA((2,)),
            ],
            compiler_params=limit(12),
            cost_estimate=cost(2 * slots * width * tile_len * tile_len),
        )(
            place,
            tile_counts,
            in_hbm(tile_rows.reshape(1, slots)),
            in_hbm(tile_cols.reshape(1, slots)),
            in_hbm(tile_values),
            panels[0],
            panels[1],
        )

    with jax.named_scope("gather"):
        for m in range(col_devs - 2, 0, -2):
            panels[m] = after(panels[m], early)
            panels[m + 1] = swap(panels[m], "col", 1)

    with jax.named_scope("late"):
        part = jax.ShapeDtypeStruct((width, slab_len), bf16)
        first, gathered = pl.pallas_call(
            functools.partial(first_late_kernel, row_devs - 1),
            out_shape=[part, pltpu.VMEM(panel_shape, bf16)],
            in_specs=smem(2) + anywhere * col_devs + vmem(2),
            out_specs=vmem(2),
            scratch_shapes=[part_acc, pltpu.SemaphoreType.DMA((col_devs,))],
            compiler_params=limit(8),
            cost_estimate=cost(width),
        )(place, plan, *panels, held, early)
        first = swap(first, "row", row_devs - 1)
        masks = list(range(row_devs - 2, 0, -1))
        others = pl.pallas_call(
            functools.partial(late_kernel, masks),
            out_shape=[part] * len(masks),
            in_specs=smem(2) + vmem(3),
            out_specs=vmem(len(masks)),
            scratch_shapes=[part_acc],
            compiler_params=limit(8),
            cost_estimate=cost(width),
        )(place, plan, gathered, held, early)
        received = [swap(other, "row", m) for m, other in zip(masks, others)]
        base = pl.pallas_call(
            own_kernel,
            out_shape=slab,
            in_specs=smem(2) + vmem(8),
            out_specs=vmem(1)[0],
            scratch_shapes=[part_acc],
            compiler_params=limit(8),
            cost_estimate=cost(width),
        )(place, plan, gathered, held, early, first, current_block, previous_block, previous_coupling, diag)

    basis_rows = (stored_count + 1) * width
    padded = (width, -(-basis_rows // LANES) * LANES)
    half = (-(-len(blocks(padded)) // 2), 8, LANES)
    with jax.named_scope("coefficients"):
        recurrence, keep, give = pl.pallas_call(
            functools.partial(coefficient_kernel, cells, len(received)),
            out_shape=[slab] + [jax.ShapeDtypeStruct(half, f32)] * 2,
            in_specs=smem(1) + vmem(len(received) + 4),
            out_specs=vmem(3),
            scratch_shapes=[pltpu.VMEM((2,) + half, f32)],
            compiler_params=limit(24),
        )(place, base, *received, mass, current_block, stored)
        mine = keep + swap(give, "col", 1)
        mine = total(total(mine, "col", 2), "row", 1)
        other = swap(mine, "col", 1)

    with jax.named_scope("residual"):
        residual_block, coef, gram = pl.pallas_call(
            functools.partial(residual_kernel, cells),
            out_shape=[
                slab,
                jax.ShapeDtypeStruct((width, basis_rows), f32),
                jax.ShapeDtypeStruct((width // 2, LANES), f32),
            ],
            in_specs=smem(1) + vmem(6),
            out_specs=vmem(3),
            scratch_shapes=[pltpu.VMEM((2,) + half, f32), pltpu.VMEM(padded, f32)],
            compiler_params=limit(24),
        )(place, mine, other, recurrence, mass, current_block, stored)
        coefficients = coef.T.reshape(stored_count + 1, width, width)

    with jax.named_scope("gram"):
        gram = gram + swap(gram, "col", 1)
        gram = total(total(gram, "col", 2), "row", 1)
        gram = jnp.concatenate(
            [gram[:, :width], gram[:, LANES // 2 : LANES // 2 + width]], axis=0
        )
    return (residual_block, coefficients, gram)


def solution(mesh):
    return jax.shard_map(
        local,
        mesh=mesh,
        in_specs=(
            P(None, ("row", "col")),
            P(None, ("row", "col")),
            P(),
            P(None, None, ("row", "col")),
            P(("row", "col")),
            P(("row", "col")),
            P(("row", "col"), None, None),
            P(("row", "col")),
            P(("row", "col")),
            P(("row", "col")),
        ),
        out_specs=(P(None, ("row", "col")), P(), P()),
        check_vma=False,
    )
```

```python
import functools

import jax
import jax.numpy as jnp
from jax import lax
from jax.experimental import pallas as pl
from jax.experimental.pallas import tpu as pltpu
from jax.sharding import PartitionSpec as P

LANES = 128
CHUNK = 32
GROUP = 2
UNROLL = 8
TILE_BIT, SOURCE_BIT, ROW_BIT = 10, 15, 20
NT = (((1,), (1,)), ((), ()))
MIB = 1 << 20


def swap(value, axis, mask):
    count = lax.axis_size(axis)
    return lax.ppermute(value, axis, [(i, i ^ mask) for i in range(count)])


def total(value, axis, step):
    values = [value] + [swap(value, axis, m) for m in range(step, lax.axis_size(axis), step)]
    while len(values) > 1:
        values = [values[i] + values[i + 1] for i in range(0, len(values), 2)]
    return values[0]


def split(value):
    high = value.astype(jnp.bfloat16)
    low = (value - high.astype(jnp.float32)).astype(jnp.bfloat16)
    return high, low


def mm(a, b, dims=(((1,), (0,)), ((), ()))):
    return lax.dot_general(a, b, dims, preferred_element_type=jnp.float32)


def dot_split(a, b, dims=(((1,), (0,)), ((), ()))):
    rows = a.shape[0]
    a_high, a_low = split(a)
    b_high, b_low = split(b)
    both = mm(jnp.concatenate([a_high, a_low], axis=0), b_high, dims)
    return both[:rows] + both[rows:] + mm(a_high, b_low, dims)


def blocks(shape):
    return [(q, k) for q in range(0, shape[0], 8) for k in range(0, shape[1], LANES)]


def early_kernel(
    row_devs,
    col_devs,
    slab_tiles,
    place,
    counts,
    rows_hbm,
    cols_hbm,
    tiles,
    own_panel,
    near_panel,
    out,
    held,
    acc,
    panel_buf,
    rows,
    cols,
    plan,
    tile_sem,
    list_sem,
    panel_sem,
):
    chunks = (counts[0] + CHUNK - 1) // CHUNK
    row_copy = pltpu.make_async_copy(rows_hbm, rows, list_sem.at[0])
    col_copy = pltpu.make_async_copy(cols_hbm, cols, list_sem.at[1])
    row_copy.start()
    col_copy.start()

    def tile_copy(k):
        window = pl.ds(k * CHUNK, CHUNK)
        return pltpu.make_async_copy(tiles.at[window], held.at[window], tile_sem.at[k])

    @pl.loop(0, chunks)
    def _(k):
        tile_copy(k).start()

    copies = load_panels({0: own_panel, 1: near_panel}, panel_buf, panel_sem)
    zero_panel = panel_buf.shape[0] - 1
    panel_buf[zero_panel, :, :LANES] = jnp.zeros((panel_buf.shape[1], LANES), jnp.bfloat16)
    f32, bf16, i32 = jnp.float32, jnp.bfloat16, jnp.int32
    slots, places = rows.shape[1], out.shape[1] - LANES
    targets = row_devs * slab_tiles
    bins = 2 * targets

    def iota(shape, dim):
        return lax.broadcasted_iota(i32, shape, dim)

    slot = iota((1, slots), 1)
    occupied = slot < counts[0]
    earlier = (iota((slots, slots), 0) < iota((slots, slots), 1)).astype(f32).astype(bf16)
    row_copy.wait()
    col_copy.wait()
    row = rows[...]
    row_owner = jnp.floor(row.astype(f32) * (1.0 / slab_tiles)).astype(i32)
    col_f = cols[...].astype(f32)
    source_f = jnp.floor(col_f * (1.0 / slab_tiles))
    source = source_f.astype(i32) ^ place[1]
    tile_f = col_f - slab_tiles * source_f
    far = row_devs - 1 - (row_owner ^ place[0])
    late_bin = targets + far * slab_tiles + row - row_owner * slab_tiles
    bin_of = jnp.where(occupied, jnp.where(source < 2, row, late_bin), -1)
    member = (iota((bins, slots), 0) == bin_of).astype(f32)
    member_bf = member.astype(bf16)
    rank = jnp.sum(member * mm(member_bf, earlier), axis=0, keepdims=True)
    sizes = mm(jnp.ones((8, slots), bf16), member_bf, NT)
    sizes = GROUP * jnp.floor((sizes + (GROUP - 1.0)) * (1.0 / GROUP))
    before = (iota((bins, bins), 1) < iota((bins, bins), 0)).astype(f32)
    begin = jnp.sum(before * sizes[:1], axis=1, keepdims=True)
    position = jnp.sum(member * begin, axis=0, keepdims=True) + rank
    position = jnp.where(occupied, position.astype(i32), -1)
    chosen = (iota((places, slots), 0) == position).astype(f32).astype(bf16)
    slot_f = slot.astype(f32)
    slot_high = jnp.floor(slot_f * (1.0 / 16.0))
    facts = [slot_high, slot_f - 16.0 * slot_high, source.astype(f32), tile_f, row.astype(f32), jnp.ones((1, slots), f32)]
    facts = jnp.concatenate(facts + [jnp.zeros((2, slots), f32)], axis=0).astype(bf16)
    found = mm(facts, chosen, NT).astype(i32)
    source = jnp.where(found[5:6] > 0, found[2:3], col_devs)
    words = (found[4:5] << ROW_BIT) + (source << SOURCE_BIT) + (found[3:4] << TILE_BIT)
    out[:, :places] = words + (found[0:1] << 4) + found[1:2]
    phase = iota((bins, LANES), 1)
    edge = jnp.where(phase > 0, targets + (phase - 1) * slab_tiles, 0)
    inside = (iota((bins, LANES), 0) < edge).astype(f32).astype(bf16)
    out[:, places:] = mm(sizes.astype(bf16), inside)[:1].astype(i32)
    plan_copy = pltpu.make_async_copy(out, plan, list_sem.at[2])
    plan_copy.start()
    acc[...] = jnp.zeros_like(acc)
    for copy in copies + [plan_copy]:
        copy.wait()

    @pl.loop(0, chunks)
    def _(k):
        tile_copy(k).wait()

    add_products(plan, 0, 0, targets, held, panel_buf, acc)


def field(word, low, high):
    return (word >> low) & ((1 << (high - low)) - 1)


def add_products(plan, phase, first_row, spare_row, tiles, panel_buf, acc):
    phases = plan.shape[1] - LANES
    begin, end = plan[0, phases + phase], plan[0, phases + phase + 1]

    def panel(word):
        where = pl.multiple_of(field(word, TILE_BIT, SOURCE_BIT) * LANES, LANES)
        return panel_buf[field(word, SOURCE_BIT, ROW_BIT), :, pl.ds(where, LANES)]

    @pl.loop(0, (end - begin + GROUP * UNROLL - 1) // (GROUP * UNROLL))
    def _(g):
        first = begin + g * GROUP * UNROLL
        parts = []
        for u in range(UNROLL):
            words = [plan[0, first + GROUP * u + i] for i in range(GROUP)]
            left = jnp.concatenate([panel(word) for word in words], axis=1)
            right = jnp.concatenate([tiles[field(word, 0, TILE_BIT)] for word in words], axis=1)
            parts.append(mm(left, right, NT))
        for u in range(UNROLL):
            p = first + GROUP * u
            a = jnp.where(p < end, (plan[0, p] >> ROW_BIT) - first_row, spare_row)
            acc[a] += parts[u]


def load_panels(panels, panel_buf, sem):
    copies = [pltpu.make_async_copy(ref, panel_buf.at[m], sem.at[i]) for i, (m, ref) in enumerate(panels.items())]
    for copy in copies:
        copy.start()
    return copies


def collect_kernel(masks, *refs):
    panels, (_, panel_buf, sem) = refs[: len(masks)], refs[len(masks) :]
    for copy in load_panels(dict(zip(masks, panels)), panel_buf, sem):
        copy.wait()


def first_late_kernel(masks, odd, place, plan, *refs):
    panels = dict(zip(odd, refs))
    tiles, early, _ = refs[len(odd) : len(odd) + 3]
    sends = refs[len(odd) + 3 : -3]
    panel_buf, acc, sem = refs[-3:]
    copies = load_panels(panels, panel_buf, sem)
    for mask, send in zip(late_masks(masks, place), sends):
        late_part(mask, place, plan, tiles, early, panel_buf, acc, copies)
        put(send, acc)
        copies = ()


def late_masks(masks, place):
    inner = (place[0] == 1) | (place[0] == 2)
    change = {"x": jnp.where(inner, 1, 2), "y": jnp.where(inner, 2, 1)}
    return [change.get(mask, mask) for mask in masks]


def late_kernel(masks, place, plan, panel_buf, tiles, early, current, previous, coupling, diag, *refs):
    sends, base, acc = refs[:-2], refs[-2], refs[-1]
    for mask, send in zip(late_masks(masks, place), sends):
        late_part(mask, place, plan, tiles, early, panel_buf, acc, ())
        put(send, acc)
    late_part(0, place, plan, tiles, early, panel_buf, acc, ())
    put(base, acc)
    base[...] += diag[...] * current[...] - jnp.dot(
        coupling[...],
        previous[...],
        precision=lax.Precision.HIGHEST,
        preferred_element_type=jnp.float32,
    )


def late_part(mask, place, plan, tiles, early, panel_buf, acc, copies):
    slab_tiles = acc.shape[0] - 1
    row_devs = (early.shape[0] - 1) // slab_tiles
    first_row = (place[0] ^ mask) * slab_tiles
    for s in range(slab_tiles):
        acc[s] = early[first_row + s]
    for copy in copies:
        copy.wait()
    add_products(plan, row_devs - mask, first_row, slab_tiles, tiles, panel_buf, acc)


def put(out, acc):
    for s in range(acc.shape[0] - 1):
        out[:, s * LANES : (s + 1) * LANES] = acc[s].astype(out.dtype)


def coefficient_kernel(cells, received_count, place, base, *refs):
    received = refs[:received_count]
    mass, current, stored, recurrence, keep, give, halves = refs[received_count:]
    total = base[...]
    for ref in received:
        total = total + ref[...].astype(jnp.float32)
    recurrence[...] = total
    weighted = total * (mass[...] * (1.0 / cells))
    basis = jnp.concatenate([current[...], stored[...]], axis=0)
    coef = dot_split(weighted, basis, NT)
    spare = -coef.shape[1] % LANES
    coef = jnp.concatenate([coef, jnp.zeros((coef.shape[0], spare), jnp.float32)], axis=1)
    halves[...] = jnp.zeros_like(halves)
    for p, (q, k) in enumerate(blocks(coef.shape)):
        halves[p // halves.shape[1], p % halves.shape[1]] = coef[q : q + 8, k : k + LANES]
    core = place[1] & 1
    keep[...] = halves[core]
    give[...] = halves[1 - core]


def residual_kernel(
    cells, place, mine, other, recurrence, mass, current, stored, residual, coef_out, gram, halves, packed
):
    width = recurrence.shape[0]
    core = place[1] & 1
    halves[core] = mine[...]
    halves[1 - core] = other[...]
    for p, (q, k) in enumerate(blocks(packed.shape)):
        packed[q : q + 8, k : k + LANES] = halves[p // halves.shape[1], p % halves.shape[1]]
    coef = packed[...]
    basis = jnp.concatenate([current[...], stored[...]], axis=0)
    coef = coef[:, : basis.shape[0]]
    coef_out[...] = coef
    value = recurrence[...] - dot_split(coef, basis)
    residual[...] = value
    local = dot_split(value * (mass[...] * (1.0 / cells)), value, NT)
    half = width // 2
    gram[...] = jnp.zeros_like(gram)
    gram[:, :width] = local[:half]
    gram[:, LANES // 2 : LANES // 2 + width] = local[half:]


def after_kernel(value, earlier, out):
    pass


def after(value, earlier):
    anywhere = pl.BlockSpec(memory_space=pl.ANY)
    return pl.pallas_call(
        after_kernel,
        out_shape=jax.ShapeDtypeStruct(value.shape, value.dtype),
        in_specs=[anywhere, anywhere],
        out_specs=anywhere,
        input_output_aliases={0: 0},
        compiler_params=limit(1),
    )(value, earlier)


def in_hbm(value):
    return pltpu.with_memory_space_constraint(value, pltpu.HBM)


def limit(mib):
    return pltpu.CompilerParams(vmem_limit_bytes=mib * MIB)


def vmem(count):
    return [pl.BlockSpec(memory_space=pltpu.VMEM)] * count


def smem(count):
    return [pl.BlockSpec(memory_space=pltpu.SMEM)] * count


def local(
    current_block,
    previous_block,
    previous_coupling,
    stored_blocks,
    stiffness_diag,
    lumped_mass,
    tile_values,
    tile_rows,
    tile_cols,
    tile_counts,
):
    row_devs = lax.axis_size("row")
    col_devs = lax.axis_size("col")
    width, slab_len = current_block.shape
    stored_count = stored_blocks.shape[0]
    slots, tile_len, _ = tile_values.shape
    slab_tiles = slab_len // tile_len
    cells = slab_len * row_devs * col_devs
    f32, bf16 = jnp.float32, jnp.bfloat16
    place = jnp.stack([lax.axis_index("row"), lax.axis_index("col")]).astype(jnp.int32)
    stored = stored_blocks.reshape(stored_count * width, slab_len)
    mass = lumped_mass.reshape(1, slab_len)
    diag = stiffness_diag.reshape(1, slab_len)
    slab = jax.ShapeDtypeStruct((width, slab_len), f32)

    targets = row_devs * slab_tiles
    anywhere = [pl.BlockSpec(memory_space=pl.ANY)]
    panel_shape = (col_devs + 1, width, slab_len)
    early_shape = (targets + 1, width, tile_len)
    part_acc = pltpu.VMEM((slab_tiles + 1, width, tile_len), f32)

    def cost(flops):
        return pl.CostEstimate(flops=flops, bytes_accessed=flops // width, transcendentals=0)

    with jax.named_scope("gather"):
        rounded = current_block.astype(bf16)
        panels = [rounded] + [None] * (col_devs - 1)
        for m in range(col_devs - 2, 0, -2):
            panels[m] = swap(rounded, "col", m)
        panels[1] = swap(rounded, "col", 1)

    with jax.named_scope("early"):
        places = -(-(slots + (GROUP - 1) * 2 * targets + GROUP * UNROLL) // LANES) * LANES
        plan_shape = (1, places + LANES)
        plan, held, early, gathered = pl.pallas_call(
            functools.partial(early_kernel, row_devs, col_devs, slab_tiles),
            out_shape=[
                jax.ShapeDtypeStruct(plan_shape, jnp.int32),
                pltpu.VMEM(tile_values.shape, bf16),
                pltpu.VMEM(early_shape, f32),
                pltpu.VMEM(panel_shape, bf16),
            ],
            in_specs=smem(2) + [pl.BlockSpec(memory_space=pltpu.HBM)] * 3 + anywhere * 2,
            out_specs=vmem(4),
            scratch_shapes=[
                pltpu.VMEM((1, slots), jnp.int32),
                pltpu.VMEM((1, slots), jnp.int32),
                pltpu.SMEM(plan_shape, jnp.int32),
                pltpu.SemaphoreType.DMA((slots // CHUNK,)),
                pltpu.SemaphoreType.DMA((3,)),
                pltpu.SemaphoreType.DMA((2,)),
            ],
            compiler_params=limit(12),
            cost_estimate=cost(2 * slots * width * tile_len * tile_len),
        )(
            place,
            tile_counts,
            in_hbm(tile_rows.reshape(1, slots)),
            in_hbm(tile_cols.reshape(1, slots)),
            in_hbm(tile_values),
            panels[0],
            panels[1],
        )

    with jax.named_scope("gather"):
        for m in range(col_devs - 2, 0, -2):
            panels[m] = after(panels[m], early)
            panels[m + 1] = swap(panels[m], "col", 1)
        even, odd = list(range(2, col_devs, 2)), list(range(3, col_devs, 2))
        gathered = pl.pallas_call(
            functools.partial(collect_kernel, even),
            out_shape=pltpu.VMEM(panel_shape, bf16),
            in_specs=anywhere * len(even) + vmem(1),
            out_specs=vmem(1)[0],
            scratch_shapes=[pltpu.SemaphoreType.DMA((len(even),))],
            input_output_aliases={len(even): 0},
            compiler_params=limit(1),
            cost_estimate=cost(width),
        )(*[panels[m] for m in even], gathered)

    with jax.named_scope("late"):
        relay = row_devs == 4
        first_masks = [3, "x"] if relay else [row_devs - 1]
        last_masks = ["y"] if relay else list(range(row_devs - 2, 0, -1))
        part = jax.ShapeDtypeStruct((width, slab_len), bf16)
        *firsts, gathered = pl.pallas_call(
            functools.partial(first_late_kernel, first_masks, odd),
            out_shape=[part] * len(first_masks) + [pltpu.VMEM(panel_shape, bf16)],
            in_specs=smem(2) + anywhere * len(odd) + vmem(3),
            out_specs=vmem(len(first_masks) + 1),
            scratch_shapes=[part_acc, pltpu.SemaphoreType.DMA((len(odd),))],
            input_output_aliases={4 + len(odd): len(first_masks)},
            compiler_params=limit(8),
            cost_estimate=cost(width),
        )(place, plan, *[panels[m] for m in odd], held, early, gathered)
        lasts = [slab] if relay else [part] * len(last_masks)
        *lasts, base = pl.pallas_call(
            functools.partial(late_kernel, last_masks),
            out_shape=lasts + [slab],
            in_specs=smem(2) + vmem(7),
            out_specs=vmem(len(lasts) + 1),
            scratch_shapes=[part_acc],
            compiler_params=limit(8),
            cost_estimate=cost(width),
        )(place, plan, gathered, held, early, current_block, previous_block, previous_coupling, diag)
        if relay:
            passing = lax.ppermute(firsts[0], "row", [(0, 1), (3, 2)])
            received = [lax.ppermute(firsts[0], "row", [(1, 2), (2, 1)])]
            received.append(lax.ppermute(firsts[1], "row", [(0, 2), (3, 1), (1, 0), (2, 3)]))
            joined = (lasts[0] + passing.astype(f32)).astype(bf16)
            received.append(lax.ppermute(joined, "row", [(0, 1), (1, 3), (3, 2), (2, 0)]))
        else:
            received = [swap(firsts[0], "row", first_masks[0])]
            received += [swap(last, "row", m) for m, last in zip(last_masks, lasts)]

    basis_rows = (stored_count + 1) * width
    padded = (width, -(-basis_rows // LANES) * LANES)
    half = (-(-len(blocks(padded)) // 2), 8, LANES)
    with jax.named_scope("coefficients"):
        recurrence, keep, give = pl.pallas_call(
            functools.partial(coefficient_kernel, cells, len(received)),
            out_shape=[slab] + [jax.ShapeDtypeStruct(half, f32)] * 2,
            in_specs=smem(1) + vmem(len(received) + 4),
            out_specs=vmem(3),
            scratch_shapes=[pltpu.VMEM((2,) + half, f32)],
            compiler_params=limit(24),
        )(place, base, *received, mass, current_block, stored)
        mine = keep + swap(give, "col", 1)
        mine = total(total(mine, "col", 2), "row", 1)
        other = swap(mine, "col", 1)

    with jax.named_scope("residual"):
        residual_block, coef, gram = pl.pallas_call(
            functools.partial(residual_kernel, cells),
            out_shape=[
                slab,
                jax.ShapeDtypeStruct((width, basis_rows), f32),
                jax.ShapeDtypeStruct((width // 2, LANES), f32),
            ],
            in_specs=smem(1) + vmem(6),
            out_specs=vmem(3),
            scratch_shapes=[pltpu.VMEM((2,) + half, f32), pltpu.VMEM(padded, f32)],
            compiler_params=limit(24),
        )(place, mine, other, recurrence, mass, current_block, stored)
        coefficients = coef.T.reshape(stored_count + 1, width, width)

    with jax.named_scope("gram"):
        gram = gram + swap(gram, "col", 1)
        gram = total(total(gram, "col", 2), "row", 1)
        gram = jnp.concatenate(
            [gram[:, :width], gram[:, LANES // 2 : LANES // 2 + width]], axis=0
        )
    return (residual_block, coefficients, gram)


def solution(mesh):
    return jax.shard_map(
        local,
        mesh=mesh,
        in_specs=(
            P(None, ("row", "col")),
            P(None, ("row", "col")),
            P(),
            P(None, None, ("row", "col")),
            P(("row", "col")),
            P(("row", "col")),
            P(("row", "col"), None, None),
            P(("row", "col")),
            P(("row", "col")),
            P(("row", "col")),
        ),
        out_specs=(P(None, ("row", "col")), P(), P()),
        check_vma=False,
    )
```

```python
import functools

import jax
import jax.numpy as jnp
from jax import lax
from jax.experimental import pallas as pl
from jax.experimental.pallas import tpu as pltpu
from jax.sharding import PartitionSpec as P

LANES = 128
CHUNK = 32
GROUP = 2
UNROLL = 8
TILE_BIT, SOURCE_BIT, ROW_BIT = 10, 15, 20
NT = (((1,), (1,)), ((), ()))
MIB = 1 << 20


def swap(value, axis, mask):
    count = lax.axis_size(axis)
    return lax.ppermute(value, axis, [(i, i ^ mask) for i in range(count)])


def total(value, axis, step):
    values = [value] + [swap(value, axis, m) for m in range(step, lax.axis_size(axis), step)]
    while len(values) > 1:
        values = [values[i] + values[i + 1] for i in range(0, len(values), 2)]
    return values[0]


def split(value):
    high = value.astype(jnp.bfloat16)
    low = (value - high.astype(jnp.float32)).astype(jnp.bfloat16)
    return high, low


def mm(a, b, dims=(((1,), (0,)), ((), ()))):
    return lax.dot_general(a, b, dims, preferred_element_type=jnp.float32)


def dot_split(a, b_parts, dims=(((1,), (0,)), ((), ()))):
    rows = a.shape[0]
    a_high, a_low = split(a)
    b_high, b_low = b_parts
    both = mm(jnp.concatenate([a_high, a_low], axis=0), b_high, dims)
    return both[:rows] + both[rows:] + mm(a_high, b_low, dims)


def blocks(shape):
    return [(q, k) for q in range(0, shape[0], 8) for k in range(0, shape[1], LANES)]


def early_kernel(
    row_devs,
    col_devs,
    slab_tiles,
    place,
    counts,
    rows_hbm,
    cols_hbm,
    tiles,
    own_panel,
    near_panel,
    out,
    held,
    acc,
    panel_buf,
    rows,
    cols,
    plan,
    tile_sem,
    list_sem,
    panel_sem,
):
    chunks = (counts[0] + CHUNK - 1) // CHUNK
    row_copy = pltpu.make_async_copy(rows_hbm, rows, list_sem.at[0])
    col_copy = pltpu.make_async_copy(cols_hbm, cols, list_sem.at[1])
    row_copy.start()
    col_copy.start()

    def tile_copy(k):
        window = pl.ds(k * CHUNK, CHUNK)
        return pltpu.make_async_copy(tiles.at[window], held.at[window], tile_sem.at[k])

    @pl.loop(0, chunks)
    def _(k):
        tile_copy(k).start()

    copies = load_panels({0: own_panel, 1: near_panel}, panel_buf, panel_sem)
    zero_panel = panel_buf.shape[0] - 1
    panel_buf[zero_panel, :, :LANES] = jnp.zeros((panel_buf.shape[1], LANES), jnp.bfloat16)
    f32, bf16, i32 = jnp.float32, jnp.bfloat16, jnp.int32
    slots, places = rows.shape[1], out.shape[1] - LANES
    targets = row_devs * slab_tiles
    bins = 2 * targets

    def iota(shape, dim):
        return lax.broadcasted_iota(i32, shape, dim)

    slot = iota((1, slots), 1)
    occupied = slot < counts[0]
    earlier = (iota((slots, slots), 0) < iota((slots, slots), 1)).astype(f32).astype(bf16)
    row_copy.wait()
    col_copy.wait()
    row = rows[...]
    row_owner = jnp.floor(row.astype(f32) * (1.0 / slab_tiles)).astype(i32)
    col_f = cols[...].astype(f32)
    source_f = jnp.floor(col_f * (1.0 / slab_tiles))
    source = source_f.astype(i32) ^ place[1]
    tile_f = col_f - slab_tiles * source_f
    far = row_devs - 1 - (row_owner ^ place[0])
    late_bin = targets + far * slab_tiles + row - row_owner * slab_tiles
    bin_of = jnp.where(occupied, jnp.where(source < 2, row, late_bin), -1)
    member = (iota((bins, slots), 0) == bin_of).astype(f32)
    member_bf = member.astype(bf16)
    rank = jnp.sum(member * mm(member_bf, earlier), axis=0, keepdims=True)
    sizes = mm(jnp.ones((8, slots), bf16), member_bf, NT)
    sizes = GROUP * jnp.floor((sizes + (GROUP - 1.0)) * (1.0 / GROUP))
    before = (iota((bins, bins), 1) < iota((bins, bins), 0)).astype(f32)
    begin = jnp.sum(before * sizes[:1], axis=1, keepdims=True)
    position = jnp.sum(member * begin, axis=0, keepdims=True) + rank
    position = jnp.where(occupied, position.astype(i32), -1)
    chosen = (iota((places, slots), 0) == position).astype(f32).astype(bf16)
    slot_f = slot.astype(f32)
    slot_high = jnp.floor(slot_f * (1.0 / 16.0))
    facts = [slot_high, slot_f - 16.0 * slot_high, source.astype(f32), tile_f, row.astype(f32), jnp.ones((1, slots), f32)]
    facts = jnp.concatenate(facts + [jnp.zeros((2, slots), f32)], axis=0).astype(bf16)
    found = mm(facts, chosen, NT).astype(i32)
    source = jnp.where(found[5:6] > 0, found[2:3], col_devs)
    words = (found[4:5] << ROW_BIT) + (source << SOURCE_BIT) + (found[3:4] << TILE_BIT)
    out[:, :places] = words + (found[0:1] << 4) + found[1:2]
    phase = iota((bins, LANES), 1)
    edge = jnp.where(phase > 0, targets + (phase - 1) * slab_tiles, 0)
    inside = (iota((bins, LANES), 0) < edge).astype(f32).astype(bf16)
    out[:, places:] = mm(sizes.astype(bf16), inside)[:1].astype(i32)
    plan_copy = pltpu.make_async_copy(out, plan, list_sem.at[2])
    plan_copy.start()
    acc[...] = jnp.zeros_like(acc)
    for copy in copies + [plan_copy]:
        copy.wait()

    @pl.loop(0, chunks)
    def _(k):
        tile_copy(k).wait()

    add_products(plan, 0, 0, targets, held, panel_buf, acc)


def field(word, low, high):
    return (word >> low) & ((1 << (high - low)) - 1)


def add_products(plan, phase, first_row, spare_row, tiles, panel_buf, acc):
    phases = plan.shape[1] - LANES
    begin, end = plan[0, phases + phase], plan[0, phases + phase + 1]

    def panel(word):
        where = pl.multiple_of(field(word, TILE_BIT, SOURCE_BIT) * LANES, LANES)
        return panel_buf[field(word, SOURCE_BIT, ROW_BIT), :, pl.ds(where, LANES)]

    @pl.loop(0, (end - begin + GROUP * UNROLL - 1) // (GROUP * UNROLL))
    def _(g):
        first = begin + g * GROUP * UNROLL
        parts = []
        for u in range(UNROLL):
            words = [plan[0, first + GROUP * u + i] for i in range(GROUP)]
            left = jnp.concatenate([panel(word) for word in words], axis=1)
            right = jnp.concatenate([tiles[field(word, 0, TILE_BIT)] for word in words], axis=1)
            parts.append(mm(left, right, NT))
        for u in range(UNROLL):
            p = first + GROUP * u
            a = jnp.where(p < end, (plan[0, p] >> ROW_BIT) - first_row, spare_row)
            acc[a] += parts[u]


def load_panels(panels, panel_buf, sem):
    copies = [pltpu.make_async_copy(ref, panel_buf.at[m], sem.at[i]) for i, (m, ref) in enumerate(panels.items())]
    for copy in copies:
        copy.start()
    return copies


def collect_kernel(masks, *refs):
    panels, (_, panel_buf, sem) = refs[: len(masks)], refs[len(masks) :]
    for copy in load_panels(dict(zip(masks, panels)), panel_buf, sem):
        copy.wait()


def first_late_kernel(masks, odd, place, plan, *refs):
    panels = dict(zip(odd, refs))
    tiles, early, _ = refs[len(odd) : len(odd) + 3]
    sends = refs[len(odd) + 3 : -3]
    panel_buf, acc, sem = refs[-3:]
    copies = load_panels(panels, panel_buf, sem)
    for mask, send in zip(late_masks(masks, place), sends):
        late_part(mask, place, plan, tiles, early, panel_buf, acc, copies)
        put(send, acc)
        copies = ()


def late_masks(masks, place):
    inner = (place[0] == 1) | (place[0] == 2)
    change = {"x": jnp.where(inner, 1, 2), "y": jnp.where(inner, 2, 1)}
    return [change.get(mask, mask) for mask in masks]


def late_kernel(masks, place, plan, panel_buf, tiles, early, *refs):
    sends, acc = refs[:-1], refs[-1]
    for mask, send in zip(late_masks(masks, place), sends):
        late_part(mask, place, plan, tiles, early, panel_buf, acc, ())
        put(send, acc)


def own_kernel(
    place, plan, panel_buf, tiles, early, current, previous, coupling, diag, stored, base, basis_high, basis_low, acc
):
    late_part(0, place, plan, tiles, early, panel_buf, acc, ())
    put(base, acc)
    base[...] += diag[...] * current[...] - jnp.dot(
        coupling[...],
        previous[...],
        precision=lax.Precision.HIGHEST,
        preferred_element_type=jnp.float32,
    )
    width = current.shape[0]
    basis_high[:width], basis_low[:width] = split(current[...])
    basis_high[width:], basis_low[width:] = split(stored[...])


def late_part(mask, place, plan, tiles, early, panel_buf, acc, copies):
    slab_tiles = acc.shape[0] - 1
    row_devs = (early.shape[0] - 1) // slab_tiles
    first_row = (place[0] ^ mask) * slab_tiles
    for s in range(slab_tiles):
        acc[s] = early[first_row + s]
    for copy in copies:
        copy.wait()
    add_products(plan, row_devs - mask, first_row, slab_tiles, tiles, panel_buf, acc)


def put(out, acc):
    for s in range(acc.shape[0] - 1):
        out[:, s * LANES : (s + 1) * LANES] = acc[s].astype(out.dtype)


def coefficient_kernel(cells, received_count, place, base, *refs):
    received = refs[:received_count]
    mass, basis_high, basis_low, recurrence, keep, give, halves = refs[received_count:]
    total = base[...]
    for ref in received:
        total = total + ref[...].astype(jnp.float32)
    recurrence[...] = total
    weighted = total * (mass[...] * (1.0 / cells))
    coef = dot_split(weighted, (basis_high[...], basis_low[...]), NT)
    spare = -coef.shape[1] % LANES
    coef = jnp.concatenate([coef, jnp.zeros((coef.shape[0], spare), jnp.float32)], axis=1)
    halves[...] = jnp.zeros_like(halves)
    for p, (q, k) in enumerate(blocks(coef.shape)):
        halves[p // halves.shape[1], p % halves.shape[1]] = coef[q : q + 8, k : k + LANES]
    core = place[1] & 1
    keep[...] = halves[core]
    give[...] = halves[1 - core]


def residual_kernel(
    cells, place, mine, other, recurrence, mass, basis_high, basis_low, residual, coef_out, gram, halves, packed
):
    width = recurrence.shape[0]
    core = place[1] & 1
    halves[core] = mine[...]
    halves[1 - core] = other[...]
    for p, (q, k) in enumerate(blocks(packed.shape)):
        packed[q : q + 8, k : k + LANES] = halves[p // halves.shape[1], p % halves.shape[1]]
    coef = packed[...]
    coef = coef[:, : basis_high.shape[0]]
    coef_out[...] = coef
    value = recurrence[...] - dot_split(coef, (basis_high[...], basis_low[...]))
    residual[...] = value
    local = dot_split(value * (mass[...] * (1.0 / cells)), split(value), NT)
    half = width // 2
    gram[...] = jnp.zeros_like(gram)
    gram[:, :width] = local[:half]
    gram[:, LANES // 2 : LANES // 2 + width] = local[half:]


def after_kernel(value, earlier, out):
    pass


def after(value, earlier):
    anywhere = pl.BlockSpec(memory_space=pl.ANY)
    return pl.pallas_call(
        after_kernel,
        out_shape=jax.ShapeDtypeStruct(value.shape, value.dtype),
        in_specs=[anywhere, anywhere],
        out_specs=anywhere,
        input_output_aliases={0: 0},
        compiler_params=limit(1),
    )(value, earlier)


def in_hbm(value):
    return pltpu.with_memory_space_constraint(value, pltpu.HBM)


def limit(mib):
    return pltpu.CompilerParams(vmem_limit_bytes=mib * MIB)


def vmem(count):
    return [pl.BlockSpec(memory_space=pltpu.VMEM)] * count


def smem(count):
    return [pl.BlockSpec(memory_space=pltpu.SMEM)] * count


def local(
    current_block,
    previous_block,
    previous_coupling,
    stored_blocks,
    stiffness_diag,
    lumped_mass,
    tile_values,
    tile_rows,
    tile_cols,
    tile_counts,
):
    row_devs = lax.axis_size("row")
    col_devs = lax.axis_size("col")
    width, slab_len = current_block.shape
    stored_count = stored_blocks.shape[0]
    slots, tile_len, _ = tile_values.shape
    slab_tiles = slab_len // tile_len
    cells = slab_len * row_devs * col_devs
    f32, bf16 = jnp.float32, jnp.bfloat16
    place = jnp.stack([lax.axis_index("row"), lax.axis_index("col")]).astype(jnp.int32)
    stored = stored_blocks.reshape(stored_count * width, slab_len)
    mass = lumped_mass.reshape(1, slab_len)
    diag = stiffness_diag.reshape(1, slab_len)
    slab = jax.ShapeDtypeStruct((width, slab_len), f32)

    targets = row_devs * slab_tiles
    anywhere = [pl.BlockSpec(memory_space=pl.ANY)]
    panel_shape = (col_devs + 1, width, slab_len)
    early_shape = (targets + 1, width, tile_len)
    part_acc = pltpu.VMEM((slab_tiles + 1, width, tile_len), f32)

    def cost(flops):
        return pl.CostEstimate(flops=flops, bytes_accessed=flops // width, transcendentals=0)

    with jax.named_scope("gather"):
        rounded = current_block.astype(bf16)
        panels = [rounded] + [None] * (col_devs - 1)
        for m in range(col_devs - 2, 0, -2):
            panels[m] = swap(rounded, "col", m)
        panels[1] = swap(rounded, "col", 1)

    with jax.named_scope("early"):
        places = -(-(slots + (GROUP - 1) * 2 * targets + GROUP * UNROLL) // LANES) * LANES
        plan_shape = (1, places + LANES)
        plan, held, early, gathered = pl.pallas_call(
            functools.partial(early_kernel, row_devs, col_devs, slab_tiles),
            out_shape=[
                jax.ShapeDtypeStruct(plan_shape, jnp.int32),
                pltpu.VMEM(tile_values.shape, bf16),
                pltpu.VMEM(early_shape, f32),
                pltpu.VMEM(panel_shape, bf16),
            ],
            in_specs=smem(2) + [pl.BlockSpec(memory_space=pltpu.HBM)] * 3 + anywhere * 2,
            out_specs=vmem(4),
            scratch_shapes=[
                pltpu.VMEM((1, slots), jnp.int32),
                pltpu.VMEM((1, slots), jnp.int32),
                pltpu.SMEM(plan_shape, jnp.int32),
                pltpu.SemaphoreType.DMA((slots // CHUNK,)),
                pltpu.SemaphoreType.DMA((3,)),
                pltpu.SemaphoreType.DMA((2,)),
            ],
            compiler_params=limit(12),
            cost_estimate=cost(2 * slots * width * tile_len * tile_len),
        )(
            place,
            tile_counts,
            in_hbm(tile_rows.reshape(1, slots)),
            in_hbm(tile_cols.reshape(1, slots)),
            in_hbm(tile_values),
            panels[0],
            panels[1],
        )

    with jax.named_scope("gather"):
        for m in range(col_devs - 2, 0, -2):
            panels[m] = after(panels[m], early)
            panels[m + 1] = swap(panels[m], "col", 1)
        even, odd = list(range(2, col_devs, 2)), list(range(3, col_devs, 2))
        gathered = pl.pallas_call(
            functools.partial(collect_kernel, even),
            out_shape=pltpu.VMEM(panel_shape, bf16),
            in_specs=anywhere * len(even) + vmem(1),
            out_specs=vmem(1)[0],
            scratch_shapes=[pltpu.SemaphoreType.DMA((len(even),))],
            input_output_aliases={len(even): 0},
            compiler_params=limit(1),
            cost_estimate=cost(width),
        )(*[panels[m] for m in even], gathered)

    with jax.named_scope("late"):
        relay = row_devs == 4
        others = ["x", "y"] if relay else list(range(row_devs - 2, 0, -1))
        part = jax.ShapeDtypeStruct((width, slab_len), bf16)
        first, gathered = pl.pallas_call(
            functools.partial(first_late_kernel, [row_devs - 1], odd),
            out_shape=[part, pltpu.VMEM(panel_shape, bf16)],
            in_specs=smem(2) + anywhere * len(odd) + vmem(3),
            out_specs=vmem(2),
            scratch_shapes=[part_acc, pltpu.SemaphoreType.DMA((len(odd),))],
            input_output_aliases={4 + len(odd): 1},
            compiler_params=limit(8),
            cost_estimate=cost(width),
        )(place, plan, *[panels[m] for m in odd], held, early, gathered)
        parts = pl.pallas_call(
            functools.partial(late_kernel, others),
            out_shape=[part, slab] if relay else [part] * len(others),
            in_specs=smem(2) + vmem(3),
            out_specs=vmem(len(others)),
            scratch_shapes=[part_acc],
            compiler_params=limit(8),
            cost_estimate=cost(width),
        )(place, plan, gathered, held, early)
        if relay:
            passing = lax.ppermute(first, "row", [(0, 1), (3, 2)])
            received = [lax.ppermute(first, "row", [(1, 2), (2, 1)])]
            received.append(lax.ppermute(parts[0], "row", [(0, 2), (3, 1), (1, 0), (2, 3)]))
            joined = (parts[1] + passing.astype(f32)).astype(bf16)
            received.append(lax.ppermute(joined, "row", [(0, 1), (1, 3), (3, 2), (2, 0)]))
        else:
            received = [swap(first, "row", row_devs - 1)]
            received += [swap(part, "row", m) for m, part in zip(others, parts)]
        basis_part = pltpu.VMEM(((stored_count + 1) * width, slab_len), bf16)
        base, *basis = pl.pallas_call(
            own_kernel,
            out_shape=[slab, basis_part, basis_part],
            in_specs=smem(2) + vmem(8),
            out_specs=vmem(3),
            scratch_shapes=[part_acc],
            compiler_params=limit(8),
            cost_estimate=cost(width),
        )(place, plan, gathered, held, early, current_block, previous_block, previous_coupling, diag, stored)

    basis_rows = (stored_count + 1) * width
    padded = (width, -(-basis_rows // LANES) * LANES)
    half = (-(-len(blocks(padded)) // 2), 8, LANES)
    with jax.named_scope("coefficients"):
        recurrence, keep, give = pl.pallas_call(
            functools.partial(coefficient_kernel, cells, len(received)),
            out_shape=[slab] + [jax.ShapeDtypeStruct(half, f32)] * 2,
            in_specs=smem(1) + vmem(len(received) + 4),
            out_specs=vmem(3),
            scratch_shapes=[pltpu.VMEM((2,) + half, f32)],
            compiler_params=limit(12),
        )(place, base, *received, mass, *basis)
        mine = keep + swap(give, "col", 1)
        mine = total(total(mine, "col", 2), "row", 1)
        other = swap(mine, "col", 1)

    with jax.named_scope("residual"):
        residual_block, coef, gram = pl.pallas_call(
            functools.partial(residual_kernel, cells),
            out_shape=[
                slab,
                jax.ShapeDtypeStruct((width, basis_rows), f32),
                jax.ShapeDtypeStruct((width // 2, LANES), f32),
            ],
            in_specs=smem(1) + vmem(6),
            out_specs=vmem(3),
            scratch_shapes=[pltpu.VMEM((2,) + half, f32), pltpu.VMEM(padded, f32)],
            compiler_params=limit(12),
        )(place, mine, other, recurrence, mass, *basis)
        coefficients = coef.T.reshape(stored_count + 1, width, width)

    with jax.named_scope("gram"):
        gram = gram + swap(gram, "col", 1)
        gram = total(total(gram, "col", 2), "row", 1)
        gram = jnp.concatenate(
            [gram[:, :width], gram[:, LANES // 2 : LANES // 2 + width]], axis=0
        )
    return (residual_block, coefficients, gram)


def solution(mesh):
    return jax.shard_map(
        local,
        mesh=mesh,
        in_specs=(
            P(None, ("row", "col")),
            P(None, ("row", "col")),
            P(),
            P(None, None, ("row", "col")),
            P(("row", "col")),
            P(("row", "col")),
            P(("row", "col"), None, None),
            P(("row", "col")),
            P(("row", "col")),
            P(("row", "col")),
        ),
        out_specs=(P(None, ("row", "col")), P(), P()),
        check_vma=False,
    )
```

```python
import functools

import jax
import jax.numpy as jnp
from jax import lax
from jax.experimental import pallas as pl
from jax.experimental.pallas import tpu as pltpu
from jax.sharding import PartitionSpec as P

LANES = 128
CHUNK = 32
GROUP = 2
UNROLL = 8
TILE_BIT, SOURCE_BIT, ROW_BIT = 10, 15, 20
NT = (((1,), (1,)), ((), ()))
MIB = 1 << 20


def swap(value, axis, mask):
    count = lax.axis_size(axis)
    return lax.ppermute(value, axis, [(i, i ^ mask) for i in range(count)])


def total(value, axis, step):
    values = [value] + [swap(value, axis, m) for m in range(step, lax.axis_size(axis), step)]
    while len(values) > 1:
        values = [values[i] + values[i + 1] for i in range(0, len(values), 2)]
    return values[0]


def split(value):
    high = value.astype(jnp.bfloat16)
    low = (value - high.astype(jnp.float32)).astype(jnp.bfloat16)
    return high, low


def mm(a, b, dims=(((1,), (0,)), ((), ()))):
    return lax.dot_general(a, b, dims, preferred_element_type=jnp.float32)


def dot_split(a, b, dims=(((1,), (0,)), ((), ()))):
    rows = a.shape[0]
    a_high, a_low = split(a)
    b_high, b_low = split(b)
    both = mm(jnp.concatenate([a_high, a_low], axis=0), b_high, dims)
    return both[:rows] + both[rows:] + mm(a_high, b_low, dims)


def blocks(shape):
    return [(q, k) for q in range(0, shape[0], 8) for k in range(0, shape[1], LANES)]


def early_kernel(
    row_devs,
    col_devs,
    slab_tiles,
    place,
    counts,
    rows_hbm,
    cols_hbm,
    tiles,
    own_panel,
    near_panel,
    out,
    held,
    acc,
    panel_buf,
    rows,
    cols,
    plan,
    tile_sem,
    list_sem,
    panel_sem,
):
    chunks = (counts[0] + CHUNK - 1) // CHUNK
    row_copy = pltpu.make_async_copy(rows_hbm, rows, list_sem.at[0])
    col_copy = pltpu.make_async_copy(cols_hbm, cols, list_sem.at[1])
    row_copy.start()
    col_copy.start()

    def tile_copy(k):
        window = pl.ds(k * CHUNK, CHUNK)
        return pltpu.make_async_copy(tiles.at[window], held.at[window], tile_sem.at[k])

    @pl.loop(0, chunks)
    def _(k):
        tile_copy(k).start()

    copies = load_panels({0: own_panel, 1: near_panel}, panel_buf, panel_sem)
    zero_panel = panel_buf.shape[0] - 1
    panel_buf[zero_panel, :, :LANES] = jnp.zeros((panel_buf.shape[1], LANES), jnp.bfloat16)
    f32, bf16, i32 = jnp.float32, jnp.bfloat16, jnp.int32
    slots, places = rows.shape[1], out.shape[1] - LANES
    targets = row_devs * slab_tiles
    bins = 2 * targets

    def iota(shape, dim):
        return lax.broadcasted_iota(i32, shape, dim)

    slot = iota((1, slots), 1)
    occupied = slot < counts[0]
    earlier = (iota((slots, slots), 0) < iota((slots, slots), 1)).astype(f32).astype(bf16)
    row_copy.wait()
    col_copy.wait()
    row = rows[...]
    row_owner = jnp.floor(row.astype(f32) * (1.0 / slab_tiles)).astype(i32)
    col_f = cols[...].astype(f32)
    source_f = jnp.floor(col_f * (1.0 / slab_tiles))
    source = source_f.astype(i32) ^ place[1]
    tile_f = col_f - slab_tiles * source_f
    far = row_devs - 1 - (row_owner ^ place[0])
    late_bin = targets + far * slab_tiles + row - row_owner * slab_tiles
    bin_of = jnp.where(occupied, jnp.where(source < 2, row, late_bin), -1)
    member = (iota((bins, slots), 0) == bin_of).astype(f32)
    member_bf = member.astype(bf16)
    rank = jnp.sum(member * mm(member_bf, earlier), axis=0, keepdims=True)
    sizes = mm(jnp.ones((8, slots), bf16), member_bf, NT)
    sizes = GROUP * jnp.floor((sizes + (GROUP - 1.0)) * (1.0 / GROUP))
    before = (iota((bins, bins), 1) < iota((bins, bins), 0)).astype(f32)
    begin = jnp.sum(before * sizes[:1], axis=1, keepdims=True)
    position = jnp.sum(member * begin, axis=0, keepdims=True) + rank
    position = jnp.where(occupied, position.astype(i32), -1)
    chosen = (iota((places, slots), 0) == position).astype(f32).astype(bf16)
    slot_f = slot.astype(f32)
    slot_high = jnp.floor(slot_f * (1.0 / 16.0))
    facts = [slot_high, slot_f - 16.0 * slot_high, source.astype(f32), tile_f, row.astype(f32), jnp.ones((1, slots), f32)]
    facts = jnp.concatenate(facts + [jnp.zeros((2, slots), f32)], axis=0).astype(bf16)
    found = mm(facts, chosen, NT).astype(i32)
    source = jnp.where(found[5:6] > 0, found[2:3], col_devs)
    words = (found[4:5] << ROW_BIT) + (source << SOURCE_BIT) + (found[3:4] << TILE_BIT)
    out[:, :places] = words + (found[0:1] << 4) + found[1:2]
    phase = iota((bins, LANES), 1)
    edge = jnp.where(phase > 0, targets + (phase - 1) * slab_tiles, 0)
    inside = (iota((bins, LANES), 0) < edge).astype(f32).astype(bf16)
    out[:, places:] = mm(sizes.astype(bf16), inside)[:1].astype(i32)
    plan_copy = pltpu.make_async_copy(out, plan, list_sem.at[2])
    plan_copy.start()
    acc[...] = jnp.zeros_like(acc)
    for copy in copies + [plan_copy]:
        copy.wait()

    @pl.loop(0, chunks)
    def _(k):
        tile_copy(k).wait()

    add_products(plan, 0, 0, targets, held, panel_buf, acc)


def field(word, low, high):
    return (word >> low) & ((1 << (high - low)) - 1)


def add_products(plan, phase, first_row, spare_row, tiles, panel_buf, acc):
    phases = plan.shape[1] - LANES
    begin, end = plan[0, phases + phase], plan[0, phases + phase + 1]

    def panel(word):
        where = pl.multiple_of(field(word, TILE_BIT, SOURCE_BIT) * LANES, LANES)
        return panel_buf[field(word, SOURCE_BIT, ROW_BIT), :, pl.ds(where, LANES)]

    @pl.loop(0, (end - begin + GROUP * UNROLL - 1) // (GROUP * UNROLL))
    def _(g):
        first = begin + g * GROUP * UNROLL
        parts = []
        for u in range(UNROLL):
            words = [plan[0, first + GROUP * u + i] for i in range(GROUP)]
            left = jnp.concatenate([panel(word) for word in words], axis=1)
            right = jnp.concatenate([tiles[field(word, 0, TILE_BIT)] for word in words], axis=1)
            parts.append(mm(left, right, NT))
        for u in range(UNROLL):
            p = first + GROUP * u
            a = jnp.where(p < end, (plan[0, p] >> ROW_BIT) - first_row, spare_row)
            acc[a] += parts[u]


def load_panels(panels, panel_buf, sem):
    copies = [pltpu.make_async_copy(ref, panel_buf.at[m], sem.at[i]) for i, (m, ref) in enumerate(panels.items())]
    for copy in copies:
        copy.start()
    return copies


def collect_kernel(masks, *refs):
    panels, (_, panel_buf, sem) = refs[: len(masks)], refs[len(masks) :]
    for copy in load_panels(dict(zip(masks, panels)), panel_buf, sem):
        copy.wait()


def first_late_kernel(masks, odd, place, plan, *refs):
    panels = dict(zip(odd, refs))
    tiles, early, _ = refs[len(odd) : len(odd) + 3]
    sends = refs[len(odd) + 3 : -3]
    panel_buf, acc, sem = refs[-3:]
    copies = load_panels(panels, panel_buf, sem)
    for mask, send in zip(masks, sends):
        late_part(mask, place, plan, tiles, early, panel_buf, acc, copies)
        put(send, acc)
        copies = ()


def late_kernel(masks, place, plan, panel_buf, tiles, early, *refs):
    sends, acc = refs[:-1], refs[-1]
    for i, (mask, send) in enumerate(zip(masks, sends)):
        if i == 0 or mask != masks[i - 1]:
            late_part(mask, place, plan, tiles, early, panel_buf, acc, ())
        put(send, acc)


def own_kernel(place, plan, panel_buf, tiles, early, current, previous, coupling, diag, base, acc):
    late_part(0, place, plan, tiles, early, panel_buf, acc, ())
    put(base, acc)
    base[...] += diag[...] * current[...] - jnp.dot(
        coupling[...],
        previous[...],
        precision=lax.Precision.HIGHEST,
        preferred_element_type=jnp.float32,
    )


def late_part(mask, place, plan, tiles, early, panel_buf, acc, copies):
    slab_tiles = acc.shape[0] - 1
    row_devs = (early.shape[0] - 1) // slab_tiles
    first_row = (place[0] ^ mask) * slab_tiles
    for s in range(slab_tiles):
        acc[s] = early[first_row + s]
    for copy in copies:
        copy.wait()
    add_products(plan, row_devs - mask, first_row, slab_tiles, tiles, panel_buf, acc)


def put(out, acc):
    for s in range(acc.shape[0] - 1):
        out[:, s * LANES : (s + 1) * LANES] = acc[s].astype(out.dtype)


def coefficient_kernel(cells, received_count, relay, place, base, *refs):
    received = refs[:received_count]
    mass, current, stored, recurrence, keep, give, halves = refs[received_count:]
    total = base[...]
    for i, ref in enumerate(received):
        value = ref[...].astype(jnp.float32)
        if relay and i == 0:
            value = jnp.where((place[0] == 1) | (place[0] == 2), 0.0, value)
        total = total + value
    recurrence[...] = total
    weighted = total * (mass[...] * (1.0 / cells))
    basis = jnp.concatenate([current[...], stored[...]], axis=0)
    coef = dot_split(weighted, basis, NT)
    spare = -coef.shape[1] % LANES
    coef = jnp.concatenate([coef, jnp.zeros((coef.shape[0], spare), jnp.float32)], axis=1)
    halves[...] = jnp.zeros_like(halves)
    for p, (q, k) in enumerate(blocks(coef.shape)):
        halves[p // halves.shape[1], p % halves.shape[1]] = coef[q : q + 8, k : k + LANES]
    core = place[1] & 1
    keep[...] = halves[core]
    give[...] = halves[1 - core]


def residual_kernel(
    cells, place, mine, other, recurrence, mass, current, stored, residual, coef_out, gram, halves, packed
):
    width = recurrence.shape[0]
    core = place[1] & 1
    halves[core] = mine[...]
    halves[1 - core] = other[...]
    for p, (q, k) in enumerate(blocks(packed.shape)):
        packed[q : q + 8, k : k + LANES] = halves[p // halves.shape[1], p % halves.shape[1]]
    coef = packed[...]
    basis = jnp.concatenate([current[...], stored[...]], axis=0)
    coef = coef[:, : basis.shape[0]]
    coef_out[...] = coef
    value = recurrence[...] - dot_split(coef, basis)
    residual[...] = value
    local = dot_split(value * (mass[...] * (1.0 / cells)), value, NT)
    half = width // 2
    gram[...] = jnp.zeros_like(gram)
    gram[:, :width] = local[:half]
    gram[:, LANES // 2 : LANES // 2 + width] = local[half:]


def after_kernel(value, earlier, out):
    pass


def after(value, earlier):
    anywhere = pl.BlockSpec(memory_space=pl.ANY)
    return pl.pallas_call(
        after_kernel,
        out_shape=jax.ShapeDtypeStruct(value.shape, value.dtype),
        in_specs=[anywhere, anywhere],
        out_specs=anywhere,
        input_output_aliases={0: 0},
        compiler_params=limit(1),
    )(value, earlier)


def in_hbm(value):
    return pltpu.with_memory_space_constraint(value, pltpu.HBM)


def limit(mib):
    return pltpu.CompilerParams(vmem_limit_bytes=mib * MIB)


def vmem(count):
    return [pl.BlockSpec(memory_space=pltpu.VMEM)] * count


def smem(count):
    return [pl.BlockSpec(memory_space=pltpu.SMEM)] * count


def local(
    current_block,
    previous_block,
    previous_coupling,
    stored_blocks,
    stiffness_diag,
    lumped_mass,
    tile_values,
    tile_rows,
    tile_cols,
    tile_counts,
):
    row_devs = lax.axis_size("row")
    col_devs = lax.axis_size("col")
    width, slab_len = current_block.shape
    stored_count = stored_blocks.shape[0]
    slots, tile_len, _ = tile_values.shape
    slab_tiles = slab_len // tile_len
    cells = slab_len * row_devs * col_devs
    f32, bf16 = jnp.float32, jnp.bfloat16
    place = jnp.stack([lax.axis_index("row"), lax.axis_index("col")]).astype(jnp.int32)
    stored = stored_blocks.reshape(stored_count * width, slab_len)
    mass = lumped_mass.reshape(1, slab_len)
    diag = stiffness_diag.reshape(1, slab_len)
    slab = jax.ShapeDtypeStruct((width, slab_len), f32)

    targets = row_devs * slab_tiles
    anywhere = [pl.BlockSpec(memory_space=pl.ANY)]
    panel_shape = (col_devs + 1, width, slab_len)
    early_shape = (targets + 1, width, tile_len)
    part_acc = pltpu.VMEM((slab_tiles + 1, width, tile_len), f32)

    def cost(flops):
        return pl.CostEstimate(flops=flops, bytes_accessed=flops // width, transcendentals=0)

    with jax.named_scope("gather"):
        rounded = current_block.astype(bf16)
        panels = [rounded] + [None] * (col_devs - 1)
        for m in range(col_devs - 2, 0, -2):
            panels[m] = swap(rounded, "col", m)
        panels[1] = swap(rounded, "col", 1)

    with jax.named_scope("early"):
        places = -(-(slots + (GROUP - 1) * 2 * targets + GROUP * UNROLL) // LANES) * LANES
        plan_shape = (1, places + LANES)
        plan, held, early, gathered = pl.pallas_call(
            functools.partial(early_kernel, row_devs, col_devs, slab_tiles),
            out_shape=[
                jax.ShapeDtypeStruct(plan_shape, jnp.int32),
                pltpu.VMEM(tile_values.shape, bf16),
                pltpu.VMEM(early_shape, f32),
                pltpu.VMEM(panel_shape, bf16),
            ],
            in_specs=smem(2) + [pl.BlockSpec(memory_space=pltpu.HBM)] * 3 + anywhere * 2,
            out_specs=vmem(4),
            scratch_shapes=[
                pltpu.VMEM((1, slots), jnp.int32),
                pltpu.VMEM((1, slots), jnp.int32),
                pltpu.SMEM(plan_shape, jnp.int32),
                pltpu.SemaphoreType.DMA((slots // CHUNK,)),
                pltpu.SemaphoreType.DMA((3,)),
                pltpu.SemaphoreType.DMA((2,)),
            ],
            compiler_params=limit(12),
            cost_estimate=cost(2 * slots * width * tile_len * tile_len),
        )(
            place,
            tile_counts,
            in_hbm(tile_rows.reshape(1, slots)),
            in_hbm(tile_cols.reshape(1, slots)),
            in_hbm(tile_values),
            panels[0],
            panels[1],
        )

    with jax.named_scope("gather"):
        for m in range(col_devs - 2, 0, -2):
            panels[m] = after(panels[m], early)
            panels[m + 1] = swap(panels[m], "col", 1)
        even, odd = list(range(2, col_devs, 2)), list(range(3, col_devs, 2))
        gathered = pl.pallas_call(
            functools.partial(collect_kernel, even),
            out_shape=pltpu.VMEM(panel_shape, bf16),
            in_specs=anywhere * len(even) + vmem(1),
            out_specs=vmem(1)[0],
            scratch_shapes=[pltpu.SemaphoreType.DMA((len(even),))],
            input_output_aliases={len(even): 0},
            compiler_params=limit(1),
            cost_estimate=cost(width),
        )(*[panels[m] for m in even], gathered)

    with jax.named_scope("late"):
        relay = row_devs == 4
        first_mask = 2 if relay else row_devs - 1
        masks = [3, 3, 1] if relay else list(range(row_devs - 2, 0, -1))
        part = jax.ShapeDtypeStruct((width, slab_len), bf16)
        first, gathered = pl.pallas_call(
            functools.partial(first_late_kernel, [first_mask], odd),
            out_shape=[part, pltpu.VMEM(panel_shape, bf16)],
            in_specs=smem(2) + anywhere * len(odd) + vmem(3),
            out_specs=vmem(2),
            scratch_shapes=[part_acc, pltpu.SemaphoreType.DMA((len(odd),))],
            input_output_aliases={4 + len(odd): 1},
            compiler_params=limit(8),
            cost_estimate=cost(width),
        )(place, plan, *[panels[m] for m in odd], held, early, gathered)
        parts = pl.pallas_call(
            functools.partial(late_kernel, masks),
            out_shape=[part, slab, part] if relay else [part] * len(masks),
            in_specs=smem(2) + vmem(3),
            out_specs=vmem(len(masks)),
            scratch_shapes=[part_acc],
            compiler_params=limit(8),
            cost_estimate=cost(width),
        )(place, plan, gathered, held, early)
        if relay:
            first = lax.ppermute(first, "row", [(0, 1), (3, 2), (1, 3), (2, 0)])
            joined = (parts[1] + first.astype(f32)).astype(bf16)
            received = [
                first,
                lax.ppermute(parts[0], "row", [(0, 3), (3, 0)]),
                lax.ppermute(joined, "row", [(1, 2), (2, 1)]),
                swap(parts[2], "row", 1),
            ]
        else:
            received = [swap(first, "row", first_mask)]
            received += [swap(part, "row", m) for m, part in zip(masks, parts)]
        base = pl.pallas_call(
            own_kernel,
            out_shape=slab,
            in_specs=smem(2) + vmem(7),
            out_specs=vmem(1)[0],
            scratch_shapes=[part_acc],
            compiler_params=limit(8),
            cost_estimate=cost(width),
        )(place, plan, gathered, held, early, current_block, previous_block, previous_coupling, diag)

    basis_rows = (stored_count + 1) * width
    padded = (width, -(-basis_rows // LANES) * LANES)
    half = (-(-len(blocks(padded)) // 2), 8, LANES)
    with jax.named_scope("coefficients"):
        recurrence, keep, give = pl.pallas_call(
            functools.partial(coefficient_kernel, cells, len(received), relay),
            out_shape=[slab] + [jax.ShapeDtypeStruct(half, f32)] * 2,
            in_specs=smem(1) + vmem(len(received) + 4),
            out_specs=vmem(3),
            scratch_shapes=[pltpu.VMEM((2,) + half, f32)],
            compiler_params=limit(24),
        )(place, base, *received, mass, current_block, stored)
        mine = keep + swap(give, "col", 1)
        mine = total(total(mine, "col", 2), "row", 1)
        other = swap(mine, "col", 1)

    with jax.named_scope("residual"):
        residual_block, coef, gram = pl.pallas_call(
            functools.partial(residual_kernel, cells),
            out_shape=[
                slab,
                jax.ShapeDtypeStruct((width, basis_rows), f32),
                jax.ShapeDtypeStruct((width // 2, LANES), f32),
            ],
            in_specs=smem(1) + vmem(6),
            out_specs=vmem(3),
            scratch_shapes=[pltpu.VMEM((2,) + half, f32), pltpu.VMEM(padded, f32)],
            compiler_params=limit(24),
        )(place, mine, other, recurrence, mass, current_block, stored)
        coefficients = coef.T.reshape(stored_count + 1, width, width)

    with jax.named_scope("gram"):
        gram = gram + swap(gram, "col", 1)
        gram = total(total(gram, "col", 2), "row", 1)
        gram = jnp.concatenate(
            [gram[:, :width], gram[:, LANES // 2 : LANES // 2 + width]], axis=0
        )
    return (residual_block, coefficients, gram)


def solution(mesh):
    return jax.shard_map(
        local,
        mesh=mesh,
        in_specs=(
            P(None, ("row", "col")),
            P(None, ("row", "col")),
            P(),
            P(None, None, ("row", "col")),
            P(("row", "col")),
            P(("row", "col")),
            P(("row", "col"), None, None),
            P(("row", "col")),
            P(("row", "col")),
            P(("row", "col")),
        ),
        out_specs=(P(None, ("row", "col")), P(), P()),
        check_vma=False,
    )
```

```python
import functools

import jax
import jax.numpy as jnp
from jax import lax
from jax.experimental import pallas as pl
from jax.experimental.pallas import tpu as pltpu
from jax.sharding import PartitionSpec as P

LANES = 128
CHUNK = 32
GROUP = 2
UNROLL = 8
TILE_BIT, SOURCE_BIT, ROW_BIT = 10, 15, 20
NT = (((1,), (1,)), ((), ()))
MIB = 1 << 20


def swap(value, axis, mask):
    count = lax.axis_size(axis)
    return lax.ppermute(value, axis, [(i, i ^ mask) for i in range(count)])


def tree_sum(values):
    while len(values) > 1:
        values = [values[i] + values[i + 1] for i in range(0, len(values), 2)]
    return values[0]


def total(value, axis, step):
    return tree_sum([value] + [swap(value, axis, m) for m in range(step, lax.axis_size(axis), step)])


def total_by_core(value):
    row_devs, col_devs = lax.axis_size("row"), lax.axis_size("col")
    if col_devs != 2 * row_devs:
        return total(total(value, "col", 2), "row", 1)
    places = [(r, c) for r in range(row_devs) for c in range(col_devs)]
    for turn in range(2):
        values = [value]
        for m in range(1, row_devs):
            partners = [(r, c ^ (2 * m)) if c % 2 == turn else (r ^ m, c) for r, c in places]
            trades = [(i, r * col_devs + c) for i, (r, c) in enumerate(partners)]
            values.append(lax.ppermute(value, ("row", "col"), trades))
        value = tree_sum(values)
    return value


def split(value):
    high = value.astype(jnp.bfloat16)
    low = (value - high.astype(jnp.float32)).astype(jnp.bfloat16)
    return high, low


def mm(a, b, dims=(((1,), (0,)), ((), ()))):
    return lax.dot_general(a, b, dims, preferred_element_type=jnp.float32)


def dot_split(a, b, dims=(((1,), (0,)), ((), ()))):
    rows = a.shape[0]
    a_high, a_low = split(a)
    b_high, b_low = split(b)
    both = mm(jnp.concatenate([a_high, a_low], axis=0), b_high, dims)
    return both[:rows] + both[rows:] + mm(a_high, b_low, dims)


def blocks(shape):
    return [(q, k) for q in range(0, shape[0], 8) for k in range(0, shape[1], LANES)]


def early_kernel(
    row_devs,
    col_devs,
    slab_tiles,
    place,
    counts,
    rows_hbm,
    cols_hbm,
    tiles,
    own_panel,
    near_panel,
    out,
    held,
    acc,
    panel_buf,
    rows,
    cols,
    plan,
    tile_sem,
    list_sem,
    panel_sem,
):
    chunks = (counts[0] + CHUNK - 1) // CHUNK
    row_copy = pltpu.make_async_copy(rows_hbm, rows, list_sem.at[0])
    col_copy = pltpu.make_async_copy(cols_hbm, cols, list_sem.at[1])
    row_copy.start()
    col_copy.start()

    def tile_copy(k):
        window = pl.ds(k * CHUNK, CHUNK)
        return pltpu.make_async_copy(tiles.at[window], held.at[window], tile_sem.at[k])

    @pl.loop(0, chunks)
    def _(k):
        tile_copy(k).start()

    copies = load_panels({0: own_panel, 1: near_panel}, panel_buf, panel_sem)
    zero_panel = panel_buf.shape[0] - 1
    panel_buf[zero_panel, :, :LANES] = jnp.zeros((panel_buf.shape[1], LANES), jnp.bfloat16)
    f32, bf16, i32 = jnp.float32, jnp.bfloat16, jnp.int32
    slots, places = rows.shape[1], out.shape[1] - LANES
    targets = row_devs * slab_tiles
    bins = 2 * targets

    def iota(shape, dim):
        return lax.broadcasted_iota(i32, shape, dim)

    slot = iota((1, slots), 1)
    occupied = slot < counts[0]
    earlier = (iota((slots, slots), 0) < iota((slots, slots), 1)).astype(f32).astype(bf16)
    row_copy.wait()
    col_copy.wait()
    row = rows[...]
    row_owner = jnp.floor(row.astype(f32) * (1.0 / slab_tiles)).astype(i32)
    col_f = cols[...].astype(f32)
    source_f = jnp.floor(col_f * (1.0 / slab_tiles))
    source = source_f.astype(i32) ^ place[1]
    tile_f = col_f - slab_tiles * source_f
    far = row_devs - 1 - (row_owner ^ place[0])
    late_bin = targets + far * slab_tiles + row - row_owner * slab_tiles
    bin_of = jnp.where(occupied, jnp.where(source < 2, row, late_bin), -1)
    member = (iota((bins, slots), 0) == bin_of).astype(f32)
    member_bf = member.astype(bf16)
    rank = jnp.sum(member * mm(member_bf, earlier), axis=0, keepdims=True)
    sizes = mm(jnp.ones((8, slots), bf16), member_bf, NT)
    sizes = GROUP * jnp.floor((sizes + (GROUP - 1.0)) * (1.0 / GROUP))
    before = (iota((bins, bins), 1) < iota((bins, bins), 0)).astype(f32)
    begin = jnp.sum(before * sizes[:1], axis=1, keepdims=True)
    position = jnp.sum(member * begin, axis=0, keepdims=True) + rank
    position = jnp.where(occupied, position.astype(i32), -1)
    chosen = (iota((places, slots), 0) == position).astype(f32).astype(bf16)
    slot_f = slot.astype(f32)
    slot_high = jnp.floor(slot_f * (1.0 / 16.0))
    facts = [slot_high, slot_f - 16.0 * slot_high, source.astype(f32), tile_f, row.astype(f32), jnp.ones((1, slots), f32)]
    facts = jnp.concatenate(facts + [jnp.zeros((2, slots), f32)], axis=0).astype(bf16)
    found = mm(facts, chosen, NT).astype(i32)
    source = jnp.where(found[5:6] > 0, found[2:3], col_devs)
    words = (found[4:5] << ROW_BIT) + (source << SOURCE_BIT) + (found[3:4] << TILE_BIT)
    out[:, :places] = words + (found[0:1] << 4) + found[1:2]
    phase = iota((bins, LANES), 1)
    edge = jnp.where(phase > 0, targets + (phase - 1) * slab_tiles, 0)
    inside = (iota((bins, LANES), 0) < edge).astype(f32).astype(bf16)
    out[:, places:] = mm(sizes.astype(bf16), inside)[:1].astype(i32)
    plan_copy = pltpu.make_async_copy(out, plan, list_sem.at[2])
    plan_copy.start()
    acc[...] = jnp.zeros_like(acc)
    for copy in copies + [plan_copy]:
        copy.wait()

    @pl.loop(0, chunks)
    def _(k):
        tile_copy(k).wait()

    add_products(plan, 0, 0, targets, held, panel_buf, acc)


def field(word, low, high):
    return (word >> low) & ((1 << (high - low)) - 1)


def add_products(plan, phase, first_row, spare_row, tiles, panel_buf, acc):
    phases = plan.shape[1] - LANES
    begin, end = plan[0, phases + phase], plan[0, phases + phase + 1]

    def panel(word):
        where = pl.multiple_of(field(word, TILE_BIT, SOURCE_BIT) * LANES, LANES)
        return panel_buf[field(word, SOURCE_BIT, ROW_BIT), :, pl.ds(where, LANES)]

    @pl.loop(0, (end - begin + GROUP * UNROLL - 1) // (GROUP * UNROLL))
    def _(g):
        first = begin + g * GROUP * UNROLL
        parts = []
        for u in range(UNROLL):
            words = [plan[0, first + GROUP * u + i] for i in range(GROUP)]
            left = jnp.concatenate([panel(word) for word in words], axis=1)
            right = jnp.concatenate([tiles[field(word, 0, TILE_BIT)] for word in words], axis=1)
            parts.append(mm(left, right, NT))
        for u in range(UNROLL):
            p = first + GROUP * u
            a = jnp.where(p < end, (plan[0, p] >> ROW_BIT) - first_row, spare_row)
            acc[a] += parts[u]


def load_panels(panels, panel_buf, sem):
    copies = [pltpu.make_async_copy(ref, panel_buf.at[m], sem.at[i]) for i, (m, ref) in enumerate(panels.items())]
    for copy in copies:
        copy.start()
    return copies


def collect_kernel(masks, *refs):
    panels, (_, panel_buf, sem) = refs[: len(masks)], refs[len(masks) :]
    for copy in load_panels(dict(zip(masks, panels)), panel_buf, sem):
        copy.wait()


def first_late_kernel(masks, odd, place, plan, *refs):
    panels = dict(zip(odd, refs))
    tiles, early, _ = refs[len(odd) : len(odd) + 3]
    sends = refs[len(odd) + 3 : -3]
    panel_buf, acc, sem = refs[-3:]
    copies = load_panels(panels, panel_buf, sem)
    for mask, send in zip(masks, sends):
        late_part(mask, place, plan, tiles, early, panel_buf, acc, copies)
        put(send, acc)
        copies = ()


def late_kernel(masks, place, plan, panel_buf, tiles, early, *refs):
    sends, acc = refs[:-1], refs[-1]
    for i, (mask, send) in enumerate(zip(masks, sends)):
        if i == 0 or mask != masks[i - 1]:
            late_part(mask, place, plan, tiles, early, panel_buf, acc, ())
        put(send, acc)


def own_kernel(place, plan, panel_buf, tiles, early, current, previous, coupling, diag, base, acc):
    late_part(0, place, plan, tiles, early, panel_buf, acc, ())
    put(base, acc)
    base[...] += diag[...] * current[...] - jnp.dot(
        coupling[...],
        previous[...],
        precision=lax.Precision.HIGHEST,
        preferred_element_type=jnp.float32,
    )


def late_part(mask, place, plan, tiles, early, panel_buf, acc, copies):
    slab_tiles = acc.shape[0] - 1
    row_devs = (early.shape[0] - 1) // slab_tiles
    first_row = (place[0] ^ mask) * slab_tiles
    for s in range(slab_tiles):
        acc[s] = early[first_row + s]
    for copy in copies:
        copy.wait()
    add_products(plan, row_devs - mask, first_row, slab_tiles, tiles, panel_buf, acc)


def put(out, acc):
    for s in range(acc.shape[0] - 1):
        out[:, s * LANES : (s + 1) * LANES] = acc[s].astype(out.dtype)


def coefficient_kernel(cells, received_count, relay, place, base, *refs):
    received = refs[:received_count]
    mass, current, stored, recurrence, keep, give, halves = refs[received_count:]
    total = base[...]
    for i, ref in enumerate(received):
        value = ref[...].astype(jnp.float32)
        if relay and i == 0:
            value = jnp.where((place[0] == 1) | (place[0] == 2), 0.0, value)
        total = total + value
    recurrence[...] = total
    weighted = total * (mass[...] * (1.0 / cells))
    basis = jnp.concatenate([current[...], stored[...]], axis=0)
    coef = dot_split(weighted, basis, NT)
    spare = -coef.shape[1] % LANES
    coef = jnp.concatenate([coef, jnp.zeros((coef.shape[0], spare), jnp.float32)], axis=1)
    halves[...] = jnp.zeros_like(halves)
    for p, (q, k) in enumerate(blocks(coef.shape)):
        halves[p // halves.shape[1], p % halves.shape[1]] = coef[q : q + 8, k : k + LANES]
    core = place[1] & 1
    keep[...] = halves[core]
    give[...] = halves[1 - core]


def residual_kernel(
    cells, place, mine, other, recurrence, mass, current, stored, residual, coef_out, gram, halves, packed
):
    width = recurrence.shape[0]
    core = place[1] & 1
    halves[core] = mine[...]
    halves[1 - core] = other[...]
    for p, (q, k) in enumerate(blocks(packed.shape)):
        packed[q : q + 8, k : k + LANES] = halves[p // halves.shape[1], p % halves.shape[1]]
    coef = packed[...]
    basis = jnp.concatenate([current[...], stored[...]], axis=0)
    coef = coef[:, : basis.shape[0]]
    coef_out[...] = coef
    value = recurrence[...] - dot_split(coef, basis)
    residual[...] = value
    local = dot_split(value * (mass[...] * (1.0 / cells)), value, NT)
    half = width // 2
    gram[...] = jnp.zeros_like(gram)
    gram[:, :width] = local[:half]
    gram[:, LANES // 2 : LANES // 2 + width] = local[half:]


def after_kernel(value, earlier, out):
    pass


def after(value, earlier):
    anywhere = pl.BlockSpec(memory_space=pl.ANY)
    return pl.pallas_call(
        after_kernel,
        out_shape=jax.ShapeDtypeStruct(value.shape, value.dtype),
        in_specs=[anywhere, anywhere],
        out_specs=anywhere,
        input_output_aliases={0: 0},
        compiler_params=limit(1),
    )(value, earlier)


def in_hbm(value):
    return pltpu.with_memory_space_constraint(value, pltpu.HBM)


def limit(mib):
    return pltpu.CompilerParams(vmem_limit_bytes=mib * MIB)


def vmem(count):
    return [pl.BlockSpec(memory_space=pltpu.VMEM)] * count


def smem(count):
    return [pl.BlockSpec(memory_space=pltpu.SMEM)] * count


def local(
    current_block,
    previous_block,
    previous_coupling,
    stored_blocks,
    stiffness_diag,
    lumped_mass,
    tile_values,
    tile_rows,
    tile_cols,
    tile_counts,
):
    row_devs = lax.axis_size("row")
    col_devs = lax.axis_size("col")
    width, slab_len = current_block.shape
    stored_count = stored_blocks.shape[0]
    slots, tile_len, _ = tile_values.shape
    slab_tiles = slab_len // tile_len
    cells = slab_len * row_devs * col_devs
    f32, bf16 = jnp.float32, jnp.bfloat16
    place = jnp.stack([lax.axis_index("row"), lax.axis_index("col")]).astype(jnp.int32)
    stored = stored_blocks.reshape(stored_count * width, slab_len)
    mass = lumped_mass.reshape(1, slab_len)
    diag = stiffness_diag.reshape(1, slab_len)
    slab = jax.ShapeDtypeStruct((width, slab_len), f32)

    targets = row_devs * slab_tiles
    anywhere = [pl.BlockSpec(memory_space=pl.ANY)]
    panel_shape = (col_devs + 1, width, slab_len)
    early_shape = (targets + 1, width, tile_len)
    part_acc = pltpu.VMEM((slab_tiles + 1, width, tile_len), f32)

    def cost(flops):
        return pl.CostEstimate(flops=flops, bytes_accessed=flops // width, transcendentals=0)

    with jax.named_scope("gather"):
        rounded = current_block.astype(bf16)
        panels = [rounded] + [None] * (col_devs - 1)
        for m in range(col_devs - 2, 0, -2):
            panels[m] = swap(rounded, "col", m)
        panels[1] = swap(rounded, "col", 1)

    with jax.named_scope("early"):
        places = -(-(slots + (GROUP - 1) * 2 * targets + GROUP * UNROLL) // LANES) * LANES
        plan_shape = (1, places + LANES)
        plan, held, early, gathered = pl.pallas_call(
            functools.partial(early_kernel, row_devs, col_devs, slab_tiles),
            out_shape=[
                jax.ShapeDtypeStruct(plan_shape, jnp.int32),
                pltpu.VMEM(tile_values.shape, bf16),
                pltpu.VMEM(early_shape, f32),
                pltpu.VMEM(panel_shape, bf16),
            ],
            in_specs=smem(2) + [pl.BlockSpec(memory_space=pltpu.HBM)] * 3 + anywhere * 2,
            out_specs=vmem(4),
            scratch_shapes=[
                pltpu.VMEM((1, slots), jnp.int32),
                pltpu.VMEM((1, slots), jnp.int32),
                pltpu.SMEM(plan_shape, jnp.int32),
                pltpu.SemaphoreType.DMA((slots // CHUNK,)),
                pltpu.SemaphoreType.DMA((3,)),
                pltpu.SemaphoreType.DMA((2,)),
            ],
            compiler_params=limit(12),
            cost_estimate=cost(2 * slots * width * tile_len * tile_len),
        )(
            place,
            tile_counts,
            in_hbm(tile_rows.reshape(1, slots)),
            in_hbm(tile_cols.reshape(1, slots)),
            in_hbm(tile_values),
            panels[0],
            panels[1],
        )

    with jax.named_scope("gather"):
        for m in range(col_devs - 2, 0, -2):
            panels[m] = after(panels[m], early)
            panels[m + 1] = swap(panels[m], "col", 1)
        even, odd = list(range(2, col_devs, 2)), list(range(3, col_devs, 2))
        gathered = pl.pallas_call(
            functools.partial(collect_kernel, even),
            out_shape=pltpu.VMEM(panel_shape, bf16),
            in_specs=anywhere * len(even) + vmem(1),
            out_specs=vmem(1)[0],
            scratch_shapes=[pltpu.SemaphoreType.DMA((len(even),))],
            input_output_aliases={len(even): 0},
            compiler_params=limit(1),
            cost_estimate=cost(width),
        )(*[panels[m] for m in even], gathered)

    with jax.named_scope("late"):
        relay = row_devs == 4
        first_mask = 2 if relay else row_devs - 1
        masks = [3, 3, 1] if relay else list(range(row_devs - 2, 0, -1))
        part = jax.ShapeDtypeStruct((width, slab_len), bf16)
        first, gathered = pl.pallas_call(
            functools.partial(first_late_kernel, [first_mask], odd),
            out_shape=[part, pltpu.VMEM(panel_shape, bf16)],
            in_specs=smem(2) + anywhere * len(odd) + vmem(3),
            out_specs=vmem(2),
            scratch_shapes=[part_acc, pltpu.SemaphoreType.DMA((len(odd),))],
            input_output_aliases={4 + len(odd): 1},
            compiler_params=limit(8),
            cost_estimate=cost(width),
        )(place, plan, *[panels[m] for m in odd], held, early, gathered)
        parts = pl.pallas_call(
            functools.partial(late_kernel, masks),
            out_shape=[part, slab, part] if relay else [part] * len(masks),
            in_specs=smem(2) + vmem(3),
            out_specs=vmem(len(masks)),
            scratch_shapes=[part_acc],
            compiler_params=limit(8),
            cost_estimate=cost(width),
        )(place, plan, gathered, held, early)
        if relay:
            first = lax.ppermute(first, "row", [(0, 1), (3, 2), (1, 3), (2, 0)])
            joined = (parts[1] + first.astype(f32)).astype(bf16)
            received = [
                first,
                lax.ppermute(parts[0], "row", [(0, 3), (3, 0)]),
                lax.ppermute(joined, "row", [(1, 2), (2, 1)]),
                swap(parts[2], "row", 1),
            ]
        else:
            received = [swap(first, "row", first_mask)]
            received += [swap(part, "row", m) for m, part in zip(masks, parts)]
        base = pl.pallas_call(
            own_kernel,
            out_shape=slab,
            in_specs=smem(2) + vmem(7),
            out_specs=vmem(1)[0],
            scratch_shapes=[part_acc],
            compiler_params=limit(8),
            cost_estimate=cost(width),
        )(place, plan, gathered, held, early, current_block, previous_block, previous_coupling, diag)

    basis_rows = (stored_count + 1) * width
    padded = (width, -(-basis_rows // LANES) * LANES)
    half = (-(-len(blocks(padded)) // 2), 8, LANES)
    with jax.named_scope("coefficients"):
        recurrence, keep, give = pl.pallas_call(
            functools.partial(coefficient_kernel, cells, len(received), relay),
            out_shape=[slab] + [jax.ShapeDtypeStruct(half, f32)] * 2,
            in_specs=smem(1) + vmem(len(received) + 4),
            out_specs=vmem(3),
            scratch_shapes=[pltpu.VMEM((2,) + half, f32)],
            compiler_params=limit(24),
        )(place, base, *received, mass, current_block, stored)
        mine = keep + swap(give, "col", 1)
        mine = total_by_core(mine)
        other = swap(mine, "col", 1)

    with jax.named_scope("residual"):
        residual_block, coef, gram = pl.pallas_call(
            functools.partial(residual_kernel, cells),
            out_shape=[
                pltpu.VMEM((width, slab_len), f32),
                jax.ShapeDtypeStruct((width, basis_rows), f32),
                jax.ShapeDtypeStruct((width // 2, LANES), f32),
            ],
            in_specs=smem(1) + vmem(6),
            out_specs=vmem(3),
            scratch_shapes=[pltpu.VMEM((2,) + half, f32), pltpu.VMEM(padded, f32)],
            compiler_params=limit(24),
        )(place, mine, other, recurrence, mass, current_block, stored)
        coefficients = coef.T.reshape(stored_count + 1, width, width)

    with jax.named_scope("gram"):
        gram = gram + swap(gram, "col", 1)
        gram = total(total(gram, "col", 2), "row", 1)
        gram = jnp.concatenate(
            [gram[:, :width], gram[:, LANES // 2 : LANES // 2 + width]], axis=0
        )
    return (residual_block, coefficients, gram)


def solution(mesh):
    return jax.shard_map(
        local,
        mesh=mesh,
        in_specs=(
            P(None, ("row", "col")),
            P(None, ("row", "col")),
            P(),
            P(None, None, ("row", "col")),
            P(("row", "col")),
            P(("row", "col")),
            P(("row", "col"), None, None),
            P(("row", "col")),
            P(("row", "col")),
            P(("row", "col")),
        ),
        out_specs=(P(None, ("row", "col")), P(), P()),
        check_vma=False,
    )
```

```python
import functools

import jax
import jax.numpy as jnp
from jax import lax
from jax.experimental import pallas as pl
from jax.experimental.pallas import tpu as pltpu
from jax.sharding import PartitionSpec as P

LANES = 128
CHUNK = 32
GROUP = 2
UNROLL = 8
TILE_BIT, SOURCE_BIT, ROW_BIT = 10, 15, 20
NT = (((1,), (1,)), ((), ()))
MIB = 1 << 20


def swap(value, axis, mask):
    count = lax.axis_size(axis)
    return lax.ppermute(value, axis, [(i, i ^ mask) for i in range(count)])


def tree_sum(values):
    while len(values) > 1:
        values = [values[i] + values[i + 1] for i in range(0, len(values), 2)]
    return values[0]


def total(value, axis, step):
    return tree_sum([value] + [swap(value, axis, m) for m in range(step, lax.axis_size(axis), step)])


def total_by_core(value):
    row_devs, col_devs = lax.axis_size("row"), lax.axis_size("col")
    if col_devs != 2 * row_devs:
        return total(total(value, "col", 2), "row", 1)
    places = [(r, c) for r in range(row_devs) for c in range(col_devs)]
    for turn in range(2):
        values = [value]
        for m in range(1, row_devs):
            partners = [(r, c ^ (2 * m)) if c % 2 == turn else (r ^ m, c) for r, c in places]
            trades = [(i, r * col_devs + c) for i, (r, c) in enumerate(partners)]
            values.append(lax.ppermute(value, ("row", "col"), trades))
        value = tree_sum(values)
    return value


def split(value):
    high = value.astype(jnp.bfloat16)
    low = (value - high.astype(jnp.float32)).astype(jnp.bfloat16)
    return high, low


def mm(a, b, dims=(((1,), (0,)), ((), ()))):
    return lax.dot_general(a, b, dims, preferred_element_type=jnp.float32)


def dot_split(a, b, dims=(((1,), (0,)), ((), ()))):
    rows = a.shape[0]
    a_high, a_low = split(a)
    b_high, b_low = split(b)
    both = mm(jnp.concatenate([a_high, a_low], axis=0), b_high, dims)
    return both[:rows] + both[rows:] + mm(a_high, b_low, dims)


def blocks(shape):
    return [(q, k) for q in range(0, shape[0], 8) for k in range(0, shape[1], LANES)]


def early_kernel(
    row_devs,
    col_devs,
    slab_tiles,
    place,
    counts,
    rows_hbm,
    cols_hbm,
    tiles,
    own_panel,
    near_panel,
    out,
    held,
    acc,
    panel_buf,
    rows,
    cols,
    plan,
    tile_sem,
    list_sem,
    panel_sem,
):
    chunks = (counts[0] + CHUNK - 1) // CHUNK
    row_copy = pltpu.make_async_copy(rows_hbm, rows, list_sem.at[0])
    col_copy = pltpu.make_async_copy(cols_hbm, cols, list_sem.at[1])
    row_copy.start()
    col_copy.start()

    def tile_copy(k):
        window = pl.ds(k * CHUNK, CHUNK)
        return pltpu.make_async_copy(tiles.at[window], held.at[window], tile_sem.at[k])

    @pl.loop(0, chunks)
    def _(k):
        tile_copy(k).start()

    copies = load_panels({0: own_panel, 1: near_panel}, panel_buf, panel_sem)
    zero_panel = panel_buf.shape[0] - 1
    panel_buf[zero_panel, :, :LANES] = jnp.zeros((panel_buf.shape[1], LANES), jnp.bfloat16)
    f32, bf16, i32 = jnp.float32, jnp.bfloat16, jnp.int32
    slots, places = rows.shape[1], out.shape[1] - LANES
    early_chunks = 3 * slots // CHUNK // 4
    targets = row_devs * slab_tiles
    bins = 2 * targets

    def iota(shape, dim):
        return lax.broadcasted_iota(i32, shape, dim)

    slot = iota((1, slots), 1)
    occupied = slot < counts[0]
    earlier = (iota((slots, slots), 0) < iota((slots, slots), 1)).astype(f32).astype(bf16)
    row_copy.wait()
    col_copy.wait()
    row = rows[...]
    row_owner = jnp.floor(row.astype(f32) * (1.0 / slab_tiles)).astype(i32)
    col_f = cols[...].astype(f32)
    source_f = jnp.floor(col_f * (1.0 / slab_tiles))
    source = source_f.astype(i32) ^ place[1]
    tile_f = col_f - slab_tiles * source_f
    far = row_devs - 1 - (row_owner ^ place[0])
    late_bin = targets + far * slab_tiles + row - row_owner * slab_tiles
    early = (source < 2) & (slot < early_chunks * CHUNK)
    bin_of = jnp.where(occupied, jnp.where(early, row, late_bin), -1)
    member = (iota((bins, slots), 0) == bin_of).astype(f32)
    member_bf = member.astype(bf16)
    rank = jnp.sum(member * mm(member_bf, earlier), axis=0, keepdims=True)
    sizes = mm(jnp.ones((8, slots), bf16), member_bf, NT)
    sizes = GROUP * jnp.floor((sizes + (GROUP - 1.0)) * (1.0 / GROUP))
    before = (iota((bins, bins), 1) < iota((bins, bins), 0)).astype(f32)
    begin = jnp.sum(before * sizes[:1], axis=1, keepdims=True)
    position = jnp.sum(member * begin, axis=0, keepdims=True) + rank
    position = jnp.where(occupied, position.astype(i32), -1)
    chosen = (iota((places, slots), 0) == position).astype(f32).astype(bf16)
    slot_f = slot.astype(f32)
    slot_high = jnp.floor(slot_f * (1.0 / 16.0))
    facts = [slot_high, slot_f - 16.0 * slot_high, source.astype(f32), tile_f, row.astype(f32), jnp.ones((1, slots), f32)]
    facts = jnp.concatenate(facts + [jnp.zeros((2, slots), f32)], axis=0).astype(bf16)
    found = mm(facts, chosen, NT).astype(i32)
    source = jnp.where(found[5:6] > 0, found[2:3], col_devs)
    words = (found[4:5] << ROW_BIT) + (source << SOURCE_BIT) + (found[3:4] << TILE_BIT)
    out[:, :places] = words + (found[0:1] << 4) + found[1:2]
    phase = iota((bins, LANES), 1)
    edge = jnp.where(phase > 0, targets + (phase - 1) * slab_tiles, 0)
    inside = (iota((bins, LANES), 0) < edge).astype(f32).astype(bf16)
    out[:, places:] = mm(sizes.astype(bf16), inside)[:1].astype(i32)
    plan_copy = pltpu.make_async_copy(out, plan, list_sem.at[2])
    plan_copy.start()
    acc[...] = jnp.zeros_like(acc)
    for copy in copies + [plan_copy]:
        copy.wait()

    @pl.loop(0, jnp.minimum(chunks, early_chunks))
    def _(k):
        tile_copy(k).wait()

    add_products(plan, 0, 0, targets, held, panel_buf, acc)

    @pl.loop(early_chunks, chunks)
    def _(k):
        tile_copy(k).wait()


def field(word, low, high):
    return (word >> low) & ((1 << (high - low)) - 1)


def add_products(plan, phase, first_row, spare_row, tiles, panel_buf, acc):
    phases = plan.shape[1] - LANES
    begin, end = plan[0, phases + phase], plan[0, phases + phase + 1]

    def panel(word):
        where = pl.multiple_of(field(word, TILE_BIT, SOURCE_BIT) * LANES, LANES)
        return panel_buf[field(word, SOURCE_BIT, ROW_BIT), :, pl.ds(where, LANES)]

    @pl.loop(0, (end - begin + GROUP * UNROLL - 1) // (GROUP * UNROLL))
    def _(g):
        first = begin + g * GROUP * UNROLL
        parts = []
        for u in range(UNROLL):
            words = [plan[0, first + GROUP * u + i] for i in range(GROUP)]
            left = jnp.concatenate([panel(word) for word in words], axis=1)
            right = jnp.concatenate([tiles[field(word, 0, TILE_BIT)] for word in words], axis=1)
            parts.append(mm(left, right, NT))
        for u in range(UNROLL):
            p = first + GROUP * u
            a = jnp.where(p < end, (plan[0, p] >> ROW_BIT) - first_row, spare_row)
            acc[a] += parts[u]


def load_panels(panels, panel_buf, sem):
    copies = [pltpu.make_async_copy(ref, panel_buf.at[m], sem.at[i]) for i, (m, ref) in enumerate(panels.items())]
    for copy in copies:
        copy.start()
    return copies


def collect_kernel(masks, *refs):
    panels, (_, panel_buf, sem) = refs[: len(masks)], refs[len(masks) :]
    for copy in load_panels(dict(zip(masks, panels)), panel_buf, sem):
        copy.wait()


def first_late_kernel(masks, odd, place, plan, *refs):
    panels = dict(zip(odd, refs))
    tiles, early, _ = refs[len(odd) : len(odd) + 3]
    sends = refs[len(odd) + 3 : -3]
    panel_buf, acc, sem = refs[-3:]
    copies = load_panels(panels, panel_buf, sem)
    make_parts(masks, place, plan, tiles, early, panel_buf, acc, sends, copies)


def make_parts(masks, place, plan, tiles, early, panel_buf, acc, sends, copies):
    for i, (mask, send) in enumerate(zip(masks, sends)):
        if i == 0 or mask != masks[i - 1]:
            late_part(mask, place, plan, tiles, early, panel_buf, acc, copies)
            copies = ()
        put(send, acc)


def late_kernel(masks, place, plan, panel_buf, tiles, early, current, previous, coupling, diag, *refs):
    sends, base, acc = refs[:-2], refs[-2], refs[-1]
    make_parts(masks + [0], place, plan, tiles, early, panel_buf, acc, sends + (base,), ())
    base[...] += diag[...] * current[...] - jnp.dot(
        coupling[...],
        previous[...],
        precision=lax.Precision.HIGHEST,
        preferred_element_type=jnp.float32,
    )


def late_part(mask, place, plan, tiles, early, panel_buf, acc, copies):
    slab_tiles = acc.shape[0] - 1
    row_devs = (early.shape[0] - 1) // slab_tiles
    first_row = (place[0] ^ mask) * slab_tiles
    for s in range(slab_tiles):
        acc[s] = early[first_row + s]
    for copy in copies:
        copy.wait()
    add_products(plan, row_devs - mask, first_row, slab_tiles, tiles, panel_buf, acc)


def put(out, acc):
    for s in range(acc.shape[0] - 1):
        out[:, s * LANES : (s + 1) * LANES] = acc[s].astype(out.dtype)


def coefficient_kernel(cells, received_count, relay, place, base, *refs):
    received = refs[:received_count]
    mass, current, stored, recurrence, keep, give, halves = refs[received_count:]
    total = base[...]
    for i, ref in enumerate(received):
        value = ref[...].astype(jnp.float32)
        if relay and i == 0:
            value = jnp.where((place[0] == 1) | (place[0] == 2), 0.0, value)
        total = total + value
    recurrence[...] = total
    weighted = total * (mass[...] * (1.0 / cells))
    basis = jnp.concatenate([current[...], stored[...]], axis=0)
    coef = dot_split(weighted, basis, NT)
    spare = -coef.shape[1] % LANES
    coef = jnp.concatenate([coef, jnp.zeros((coef.shape[0], spare), jnp.float32)], axis=1)
    halves[...] = jnp.zeros_like(halves)
    for p, (q, k) in enumerate(blocks(coef.shape)):
        halves[p // halves.shape[1], p % halves.shape[1]] = coef[q : q + 8, k : k + LANES]
    core = place[1] & 1
    keep[...] = halves[core]
    give[...] = halves[1 - core]


def residual_kernel(
    cells, place, mine, other, recurrence, mass, current, stored, residual, coef_out, gram, halves, packed
):
    width = recurrence.shape[0]
    core = place[1] & 1
    halves[core] = mine[...]
    halves[1 - core] = other[...]
    for p, (q, k) in enumerate(blocks(packed.shape)):
        packed[q : q + 8, k : k + LANES] = halves[p // halves.shape[1], p % halves.shape[1]]
    coef = packed[...]
    basis = jnp.concatenate([current[...], stored[...]], axis=0)
    coef = coef[:, : basis.shape[0]]
    coef_out[...] = coef
    value = recurrence[...] - dot_split(coef, basis)
    residual[...] = value
    local = dot_split(value * (mass[...] * (1.0 / cells)), value, NT)
    half = width // 2
    gram[...] = jnp.zeros_like(gram)
    gram[:, :width] = local[:half]
    gram[:, LANES // 2 : LANES // 2 + width] = local[half:]


def after_kernel(value, earlier, out):
    pass


def after(value, earlier):
    anywhere = pl.BlockSpec(memory_space=pl.ANY)
    return pl.pallas_call(
        after_kernel,
        out_shape=jax.ShapeDtypeStruct(value.shape, value.dtype),
        in_specs=[anywhere, anywhere],
        out_specs=anywhere,
        input_output_aliases={0: 0},
        compiler_params=limit(1),
    )(value, earlier)


def in_hbm(value):
    return pltpu.with_memory_space_constraint(value, pltpu.HBM)


def limit(mib):
    return pltpu.CompilerParams(vmem_limit_bytes=mib * MIB)


def vmem(count):
    return [pl.BlockSpec(memory_space=pltpu.VMEM)] * count


def smem(count):
    return [pl.BlockSpec(memory_space=pltpu.SMEM)] * count


def local(
    current_block,
    previous_block,
    previous_coupling,
    stored_blocks,
    stiffness_diag,
    lumped_mass,
    tile_values,
    tile_rows,
    tile_cols,
    tile_counts,
):
    row_devs = lax.axis_size("row")
    col_devs = lax.axis_size("col")
    width, slab_len = current_block.shape
    stored_count = stored_blocks.shape[0]
    slots, tile_len, _ = tile_values.shape
    slab_tiles = slab_len // tile_len
    cells = slab_len * row_devs * col_devs
    f32, bf16 = jnp.float32, jnp.bfloat16
    place = jnp.stack([lax.axis_index("row"), lax.axis_index("col")]).astype(jnp.int32)
    stored = stored_blocks.reshape(stored_count * width, slab_len)
    mass = lumped_mass.reshape(1, slab_len)
    diag = stiffness_diag.reshape(1, slab_len)
    slab = jax.ShapeDtypeStruct((width, slab_len), f32)

    targets = row_devs * slab_tiles
    anywhere = [pl.BlockSpec(memory_space=pl.ANY)]
    panel_shape = (col_devs + 1, width, slab_len)
    early_shape = (targets + 1, width, tile_len)
    part_acc = pltpu.VMEM((slab_tiles + 1, width, tile_len), f32)

    def cost(flops):
        return pl.CostEstimate(flops=flops, bytes_accessed=flops // width, transcendentals=0)

    with jax.named_scope("gather"):
        rounded = current_block.astype(bf16)
        panels = [rounded] + [None] * (col_devs - 1)
        for m in range(col_devs - 2, 0, -2):
            panels[m] = swap(rounded, "col", m)
        panels[1] = swap(rounded, "col", 1)

    with jax.named_scope("early"):
        places = -(-(slots + (GROUP - 1) * 2 * targets + GROUP * UNROLL) // LANES) * LANES
        plan_shape = (1, places + LANES)
        plan, held, early, gathered = pl.pallas_call(
            functools.partial(early_kernel, row_devs, col_devs, slab_tiles),
            out_shape=[
                jax.ShapeDtypeStruct(plan_shape, jnp.int32),
                pltpu.VMEM(tile_values.shape, bf16),
                pltpu.VMEM(early_shape, f32),
                pltpu.VMEM(panel_shape, bf16),
            ],
            in_specs=smem(2) + [pl.BlockSpec(memory_space=pltpu.HBM)] * 3 + anywhere * 2,
            out_specs=vmem(4),
            scratch_shapes=[
                pltpu.VMEM((1, slots), jnp.int32),
                pltpu.VMEM((1, slots), jnp.int32),
                pltpu.SMEM(plan_shape, jnp.int32),
                pltpu.SemaphoreType.DMA((slots // CHUNK,)),
                pltpu.SemaphoreType.DMA((3,)),
                pltpu.SemaphoreType.DMA((2,)),
            ],
            compiler_params=limit(12),
            cost_estimate=cost(2 * slots * width * tile_len * tile_len),
        )(
            place,
            tile_counts,
            in_hbm(tile_rows.reshape(1, slots)),
            in_hbm(tile_cols.reshape(1, slots)),
            in_hbm(tile_values),
            panels[0],
            panels[1],
        )

    with jax.named_scope("gather"):
        for m in range(col_devs - 2, 0, -2):
            panels[m] = after(panels[m], early)
            panels[m + 1] = swap(panels[m], "col", 1)
        even, odd = list(range(2, col_devs, 2)), list(range(3, col_devs, 2))
        gathered = pl.pallas_call(
            functools.partial(collect_kernel, even),
            out_shape=pltpu.VMEM(panel_shape, bf16),
            in_specs=anywhere * len(even) + vmem(1),
            out_specs=vmem(1)[0],
            scratch_shapes=[pltpu.SemaphoreType.DMA((len(even),))],
            input_output_aliases={len(even): 0},
            compiler_params=limit(1),
            cost_estimate=cost(width),
        )(*[panels[m] for m in even], gathered)

    with jax.named_scope("late"):
        relay = row_devs == 4
        first_masks = [2, 3, 3] if relay else [row_devs - 1]
        last_masks = [1] if relay else list(range(row_devs - 2, 0, -1))
        part = jax.ShapeDtypeStruct((width, slab_len), bf16)
        *firsts, gathered = pl.pallas_call(
            functools.partial(first_late_kernel, first_masks, odd),
            out_shape=([part, part, slab] if relay else [part]) + [pltpu.VMEM(panel_shape, bf16)],
            in_specs=smem(2) + anywhere * len(odd) + vmem(3),
            out_specs=vmem(len(first_masks) + 1),
            scratch_shapes=[part_acc, pltpu.SemaphoreType.DMA((len(odd),))],
            input_output_aliases={4 + len(odd): len(first_masks)},
            compiler_params=limit(8),
            cost_estimate=cost(width),
        )(place, plan, *[panels[m] for m in odd], held, early, gathered)
        *lasts, base = pl.pallas_call(
            functools.partial(late_kernel, last_masks),
            out_shape=[part] * len(last_masks) + [slab],
            in_specs=smem(2) + vmem(7),
            out_specs=vmem(len(last_masks) + 1),
            scratch_shapes=[part_acc],
            compiler_params=limit(8),
            cost_estimate=cost(width),
        )(place, plan, gathered, held, early, current_block, previous_block, previous_coupling, diag)
        if relay:
            first = lax.ppermute(firsts[0], "row", [(0, 1), (3, 2), (1, 3), (2, 0)])
            joined = (firsts[2] + first.astype(f32)).astype(bf16)
            received = [
                first,
                lax.ppermute(firsts[1], "row", [(0, 3), (3, 0)]),
                swap(after(lasts[0], joined), "row", 1),
                lax.ppermute(joined, "row", [(1, 2), (2, 1)]),
            ]
        else:
            received = [swap(firsts[0], "row", first_masks[0])]
            received += [swap(last, "row", m) for m, last in zip(last_masks, lasts)]

    basis_rows = (stored_count + 1) * width
    padded = (width, -(-basis_rows // LANES) * LANES)
    half = (-(-len(blocks(padded)) // 2), 8, LANES)
    with jax.named_scope("coefficients"):
        recurrence, keep, give = pl.pallas_call(
            functools.partial(coefficient_kernel, cells, len(received), relay),
            out_shape=[slab] + [jax.ShapeDtypeStruct(half, f32)] * 2,
            in_specs=smem(1) + vmem(len(received) + 4),
            out_specs=vmem(3),
            scratch_shapes=[pltpu.VMEM((2,) + half, f32)],
            compiler_params=limit(24),
        )(place, base, *received, mass, current_block, stored)
        mine = keep + swap(give, "col", 1)
        mine = total_by_core(mine)
        other = swap(mine, "col", 1)

    with jax.named_scope("residual"):
        residual_block, coef, gram = pl.pallas_call(
            functools.partial(residual_kernel, cells),
            out_shape=[
                pltpu.VMEM((width, slab_len), f32),
                jax.ShapeDtypeStruct((width, basis_rows), f32),
                jax.ShapeDtypeStruct((width // 2, LANES), f32),
            ],
            in_specs=smem(1) + vmem(6),
            out_specs=vmem(3),
            scratch_shapes=[pltpu.VMEM((2,) + half, f32), pltpu.VMEM(padded, f32)],
            compiler_params=limit(24),
        )(place, mine, other, recurrence, mass, current_block, stored)
        coefficients = coef.T.reshape(stored_count + 1, width, width)

    with jax.named_scope("gram"):
        gram = gram + swap(gram, "col", 1)
        gram = total(total(gram, "col", 2), "row", 1)
        gram = jnp.concatenate(
            [gram[:, :width], gram[:, LANES // 2 : LANES // 2 + width]], axis=0
        )
    return (residual_block, coefficients, gram)


def solution(mesh):
    return jax.shard_map(
        local,
        mesh=mesh,
        in_specs=(
            P(None, ("row", "col")),
            P(None, ("row", "col")),
            P(),
            P(None, None, ("row", "col")),
            P(("row", "col")),
            P(("row", "col")),
            P(("row", "col"), None, None),
            P(("row", "col")),
            P(("row", "col")),
            P(("row", "col")),
        ),
        out_specs=(P(None, ("row", "col")), P(), P()),
        check_vma=False,
    )
```

```python
import functools

import jax
import jax.numpy as jnp
from jax import lax
from jax.experimental import pallas as pl
from jax.experimental.pallas import tpu as pltpu
from jax.sharding import PartitionSpec as P

LANES = 128
CHUNK = 32
GROUP = 2
UNROLL = 8
TILE_BIT, SOURCE_BIT, ROW_BIT = 10, 15, 20
NT = (((1,), (1,)), ((), ()))
MIB = 1 << 20


def swap(value, axis, mask):
    count = lax.axis_size(axis)
    return lax.ppermute(value, axis, [(i, i ^ mask) for i in range(count)])


def tree_sum(values):
    while len(values) > 1:
        values = [values[i] + values[i + 1] for i in range(0, len(values), 2)]
    return values[0]


def total(value, axis, step):
    return tree_sum([value] + [swap(value, axis, m) for m in range(step, lax.axis_size(axis), step)])


def total_by_core(value):
    row_devs, col_devs = lax.axis_size("row"), lax.axis_size("col")
    if col_devs != 2 * row_devs:
        return total(total(value, "col", 2), "row", 1)
    places = [(r, c) for r in range(row_devs) for c in range(col_devs)]
    for turn in range(2):
        values = [value]
        for m in range(1, row_devs):
            partners = [(r, c ^ (2 * m)) if c % 2 == turn else (r ^ m, c) for r, c in places]
            trades = [(i, r * col_devs + c) for i, (r, c) in enumerate(partners)]
            values.append(lax.ppermute(value, ("row", "col"), trades))
        value = tree_sum(values)
    return value


def split(value):
    high = value.astype(jnp.bfloat16)
    low = (value - high.astype(jnp.float32)).astype(jnp.bfloat16)
    return high, low


def mm(a, b, dims=(((1,), (0,)), ((), ()))):
    return lax.dot_general(a, b, dims, preferred_element_type=jnp.float32)


def dot_split(a, b, dims=(((1,), (0,)), ((), ()))):
    rows = a.shape[0]
    a_high, a_low = split(a)
    b_high, b_low = split(b)
    both = mm(jnp.concatenate([a_high, a_low], axis=0), b_high, dims)
    return both[:rows] + both[rows:] + mm(a_high, b_low, dims)


def blocks(shape):
    return [(q, k) for q in range(0, shape[0], 8) for k in range(0, shape[1], LANES)]


def early_kernel(
    row_devs,
    col_devs,
    slab_tiles,
    place,
    counts,
    rows_hbm,
    cols_hbm,
    tiles,
    own_panel,
    near_panel,
    out,
    held,
    acc,
    panel_buf,
    rows,
    cols,
    plan,
    tile_sem,
    list_sem,
    panel_sem,
):
    chunks = (counts[0] + CHUNK - 1) // CHUNK
    row_copy = pltpu.make_async_copy(rows_hbm, rows, list_sem.at[0])
    col_copy = pltpu.make_async_copy(cols_hbm, cols, list_sem.at[1])
    row_copy.start()
    col_copy.start()

    def tile_copy(k):
        window = pl.ds(k * CHUNK, CHUNK)
        return pltpu.make_async_copy(tiles.at[window], held.at[window], tile_sem.at[k])

    @pl.loop(0, chunks)
    def _(k):
        tile_copy(k).start()

    copies = load_panels({0: own_panel, 1: near_panel}, panel_buf, panel_sem)
    zero_panel = panel_buf.shape[0] - 1
    panel_buf[zero_panel, :, :LANES] = jnp.zeros((panel_buf.shape[1], LANES), jnp.bfloat16)
    f32, bf16, i32 = jnp.float32, jnp.bfloat16, jnp.int32
    slots, places = rows.shape[1], out.shape[1] - LANES
    early_chunks = 3 * slots // CHUNK // 4
    targets = row_devs * slab_tiles
    bins = 2 * targets

    def iota(shape, dim):
        return lax.broadcasted_iota(i32, shape, dim)

    slot = iota((1, slots), 1)
    occupied = slot < counts[0]
    earlier = (iota((slots, slots), 0) < iota((slots, slots), 1)).astype(f32).astype(bf16)
    row_copy.wait()
    col_copy.wait()
    row = rows[...]
    row_owner = jnp.floor(row.astype(f32) * (1.0 / slab_tiles)).astype(i32)
    col_f = cols[...].astype(f32)
    source_f = jnp.floor(col_f * (1.0 / slab_tiles))
    source = source_f.astype(i32) ^ place[1]
    tile_f = col_f - slab_tiles * source_f
    far = row_devs - 1 - (row_owner ^ place[0])
    late_bin = targets + far * slab_tiles + row - row_owner * slab_tiles
    early = (source < 2) & (slot < early_chunks * CHUNK)
    bin_of = jnp.where(occupied, jnp.where(early, row, late_bin), -1)
    member = (iota((bins, slots), 0) == bin_of).astype(f32)
    member_bf = member.astype(bf16)
    rank = jnp.sum(member * mm(member_bf, earlier), axis=0, keepdims=True)
    sizes = mm(jnp.ones((8, slots), bf16), member_bf, NT)
    sizes = GROUP * jnp.floor((sizes + (GROUP - 1.0)) * (1.0 / GROUP))
    before = (iota((bins, bins), 1) < iota((bins, bins), 0)).astype(f32)
    begin = jnp.sum(before * sizes[:1], axis=1, keepdims=True)
    position = jnp.sum(member * begin, axis=0, keepdims=True) + rank
    position = jnp.where(occupied, position.astype(i32), -1)
    chosen = (iota((places, slots), 0) == position).astype(f32).astype(bf16)
    slot_f = slot.astype(f32)
    slot_high = jnp.floor(slot_f * (1.0 / 16.0))
    facts = [slot_high, slot_f - 16.0 * slot_high, source.astype(f32), tile_f, row.astype(f32), jnp.ones((1, slots), f32)]
    facts = jnp.concatenate(facts + [jnp.zeros((2, slots), f32)], axis=0).astype(bf16)
    found = mm(facts, chosen, NT).astype(i32)
    source = jnp.where(found[5:6] > 0, found[2:3], col_devs)
    words = (found[4:5] << ROW_BIT) + (source << SOURCE_BIT) + (found[3:4] << TILE_BIT)
    out[:, :places] = words + (found[0:1] << 4) + found[1:2]
    phase = iota((bins, LANES), 1)
    edge = jnp.where(phase > 0, targets + (phase - 1) * slab_tiles, 0)
    inside = (iota((bins, LANES), 0) < edge).astype(f32).astype(bf16)
    out[:, places:] = mm(sizes.astype(bf16), inside)[:1].astype(i32)
    plan_copy = pltpu.make_async_copy(out, plan, list_sem.at[2])
    plan_copy.start()
    acc[...] = jnp.zeros_like(acc)
    for copy in copies + [plan_copy]:
        copy.wait()

    @pl.loop(0, jnp.minimum(chunks, early_chunks))
    def _(k):
        tile_copy(k).wait()

    add_products(plan, 0, 0, targets, held, panel_buf, acc)

    @pl.loop(early_chunks, chunks)
    def _(k):
        tile_copy(k).wait()


def field(word, low, high):
    return (word >> low) & ((1 << (high - low)) - 1)


def add_products(plan, phase, first_row, spare_row, tiles, panel_buf, acc):
    phases = plan.shape[1] - LANES
    begin, end = plan[0, phases + phase], plan[0, phases + phase + 1]

    def panel(word):
        where = pl.multiple_of(field(word, TILE_BIT, SOURCE_BIT) * LANES, LANES)
        return panel_buf[field(word, SOURCE_BIT, ROW_BIT), :, pl.ds(where, LANES)]

    @pl.loop(0, (end - begin + GROUP * UNROLL - 1) // (GROUP * UNROLL))
    def _(g):
        first = begin + g * GROUP * UNROLL
        parts = []
        for u in range(UNROLL):
            words = [plan[0, first + GROUP * u + i] for i in range(GROUP)]
            left = jnp.concatenate([panel(word) for word in words], axis=1)
            right = jnp.concatenate([tiles[field(word, 0, TILE_BIT)] for word in words], axis=1)
            parts.append(mm(left, right, NT))
        for u in range(UNROLL):
            p = first + GROUP * u
            a = jnp.where(p < end, (plan[0, p] >> ROW_BIT) - first_row, spare_row)
            acc[a] += parts[u]


def load_panels(panels, panel_buf, sem):
    copies = [pltpu.make_async_copy(ref, panel_buf.at[m], sem.at[i]) for i, (m, ref) in enumerate(panels.items())]
    for copy in copies:
        copy.start()
    return copies


def collect_kernel(masks, *refs):
    panels, (_, panel_buf, sem) = refs[: len(masks)], refs[len(masks) :]
    for copy in load_panels(dict(zip(masks, panels)), panel_buf, sem):
        copy.wait()


def first_late_kernel(masks, odd, place, plan, *refs):
    panels = dict(zip(odd, refs))
    tiles, early, _ = refs[len(odd) : len(odd) + 3]
    sends = refs[len(odd) + 3 : -3]
    panel_buf, acc, sem = refs[-3:]
    copies = load_panels(panels, panel_buf, sem)
    for mask, send in zip(masks, sends):
        late_part(mask, place, plan, tiles, early, panel_buf, acc, copies)
        put(send, acc)
        copies = ()


def late_kernel(masks, place, plan, panel_buf, tiles, early, *refs):
    sends, acc = refs[:-1], refs[-1]
    for i, (mask, send) in enumerate(zip(masks, sends)):
        if i == 0 or mask != masks[i - 1]:
            late_part(mask, place, plan, tiles, early, panel_buf, acc, ())
        put(send, acc)


def own_kernel(place, plan, panel_buf, tiles, early, current, previous, coupling, diag, base, acc):
    late_part(0, place, plan, tiles, early, panel_buf, acc, ())
    put(base, acc)
    base[...] += diag[...] * current[...] - jnp.dot(
        coupling[...],
        previous[...],
        precision=lax.Precision.HIGHEST,
        preferred_element_type=jnp.float32,
    )


def late_part(mask, place, plan, tiles, early, panel_buf, acc, copies):
    slab_tiles = acc.shape[0] - 1
    row_devs = (early.shape[0] - 1) // slab_tiles
    first_row = (place[0] ^ mask) * slab_tiles
    for s in range(slab_tiles):
        acc[s] = early[first_row + s]
    for copy in copies:
        copy.wait()
    add_products(plan, row_devs - mask, first_row, slab_tiles, tiles, panel_buf, acc)


def put(out, acc):
    for s in range(acc.shape[0] - 1):
        out[:, s * LANES : (s + 1) * LANES] = acc[s].astype(out.dtype)


def coefficient_kernel(cells, received_count, relay, place, base, *refs):
    received = refs[:received_count]
    mass, current, stored, recurrence, keep, give, halves = refs[received_count:]
    total = base[...]
    for i, ref in enumerate(received):
        value = ref[...].astype(jnp.float32)
        if relay and i == 0:
            value = jnp.where((place[0] == 1) | (place[0] == 2), 0.0, value)
        total = total + value
    recurrence[...] = total
    weighted = total * (mass[...] * (1.0 / cells))
    basis = jnp.concatenate([current[...], stored[...]], axis=0)
    coef = dot_split(weighted, basis, NT)
    spare = -coef.shape[1] % LANES
    coef = jnp.concatenate([coef, jnp.zeros((coef.shape[0], spare), jnp.float32)], axis=1)
    halves[...] = jnp.zeros_like(halves)
    for p, (q, k) in enumerate(blocks(coef.shape)):
        halves[p // halves.shape[1], p % halves.shape[1]] = coef[q : q + 8, k : k + LANES]
    core = place[1] & 1
    keep[...] = halves[core]
    give[...] = halves[1 - core]


def residual_kernel(
    cells, place, mine, other, recurrence, mass, current, stored, residual, coef_out, gram, halves, packed
):
    width = recurrence.shape[0]
    core = place[1] & 1
    halves[core] = mine[...]
    halves[1 - core] = other[...]
    for p, (q, k) in enumerate(blocks(packed.shape)):
        packed[q : q + 8, k : k + LANES] = halves[p // halves.shape[1], p % halves.shape[1]]
    coef = packed[...]
    basis = jnp.concatenate([current[...], stored[...]], axis=0)
    coef = coef[:, : basis.shape[0]]
    coef_out[...] = coef
    value = recurrence[...] - dot_split(coef, basis)
    residual[...] = value
    local = dot_split(value * (mass[...] * (1.0 / cells)), value, NT)
    half = width // 2
    gram[...] = jnp.zeros_like(gram)
    gram[:, :width] = local[:half]
    gram[:, LANES // 2 : LANES // 2 + width] = local[half:]


def after_kernel(value, earlier, out):
    pass


def after(value, earlier):
    anywhere = pl.BlockSpec(memory_space=pl.ANY)
    return pl.pallas_call(
        after_kernel,
        out_shape=jax.ShapeDtypeStruct(value.shape, value.dtype),
        in_specs=[anywhere, anywhere],
        out_specs=anywhere,
        input_output_aliases={0: 0},
        compiler_params=limit(1),
    )(value, earlier)


def in_hbm(value):
    return pltpu.with_memory_space_constraint(value, pltpu.HBM)


def limit(mib):
    return pltpu.CompilerParams(vmem_limit_bytes=mib * MIB)


def vmem(count):
    return [pl.BlockSpec(memory_space=pltpu.VMEM)] * count


def smem(count):
    return [pl.BlockSpec(memory_space=pltpu.SMEM)] * count


def local(
    current_block,
    previous_block,
    previous_coupling,
    stored_blocks,
    stiffness_diag,
    lumped_mass,
    tile_values,
    tile_rows,
    tile_cols,
    tile_counts,
):
    row_devs = lax.axis_size("row")
    col_devs = lax.axis_size("col")
    width, slab_len = current_block.shape
    stored_count = stored_blocks.shape[0]
    slots, tile_len, _ = tile_values.shape
    slab_tiles = slab_len // tile_len
    cells = slab_len * row_devs * col_devs
    f32, bf16 = jnp.float32, jnp.bfloat16
    place = jnp.stack([lax.axis_index("row"), lax.axis_index("col")]).astype(jnp.int32)
    stored = stored_blocks.reshape(stored_count * width, slab_len)
    mass = lumped_mass.reshape(1, slab_len)
    diag = stiffness_diag.reshape(1, slab_len)
    slab = jax.ShapeDtypeStruct((width, slab_len), f32)

    targets = row_devs * slab_tiles
    anywhere = [pl.BlockSpec(memory_space=pl.ANY)]
    panel_shape = (col_devs + 1, width, slab_len)
    early_shape = (targets + 1, width, tile_len)
    part_acc = pltpu.VMEM((slab_tiles + 1, width, tile_len), f32)

    def cost(flops):
        return pl.CostEstimate(flops=flops, bytes_accessed=flops // width, transcendentals=0)

    with jax.named_scope("gather"):
        rounded = current_block.astype(bf16)
        panels = [rounded] + [None] * (col_devs - 1)
        for m in range(col_devs - 2, 0, -2):
            panels[m] = swap(rounded, "col", m)
        panels[1] = swap(rounded, "col", 1)

    with jax.named_scope("early"):
        places = -(-(slots + (GROUP - 1) * 2 * targets + GROUP * UNROLL) // LANES) * LANES
        plan_shape = (1, places + LANES)
        plan, held, early, gathered = pl.pallas_call(
            functools.partial(early_kernel, row_devs, col_devs, slab_tiles),
            out_shape=[
                jax.ShapeDtypeStruct(plan_shape, jnp.int32),
                pltpu.VMEM(tile_values.shape, bf16),
                pltpu.VMEM(early_shape, f32),
                pltpu.VMEM(panel_shape, bf16),
            ],
            in_specs=smem(2) + [pl.BlockSpec(memory_space=pltpu.HBM)] * 3 + anywhere * 2,
            out_specs=vmem(4),
            scratch_shapes=[
                pltpu.VMEM((1, slots), jnp.int32),
                pltpu.VMEM((1, slots), jnp.int32),
                pltpu.SMEM(plan_shape, jnp.int32),
                pltpu.SemaphoreType.DMA((slots // CHUNK,)),
                pltpu.SemaphoreType.DMA((3,)),
                pltpu.SemaphoreType.DMA((2,)),
            ],
            compiler_params=limit(12),
            cost_estimate=cost(2 * slots * width * tile_len * tile_len),
        )(
            place,
            tile_counts,
            in_hbm(tile_rows.reshape(1, slots)),
            in_hbm(tile_cols.reshape(1, slots)),
            in_hbm(tile_values),
            panels[0],
            panels[1],
        )

    with jax.named_scope("gather"):
        for m in range(col_devs - 2, 0, -2):
            panels[m] = after(panels[m], early)
            panels[m + 1] = swap(panels[m], "col", 1)
        even, odd = list(range(2, col_devs, 2)), list(range(3, col_devs, 2))
        gathered = pl.pallas_call(
            functools.partial(collect_kernel, even),
            out_shape=pltpu.VMEM(panel_shape, bf16),
            in_specs=anywhere * len(even) + vmem(1),
            out_specs=vmem(1)[0],
            scratch_shapes=[pltpu.SemaphoreType.DMA((len(even),))],
            input_output_aliases={len(even): 0},
            compiler_params=limit(1),
            cost_estimate=cost(width),
        )(*[panels[m] for m in even], gathered)

    with jax.named_scope("late"):
        relay = row_devs == 4
        first_mask = 2 if relay else row_devs - 1
        masks = [3, 3, 1] if relay else list(range(row_devs - 2, 0, -1))
        part = jax.ShapeDtypeStruct((width, slab_len), bf16)
        first, gathered = pl.pallas_call(
            functools.partial(first_late_kernel, [first_mask], odd),
            out_shape=[part, pltpu.VMEM(panel_shape, bf16)],
            in_specs=smem(2) + anywhere * len(odd) + vmem(3),
            out_specs=vmem(2),
            scratch_shapes=[part_acc, pltpu.SemaphoreType.DMA((len(odd),))],
            input_output_aliases={4 + len(odd): 1},
            compiler_params=limit(8),
            cost_estimate=cost(width),
        )(place, plan, *[panels[m] for m in odd], held, early, gathered)
        parts = pl.pallas_call(
            functools.partial(late_kernel, masks),
            out_shape=[part, slab, part] if relay else [part] * len(masks),
            in_specs=smem(2) + vmem(3),
            out_specs=vmem(len(masks)),
            scratch_shapes=[part_acc],
            compiler_params=limit(8),
            cost_estimate=cost(width),
        )(place, plan, gathered, held, early)
        if relay:
            first = lax.ppermute(first, "row", [(0, 1), (3, 2), (1, 3), (2, 0)])
            joined = (parts[1] + first.astype(f32)).astype(bf16)
            received = [
                first,
                swap(parts[2], "row", 1),
                lax.ppermute(joined, "row", [(1, 2), (2, 1)]),
                lax.ppermute(parts[0], "row", [(0, 3), (3, 0)]),
            ]
        else:
            received = [swap(first, "row", first_mask)]
            received += [swap(part, "row", m) for m, part in zip(masks, parts)]
        base = pl.pallas_call(
            own_kernel,
            out_shape=slab,
            in_specs=smem(2) + vmem(7),
            out_specs=vmem(1)[0],
            scratch_shapes=[part_acc],
            compiler_params=limit(8),
            cost_estimate=cost(width),
        )(place, plan, gathered, held, early, current_block, previous_block, previous_coupling, diag)

    basis_rows = (stored_count + 1) * width
    padded = (width, -(-basis_rows // LANES) * LANES)
    half = (-(-len(blocks(padded)) // 2), 8, LANES)
    with jax.named_scope("coefficients"):
        recurrence, keep, give = pl.pallas_call(
            functools.partial(coefficient_kernel, cells, len(received), relay),
            out_shape=[slab] + [jax.ShapeDtypeStruct(half, f32)] * 2,
            in_specs=smem(1) + vmem(len(received) + 4),
            out_specs=vmem(3),
            scratch_shapes=[pltpu.VMEM((2,) + half, f32)],
            compiler_params=limit(24),
        )(place, base, *received, mass, current_block, stored)
        mine = keep + swap(give, "col", 1)
        mine = total_by_core(mine)
        other = swap(mine, "col", 1)

    with jax.named_scope("residual"):
        residual_block, coef, gram = pl.pallas_call(
            functools.partial(residual_kernel, cells),
            out_shape=[
                pltpu.VMEM((width, slab_len), f32),
                jax.ShapeDtypeStruct((width, basis_rows), f32),
                jax.ShapeDtypeStruct((width // 2, LANES), f32),
            ],
            in_specs=smem(1) + vmem(6),
            out_specs=vmem(3),
            scratch_shapes=[pltpu.VMEM((2,) + half, f32), pltpu.VMEM(padded, f32)],
            compiler_params=limit(24),
        )(place, mine, other, recurrence, mass, current_block, stored)
        coefficients = coef.T.reshape(stored_count + 1, width, width)

    with jax.named_scope("gram"):
        gram = gram + swap(gram, "col", 1)
        gram = total(total(gram, "col", 2), "row", 1)
        gram = jnp.concatenate(
            [gram[:, :width], gram[:, LANES // 2 : LANES // 2 + width]], axis=0
        )
    return (residual_block, coefficients, gram)


def solution(mesh):
    return jax.shard_map(
        local,
        mesh=mesh,
        in_specs=(
            P(None, ("row", "col")),
            P(None, ("row", "col")),
            P(),
            P(None, None, ("row", "col")),
            P(("row", "col")),
            P(("row", "col")),
            P(("row", "col"), None, None),
            P(("row", "col")),
            P(("row", "col")),
            P(("row", "col")),
        ),
        out_specs=(P(None, ("row", "col")), P(), P()),
        check_vma=False,
    )
```

```python
import functools

import jax
import jax.numpy as jnp
from jax import lax
from jax.experimental import pallas as pl
from jax.experimental.pallas import tpu as pltpu
from jax.sharding import PartitionSpec as P

LANES = 128
CHUNK = 32
GROUP = 2
UNROLL = 8
TILE_BIT, SOURCE_BIT, ROW_BIT = 10, 15, 20
NT = (((1,), (1,)), ((), ()))
MIB = 1 << 20


def swap(value, axis, mask):
    count = lax.axis_size(axis)
    return lax.ppermute(value, axis, [(i, i ^ mask) for i in range(count)])


def tree_sum(values):
    while len(values) > 1:
        values = [values[i] + values[i + 1] for i in range(0, len(values), 2)]
    return values[0]


def total(value, axis, step):
    return tree_sum([value] + [swap(value, axis, m) for m in range(step, lax.axis_size(axis), step)])


def total_by_core(value):
    row_devs, col_devs = lax.axis_size("row"), lax.axis_size("col")
    if col_devs != 2 * row_devs:
        return total(total(value, "col", 2), "row", 1)
    places = [(r, c) for r in range(row_devs) for c in range(col_devs)]
    for turn in range(2):
        values = [value]
        for m in range(1, row_devs):
            partners = [(r, c ^ (2 * m)) if c % 2 == turn else (r ^ m, c) for r, c in places]
            trades = [(i, r * col_devs + c) for i, (r, c) in enumerate(partners)]
            values.append(lax.ppermute(value, ("row", "col"), trades))
        value = tree_sum(values)
    return value


def split(value):
    high = value.astype(jnp.bfloat16)
    low = (value - high.astype(jnp.float32)).astype(jnp.bfloat16)
    return high, low


def mm(a, b, dims=(((1,), (0,)), ((), ()))):
    return lax.dot_general(a, b, dims, preferred_element_type=jnp.float32)


def dot_split(a, b, dims=(((1,), (0,)), ((), ()))):
    rows = a.shape[0]
    a_high, a_low = split(a)
    b_high, b_low = split(b)
    both = mm(jnp.concatenate([a_high, a_low], axis=0), b_high, dims)
    return both[:rows] + both[rows:] + mm(a_high, b_low, dims)


def blocks(shape):
    return [(q, k) for q in range(0, shape[0], 8) for k in range(0, shape[1], LANES)]


def early_kernel(
    row_devs,
    col_devs,
    slab_tiles,
    place,
    counts,
    rows_hbm,
    cols_hbm,
    tiles,
    own_panel,
    near_panel,
    plan,
    held,
    acc,
    panel_buf,
    rows,
    cols,
    out,
    tile_sem,
    list_sem,
    panel_sem,
):
    chunks = (counts[0] + CHUNK - 1) // CHUNK
    row_copy = pltpu.make_async_copy(rows_hbm, rows, list_sem.at[0])
    col_copy = pltpu.make_async_copy(cols_hbm, cols, list_sem.at[1])
    row_copy.start()
    col_copy.start()

    def tile_copy(k):
        window = pl.ds(k * CHUNK, CHUNK)
        return pltpu.make_async_copy(tiles.at[window], held.at[window], tile_sem.at[k])

    @pl.loop(0, chunks)
    def _(k):
        tile_copy(k).start()

    copies = load_panels({0: own_panel, 1: near_panel}, panel_buf, panel_sem)
    zero_panel = panel_buf.shape[0] - 1
    panel_buf[zero_panel, :, :LANES] = jnp.zeros((panel_buf.shape[1], LANES), jnp.bfloat16)
    f32, bf16, i32 = jnp.float32, jnp.bfloat16, jnp.int32
    slots, places = rows.shape[1], out.shape[1] - LANES
    early_chunks = 3 * slots // CHUNK // 4
    targets = row_devs * slab_tiles
    bins = 2 * targets

    def iota(shape, dim):
        return lax.broadcasted_iota(i32, shape, dim)

    slot = iota((1, slots), 1)
    occupied = slot < counts[0]
    earlier = (iota((slots, slots), 0) < iota((slots, slots), 1)).astype(f32).astype(bf16)
    row_copy.wait()
    col_copy.wait()
    row = rows[...]
    row_owner = jnp.floor(row.astype(f32) * (1.0 / slab_tiles)).astype(i32)
    col_f = cols[...].astype(f32)
    source_f = jnp.floor(col_f * (1.0 / slab_tiles))
    source = source_f.astype(i32) ^ place[1]
    tile_f = col_f - slab_tiles * source_f
    far = row_devs - 1 - (row_owner ^ place[0])
    late_bin = targets + far * slab_tiles + row - row_owner * slab_tiles
    early = (source < 2) & (slot < early_chunks * CHUNK)
    bin_of = jnp.where(occupied, jnp.where(early, row, late_bin), -1)
    member = (iota((bins, slots), 0) == bin_of).astype(f32)
    member_bf = member.astype(bf16)
    rank = jnp.sum(member * mm(member_bf, earlier), axis=0, keepdims=True)
    sizes = mm(jnp.ones((8, slots), bf16), member_bf, NT)
    sizes = GROUP * jnp.floor((sizes + (GROUP - 1.0)) * (1.0 / GROUP))
    before = (iota((bins, bins), 1) < iota((bins, bins), 0)).astype(f32)
    begin = jnp.sum(before * sizes[:1], axis=1, keepdims=True)
    position = jnp.sum(member * begin, axis=0, keepdims=True) + rank
    position = jnp.where(occupied, position.astype(i32), -1)
    chosen = (iota((places, slots), 0) == position).astype(f32).astype(bf16)
    slot_f = slot.astype(f32)
    slot_high = jnp.floor(slot_f * (1.0 / 16.0))
    facts = [slot_high, slot_f - 16.0 * slot_high, source.astype(f32), tile_f, row.astype(f32), jnp.ones((1, slots), f32)]
    facts = jnp.concatenate(facts + [jnp.zeros((2, slots), f32)], axis=0).astype(bf16)
    found = mm(facts, chosen, NT).astype(i32)
    source = jnp.where(found[5:6] > 0, found[2:3], col_devs)
    words = (found[4:5] << ROW_BIT) + (source << SOURCE_BIT) + (found[3:4] << TILE_BIT)
    out[:, :places] = words + (found[0:1] << 4) + found[1:2]
    phase = iota((bins, LANES), 1)
    edge = jnp.where(phase > 0, targets + (phase - 1) * slab_tiles, 0)
    inside = (iota((bins, LANES), 0) < edge).astype(f32).astype(bf16)
    edges = mm(sizes.astype(bf16), inside)[:1].astype(i32)
    lane = iota((1, LANES), 1)
    edges = jnp.where(lane == LANES - 2, place[0], jnp.where(lane == LANES - 1, place[1], edges))
    out[:, places:] = edges
    plan_copy = pltpu.make_async_copy(out, plan, list_sem.at[2])
    plan_copy.start()
    acc[...] = jnp.zeros_like(acc)
    for copy in copies + [plan_copy]:
        copy.wait()

    @pl.loop(0, jnp.minimum(chunks, early_chunks))
    def _(k):
        tile_copy(k).wait()

    add_products(plan, 0, 0, targets, held, panel_buf, acc)

    @pl.loop(early_chunks, chunks)
    def _(k):
        tile_copy(k).wait()


def row_of(plan):
    return plan[0, plan.shape[1] - 2]


def core_of(plan):
    return plan[0, plan.shape[1] - 1] & 1


def field(word, low, high):
    return (word >> low) & ((1 << (high - low)) - 1)


def add_products(plan, phase, first_row, spare_row, tiles, panel_buf, acc):
    phases = plan.shape[1] - LANES
    begin, end = plan[0, phases + phase], plan[0, phases + phase + 1]

    def panel(word):
        where = pl.multiple_of(field(word, TILE_BIT, SOURCE_BIT) * LANES, LANES)
        return panel_buf[field(word, SOURCE_BIT, ROW_BIT), :, pl.ds(where, LANES)]

    @pl.loop(0, (end - begin + GROUP * UNROLL - 1) // (GROUP * UNROLL))
    def _(g):
        first = begin + g * GROUP * UNROLL
        parts = []
        for u in range(UNROLL):
            words = [plan[0, first + GROUP * u + i] for i in range(GROUP)]
            left = jnp.concatenate([panel(word) for word in words], axis=1)
            right = jnp.concatenate([tiles[field(word, 0, TILE_BIT)] for word in words], axis=1)
            parts.append(mm(left, right, NT))
        for u in range(UNROLL):
            p = first + GROUP * u
            a = jnp.where(p < end, (plan[0, p] >> ROW_BIT) - first_row, spare_row)
            acc[a] += parts[u]


def load_panels(panels, panel_buf, sem):
    copies = [pltpu.make_async_copy(ref, panel_buf.at[m], sem.at[i]) for i, (m, ref) in enumerate(panels.items())]
    for copy in copies:
        copy.start()
    return copies


def collect_kernel(masks, *refs):
    panels, (_, panel_buf, sem) = refs[: len(masks)], refs[len(masks) :]
    for copy in load_panels(dict(zip(masks, panels)), panel_buf, sem):
        copy.wait()


def first_late_kernel(masks, odd, plan, *refs):
    panels = dict(zip(odd, refs))
    tiles, early, _ = refs[len(odd) : len(odd) + 3]
    sends = refs[len(odd) + 3 : -3]
    panel_buf, acc, sem = refs[-3:]
    copies = load_panels(panels, panel_buf, sem)
    for mask, send in zip(masks, sends):
        late_part(mask, plan, tiles, early, panel_buf, acc, copies)
        put(send, acc)
        copies = ()


def late_kernel(masks, plan, panel_buf, tiles, early, *refs):
    sends, acc = refs[:-1], refs[-1]
    for i, (mask, send) in enumerate(zip(masks, sends)):
        if i == 0 or mask != masks[i - 1]:
            late_part(mask, plan, tiles, early, panel_buf, acc, ())
        put(send, acc)


def own_kernel(plan, panel_buf, tiles, early, current, previous, coupling, diag, base, acc):
    late_part(0, plan, tiles, early, panel_buf, acc, ())
    put(base, acc)
    base[...] += diag[...] * current[...] - jnp.dot(
        coupling[...],
        previous[...],
        precision=lax.Precision.HIGHEST,
        preferred_element_type=jnp.float32,
    )


def late_part(mask, plan, tiles, early, panel_buf, acc, copies):
    slab_tiles = acc.shape[0] - 1
    row_devs = (early.shape[0] - 1) // slab_tiles
    first_row = (row_of(plan) ^ mask) * slab_tiles
    for s in range(slab_tiles):
        acc[s] = early[first_row + s]
    for copy in copies:
        copy.wait()
    add_products(plan, row_devs - mask, first_row, slab_tiles, tiles, panel_buf, acc)


def put(out, acc):
    for s in range(acc.shape[0] - 1):
        out[:, s * LANES : (s + 1) * LANES] = acc[s].astype(out.dtype)


def coefficient_kernel(cells, received_count, relay, plan, base, *refs):
    received = refs[:received_count]
    mass, current, stored, recurrence, keep, give, halves = refs[received_count:]
    total = base[...]
    for i, ref in enumerate(received):
        value = ref[...].astype(jnp.float32)
        if relay and i == 0:
            value = jnp.where((row_of(plan) == 1) | (row_of(plan) == 2), 0.0, value)
        total = total + value
    recurrence[...] = total
    weighted = total * (mass[...] * (1.0 / cells))
    basis = jnp.concatenate([current[...], stored[...]], axis=0)
    coef = dot_split(weighted, basis, NT)
    spare = -coef.shape[1] % LANES
    coef = jnp.concatenate([coef, jnp.zeros((coef.shape[0], spare), jnp.float32)], axis=1)
    halves[...] = jnp.zeros_like(halves)
    for p, (q, k) in enumerate(blocks(coef.shape)):
        halves[p // halves.shape[1], p % halves.shape[1]] = coef[q : q + 8, k : k + LANES]
    core = core_of(plan)
    keep[...] = halves[core]
    give[...] = halves[1 - core]


def residual_kernel(
    cells, plan, mine, other, recurrence, mass, current, stored, residual, coef_out, gram, halves, packed
):
    width = recurrence.shape[0]
    core = core_of(plan)
    halves[core] = mine[...]
    halves[1 - core] = other[...]
    for p, (q, k) in enumerate(blocks(packed.shape)):
        packed[q : q + 8, k : k + LANES] = halves[p // halves.shape[1], p % halves.shape[1]]
    coef = packed[...]
    basis = jnp.concatenate([current[...], stored[...]], axis=0)
    coef = coef[:, : basis.shape[0]]
    coef_out[...] = coef
    value = recurrence[...] - dot_split(coef, basis)
    residual[...] = value
    local = dot_split(value * (mass[...] * (1.0 / cells)), value, NT)
    half = width // 2
    gram[...] = jnp.zeros_like(gram)
    gram[:, :width] = local[:half]
    gram[:, LANES // 2 : LANES // 2 + width] = local[half:]


def after_kernel(value, earlier, out):
    pass


def after(value, earlier):
    anywhere = pl.BlockSpec(memory_space=pl.ANY)
    return pl.pallas_call(
        after_kernel,
        out_shape=jax.ShapeDtypeStruct(value.shape, value.dtype),
        in_specs=[anywhere, anywhere],
        out_specs=anywhere,
        input_output_aliases={0: 0},
        compiler_params=limit(1),
    )(value, earlier)


def in_hbm(value):
    return pltpu.with_memory_space_constraint(value, pltpu.HBM)


def limit(mib):
    return pltpu.CompilerParams(vmem_limit_bytes=mib * MIB)


def vmem(count):
    return [pl.BlockSpec(memory_space=pltpu.VMEM)] * count


def smem(count):
    return [pl.BlockSpec(memory_space=pltpu.SMEM)] * count


def local(
    current_block,
    previous_block,
    previous_coupling,
    stored_blocks,
    stiffness_diag,
    lumped_mass,
    tile_values,
    tile_rows,
    tile_cols,
    tile_counts,
):
    row_devs = lax.axis_size("row")
    col_devs = lax.axis_size("col")
    width, slab_len = current_block.shape
    stored_count = stored_blocks.shape[0]
    slots, tile_len, _ = tile_values.shape
    slab_tiles = slab_len // tile_len
    cells = slab_len * row_devs * col_devs
    f32, bf16 = jnp.float32, jnp.bfloat16
    place = jnp.stack([lax.axis_index("row"), lax.axis_index("col")]).astype(jnp.int32)
    stored = stored_blocks.reshape(stored_count * width, slab_len)
    mass = lumped_mass.reshape(1, slab_len)
    diag = stiffness_diag.reshape(1, slab_len)
    slab = jax.ShapeDtypeStruct((width, slab_len), f32)

    targets = row_devs * slab_tiles
    anywhere = [pl.BlockSpec(memory_space=pl.ANY)]
    panel_shape = (col_devs + 1, width, slab_len)
    early_shape = (targets + 1, width, tile_len)
    part_acc = pltpu.VMEM((slab_tiles + 1, width, tile_len), f32)

    def cost(flops):
        return pl.CostEstimate(flops=flops, bytes_accessed=flops // width, transcendentals=0)

    with jax.named_scope("gather"):
        rounded = current_block.astype(bf16)
        panels = [rounded] + [None] * (col_devs - 1)
        for m in range(col_devs - 2, 0, -2):
            panels[m] = swap(rounded, "col", m)
        panels[1] = swap(rounded, "col", 1)

    with jax.named_scope("early"):
        places = -(-(slots + (GROUP - 1) * 2 * targets + GROUP * UNROLL) // LANES) * LANES
        plan_shape = (1, places + LANES)
        plan, held, early, gathered = pl.pallas_call(
            functools.partial(early_kernel, row_devs, col_devs, slab_tiles),
            out_shape=[
                pltpu.SMEM(plan_shape, jnp.int32),
                pltpu.VMEM(tile_values.shape, bf16),
                pltpu.VMEM(early_shape, f32),
                pltpu.VMEM(panel_shape, bf16),
            ],
            in_specs=smem(2) + [pl.BlockSpec(memory_space=pltpu.HBM)] * 3 + anywhere * 2,
            out_specs=smem(1) + vmem(3),
            scratch_shapes=[
                pltpu.VMEM((1, slots), jnp.int32),
                pltpu.VMEM((1, slots), jnp.int32),
                pltpu.VMEM(plan_shape, jnp.int32),
                pltpu.SemaphoreType.DMA((slots // CHUNK,)),
                pltpu.SemaphoreType.DMA((3,)),
                pltpu.SemaphoreType.DMA((2,)),
            ],
            compiler_params=limit(12),
            cost_estimate=cost(2 * slots * width * tile_len * tile_len),
        )(
            place,
            tile_counts,
            in_hbm(tile_rows.reshape(1, slots)),
            in_hbm(tile_cols.reshape(1, slots)),
            in_hbm(tile_values),
            panels[0],
            panels[1],
        )

    with jax.named_scope("gather"):
        for m in range(col_devs - 2, 0, -2):
            panels[m] = after(panels[m], early)
            panels[m + 1] = swap(panels[m], "col", 1)
        even, odd = list(range(2, col_devs, 2)), list(range(3, col_devs, 2))
        gathered = pl.pallas_call(
            functools.partial(collect_kernel, even),
            out_shape=pltpu.VMEM(panel_shape, bf16),
            in_specs=anywhere * len(even) + vmem(1),
            out_specs=vmem(1)[0],
            scratch_shapes=[pltpu.SemaphoreType.DMA((len(even),))],
            input_output_aliases={len(even): 0},
            compiler_params=limit(1),
            cost_estimate=cost(width),
        )(*[panels[m] for m in even], gathered)

    with jax.named_scope("late"):
        relay = row_devs == 4
        first_mask = 2 if relay else row_devs - 1
        masks = [3, 3, 1] if relay else list(range(row_devs - 2, 0, -1))
        part = jax.ShapeDtypeStruct((width, slab_len), bf16)
        first, gathered = pl.pallas_call(
            functools.partial(first_late_kernel, [first_mask], odd),
            out_shape=[part, pltpu.VMEM(panel_shape, bf16)],
            in_specs=smem(1) + anywhere * len(odd) + vmem(3),
            out_specs=vmem(2),
            scratch_shapes=[part_acc, pltpu.SemaphoreType.DMA((len(odd),))],
            input_output_aliases={3 + len(odd): 1},
            compiler_params=limit(8),
            cost_estimate=cost(width),
        )(plan, *[panels[m] for m in odd], held, early, gathered)
        parts = pl.pallas_call(
            functools.partial(late_kernel, masks),
            out_shape=[part, slab, part] if relay else [part] * len(masks),
            in_specs=smem(1) + vmem(3),
            out_specs=vmem(len(masks)),
            scratch_shapes=[part_acc],
            compiler_params=limit(8),
            cost_estimate=cost(width),
        )(plan, gathered, held, early)
        if relay:
            first = lax.ppermute(first, "row", [(0, 1), (3, 2), (1, 3), (2, 0)])
            joined = (parts[1] + first.astype(f32)).astype(bf16)
            received = [
                first,
                lax.ppermute(parts[0], "row", [(0, 3), (3, 0)]),
                lax.ppermute(joined, "row", [(1, 2), (2, 1)]),
                swap(parts[2], "row", 1),
            ]
        else:
            received = [swap(first, "row", first_mask)]
            received += [swap(part, "row", m) for m, part in zip(masks, parts)]
        base = pl.pallas_call(
            own_kernel,
            out_shape=slab,
            in_specs=smem(1) + vmem(7),
            out_specs=vmem(1)[0],
            scratch_shapes=[part_acc],
            compiler_params=limit(8),
            cost_estimate=cost(width),
        )(plan, gathered, held, early, current_block, previous_block, previous_coupling, diag)

    basis_rows = (stored_count + 1) * width
    padded = (width, -(-basis_rows // LANES) * LANES)
    half = (-(-len(blocks(padded)) // 2), 8, LANES)
    with jax.named_scope("coefficients"):
        recurrence, keep, give = pl.pallas_call(
            functools.partial(coefficient_kernel, cells, len(received), relay),
            out_shape=[slab] + [jax.ShapeDtypeStruct(half, f32)] * 2,
            in_specs=smem(1) + vmem(len(received) + 4),
            out_specs=vmem(3),
            scratch_shapes=[pltpu.VMEM((2,) + half, f32)],
            compiler_params=limit(24),
        )(plan, base, *received, mass, current_block, stored)
        mine = keep + swap(give, "col", 1)
        mine = total_by_core(mine)
        other = swap(mine, "col", 1)

    with jax.named_scope("residual"):
        residual_block, coef, gram = pl.pallas_call(
            functools.partial(residual_kernel, cells),
            out_shape=[
                pltpu.VMEM((width, slab_len), f32),
                jax.ShapeDtypeStruct((width, basis_rows), f32),
                jax.ShapeDtypeStruct((width // 2, LANES), f32),
            ],
            in_specs=smem(1) + vmem(6),
            out_specs=vmem(3),
            scratch_shapes=[pltpu.VMEM((2,) + half, f32), pltpu.VMEM(padded, f32)],
            compiler_params=limit(24),
        )(plan, mine, other, recurrence, mass, current_block, stored)
        coefficients = coef.T.reshape(stored_count + 1, width, width)

    with jax.named_scope("gram"):
        gram = gram + swap(gram, "col", 1)
        gram = total(total(gram, "col", 2), "row", 1)
        gram = jnp.concatenate(
            [gram[:, :width], gram[:, LANES // 2 : LANES // 2 + width]], axis=0
        )
    return (residual_block, coefficients, gram)


def solution(mesh):
    return jax.shard_map(
        local,
        mesh=mesh,
        in_specs=(
            P(None, ("row", "col")),
            P(None, ("row", "col")),
            P(),
            P(None, None, ("row", "col")),
            P(("row", "col")),
            P(("row", "col")),
            P(("row", "col"), None, None),
            P(("row", "col")),
            P(("row", "col")),
            P(("row", "col")),
        ),
        out_specs=(P(None, ("row", "col")), P(), P()),
        check_vma=False,
    )
```

```python
import functools

import jax
import jax.numpy as jnp
from jax import lax
from jax.experimental import pallas as pl
from jax.experimental.pallas import tpu as pltpu
from jax.sharding import PartitionSpec as P

LANES = 128
CHUNK = 32
GROUP = 2
UNROLL = 8
TILE_BIT, SOURCE_BIT, ROW_BIT = 10, 15, 20
NT = (((1,), (1,)), ((), ()))
MIB = 1 << 20


def swap(value, axis, mask):
    count = lax.axis_size(axis)
    return lax.ppermute(value, axis, [(i, i ^ mask) for i in range(count)])


def tree_sum(values):
    values = [values[m] for m in sorted(values)]
    while len(values) > 1:
        values = [values[i] + values[i + 1] for i in range(0, len(values), 2)]
    return values[0]


def total(value, axis, step):
    values = {0: value}
    for m in range(lax.axis_size(axis) - step, 0, -step):
        values[m] = swap(value, axis, m)
    return tree_sum(values)


def total_by_core(value):
    row_devs, col_devs = lax.axis_size("row"), lax.axis_size("col")
    if col_devs != 2 * row_devs:
        return total(total(value, "col", 2), "row", 1)
    places = [(r, c) for r in range(row_devs) for c in range(col_devs)]
    for turn in range(2):
        values = {0: value}
        for m in range(row_devs - 1, 0, -1):
            partners = [(r, c ^ (2 * m)) if c % 2 == turn else (r ^ m, c) for r, c in places]
            trades = [(i, r * col_devs + c) for i, (r, c) in enumerate(partners)]
            values[m] = lax.ppermute(value, ("row", "col"), trades)
        value = tree_sum(values)
    return value


def split(value):
    high = value.astype(jnp.bfloat16)
    low = (value - high.astype(jnp.float32)).astype(jnp.bfloat16)
    return high, low


def mm(a, b, dims=(((1,), (0,)), ((), ()))):
    return lax.dot_general(a, b, dims, preferred_element_type=jnp.float32)


def dot_split(a, b, dims=(((1,), (0,)), ((), ()))):
    rows = a.shape[0]
    a_high, a_low = split(a)
    b_high, b_low = split(b)
    both = mm(jnp.concatenate([a_high, a_low], axis=0), b_high, dims)
    return both[:rows] + both[rows:] + mm(a_high, b_low, dims)


def blocks(shape):
    return [(q, k) for q in range(0, shape[0], 8) for k in range(0, shape[1], LANES)]


def early_kernel(
    row_devs,
    col_devs,
    slab_tiles,
    place,
    counts,
    rows_hbm,
    cols_hbm,
    tiles,
    own_panel,
    near_panel,
    plan,
    held,
    acc,
    panel_buf,
    rows,
    cols,
    out,
    tile_sem,
    list_sem,
    panel_sem,
):
    chunks = (counts[0] + CHUNK - 1) // CHUNK
    row_copy = pltpu.make_async_copy(rows_hbm, rows, list_sem.at[0])
    col_copy = pltpu.make_async_copy(cols_hbm, cols, list_sem.at[1])
    row_copy.start()
    col_copy.start()

    def tile_copy(k):
        window = pl.ds(k * CHUNK, CHUNK)
        return pltpu.make_async_copy(tiles.at[window], held.at[window], tile_sem.at[k])

    @pl.loop(0, chunks)
    def _(k):
        tile_copy(k).start()

    copies = load_panels({0: own_panel, 1: near_panel}, panel_buf, panel_sem)
    zero_panel = panel_buf.shape[0] - 1
    panel_buf[zero_panel, :, :LANES] = jnp.zeros((panel_buf.shape[1], LANES), jnp.bfloat16)
    f32, bf16, i32 = jnp.float32, jnp.bfloat16, jnp.int32
    slots, places = rows.shape[1], out.shape[1] - LANES
    early_chunks = 3 * slots // CHUNK // 4
    targets = row_devs * slab_tiles
    bins = 2 * targets

    def iota(shape, dim):
        return lax.broadcasted_iota(i32, shape, dim)

    slot = iota((1, slots), 1)
    occupied = slot < counts[0]
    earlier = (iota((slots, slots), 0) < iota((slots, slots), 1)).astype(f32).astype(bf16)
    row_copy.wait()
    col_copy.wait()
    row = rows[...]
    row_owner = jnp.floor(row.astype(f32) * (1.0 / slab_tiles)).astype(i32)
    col_f = cols[...].astype(f32)
    source_f = jnp.floor(col_f * (1.0 / slab_tiles))
    source = source_f.astype(i32) ^ place[1]
    tile_f = col_f - slab_tiles * source_f
    far = row_devs - 1 - (row_owner ^ place[0])
    late_bin = targets + far * slab_tiles + row - row_owner * slab_tiles
    early = (source < 2) & (slot < early_chunks * CHUNK)
    bin_of = jnp.where(occupied, jnp.where(early, row, late_bin), -1)
    member = (iota((bins, slots), 0) == bin_of).astype(f32)
    member_bf = member.astype(bf16)
    rank = jnp.sum(member * mm(member_bf, earlier), axis=0, keepdims=True)
    sizes = mm(jnp.ones((8, slots), bf16), member_bf, NT)
    sizes = GROUP * jnp.floor((sizes + (GROUP - 1.0)) * (1.0 / GROUP))
    before = (iota((bins, bins), 1) < iota((bins, bins), 0)).astype(f32)
    begin = jnp.sum(before * sizes[:1], axis=1, keepdims=True)
    position = jnp.sum(member * begin, axis=0, keepdims=True) + rank
    position = jnp.where(occupied, position.astype(i32), -1)
    chosen = (iota((places, slots), 0) == position).astype(f32).astype(bf16)
    slot_f = slot.astype(f32)
    slot_high = jnp.floor(slot_f * (1.0 / 16.0))
    facts = [slot_high, slot_f - 16.0 * slot_high, source.astype(f32), tile_f, row.astype(f32), jnp.ones((1, slots), f32)]
    facts = jnp.concatenate(facts + [jnp.zeros((2, slots), f32)], axis=0).astype(bf16)
    found = mm(facts, chosen, NT).astype(i32)
    source = jnp.where(found[5:6] > 0, found[2:3], col_devs)
    words = (found[4:5] << ROW_BIT) + (source << SOURCE_BIT) + (found[3:4] << TILE_BIT)
    out[:, :places] = words + (found[0:1] << 4) + found[1:2]
    phase = iota((bins, LANES), 1)
    edge = jnp.where(phase > 0, targets + (phase - 1) * slab_tiles, 0)
    inside = (iota((bins, LANES), 0) < edge).astype(f32).astype(bf16)
    edges = mm(sizes.astype(bf16), inside)[:1].astype(i32)
    lane = iota((1, LANES), 1)
    edges = jnp.where(lane == LANES - 2, place[0], jnp.where(lane == LANES - 1, place[1], edges))
    out[:, places:] = edges
    plan_copy = pltpu.make_async_copy(out, plan, list_sem.at[2])
    plan_copy.start()
    acc[...] = jnp.zeros_like(acc)
    for copy in copies + [plan_copy]:
        copy.wait()

    @pl.loop(0, jnp.minimum(chunks, early_chunks))
    def _(k):
        tile_copy(k).wait()

    add_products(plan, 0, 0, targets, held, panel_buf, acc)

    @pl.loop(early_chunks, chunks)
    def _(k):
        tile_copy(k).wait()


def row_of(plan):
    return plan[0, plan.shape[1] - 2]


def core_of(plan):
    return plan[0, plan.shape[1] - 1] & 1


def field(word, low, high):
    return (word >> low) & ((1 << (high - low)) - 1)


def add_products(plan, phase, first_row, spare_row, tiles, panel_buf, acc):
    phases = plan.shape[1] - LANES
    begin, end = plan[0, phases + phase], plan[0, phases + phase + 1]

    def panel(word):
        where = pl.multiple_of(field(word, TILE_BIT, SOURCE_BIT) * LANES, LANES)
        return panel_buf[field(word, SOURCE_BIT, ROW_BIT), :, pl.ds(where, LANES)]

    @pl.loop(0, (end - begin + GROUP * UNROLL - 1) // (GROUP * UNROLL))
    def _(g):
        first = begin + g * GROUP * UNROLL
        parts = []
        for u in range(UNROLL):
            words = [plan[0, first + GROUP * u + i] for i in range(GROUP)]
            left = jnp.concatenate([panel(word) for word in words], axis=1)
            right = jnp.concatenate([tiles[field(word, 0, TILE_BIT)] for word in words], axis=1)
            parts.append(mm(left, right, NT))
        for u in range(UNROLL):
            p = first + GROUP * u
            a = jnp.where(p < end, (plan[0, p] >> ROW_BIT) - first_row, spare_row)
            acc[a] += parts[u]


def load_panels(panels, panel_buf, sem):
    copies = [pltpu.make_async_copy(ref, panel_buf.at[m], sem.at[i]) for i, (m, ref) in enumerate(panels.items())]
    for copy in copies:
        copy.start()
    return copies


def collect_kernel(masks, *refs):
    panels, (_, panel_buf, sem) = refs[: len(masks)], refs[len(masks) :]
    for copy in load_panels(dict(zip(masks, panels)), panel_buf, sem):
        copy.wait()


def first_late_kernel(masks, odd, plan, *refs):
    panels = dict(zip(odd, refs))
    tiles, early, _ = refs[len(odd) : len(odd) + 3]
    sends = refs[len(odd) + 3 : -3]
    panel_buf, acc, sem = refs[-3:]
    copies = load_panels(panels, panel_buf, sem)
    for mask, send in zip(masks, sends):
        late_part(mask, plan, tiles, early, panel_buf, acc, copies)
        put(send, acc)
        copies = ()


def late_kernel(masks, plan, panel_buf, tiles, early, *refs):
    sends, acc = refs[:-1], refs[-1]
    for i, (mask, send) in enumerate(zip(masks, sends)):
        if i == 0 or mask != masks[i - 1]:
            late_part(mask, plan, tiles, early, panel_buf, acc, ())
        put(send, acc)


def own_kernel(plan, panel_buf, tiles, early, current, previous, coupling, diag, base, acc):
    late_part(0, plan, tiles, early, panel_buf, acc, ())
    put(base, acc)
    base[...] += diag[...] * current[...] - jnp.dot(
        coupling[...],
        previous[...],
        precision=lax.Precision.HIGHEST,
        preferred_element_type=jnp.float32,
    )


def late_part(mask, plan, tiles, early, panel_buf, acc, copies):
    slab_tiles = acc.shape[0] - 1
    row_devs = (early.shape[0] - 1) // slab_tiles
    first_row = (row_of(plan) ^ mask) * slab_tiles
    for s in range(slab_tiles):
        acc[s] = early[first_row + s]
    for copy in copies:
        copy.wait()
    add_products(plan, row_devs - mask, first_row, slab_tiles, tiles, panel_buf, acc)


def put(out, acc):
    for s in range(acc.shape[0] - 1):
        out[:, s * LANES : (s + 1) * LANES] = acc[s].astype(out.dtype)


def half_basis(half, current, stored):
    rows = (current.shape[0] + stored.shape[0]) // 2
    cut = rows - current.shape[0]
    return jnp.where(half == 0, jnp.concatenate([current[...], stored[:cut]], axis=0), stored[cut:])


def pack(coef, out):
    spare = -coef.shape[1] % LANES
    coef = jnp.concatenate([coef, jnp.zeros((coef.shape[0], spare), jnp.float32)], axis=1)
    for p, (q, k) in enumerate(blocks(coef.shape)):
        out[p] = coef[q : q + 8, k : k + LANES]


def unpack(pieces, width, columns):
    groups = pieces.shape[0] * 8 // width
    rows = [jnp.concatenate([pieces[p + g] for g in range(groups)], axis=1) for p in range(0, pieces.shape[0], groups)]
    return jnp.concatenate(rows, axis=0)[:, :columns]


def give_kernel(cells, received_count, relay, plan, base, *refs):
    received = refs[:received_count]
    mass, current, stored, recurrence, give = refs[received_count:]
    total = base[...]
    for i, ref in enumerate(received):
        value = ref[...].astype(jnp.float32)
        if relay and i == 0:
            value = jnp.where((row_of(plan) == 1) | (row_of(plan) == 2), 0.0, value)
        total = total + value
    recurrence[...] = total
    weighted = total * (mass[...] * (1.0 / cells))
    pack(dot_split(weighted, half_basis(1 - core_of(plan), current, stored), NT), give)


def keep_kernel(cells, plan, recurrence, mass, current, stored, keep):
    weighted = recurrence[...] * (mass[...] * (1.0 / cells))
    pack(dot_split(weighted, half_basis(core_of(plan), current, stored), NT), keep)


def less_kernel(plan, mine, recurrence, current, stored, less):
    basis = half_basis(core_of(plan), current, stored)
    less[...] = recurrence[...] - dot_split(unpack(mine, recurrence.shape[0], basis.shape[0]), basis)


def residual_kernel(cells, plan, mine, other, less, mass, current, stored, residual, coef_out, gram):
    width = less.shape[0]
    core = core_of(plan)
    basis = half_basis(1 - core, current, stored)
    own_coef = unpack(mine, width, basis.shape[0])
    other_coef = unpack(other, width, basis.shape[0])
    coef_out[...] = jnp.concatenate(
        [jnp.where(core == 0, own_coef, other_coef), jnp.where(core == 0, other_coef, own_coef)], axis=1
    )
    value = less[...] - dot_split(other_coef, basis)
    residual[...] = value
    local = dot_split(value * (mass[...] * (1.0 / cells)), value, NT)
    half = width // 2
    gram[...] = jnp.zeros_like(gram)
    gram[:, :width] = local[:half]
    gram[:, LANES // 2 : LANES // 2 + width] = local[half:]


def after_kernel(value, earlier, out):
    pass


def after(value, earlier):
    anywhere = pl.BlockSpec(memory_space=pl.ANY)
    return pl.pallas_call(
        after_kernel,
        out_shape=jax.ShapeDtypeStruct(value.shape, value.dtype),
        in_specs=[anywhere, anywhere],
        out_specs=anywhere,
        input_output_aliases={0: 0},
        compiler_params=limit(1),
    )(value, earlier)


def in_hbm(value):
    return pltpu.with_memory_space_constraint(value, pltpu.HBM)


def limit(mib):
    return pltpu.CompilerParams(vmem_limit_bytes=mib * MIB)


def vmem(count):
    return [pl.BlockSpec(memory_space=pltpu.VMEM)] * count


def smem(count):
    return [pl.BlockSpec(memory_space=pltpu.SMEM)] * count


def local(
    current_block,
    previous_block,
    previous_coupling,
    stored_blocks,
    stiffness_diag,
    lumped_mass,
    tile_values,
    tile_rows,
    tile_cols,
    tile_counts,
):
    row_devs = lax.axis_size("row")
    col_devs = lax.axis_size("col")
    width, slab_len = current_block.shape
    stored_count = stored_blocks.shape[0]
    slots, tile_len, _ = tile_values.shape
    slab_tiles = slab_len // tile_len
    cells = slab_len * row_devs * col_devs
    f32, bf16 = jnp.float32, jnp.bfloat16
    place = jnp.stack([lax.axis_index("row"), lax.axis_index("col")]).astype(jnp.int32)
    stored = stored_blocks.reshape(stored_count * width, slab_len)
    mass = lumped_mass.reshape(1, slab_len)
    diag = stiffness_diag.reshape(1, slab_len)
    slab = jax.ShapeDtypeStruct((width, slab_len), f32)

    targets = row_devs * slab_tiles
    anywhere = [pl.BlockSpec(memory_space=pl.ANY)]
    panel_shape = (col_devs + 1, width, slab_len)
    early_shape = (targets + 1, width, tile_len)
    part_acc = pltpu.VMEM((slab_tiles + 1, width, tile_len), f32)

    def cost(flops):
        return pl.CostEstimate(flops=flops, bytes_accessed=flops // width, transcendentals=0)

    with jax.named_scope("gather"):
        rounded = current_block.astype(bf16)
        panels = [rounded] + [None] * (col_devs - 1)
        for m in range(2, col_devs, 2):
            panels[m] = swap(rounded, "col", m)
        panels[1] = swap(rounded, "col", 1)

    with jax.named_scope("early"):
        places = -(-(slots + (GROUP - 1) * 2 * targets + GROUP * UNROLL) // LANES) * LANES
        plan_shape = (1, places + LANES)
        plan, held, early, gathered = pl.pallas_call(
            functools.partial(early_kernel, row_devs, col_devs, slab_tiles),
            out_shape=[
                pltpu.SMEM(plan_shape, jnp.int32),
                pltpu.VMEM(tile_values.shape, bf16),
                pltpu.VMEM(early_shape, f32),
                pltpu.VMEM(panel_shape, bf16),
            ],
            in_specs=smem(2) + [pl.BlockSpec(memory_space=pltpu.HBM)] * 3 + anywhere * 2,
            out_specs=smem(1) + vmem(3),
            scratch_shapes=[
                pltpu.VMEM((1, slots), jnp.int32),
                pltpu.VMEM((1, slots), jnp.int32),
                pltpu.VMEM(plan_shape, jnp.int32),
                pltpu.SemaphoreType.DMA((slots // CHUNK,)),
                pltpu.SemaphoreType.DMA((3,)),
                pltpu.SemaphoreType.DMA((2,)),
            ],
            compiler_params=limit(12),
            cost_estimate=cost(2 * slots * width * tile_len * tile_len),
        )(
            place,
            tile_counts,
            in_hbm(tile_rows.reshape(1, slots)),
            in_hbm(tile_cols.reshape(1, slots)),
            in_hbm(tile_values),
            panels[0],
            panels[1],
        )

    with jax.named_scope("gather"):
        for m in range(2, col_devs, 2):
            panels[m] = after(panels[m], early)
            panels[m + 1] = swap(panels[m], "col", 1)
        even, odd = list(range(2, col_devs, 2)), list(range(3, col_devs, 2))
        gathered = pl.pallas_call(
            functools.partial(collect_kernel, even),
            out_shape=pltpu.VMEM(panel_shape, bf16),
            in_specs=anywhere * len(even) + vmem(1),
            out_specs=vmem(1)[0],
            scratch_shapes=[pltpu.SemaphoreType.DMA((len(even),))],
            input_output_aliases={len(even): 0},
            compiler_params=limit(1),
            cost_estimate=cost(width),
        )(*[panels[m] for m in even], gathered)

    with jax.named_scope("late"):
        relay = row_devs == 4
        first_mask = 2 if relay else row_devs - 1
        masks = [3, 3, 1] if relay else list(range(row_devs - 2, 0, -1))
        part = jax.ShapeDtypeStruct((width, slab_len), bf16)
        first, gathered = pl.pallas_call(
            functools.partial(first_late_kernel, [first_mask], odd),
            out_shape=[part, pltpu.VMEM(panel_shape, bf16)],
            in_specs=smem(1) + anywhere * len(odd) + vmem(3),
            out_specs=vmem(2),
            scratch_shapes=[part_acc, pltpu.SemaphoreType.DMA((len(odd),))],
            input_output_aliases={3 + len(odd): 1},
            compiler_params=limit(8),
            cost_estimate=cost(width),
        )(plan, *[panels[m] for m in odd], held, early, gathered)
        parts = pl.pallas_call(
            functools.partial(late_kernel, masks),
            out_shape=[part, slab, part] if relay else [part] * len(masks),
            in_specs=smem(1) + vmem(3),
            out_specs=vmem(len(masks)),
            scratch_shapes=[part_acc],
            compiler_params=limit(8),
            cost_estimate=cost(width),
        )(plan, gathered, held, early)
        if relay:
            first = lax.ppermute(first, "row", [(0, 1), (3, 2), (1, 3), (2, 0)])
            joined = (parts[1] + first.astype(f32)).astype(bf16)
            received = [
                first,
                lax.ppermute(parts[0], "row", [(0, 3), (3, 0)]),
                lax.ppermute(joined, "row", [(1, 2), (2, 1)]),
                swap(parts[2], "row", 1),
            ]
        else:
            received = [swap(first, "row", first_mask)]
            received += [swap(part, "row", m) for m, part in zip(masks, parts)]
        base = pl.pallas_call(
            own_kernel,
            out_shape=slab,
            in_specs=smem(1) + vmem(7),
            out_specs=vmem(1)[0],
            scratch_shapes=[part_acc],
            compiler_params=limit(8),
            cost_estimate=cost(width),
        )(plan, gathered, held, early, current_block, previous_block, previous_coupling, diag)

    basis_rows = (stored_count + 1) * width
    half = (width // 8 * -(-basis_rows // 2 // LANES), 8, LANES)
    half = jax.ShapeDtypeStruct(half, f32)
    with jax.named_scope("coefficients"):
        recurrence, give = pl.pallas_call(
            functools.partial(give_kernel, cells, len(received), relay),
            out_shape=[slab, half],
            in_specs=smem(1) + vmem(len(received) + 4),
            out_specs=vmem(2),
            compiler_params=limit(16),
            cost_estimate=cost(width),
        )(plan, base, *received, mass, current_block, stored)
        keep = pl.pallas_call(
            functools.partial(keep_kernel, cells),
            out_shape=half,
            in_specs=smem(1) + vmem(4),
            out_specs=vmem(1)[0],
            compiler_params=limit(16),
            cost_estimate=cost(width),
        )(plan, recurrence, mass, current_block, stored)
        mine = keep + swap(give, "col", 1)
        mine = total_by_core(mine)
        other = swap(mine, "col", 1)

    with jax.named_scope("residual"):
        less = pl.pallas_call(
            less_kernel,
            out_shape=slab,
            in_specs=smem(1) + vmem(4),
            out_specs=vmem(1)[0],
            compiler_params=limit(16),
            cost_estimate=cost(width),
        )(plan, mine, recurrence, current_block, stored)
        residual_block, coef, gram = pl.pallas_call(
            functools.partial(residual_kernel, cells),
            out_shape=[
                pltpu.VMEM((width, slab_len), f32),
                jax.ShapeDtypeStruct((width, basis_rows), f32),
                jax.ShapeDtypeStruct((width // 2, LANES), f32),
            ],
            in_specs=smem(1) + vmem(6),
            out_specs=vmem(3),
            compiler_params=limit(16),
            cost_estimate=cost(width),
        )(plan, mine, other, less, mass, current_block, stored)
        coefficients = coef.T.reshape(stored_count + 1, width, width)

    with jax.named_scope("gram"):
        gram = gram + swap(gram, "col", 1)
        gram = total(total(gram, "col", 2), "row", 1)
        gram = jnp.concatenate(
            [gram[:, :width], gram[:, LANES // 2 : LANES // 2 + width]], axis=0
        )
    return (residual_block, coefficients, gram)


def solution(mesh):
    return jax.shard_map(
        local,
        mesh=mesh,
        in_specs=(
            P(None, ("row", "col")),
            P(None, ("row", "col")),
            P(),
            P(None, None, ("row", "col")),
            P(("row", "col")),
            P(("row", "col")),
            P(("row", "col"), None, None),
            P(("row", "col")),
            P(("row", "col")),
            P(("row", "col")),
        ),
        out_specs=(P(None, ("row", "col")), P(), P()),
        check_vma=False,
    )
```

```python
import functools

import jax
import jax.numpy as jnp
from jax import lax
from jax.experimental import pallas as pl
from jax.experimental.pallas import tpu as pltpu
from jax.sharding import PartitionSpec as P

LANES = 128
CHUNK = 32
GROUP = 2
UNROLL = 8
TILE_BIT, SOURCE_BIT, ROW_BIT = 10, 15, 20
NT = (((1,), (1,)), ((), ()))
MIB = 1 << 20


def swap(value, axis, mask):
    count = lax.axis_size(axis)
    return lax.ppermute(value, axis, [(i, i ^ mask) for i in range(count)])


def tree_sum(values):
    values = [values[m] for m in sorted(values)]
    while len(values) > 1:
        values = [values[i] + values[i + 1] for i in range(0, len(values), 2)]
    return values[0]


def total(value, axis, step):
    values = {0: value}
    for m in range(lax.axis_size(axis) - step, 0, -step):
        values[m] = swap(value, axis, m)
    return tree_sum(values)


def total_by_core(value):
    row_devs, col_devs = lax.axis_size("row"), lax.axis_size("col")
    if col_devs != 2 * row_devs:
        return total(total(value, "col", 2), "row", 1)
    places = [(r, c) for r in range(row_devs) for c in range(col_devs)]
    for turn in range(2):
        values = {0: value}
        for m in range(row_devs - 1, 0, -1):
            partners = [(r, c ^ (2 * m)) if c % 2 == turn else (r ^ m, c) for r, c in places]
            trades = [(i, r * col_devs + c) for i, (r, c) in enumerate(partners)]
            values[m] = lax.ppermute(value, ("row", "col"), trades)
        value = tree_sum(values)
    return value


def split(value):
    high = value.astype(jnp.bfloat16)
    low = (value - high.astype(jnp.float32)).astype(jnp.bfloat16)
    return high, low


def mm(a, b, dims=(((1,), (0,)), ((), ()))):
    return lax.dot_general(a, b, dims, preferred_element_type=jnp.float32)


def dot_split(a, b, dims=(((1,), (0,)), ((), ()))):
    rows = a.shape[0]
    a_high, a_low = split(a)
    b_high, b_low = split(b)
    both = mm(jnp.concatenate([a_high, a_low], axis=0), b_high, dims)
    return both[:rows] + both[rows:] + mm(a_high, b_low, dims)


def blocks(shape):
    return [(q, k) for q in range(0, shape[0], 8) for k in range(0, shape[1], LANES)]


def early_kernel(
    row_devs,
    col_devs,
    slab_tiles,
    place,
    counts,
    rows_hbm,
    cols_hbm,
    tiles,
    own_panel,
    near_panel,
    plan,
    held,
    acc,
    panel_buf,
    rows,
    cols,
    out,
    tile_sem,
    list_sem,
    panel_sem,
):
    chunks = (counts[0] + CHUNK - 1) // CHUNK
    row_copy = pltpu.make_async_copy(rows_hbm, rows, list_sem.at[0])
    col_copy = pltpu.make_async_copy(cols_hbm, cols, list_sem.at[1])
    row_copy.start()
    col_copy.start()

    def tile_copy(k):
        window = pl.ds(k * CHUNK, CHUNK)
        return pltpu.make_async_copy(tiles.at[window], held.at[window], tile_sem.at[k])

    @pl.loop(0, chunks)
    def _(k):
        tile_copy(k).start()

    copies = load_panels({0: own_panel, 1: near_panel}, panel_buf, panel_sem)
    zero_panel = panel_buf.shape[0] - 1
    panel_buf[zero_panel, :, :LANES] = jnp.zeros((panel_buf.shape[1], LANES), jnp.bfloat16)
    f32, bf16, i32 = jnp.float32, jnp.bfloat16, jnp.int32
    slots, places = rows.shape[1], out.shape[1] - LANES
    early_chunks = 3 * slots // CHUNK // 4
    targets = row_devs * slab_tiles
    bins = 2 * targets

    def iota(shape, dim):
        return lax.broadcasted_iota(i32, shape, dim)

    slot = iota((1, slots), 1)
    occupied = slot < counts[0]
    earlier = (iota((slots, slots), 0) < iota((slots, slots), 1)).astype(f32).astype(bf16)
    row_copy.wait()
    col_copy.wait()
    row = rows[...]
    row_owner = jnp.floor(row.astype(f32) * (1.0 / slab_tiles)).astype(i32)
    col_f = cols[...].astype(f32)
    source_f = jnp.floor(col_f * (1.0 / slab_tiles))
    source = source_f.astype(i32) ^ place[1]
    tile_f = col_f - slab_tiles * source_f
    far = row_devs - 1 - (row_owner ^ place[0])
    late_bin = targets + far * slab_tiles + row - row_owner * slab_tiles
    early = (source < 2) & (slot < early_chunks * CHUNK)
    bin_of = jnp.where(occupied, jnp.where(early, row, late_bin), -1)
    member = (iota((bins, slots), 0) == bin_of).astype(f32)
    member_bf = member.astype(bf16)
    rank = jnp.sum(member * mm(member_bf, earlier), axis=0, keepdims=True)
    sizes = mm(jnp.ones((8, slots), bf16), member_bf, NT)
    sizes = GROUP * jnp.floor((sizes + (GROUP - 1.0)) * (1.0 / GROUP))
    before = (iota((bins, bins), 1) < iota((bins, bins), 0)).astype(f32)
    begin = jnp.sum(before * sizes[:1], axis=1, keepdims=True)
    position = jnp.sum(member * begin, axis=0, keepdims=True) + rank
    position = jnp.where(occupied, position.astype(i32), -1)
    chosen = (iota((places, slots), 0) == position).astype(f32).astype(bf16)
    slot_f = slot.astype(f32)
    slot_high = jnp.floor(slot_f * (1.0 / 16.0))
    facts = [slot_high, slot_f - 16.0 * slot_high, source.astype(f32), tile_f, row.astype(f32), jnp.ones((1, slots), f32)]
    facts = jnp.concatenate(facts + [jnp.zeros((2, slots), f32)], axis=0).astype(bf16)
    found = mm(facts, chosen, NT).astype(i32)
    source = jnp.where(found[5:6] > 0, found[2:3], col_devs)
    words = (found[4:5] << ROW_BIT) + (source << SOURCE_BIT) + (found[3:4] << TILE_BIT)
    out[:, :places] = words + (found[0:1] << 4) + found[1:2]
    phase = iota((bins, LANES), 1)
    edge = jnp.where(phase > 0, targets + (phase - 1) * slab_tiles, 0)
    inside = (iota((bins, LANES), 0) < edge).astype(f32).astype(bf16)
    edges = mm(sizes.astype(bf16), inside)[:1].astype(i32)
    lane = iota((1, LANES), 1)
    edges = jnp.where(lane == LANES - 2, place[0], jnp.where(lane == LANES - 1, place[1], edges))
    out[:, places:] = edges
    plan_copy = pltpu.make_async_copy(out, plan, list_sem.at[2])
    plan_copy.start()
    acc[...] = jnp.zeros_like(acc)
    for copy in copies + [plan_copy]:
        copy.wait()

    @pl.loop(0, jnp.minimum(chunks, early_chunks))
    def _(k):
        tile_copy(k).wait()

    add_products(plan, 0, 0, targets, held, panel_buf, acc)

    @pl.loop(early_chunks, chunks)
    def _(k):
        tile_copy(k).wait()


def row_of(plan):
    return plan[0, plan.shape[1] - 2]


def core_of(plan):
    return plan[0, plan.shape[1] - 1] & 1


def field(word, low, high):
    return (word >> low) & ((1 << (high - low)) - 1)


def add_products(plan, phase, first_row, spare_row, tiles, panel_buf, acc):
    phases = plan.shape[1] - LANES
    begin, end = plan[0, phases + phase], plan[0, phases + phase + 1]

    def panel(word):
        where = pl.multiple_of(field(word, TILE_BIT, SOURCE_BIT) * LANES, LANES)
        return panel_buf[field(word, SOURCE_BIT, ROW_BIT), :, pl.ds(where, LANES)]

    @pl.loop(0, (end - begin + GROUP * UNROLL - 1) // (GROUP * UNROLL))
    def _(g):
        first = begin + g * GROUP * UNROLL
        parts = []
        for u in range(UNROLL):
            words = [plan[0, first + GROUP * u + i] for i in range(GROUP)]
            left = jnp.concatenate([panel(word) for word in words], axis=1)
            right = jnp.concatenate([tiles[field(word, 0, TILE_BIT)] for word in words], axis=1)
            parts.append(mm(left, right, NT))
        for u in range(UNROLL):
            p = first + GROUP * u
            a = jnp.where(p < end, (plan[0, p] >> ROW_BIT) - first_row, spare_row)
            acc[a] += parts[u]


def load_panels(panels, panel_buf, sem):
    copies = [pltpu.make_async_copy(ref, panel_buf.at[m], sem.at[i]) for i, (m, ref) in enumerate(panels.items())]
    for copy in copies:
        copy.start()
    return copies


def collect_kernel(masks, *refs):
    panels, (_, panel_buf, sem) = refs[: len(masks)], refs[len(masks) :]
    for copy in load_panels(dict(zip(masks, panels)), panel_buf, sem):
        copy.wait()


def first_late_kernel(masks, odd, plan, *refs):
    panels = dict(zip(odd, refs))
    tiles, early, _ = refs[len(odd) : len(odd) + 3]
    sends = refs[len(odd) + 3 : -3]
    panel_buf, acc, sem = refs[-3:]
    copies = load_panels(panels, panel_buf, sem)
    for mask, send in zip(masks, sends):
        late_part(mask, plan, tiles, early, panel_buf, acc, copies)
        put(send, acc)
        copies = ()


def late_kernel(masks, plan, panel_buf, tiles, early, *refs):
    sends, acc = refs[:-1], refs[-1]
    for i, (mask, send) in enumerate(zip(masks, sends)):
        if i == 0 or mask != masks[i - 1]:
            late_part(mask, plan, tiles, early, panel_buf, acc, ())
        put(send, acc)


def own_kernel(plan, panel_buf, tiles, early, current, previous, coupling, diag, base, acc):
    late_part(0, plan, tiles, early, panel_buf, acc, ())
    put(base, acc)
    base[...] += diag[...] * current[...] - jnp.dot(
        coupling[...],
        previous[...],
        precision=lax.Precision.HIGHEST,
        preferred_element_type=jnp.float32,
    )


def late_part(mask, plan, tiles, early, panel_buf, acc, copies):
    slab_tiles = acc.shape[0] - 1
    row_devs = (early.shape[0] - 1) // slab_tiles
    first_row = (row_of(plan) ^ mask) * slab_tiles
    for s in range(slab_tiles):
        acc[s] = early[first_row + s]
    for copy in copies:
        copy.wait()
    add_products(plan, row_devs - mask, first_row, slab_tiles, tiles, panel_buf, acc)


def put(out, acc):
    for s in range(acc.shape[0] - 1):
        out[:, s * LANES : (s + 1) * LANES] = acc[s].astype(out.dtype)


def half_basis(half, current, stored):
    rows = (current.shape[0] + stored.shape[0]) // 2
    cut = rows - current.shape[0]
    return jnp.where(half == 0, jnp.concatenate([current[...], stored[:cut]], axis=0), stored[cut:])


def pack(coef, out):
    spare = -coef.shape[1] % LANES
    coef = jnp.concatenate([coef, jnp.zeros((coef.shape[0], spare), jnp.float32)], axis=1)
    for p, (q, k) in enumerate(blocks(coef.shape)):
        out[p] = coef[q : q + 8, k : k + LANES]


def unpack(pieces, width, columns):
    groups = pieces.shape[0] * 8 // width
    rows = [jnp.concatenate([pieces[p + g] for g in range(groups)], axis=1) for p in range(0, pieces.shape[0], groups)]
    return jnp.concatenate(rows, axis=0)[:, :columns]


def give_kernel(cells, received_count, relay, plan, base, *refs):
    received = refs[:received_count]
    mass, current, stored, recurrence, give = refs[received_count:]
    total = base[...]
    for i, ref in enumerate(received):
        value = ref[...].astype(jnp.float32)
        if relay and i == 0:
            value = jnp.where((row_of(plan) == 1) | (row_of(plan) == 2), 0.0, value)
        total = total + value
    recurrence[...] = total
    weighted = total * (mass[...] * (1.0 / cells))
    pack(dot_split(weighted, half_basis(1 - core_of(plan), current, stored), NT), give)


def keep_kernel(cells, plan, recurrence, mass, current, stored, keep):
    weighted = recurrence[...] * (mass[...] * (1.0 / cells))
    pack(dot_split(weighted, half_basis(core_of(plan), current, stored), NT), keep)


def less_kernel(plan, mine, recurrence, current, stored, less):
    basis = half_basis(core_of(plan), current, stored)
    less[...] = recurrence[...] - dot_split(unpack(mine, recurrence.shape[0], basis.shape[0]), basis)


def turned(pieces, width, rows):
    value = unpack(pieces, width, pieces.shape[0] * 8 // width * LANES)
    spare = jnp.zeros((LANES - width, value.shape[1]), jnp.float32)
    return jnp.concatenate([value, spare], axis=0).T[:rows, :width]


def coefficient_kernel(plan, mine, other, out):
    rows = out.shape[0] // 2
    core = core_of(plan)
    own_half, other_half = turned(mine, out.shape[1], rows), turned(other, out.shape[1], rows)
    out[:rows] = jnp.where(core == 0, own_half, other_half)
    out[rows:] = jnp.where(core == 0, other_half, own_half)


def store_kernel(value, out, sem):
    copy = pltpu.make_async_copy(value, out, sem.at[0])
    copy.start()
    copy.wait()


def residual_kernel(cells, plan, other, less, mass, current, stored, residual, gram):
    width = less.shape[0]
    basis = half_basis(1 - core_of(plan), current, stored)
    value = less[...] - dot_split(unpack(other, width, basis.shape[0]), basis)
    residual[...] = value
    local = dot_split(value * (mass[...] * (1.0 / cells)), value, NT)
    half = width // 2
    gram[...] = jnp.zeros_like(gram)
    gram[:, :width] = local[:half]
    gram[:, LANES // 2 : LANES // 2 + width] = local[half:]


def after_kernel(*refs):
    pass


def after(value, *earlier):
    anywhere = pl.BlockSpec(memory_space=pl.ANY)
    return pl.pallas_call(
        after_kernel,
        out_shape=jax.ShapeDtypeStruct(value.shape, value.dtype),
        in_specs=[anywhere] * (1 + len(earlier)),
        out_specs=anywhere,
        input_output_aliases={0: 0},
        compiler_params=limit(1),
    )(value, *earlier)


def in_hbm(value):
    return pltpu.with_memory_space_constraint(value, pltpu.HBM)


def limit(mib):
    return pltpu.CompilerParams(vmem_limit_bytes=mib * MIB)


def vmem(count):
    return [pl.BlockSpec(memory_space=pltpu.VMEM)] * count


def smem(count):
    return [pl.BlockSpec(memory_space=pltpu.SMEM)] * count


def local(
    current_block,
    previous_block,
    previous_coupling,
    stored_blocks,
    stiffness_diag,
    lumped_mass,
    tile_values,
    tile_rows,
    tile_cols,
    tile_counts,
):
    row_devs = lax.axis_size("row")
    col_devs = lax.axis_size("col")
    width, slab_len = current_block.shape
    stored_count = stored_blocks.shape[0]
    slots, tile_len, _ = tile_values.shape
    slab_tiles = slab_len // tile_len
    cells = slab_len * row_devs * col_devs
    f32, bf16 = jnp.float32, jnp.bfloat16
    place = jnp.stack([lax.axis_index("row"), lax.axis_index("col")]).astype(jnp.int32)
    stored = stored_blocks.reshape(stored_count * width, slab_len)
    mass = lumped_mass.reshape(1, slab_len)
    diag = stiffness_diag.reshape(1, slab_len)
    slab = jax.ShapeDtypeStruct((width, slab_len), f32)

    targets = row_devs * slab_tiles
    anywhere = [pl.BlockSpec(memory_space=pl.ANY)]
    panel_shape = (col_devs + 1, width, slab_len)
    early_shape = (targets + 1, width, tile_len)
    part_acc = pltpu.VMEM((slab_tiles + 1, width, tile_len), f32)

    def cost(flops):
        return pl.CostEstimate(flops=flops, bytes_accessed=flops // width, transcendentals=0)

    with jax.named_scope("gather"):
        rounded = current_block.astype(bf16)
        panels = [rounded] + [None] * (col_devs - 1)
        for m in range(2, col_devs, 2):
            panels[m] = swap(rounded, "col", m)
        panels[1] = swap(rounded, "col", 1)

    with jax.named_scope("early"):
        places = -(-(slots + (GROUP - 1) * 2 * targets + GROUP * UNROLL) // LANES) * LANES
        plan_shape = (1, places + LANES)
        plan, held, early, gathered = pl.pallas_call(
            functools.partial(early_kernel, row_devs, col_devs, slab_tiles),
            out_shape=[
                pltpu.SMEM(plan_shape, jnp.int32),
                pltpu.VMEM(tile_values.shape, bf16),
                pltpu.VMEM(early_shape, f32),
                pltpu.VMEM(panel_shape, bf16),
            ],
            in_specs=smem(2) + [pl.BlockSpec(memory_space=pltpu.HBM)] * 3 + anywhere * 2,
            out_specs=smem(1) + vmem(3),
            scratch_shapes=[
                pltpu.VMEM((1, slots), jnp.int32),
                pltpu.VMEM((1, slots), jnp.int32),
                pltpu.VMEM(plan_shape, jnp.int32),
                pltpu.SemaphoreType.DMA((slots // CHUNK,)),
                pltpu.SemaphoreType.DMA((3,)),
                pltpu.SemaphoreType.DMA((2,)),
            ],
            compiler_params=limit(12),
            cost_estimate=cost(2 * slots * width * tile_len * tile_len),
        )(
            place,
            tile_counts,
            in_hbm(tile_rows.reshape(1, slots)),
            in_hbm(tile_cols.reshape(1, slots)),
            in_hbm(tile_values),
            panels[0],
            panels[1],
        )

    with jax.named_scope("gather"):
        for m in range(2, col_devs, 2):
            panels[m] = after(panels[m], early)
            panels[m + 1] = swap(panels[m], "col", 1)
        even, odd = list(range(2, col_devs, 2)), list(range(3, col_devs, 2))
        gathered = pl.pallas_call(
            functools.partial(collect_kernel, even),
            out_shape=pltpu.VMEM(panel_shape, bf16),
            in_specs=anywhere * len(even) + vmem(1),
            out_specs=vmem(1)[0],
            scratch_shapes=[pltpu.SemaphoreType.DMA((len(even),))],
            input_output_aliases={len(even): 0},
            compiler_params=limit(1),
            cost_estimate=cost(width),
        )(*[panels[m] for m in even], gathered)

    with jax.named_scope("late"):
        relay = row_devs == 4
        first_mask = 2 if relay else row_devs - 1
        masks = [3, 3, 1] if relay else list(range(row_devs - 2, 0, -1))
        part = jax.ShapeDtypeStruct((width, slab_len), bf16)
        first, gathered = pl.pallas_call(
            functools.partial(first_late_kernel, [first_mask], odd),
            out_shape=[part, pltpu.VMEM(panel_shape, bf16)],
            in_specs=smem(1) + anywhere * len(odd) + vmem(3),
            out_specs=vmem(2),
            scratch_shapes=[part_acc, pltpu.SemaphoreType.DMA((len(odd),))],
            input_output_aliases={3 + len(odd): 1},
            compiler_params=limit(8),
            cost_estimate=cost(width),
        )(plan, *[panels[m] for m in odd], held, early, gathered)
        parts = pl.pallas_call(
            functools.partial(late_kernel, masks),
            out_shape=[part, slab, part] if relay else [part] * len(masks),
            in_specs=smem(1) + vmem(3),
            out_specs=vmem(len(masks)),
            scratch_shapes=[part_acc],
            compiler_params=limit(8),
            cost_estimate=cost(width),
        )(plan, gathered, held, early)
        if relay:
            first = lax.ppermute(first, "row", [(0, 1), (3, 2), (1, 3), (2, 0)])
            joined = (parts[1] + first.astype(f32)).astype(bf16)
            received = [
                first,
                lax.ppermute(parts[0], "row", [(0, 3), (3, 0)]),
                lax.ppermute(joined, "row", [(1, 2), (2, 1)]),
                swap(parts[2], "row", 1),
            ]
        else:
            received = [swap(first, "row", first_mask)]
            received += [swap(part, "row", m) for m, part in zip(masks, parts)]
        base = pl.pallas_call(
            own_kernel,
            out_shape=slab,
            in_specs=smem(1) + vmem(7),
            out_specs=vmem(1)[0],
            scratch_shapes=[part_acc],
            compiler_params=limit(8),
            cost_estimate=cost(width),
        )(plan, gathered, held, early, current_block, previous_block, previous_coupling, diag)

    basis_rows = (stored_count + 1) * width
    half = (width // 8 * -(-basis_rows // 2 // LANES), 8, LANES)
    half = jax.ShapeDtypeStruct(half, f32)
    with jax.named_scope("coefficients"):
        recurrence, give = pl.pallas_call(
            functools.partial(give_kernel, cells, len(received), relay),
            out_shape=[slab, half],
            in_specs=smem(1) + vmem(len(received) + 4),
            out_specs=vmem(2),
            compiler_params=limit(16),
            cost_estimate=cost(width),
        )(plan, base, *received, mass, current_block, stored)
        keep = pl.pallas_call(
            functools.partial(keep_kernel, cells),
            out_shape=half,
            in_specs=smem(1) + vmem(4),
            out_specs=vmem(1)[0],
            compiler_params=limit(16),
            cost_estimate=cost(width),
        )(plan, recurrence, mass, current_block, stored)
        mine = keep + swap(give, "col", 1)
        mine = total_by_core(mine)
        other = swap(mine, "col", 1)

    with jax.named_scope("residual"):
        less = pl.pallas_call(
            less_kernel,
            out_shape=slab,
            in_specs=smem(1) + vmem(4),
            out_specs=vmem(1)[0],
            compiler_params=limit(16),
            cost_estimate=cost(width),
        )(plan, mine, recurrence, current_block, stored)
        residual, gram = pl.pallas_call(
            functools.partial(residual_kernel, cells),
            out_shape=[
                pltpu.VMEM((width, slab_len), f32),
                jax.ShapeDtypeStruct((width // 2, LANES), f32),
            ],
            in_specs=smem(1) + vmem(5),
            out_specs=vmem(2),
            compiler_params=limit(16),
            cost_estimate=cost(width),
        )(plan, other, less, mass, current_block, stored)
        residual_block = pl.pallas_call(
            store_kernel,
            out_shape=slab,
            in_specs=vmem(1),
            out_specs=anywhere[0],
            scratch_shapes=[pltpu.SemaphoreType.DMA((1,))],
            compiler_params=limit(1),
            cost_estimate=cost(width),
        )(residual)
        coef = pl.pallas_call(
            coefficient_kernel,
            out_shape=jax.ShapeDtypeStruct((basis_rows, width), f32),
            in_specs=smem(1) + vmem(2),
            out_specs=vmem(1)[0],
            compiler_params=limit(4),
            cost_estimate=cost(width),
        )(plan, mine, other)
        coefficients = coef.reshape(stored_count + 1, width, width)

    with jax.named_scope("gram"):
        gram = gram + swap(gram, "col", 1)
        gram = after(total(gram, "col", 2), in_hbm(residual_block), in_hbm(coef))
        gram = total(gram, "row", 1)
        gram = jnp.concatenate(
            [gram[:, :width], gram[:, LANES // 2 : LANES // 2 + width]], axis=0
        )
    return (residual_block, coefficients, gram)


def solution(mesh):
    return jax.shard_map(
        local,
        mesh=mesh,
        in_specs=(
            P(None, ("row", "col")),
            P(None, ("row", "col")),
            P(),
            P(None, None, ("row", "col")),
            P(("row", "col")),
            P(("row", "col")),
            P(("row", "col"), None, None),
            P(("row", "col")),
            P(("row", "col")),
            P(("row", "col")),
        ),
        out_specs=(P(None, ("row", "col")), P(), P()),
        check_vma=False,
    )
```

```python
import functools

import jax
import jax.numpy as jnp
from jax import lax
from jax.experimental import pallas as pl
from jax.experimental.pallas import tpu as pltpu
from jax.sharding import PartitionSpec as P

LANES = 128
CHUNK = 32
GROUP = 2
UNROLL = 8
TILE_BIT, SOURCE_BIT, ROW_BIT = 10, 15, 20
NT = (((1,), (1,)), ((), ()))
MIB = 1 << 20


def swap(value, axis, mask):
    count = lax.axis_size(axis)
    return lax.ppermute(value, axis, [(i, i ^ mask) for i in range(count)])


def tree_sum(values):
    values = [values[m] for m in sorted(values)]
    while len(values) > 1:
        values = [values[i] + values[i + 1] for i in range(0, len(values), 2)]
    return values[0]


def total(value, axis, step):
    values = {0: value}
    for m in range(lax.axis_size(axis) - step, 0, -step):
        values[m] = swap(value, axis, m)
    return tree_sum(values)


def total_shared(value, axis, *earlier):
    row_devs, col_devs = lax.axis_size("row"), lax.axis_size("col")
    step = 2 if axis == "col" else 1
    if lax.axis_size(axis) != 4 * step:
        return after(total(value, axis, step), *earlier)

    def trade(masks):
        pairs = []
        for r in range(row_devs):
            for c in range(col_devs):
                m = step * masks[c % 2]
                there = (r, c ^ m) if axis == "col" else (r ^ m, c)
                if m:
                    pairs.append((r * col_devs + c, there[0] * col_devs + there[1]))
        return lax.ppermute(value, ("row", "col"), pairs)

    far, near = trade((1, 3)), trade((0, 2))
    part = jnp.where(lax.axis_index("col") & 1 == 0, value, near) + far
    if earlier:
        part = after(part, *earlier)
    return part + swap(part, "col", 1)


def total_by_core(value):
    row_devs, col_devs = lax.axis_size("row"), lax.axis_size("col")
    if col_devs != 2 * row_devs:
        return total(total(value, "col", 2), "row", 1)
    places = [(r, c) for r in range(row_devs) for c in range(col_devs)]
    for turn in range(2):
        values = {0: value}
        for m in range(row_devs - 1, 0, -1):
            partners = [(r, c ^ (2 * m)) if c % 2 == turn else (r ^ m, c) for r, c in places]
            trades = [(i, r * col_devs + c) for i, (r, c) in enumerate(partners)]
            values[m] = lax.ppermute(value, ("row", "col"), trades)
        value = tree_sum(values)
    return value


def split(value):
    high = value.astype(jnp.bfloat16)
    low = (value - high.astype(jnp.float32)).astype(jnp.bfloat16)
    return high, low


def mm(a, b, dims=(((1,), (0,)), ((), ()))):
    return lax.dot_general(a, b, dims, preferred_element_type=jnp.float32)


def dot_split(a, b, dims=(((1,), (0,)), ((), ()))):
    rows = a.shape[0]
    a_high, a_low = split(a)
    b_high, b_low = split(b)
    both = mm(jnp.concatenate([a_high, a_low], axis=0), b_high, dims)
    return both[:rows] + both[rows:] + mm(a_high, b_low, dims)


def blocks(shape):
    return [(q, k) for q in range(0, shape[0], 8) for k in range(0, shape[1], LANES)]


def early_kernel(
    row_devs,
    col_devs,
    slab_tiles,
    place,
    counts,
    rows_hbm,
    cols_hbm,
    tiles,
    own_panel,
    near_panel,
    plan,
    held,
    acc,
    panel_buf,
    rows,
    cols,
    out,
    tile_sem,
    list_sem,
    panel_sem,
):
    chunks = (counts[0] + CHUNK - 1) // CHUNK
    row_copy = pltpu.make_async_copy(rows_hbm, rows, list_sem.at[0])
    col_copy = pltpu.make_async_copy(cols_hbm, cols, list_sem.at[1])
    row_copy.start()
    col_copy.start()

    def tile_copy(k):
        window = pl.ds(k * CHUNK, CHUNK)
        return pltpu.make_async_copy(tiles.at[window], held.at[window], tile_sem.at[k])

    @pl.loop(0, chunks)
    def _(k):
        tile_copy(k).start()

    copies = load_panels({0: own_panel, 1: near_panel}, panel_buf, panel_sem)
    zero_panel = panel_buf.shape[0] - 1
    panel_buf[zero_panel, :, :LANES] = jnp.zeros((panel_buf.shape[1], LANES), jnp.bfloat16)
    f32, bf16, i32 = jnp.float32, jnp.bfloat16, jnp.int32
    slots, places = rows.shape[1], out.shape[1] - LANES
    early_chunks = 3 * slots // CHUNK // 4
    targets = row_devs * slab_tiles
    bins = 2 * targets

    def iota(shape, dim):
        return lax.broadcasted_iota(i32, shape, dim)

    slot = iota((1, slots), 1)
    occupied = slot < counts[0]
    earlier = (iota((slots, slots), 0) < iota((slots, slots), 1)).astype(f32).astype(bf16)
    row_copy.wait()
    col_copy.wait()
    row = rows[...]
    row_owner = jnp.floor(row.astype(f32) * (1.0 / slab_tiles)).astype(i32)
    col_f = cols[...].astype(f32)
    source_f = jnp.floor(col_f * (1.0 / slab_tiles))
    source = source_f.astype(i32) ^ place[1]
    tile_f = col_f - slab_tiles * source_f
    far = row_devs - 1 - (row_owner ^ place[0])
    late_bin = targets + far * slab_tiles + row - row_owner * slab_tiles
    early = (source < 2) & (slot < early_chunks * CHUNK)
    bin_of = jnp.where(occupied, jnp.where(early, row, late_bin), -1)
    member = (iota((bins, slots), 0) == bin_of).astype(f32)
    member_bf = member.astype(bf16)
    rank = jnp.sum(member * mm(member_bf, earlier), axis=0, keepdims=True)
    sizes = mm(jnp.ones((8, slots), bf16), member_bf, NT)
    sizes = GROUP * jnp.floor((sizes + (GROUP - 1.0)) * (1.0 / GROUP))
    before = (iota((bins, bins), 1) < iota((bins, bins), 0)).astype(f32)
    begin = jnp.sum(before * sizes[:1], axis=1, keepdims=True)
    position = jnp.sum(member * begin, axis=0, keepdims=True) + rank
    position = jnp.where(occupied, position.astype(i32), -1)
    chosen = (iota((places, slots), 0) == position).astype(f32).astype(bf16)
    slot_f = slot.astype(f32)
    slot_high = jnp.floor(slot_f * (1.0 / 16.0))
    facts = [slot_high, slot_f - 16.0 * slot_high, source.astype(f32), tile_f, row.astype(f32), jnp.ones((1, slots), f32)]
    facts = jnp.concatenate(facts + [jnp.zeros((2, slots), f32)], axis=0).astype(bf16)
    found = mm(facts, chosen, NT).astype(i32)
    source = jnp.where(found[5:6] > 0, found[2:3], col_devs)
    words = (found[4:5] << ROW_BIT) + (source << SOURCE_BIT) + (found[3:4] << TILE_BIT)
    out[:, :places] = words + (found[0:1] << 4) + found[1:2]
    phase = iota((bins, LANES), 1)
    edge = jnp.where(phase > 0, targets + (phase - 1) * slab_tiles, 0)
    inside = (iota((bins, LANES), 0) < edge).astype(f32).astype(bf16)
    edges = mm(sizes.astype(bf16), inside)[:1].astype(i32)
    lane = iota((1, LANES), 1)
    edges = jnp.where(lane == LANES - 2, place[0], jnp.where(lane == LANES - 1, place[1], edges))
    out[:, places:] = edges
    plan_copy = pltpu.make_async_copy(out, plan, list_sem.at[2])
    plan_copy.start()
    acc[...] = jnp.zeros_like(acc)
    for copy in copies + [plan_copy]:
        copy.wait()

    @pl.loop(0, jnp.minimum(chunks, early_chunks))
    def _(k):
        tile_copy(k).wait()

    add_products(plan, 0, 0, targets, held, panel_buf, acc)

    @pl.loop(early_chunks, chunks)
    def _(k):
        tile_copy(k).wait()


def row_of(plan):
    return plan[0, plan.shape[1] - 2]


def core_of(plan):
    return plan[0, plan.shape[1] - 1] & 1


def field(word, low, high):
    return (word >> low) & ((1 << (high - low)) - 1)


def add_products(plan, phase, first_row, spare_row, tiles, panel_buf, acc):
    phases = plan.shape[1] - LANES
    begin, end = plan[0, phases + phase], plan[0, phases + phase + 1]

    def panel(word):
        where = pl.multiple_of(field(word, TILE_BIT, SOURCE_BIT) * LANES, LANES)
        return panel_buf[field(word, SOURCE_BIT, ROW_BIT), :, pl.ds(where, LANES)]

    @pl.loop(0, (end - begin + GROUP * UNROLL - 1) // (GROUP * UNROLL))
    def _(g):
        first = begin + g * GROUP * UNROLL
        parts = []
        for u in range(UNROLL):
            words = [plan[0, first + GROUP * u + i] for i in range(GROUP)]
            left = jnp.concatenate([panel(word) for word in words], axis=1)
            right = jnp.concatenate([tiles[field(word, 0, TILE_BIT)] for word in words], axis=1)
            parts.append(mm(left, right, NT))
        for u in range(UNROLL):
            p = first + GROUP * u
            a = jnp.where(p < end, (plan[0, p] >> ROW_BIT) - first_row, spare_row)
            acc[a] += parts[u]


def load_panels(panels, panel_buf, sem):
    copies = [pltpu.make_async_copy(ref, panel_buf.at[m], sem.at[i]) for i, (m, ref) in enumerate(panels.items())]
    for copy in copies:
        copy.start()
    return copies


def collect_kernel(masks, *refs):
    panels, (_, panel_buf, sem) = refs[: len(masks)], refs[len(masks) :]
    for copy in load_panels(dict(zip(masks, panels)), panel_buf, sem):
        copy.wait()


def first_late_kernel(masks, odd, plan, *refs):
    panels = dict(zip(odd, refs))
    tiles, early, _ = refs[len(odd) : len(odd) + 3]
    sends = refs[len(odd) + 3 : -3]
    panel_buf, acc, sem = refs[-3:]
    copies = load_panels(panels, panel_buf, sem)
    for mask, send in zip(masks, sends):
        late_part(mask, plan, tiles, early, panel_buf, acc, copies)
        put(send, acc)
        copies = ()


def late_kernel(masks, plan, panel_buf, tiles, early, *refs):
    sends, acc = refs[:-1], refs[-1]
    for i, (mask, send) in enumerate(zip(masks, sends)):
        if i == 0 or mask != masks[i - 1]:
            late_part(mask, plan, tiles, early, panel_buf, acc, ())
        put(send, acc)


def own_kernel(plan, panel_buf, tiles, early, current, previous, coupling, diag, base, acc):
    late_part(0, plan, tiles, early, panel_buf, acc, ())
    put(base, acc)
    base[...] += diag[...] * current[...] - jnp.dot(
        coupling[...],
        previous[...],
        precision=lax.Precision.HIGHEST,
        preferred_element_type=jnp.float32,
    )


def late_part(mask, plan, tiles, early, panel_buf, acc, copies):
    slab_tiles = acc.shape[0] - 1
    row_devs = (early.shape[0] - 1) // slab_tiles
    first_row = (row_of(plan) ^ mask) * slab_tiles
    for s in range(slab_tiles):
        acc[s] = early[first_row + s]
    for copy in copies:
        copy.wait()
    add_products(plan, row_devs - mask, first_row, slab_tiles, tiles, panel_buf, acc)


def put(out, acc):
    for s in range(acc.shape[0] - 1):
        out[:, s * LANES : (s + 1) * LANES] = acc[s].astype(out.dtype)


def half_basis(half, current, stored):
    rows = (current.shape[0] + stored.shape[0]) // 2
    cut = rows - current.shape[0]
    return jnp.where(half == 0, jnp.concatenate([current[...], stored[:cut]], axis=0), stored[cut:])


def pack(coef, out):
    spare = -coef.shape[1] % LANES
    coef = jnp.concatenate([coef, jnp.zeros((coef.shape[0], spare), jnp.float32)], axis=1)
    for p, (q, k) in enumerate(blocks(coef.shape)):
        out[p] = coef[q : q + 8, k : k + LANES]


def unpack(pieces, width, columns):
    groups = pieces.shape[0] * 8 // width
    rows = [jnp.concatenate([pieces[p + g] for g in range(groups)], axis=1) for p in range(0, pieces.shape[0], groups)]
    return jnp.concatenate(rows, axis=0)[:, :columns]


def give_kernel(cells, received_count, relay, plan, base, *refs):
    received = refs[:received_count]
    mass, current, stored, recurrence, give = refs[received_count:]
    total = base[...]
    for i, ref in enumerate(received):
        value = ref[...].astype(jnp.float32)
        if relay and i == 0:
            value = jnp.where((row_of(plan) == 1) | (row_of(plan) == 2), 0.0, value)
        total = total + value
    recurrence[...] = total
    weighted = total * (mass[...] * (1.0 / cells))
    pack(dot_split(weighted, half_basis(1 - core_of(plan), current, stored), NT), give)


def keep_kernel(cells, plan, recurrence, mass, current, stored, keep):
    weighted = recurrence[...] * (mass[...] * (1.0 / cells))
    pack(dot_split(weighted, half_basis(core_of(plan), current, stored), NT), keep)


def less_kernel(plan, mine, recurrence, current, stored, less):
    basis = half_basis(core_of(plan), current, stored)
    less[...] = recurrence[...] - dot_split(unpack(mine, recurrence.shape[0], basis.shape[0]), basis)


def turned(pieces, width, rows):
    value = unpack(pieces, width, pieces.shape[0] * 8 // width * LANES)
    spare = jnp.zeros((LANES - width, value.shape[1]), jnp.float32)
    return jnp.concatenate([value, spare], axis=0).T[:rows, :width]


def coefficient_kernel(plan, mine, other, out):
    rows = out.shape[0] // 2
    core = core_of(plan)
    own_half, other_half = turned(mine, out.shape[1], rows), turned(other, out.shape[1], rows)
    out[:rows] = jnp.where(core == 0, own_half, other_half)
    out[rows:] = jnp.where(core == 0, other_half, own_half)


def store_kernel(value, out, sem):
    copy = pltpu.make_async_copy(value, out, sem.at[0])
    copy.start()
    copy.wait()


def residual_kernel(cells, plan, other, less, mass, current, stored, residual, gram):
    width = less.shape[0]
    basis = half_basis(1 - core_of(plan), current, stored)
    value = less[...] - dot_split(unpack(other, width, basis.shape[0]), basis)
    residual[...] = value
    local = dot_split(value * (mass[...] * (1.0 / cells)), value, NT)
    half = width // 2
    gram[...] = jnp.zeros_like(gram)
    gram[:, :width] = local[:half]
    gram[:, LANES // 2 : LANES // 2 + width] = local[half:]


def after_kernel(*refs):
    pass


def after(value, *earlier):
    anywhere = pl.BlockSpec(memory_space=pl.ANY)
    return pl.pallas_call(
        after_kernel,
        out_shape=jax.ShapeDtypeStruct(value.shape, value.dtype),
        in_specs=[anywhere] * (1 + len(earlier)),
        out_specs=anywhere,
        input_output_aliases={0: 0},
        compiler_params=limit(1),
    )(value, *earlier)


def in_hbm(value):
    return pltpu.with_memory_space_constraint(value, pltpu.HBM)


def limit(mib):
    return pltpu.CompilerParams(vmem_limit_bytes=mib * MIB)


def vmem(count):
    return [pl.BlockSpec(memory_space=pltpu.VMEM)] * count


def smem(count):
    return [pl.BlockSpec(memory_space=pltpu.SMEM)] * count


def local(
    current_block,
    previous_block,
    previous_coupling,
    stored_blocks,
    stiffness_diag,
    lumped_mass,
    tile_values,
    tile_rows,
    tile_cols,
    tile_counts,
):
    row_devs = lax.axis_size("row")
    col_devs = lax.axis_size("col")
    width, slab_len = current_block.shape
    stored_count = stored_blocks.shape[0]
    slots, tile_len, _ = tile_values.shape
    slab_tiles = slab_len // tile_len
    cells = slab_len * row_devs * col_devs
    f32, bf16 = jnp.float32, jnp.bfloat16
    place = jnp.stack([lax.axis_index("row"), lax.axis_index("col")]).astype(jnp.int32)
    stored = stored_blocks.reshape(stored_count * width, slab_len)
    mass = lumped_mass.reshape(1, slab_len)
    diag = stiffness_diag.reshape(1, slab_len)
    slab = jax.ShapeDtypeStruct((width, slab_len), f32)

    targets = row_devs * slab_tiles
    anywhere = [pl.BlockSpec(memory_space=pl.ANY)]
    panel_shape = (col_devs + 1, width, slab_len)
    early_shape = (targets + 1, width, tile_len)
    part_acc = pltpu.VMEM((slab_tiles + 1, width, tile_len), f32)

    def cost(flops):
        return pl.CostEstimate(flops=flops, bytes_accessed=flops // width, transcendentals=0)

    with jax.named_scope("gather"):
        rounded = current_block.astype(bf16)
        panels = [rounded] + [None] * (col_devs - 1)
        for m in range(2, col_devs, 2):
            panels[m] = swap(rounded, "col", m)
        panels[1] = swap(rounded, "col", 1)

    with jax.named_scope("early"):
        places = -(-(slots + (GROUP - 1) * 2 * targets + GROUP * UNROLL) // LANES) * LANES
        plan_shape = (1, places + LANES)
        plan, held, early, gathered = pl.pallas_call(
            functools.partial(early_kernel, row_devs, col_devs, slab_tiles),
            out_shape=[
                pltpu.SMEM(plan_shape, jnp.int32),
                pltpu.VMEM(tile_values.shape, bf16),
                pltpu.VMEM(early_shape, f32),
                pltpu.VMEM(panel_shape, bf16),
            ],
            in_specs=smem(2) + [pl.BlockSpec(memory_space=pltpu.HBM)] * 3 + anywhere * 2,
            out_specs=smem(1) + vmem(3),
            scratch_shapes=[
                pltpu.VMEM((1, slots), jnp.int32),
                pltpu.VMEM((1, slots), jnp.int32),
                pltpu.VMEM(plan_shape, jnp.int32),
                pltpu.SemaphoreType.DMA((slots // CHUNK,)),
                pltpu.SemaphoreType.DMA((3,)),
                pltpu.SemaphoreType.DMA((2,)),
            ],
            compiler_params=limit(12),
            cost_estimate=cost(2 * slots * width * tile_len * tile_len),
        )(
            place,
            tile_counts,
            in_hbm(tile_rows.reshape(1, slots)),
            in_hbm(tile_cols.reshape(1, slots)),
            in_hbm(tile_values),
            panels[0],
            panels[1],
        )

    with jax.named_scope("gather"):
        for m in range(2, col_devs, 2):
            panels[m] = after(panels[m], early)
            panels[m + 1] = swap(panels[m], "col", 1)
        even, odd = list(range(2, col_devs, 2)), list(range(3, col_devs, 2))
        gathered = pl.pallas_call(
            functools.partial(collect_kernel, even),
            out_shape=pltpu.VMEM(panel_shape, bf16),
            in_specs=anywhere * len(even) + vmem(1),
            out_specs=vmem(1)[0],
            scratch_shapes=[pltpu.SemaphoreType.DMA((len(even),))],
            input_output_aliases={len(even): 0},
            compiler_params=limit(1),
            cost_estimate=cost(width),
        )(*[panels[m] for m in even], gathered)

    with jax.named_scope("late"):
        relay = row_devs == 4
        first_mask = 2 if relay else row_devs - 1
        masks = [3, 3, 1] if relay else list(range(row_devs - 2, 0, -1))
        part = jax.ShapeDtypeStruct((width, slab_len), bf16)
        first, gathered = pl.pallas_call(
            functools.partial(first_late_kernel, [first_mask], odd),
            out_shape=[part, pltpu.VMEM(panel_shape, bf16)],
            in_specs=smem(1) + anywhere * len(odd) + vmem(3),
            out_specs=vmem(2),
            scratch_shapes=[part_acc, pltpu.SemaphoreType.DMA((len(odd),))],
            input_output_aliases={3 + len(odd): 1},
            compiler_params=limit(8),
            cost_estimate=cost(width),
        )(plan, *[panels[m] for m in odd], held, early, gathered)
        parts = pl.pallas_call(
            functools.partial(late_kernel, masks),
            out_shape=[part, slab, part] if relay else [part] * len(masks),
            in_specs=smem(1) + vmem(3),
            out_specs=vmem(len(masks)),
            scratch_shapes=[part_acc],
            compiler_params=limit(8),
            cost_estimate=cost(width),
        )(plan, gathered, held, early)
        if relay:
            first = lax.ppermute(first, "row", [(0, 1), (3, 2), (1, 3), (2, 0)])
            joined = (parts[1] + first.astype(f32)).astype(bf16)
            received = [
                first,
                lax.ppermute(parts[0], "row", [(0, 3), (3, 0)]),
                lax.ppermute(joined, "row", [(1, 2), (2, 1)]),
                swap(parts[2], "row", 1),
            ]
        else:
            received = [swap(first, "row", first_mask)]
            received += [swap(part, "row", m) for m, part in zip(masks, parts)]
        base = pl.pallas_call(
            own_kernel,
            out_shape=slab,
            in_specs=smem(1) + vmem(7),
            out_specs=vmem(1)[0],
            scratch_shapes=[part_acc],
            compiler_params=limit(8),
            cost_estimate=cost(width),
        )(plan, gathered, held, early, current_block, previous_block, previous_coupling, diag)

    basis_rows = (stored_count + 1) * width
    half = (width // 8 * -(-basis_rows // 2 // LANES), 8, LANES)
    half = jax.ShapeDtypeStruct(half, f32)
    with jax.named_scope("coefficients"):
        recurrence, give = pl.pallas_call(
            functools.partial(give_kernel, cells, len(received), relay),
            out_shape=[slab, half],
            in_specs=smem(1) + vmem(len(received) + 4),
            out_specs=vmem(2),
            compiler_params=limit(16),
            cost_estimate=cost(width),
        )(plan, base, *received, mass, current_block, stored)
        keep = pl.pallas_call(
            functools.partial(keep_kernel, cells),
            out_shape=half,
            in_specs=smem(1) + vmem(4),
            out_specs=vmem(1)[0],
            compiler_params=limit(16),
            cost_estimate=cost(width),
        )(plan, recurrence, mass, current_block, stored)
        mine = keep + swap(give, "col", 1)
        mine = total_by_core(mine)
        other = swap(mine, "col", 1)

    with jax.named_scope("residual"):
        less = pl.pallas_call(
            less_kernel,
            out_shape=slab,
            in_specs=smem(1) + vmem(4),
            out_specs=vmem(1)[0],
            compiler_params=limit(16),
            cost_estimate=cost(width),
        )(plan, mine, recurrence, current_block, stored)
        residual, gram = pl.pallas_call(
            functools.partial(residual_kernel, cells),
            out_shape=[
                pltpu.VMEM((width, slab_len), f32),
                jax.ShapeDtypeStruct((width // 2, LANES), f32),
            ],
            in_specs=smem(1) + vmem(5),
            out_specs=vmem(2),
            compiler_params=limit(16),
            cost_estimate=cost(width),
        )(plan, other, less, mass, current_block, stored)
        residual_block = pl.pallas_call(
            store_kernel,
            out_shape=slab,
            in_specs=vmem(1),
            out_specs=anywhere[0],
            scratch_shapes=[pltpu.SemaphoreType.DMA((1,))],
            compiler_params=limit(1),
            cost_estimate=cost(width),
        )(residual)
        coef = pl.pallas_call(
            coefficient_kernel,
            out_shape=jax.ShapeDtypeStruct((basis_rows, width), f32),
            in_specs=smem(1) + vmem(2),
            out_specs=vmem(1)[0],
            compiler_params=limit(4),
            cost_estimate=cost(width),
        )(plan, mine, other)
        coefficients = coef.reshape(stored_count + 1, width, width)

    with jax.named_scope("gram"):
        gram = gram + swap(gram, "col", 1)
        gram = total_shared(gram, "col", in_hbm(residual_block), in_hbm(coef))
        gram = total_shared(gram, "row")
        gram = jnp.concatenate(
            [gram[:, :width], gram[:, LANES // 2 : LANES // 2 + width]], axis=0
        )
    return (residual_block, coefficients, gram)


def solution(mesh):
    return jax.shard_map(
        local,
        mesh=mesh,
        in_specs=(
            P(None, ("row", "col")),
            P(None, ("row", "col")),
            P(),
            P(None, None, ("row", "col")),
            P(("row", "col")),
            P(("row", "col")),
            P(("row", "col"), None, None),
            P(("row", "col")),
            P(("row", "col")),
            P(("row", "col")),
        ),
        out_specs=(P(None, ("row", "col")), P(), P()),
        check_vma=False,
    )
```

```python
import functools

import jax
import jax.numpy as jnp
from jax import lax
from jax.experimental import pallas as pl
from jax.experimental.pallas import tpu as pltpu
from jax.sharding import PartitionSpec as P

LANES = 128
CHUNK = 32
GROUP = 2
UNROLL = 8
TILE_BIT, SOURCE_BIT, ROW_BIT = 10, 15, 20
NT = (((1,), (1,)), ((), ()))
MIB = 1 << 20


def swap(value, axis, mask):
    count = lax.axis_size(axis)
    return lax.ppermute(value, axis, [(i, i ^ mask) for i in range(count)])


def trade_rows(value, pairs):
    row_devs, col_devs = lax.axis_size("row"), lax.axis_size("col")
    to = dict(pairs)
    trades = []
    for r in range(row_devs):
        for c in range(col_devs):
            partner = to[r] * col_devs + c if r in to else r * col_devs + (c ^ 1)
            trades.append((r * col_devs + c, partner))
    return lax.ppermute(value, ("row", "col"), trades)


def tree_sum(values):
    values = [values[m] for m in sorted(values)]
    while len(values) > 1:
        values = [values[i] + values[i + 1] for i in range(0, len(values), 2)]
    return values[0]


def total(value, axis, step):
    values = {0: value}
    for m in range(lax.axis_size(axis) - step, 0, -step):
        values[m] = swap(value, axis, m)
    return tree_sum(values)


def total_by_core(value):
    row_devs, col_devs = lax.axis_size("row"), lax.axis_size("col")
    if col_devs != 2 * row_devs:
        return total(total(value, "col", 2), "row", 1)
    places = [(r, c) for r in range(row_devs) for c in range(col_devs)]
    for turn in range(2):
        values = {0: value}
        for m in range(row_devs - 1, 0, -1):
            partners = [(r, c ^ (2 * m)) if c % 2 == turn else (r ^ m, c) for r, c in places]
            trades = [(i, r * col_devs + c) for i, (r, c) in enumerate(partners)]
            values[m] = lax.ppermute(value, ("row", "col"), trades)
        value = tree_sum(values)
    return value


def split(value):
    high = value.astype(jnp.bfloat16)
    low = (value - high.astype(jnp.float32)).astype(jnp.bfloat16)
    return high, low


def mm(a, b, dims=(((1,), (0,)), ((), ()))):
    return lax.dot_general(a, b, dims, preferred_element_type=jnp.float32)


def dot_split(a, b, dims=(((1,), (0,)), ((), ()))):
    rows = a.shape[0]
    a_high, a_low = split(a)
    b_high, b_low = split(b)
    both = mm(jnp.concatenate([a_high, a_low], axis=0), b_high, dims)
    return both[:rows] + both[rows:] + mm(a_high, b_low, dims)


def blocks(shape):
    return [(q, k) for q in range(0, shape[0], 8) for k in range(0, shape[1], LANES)]


def early_kernel(
    row_devs,
    col_devs,
    slab_tiles,
    place,
    counts,
    rows_hbm,
    cols_hbm,
    tiles,
    own_panel,
    near_panel,
    plan,
    held,
    acc,
    panel_buf,
    rows,
    cols,
    out,
    tile_sem,
    list_sem,
    panel_sem,
):
    chunks = (counts[0] + CHUNK - 1) // CHUNK
    row_copy = pltpu.make_async_copy(rows_hbm, rows, list_sem.at[0])
    col_copy = pltpu.make_async_copy(cols_hbm, cols, list_sem.at[1])
    row_copy.start()
    col_copy.start()

    def tile_copy(k):
        window = pl.ds(k * CHUNK, CHUNK)
        return pltpu.make_async_copy(tiles.at[window], held.at[window], tile_sem.at[k])

    @pl.loop(0, chunks)
    def _(k):
        tile_copy(k).start()

    copies = load_panels({0: own_panel, 1: near_panel}, panel_buf, panel_sem)
    zero_panel = panel_buf.shape[0] - 1
    panel_buf[zero_panel, :, :LANES] = jnp.zeros((panel_buf.shape[1], LANES), jnp.bfloat16)
    f32, bf16, i32 = jnp.float32, jnp.bfloat16, jnp.int32
    slots, places = rows.shape[1], out.shape[1] - LANES
    early_chunks = 3 * slots // CHUNK // 4
    targets = row_devs * slab_tiles
    bins = 2 * targets

    def iota(shape, dim):
        return lax.broadcasted_iota(i32, shape, dim)

    slot = iota((1, slots), 1)
    occupied = slot < counts[0]
    earlier = (iota((slots, slots), 0) < iota((slots, slots), 1)).astype(f32).astype(bf16)
    row_copy.wait()
    col_copy.wait()
    row = rows[...]
    row_owner = jnp.floor(row.astype(f32) * (1.0 / slab_tiles)).astype(i32)
    col_f = cols[...].astype(f32)
    source_f = jnp.floor(col_f * (1.0 / slab_tiles))
    source = source_f.astype(i32) ^ place[1]
    tile_f = col_f - slab_tiles * source_f
    far = row_devs - 1 - (row_owner ^ place[0])
    late_bin = targets + far * slab_tiles + row - row_owner * slab_tiles
    early = (source < 2) & (slot < early_chunks * CHUNK)
    bin_of = jnp.where(occupied, jnp.where(early, row, late_bin), -1)
    member = (iota((bins, slots), 0) == bin_of).astype(f32)
    member_bf = member.astype(bf16)
    rank = jnp.sum(member * mm(member_bf, earlier), axis=0, keepdims=True)
    sizes = mm(jnp.ones((8, slots), bf16), member_bf, NT)
    sizes = GROUP * jnp.floor((sizes + (GROUP - 1.0)) * (1.0 / GROUP))
    before = (iota((bins, bins), 1) < iota((bins, bins), 0)).astype(f32)
    begin = jnp.sum(before * sizes[:1], axis=1, keepdims=True)
    position = jnp.sum(member * begin, axis=0, keepdims=True) + rank
    position = jnp.where(occupied, position.astype(i32), -1)
    chosen = (iota((places, slots), 0) == position).astype(f32).astype(bf16)
    slot_f = slot.astype(f32)
    slot_high = jnp.floor(slot_f * (1.0 / 16.0))
    facts = [slot_high, slot_f - 16.0 * slot_high, source.astype(f32), tile_f, row.astype(f32), jnp.ones((1, slots), f32)]
    facts = jnp.concatenate(facts + [jnp.zeros((2, slots), f32)], axis=0).astype(bf16)
    found = mm(facts, chosen, NT).astype(i32)
    source = jnp.where(found[5:6] > 0, found[2:3], col_devs)
    words = (found[4:5] << ROW_BIT) + (source << SOURCE_BIT) + (found[3:4] << TILE_BIT)
    out[:, :places] = words + (found[0:1] << 4) + found[1:2]
    phase = iota((bins, LANES), 1)
    edge = jnp.where(phase > 0, targets + (phase - 1) * slab_tiles, 0)
    inside = (iota((bins, LANES), 0) < edge).astype(f32).astype(bf16)
    edges = mm(sizes.astype(bf16), inside)[:1].astype(i32)
    lane = iota((1, LANES), 1)
    edges = jnp.where(lane == LANES - 2, place[0], jnp.where(lane == LANES - 1, place[1], edges))
    out[:, places:] = edges
    plan_copy = pltpu.make_async_copy(out, plan, list_sem.at[2])
    plan_copy.start()
    acc[...] = jnp.zeros_like(acc)
    for copy in copies + [plan_copy]:
        copy.wait()

    @pl.loop(0, jnp.minimum(chunks, early_chunks))
    def _(k):
        tile_copy(k).wait()

    add_products(plan, 0, 0, targets, held, panel_buf, acc)

    @pl.loop(early_chunks, chunks)
    def _(k):
        tile_copy(k).wait()


def row_of(plan):
    return plan[0, plan.shape[1] - 2]


def core_of(plan):
    return plan[0, plan.shape[1] - 1] & 1


def field(word, low, high):
    return (word >> low) & ((1 << (high - low)) - 1)


def add_products(plan, phase, first_row, spare_row, tiles, panel_buf, acc):
    phases = plan.shape[1] - LANES
    begin, end = plan[0, phases + phase], plan[0, phases + phase + 1]

    def panel(word):
        where = pl.multiple_of(field(word, TILE_BIT, SOURCE_BIT) * LANES, LANES)
        return panel_buf[field(word, SOURCE_BIT, ROW_BIT), :, pl.ds(where, LANES)]

    @pl.loop(0, (end - begin + GROUP * UNROLL - 1) // (GROUP * UNROLL))
    def _(g):
        first = begin + g * GROUP * UNROLL
        parts = []
        for u in range(UNROLL):
            words = [plan[0, first + GROUP * u + i] for i in range(GROUP)]
            left = jnp.concatenate([panel(word) for word in words], axis=1)
            right = jnp.concatenate([tiles[field(word, 0, TILE_BIT)] for word in words], axis=1)
            parts.append(mm(left, right, NT))
        for u in range(UNROLL):
            p = first + GROUP * u
            a = jnp.where(p < end, (plan[0, p] >> ROW_BIT) - first_row, spare_row)
            acc[a] += parts[u]


def load_panels(panels, panel_buf, sem):
    copies = [pltpu.make_async_copy(ref, panel_buf.at[m], sem.at[i]) for i, (m, ref) in enumerate(panels.items())]
    for copy in copies:
        copy.start()
    return copies


def collect_kernel(masks, *refs):
    panels, (_, panel_buf, sem) = refs[: len(masks)], refs[len(masks) :]
    for copy in load_panels(dict(zip(masks, panels)), panel_buf, sem):
        copy.wait()


def first_late_kernel(masks, odd, plan, *refs):
    panels = dict(zip(odd, refs))
    tiles, early, _ = refs[len(odd) : len(odd) + 3]
    sends = refs[len(odd) + 3 : -3]
    panel_buf, acc, sem = refs[-3:]
    copies = load_panels(panels, panel_buf, sem)
    for mask, send in zip(masks, sends):
        late_part(mask, plan, tiles, early, panel_buf, acc, copies)
        put(send, acc)
        copies = ()


def late_kernel(masks, plan, panel_buf, tiles, early, *refs):
    sends, acc = refs[:-1], refs[-1]
    for i, (mask, send) in enumerate(zip(masks, sends)):
        if i == 0 or mask != masks[i - 1]:
            late_part(mask, plan, tiles, early, panel_buf, acc, ())
        put(send, acc)


def own_kernel(plan, panel_buf, tiles, early, current, previous, coupling, diag, base, acc):
    late_part(0, plan, tiles, early, panel_buf, acc, ())
    put(base, acc)
    base[...] += diag[...] * current[...] - jnp.dot(
        coupling[...],
        previous[...],
        precision=lax.Precision.HIGHEST,
        preferred_element_type=jnp.float32,
    )


def late_part(mask, plan, tiles, early, panel_buf, acc, copies):
    slab_tiles = acc.shape[0] - 1
    row_devs = (early.shape[0] - 1) // slab_tiles
    first_row = (row_of(plan) ^ mask) * slab_tiles
    for s in range(slab_tiles):
        acc[s] = early[first_row + s]
    for copy in copies:
        copy.wait()
    add_products(plan, row_devs - mask, first_row, slab_tiles, tiles, panel_buf, acc)


def put(out, acc):
    for s in range(acc.shape[0] - 1):
        out[:, s * LANES : (s + 1) * LANES] = acc[s].astype(out.dtype)


def half_basis(half, current, stored):
    rows = (current.shape[0] + stored.shape[0]) // 2
    cut = rows - current.shape[0]
    return jnp.where(half == 0, jnp.concatenate([current[...], stored[:cut]], axis=0), stored[cut:])


def pack(coef, out):
    spare = -coef.shape[1] % LANES
    coef = jnp.concatenate([coef, jnp.zeros((coef.shape[0], spare), jnp.float32)], axis=1)
    for p, (q, k) in enumerate(blocks(coef.shape)):
        out[p] = coef[q : q + 8, k : k + LANES]


def unpack(pieces, width, columns):
    groups = pieces.shape[0] * 8 // width
    rows = [jnp.concatenate([pieces[p + g] for g in range(groups)], axis=1) for p in range(0, pieces.shape[0], groups)]
    return jnp.concatenate(rows, axis=0)[:, :columns]


def give_kernel(cells, received_count, relay, plan, base, *refs):
    received = refs[:received_count]
    mass, current, stored, recurrence, give = refs[received_count:]
    total = base[...]
    for i, ref in enumerate(received):
        value = ref[...].astype(jnp.float32)
        if relay and i < 3:
            inner = (row_of(plan) == 1) | (row_of(plan) == 2)
            value = jnp.where(inner if i < 2 else jnp.logical_not(inner), 0.0, value)
        total = total + value
    recurrence[...] = total
    weighted = total * (mass[...] * (1.0 / cells))
    pack(dot_split(weighted, half_basis(1 - core_of(plan), current, stored), NT), give)


def keep_kernel(cells, plan, recurrence, mass, current, stored, keep):
    weighted = recurrence[...] * (mass[...] * (1.0 / cells))
    pack(dot_split(weighted, half_basis(core_of(plan), current, stored), NT), keep)


def less_kernel(plan, mine, recurrence, current, stored, less):
    basis = half_basis(core_of(plan), current, stored)
    less[...] = recurrence[...] - dot_split(unpack(mine, recurrence.shape[0], basis.shape[0]), basis)


def turned(pieces, width, rows):
    value = unpack(pieces, width, pieces.shape[0] * 8 // width * LANES)
    spare = jnp.zeros((LANES - width, value.shape[1]), jnp.float32)
    return jnp.concatenate([value, spare], axis=0).T[:rows, :width]


def coefficient_kernel(plan, mine, other, out):
    rows = out.shape[0] // 2
    core = core_of(plan)
    own_half, other_half = turned(mine, out.shape[1], rows), turned(other, out.shape[1], rows)
    out[:rows] = jnp.where(core == 0, own_half, other_half)
    out[rows:] = jnp.where(core == 0, other_half, own_half)


def store_kernel(value, out, sem):
    copy = pltpu.make_async_copy(value, out, sem.at[0])
    copy.start()
    copy.wait()


def residual_kernel(cells, plan, other, less, mass, current, stored, residual, gram):
    width = less.shape[0]
    basis = half_basis(1 - core_of(plan), current, stored)
    value = less[...] - dot_split(unpack(other, width, basis.shape[0]), basis)
    residual[...] = value
    local = dot_split(value * (mass[...] * (1.0 / cells)), value, NT)
    half = width // 2
    gram[...] = jnp.zeros_like(gram)
    gram[:, :width] = local[:half]
    gram[:, LANES // 2 : LANES // 2 + width] = local[half:]


def after_kernel(*refs):
    pass


def after(value, *earlier):
    anywhere = pl.BlockSpec(memory_space=pl.ANY)
    return pl.pallas_call(
        after_kernel,
        out_shape=jax.ShapeDtypeStruct(value.shape, value.dtype),
        in_specs=[anywhere] * (1 + len(earlier)),
        out_specs=anywhere,
        input_output_aliases={0: 0},
        compiler_params=limit(1),
    )(value, *earlier)


def in_hbm(value):
    return pltpu.with_memory_space_constraint(value, pltpu.HBM)


def limit(mib):
    return pltpu.CompilerParams(vmem_limit_bytes=mib * MIB)


def vmem(count):
    return [pl.BlockSpec(memory_space=pltpu.VMEM)] * count


def smem(count):
    return [pl.BlockSpec(memory_space=pltpu.SMEM)] * count


def local(
    current_block,
    previous_block,
    previous_coupling,
    stored_blocks,
    stiffness_diag,
    lumped_mass,
    tile_values,
    tile_rows,
    tile_cols,
    tile_counts,
):
    row_devs = lax.axis_size("row")
    col_devs = lax.axis_size("col")
    width, slab_len = current_block.shape
    stored_count = stored_blocks.shape[0]
    slots, tile_len, _ = tile_values.shape
    slab_tiles = slab_len // tile_len
    cells = slab_len * row_devs * col_devs
    f32, bf16 = jnp.float32, jnp.bfloat16
    place = jnp.stack([lax.axis_index("row"), lax.axis_index("col")]).astype(jnp.int32)
    stored = stored_blocks.reshape(stored_count * width, slab_len)
    mass = lumped_mass.reshape(1, slab_len)
    diag = stiffness_diag.reshape(1, slab_len)
    slab = jax.ShapeDtypeStruct((width, slab_len), f32)

    targets = row_devs * slab_tiles
    anywhere = [pl.BlockSpec(memory_space=pl.ANY)]
    panel_shape = (col_devs + 1, width, slab_len)
    early_shape = (targets + 1, width, tile_len)
    part_acc = pltpu.VMEM((slab_tiles + 1, width, tile_len), f32)

    def cost(flops):
        return pl.CostEstimate(flops=flops, bytes_accessed=flops // width, transcendentals=0)

    with jax.named_scope("gather"):
        rounded = current_block.astype(bf16)
        panels = [rounded] + [None] * (col_devs - 1)
        for m in range(2, col_devs, 2):
            panels[m] = swap(rounded, "col", m)
        panels[1] = swap(rounded, "col", 1)

    with jax.named_scope("early"):
        places = -(-(slots + (GROUP - 1) * 2 * targets + GROUP * UNROLL) // LANES) * LANES
        plan_shape = (1, places + LANES)
        plan, held, early, gathered = pl.pallas_call(
            functools.partial(early_kernel, row_devs, col_devs, slab_tiles),
            out_shape=[
                pltpu.SMEM(plan_shape, jnp.int32),
                pltpu.VMEM(tile_values.shape, bf16),
                pltpu.VMEM(early_shape, f32),
                pltpu.VMEM(panel_shape, bf16),
            ],
            in_specs=smem(2) + [pl.BlockSpec(memory_space=pltpu.HBM)] * 3 + anywhere * 2,
            out_specs=smem(1) + vmem(3),
            scratch_shapes=[
                pltpu.VMEM((1, slots), jnp.int32),
                pltpu.VMEM((1, slots), jnp.int32),
                pltpu.VMEM(plan_shape, jnp.int32),
                pltpu.SemaphoreType.DMA((slots // CHUNK,)),
                pltpu.SemaphoreType.DMA((3,)),
                pltpu.SemaphoreType.DMA((2,)),
            ],
            compiler_params=limit(12),
            cost_estimate=cost(2 * slots * width * tile_len * tile_len),
        )(
            place,
            tile_counts,
            in_hbm(tile_rows.reshape(1, slots)),
            in_hbm(tile_cols.reshape(1, slots)),
            in_hbm(tile_values),
            panels[0],
            panels[1],
        )

    with jax.named_scope("gather"):
        for m in range(2, col_devs, 2):
            panels[m] = after(panels[m], early)
            panels[m + 1] = swap(panels[m], "col", 1)
        even, odd = list(range(2, col_devs, 2)), list(range(3, col_devs, 2))
        gathered = pl.pallas_call(
            functools.partial(collect_kernel, even),
            out_shape=pltpu.VMEM(panel_shape, bf16),
            in_specs=anywhere * len(even) + vmem(1),
            out_specs=vmem(1)[0],
            scratch_shapes=[pltpu.SemaphoreType.DMA((len(even),))],
            input_output_aliases={len(even): 0},
            compiler_params=limit(1),
            cost_estimate=cost(width),
        )(*[panels[m] for m in even], gathered)

    with jax.named_scope("late"):
        relay = row_devs == 4
        first_mask = 2 if relay else row_devs - 1
        masks = [3, 3, 1] if relay else list(range(row_devs - 2, 0, -1))
        part = jax.ShapeDtypeStruct((width, slab_len), bf16)
        first, gathered = pl.pallas_call(
            functools.partial(first_late_kernel, [first_mask], odd),
            out_shape=[part, pltpu.VMEM(panel_shape, bf16)],
            in_specs=smem(1) + anywhere * len(odd) + vmem(3),
            out_specs=vmem(2),
            scratch_shapes=[part_acc, pltpu.SemaphoreType.DMA((len(odd),))],
            input_output_aliases={3 + len(odd): 1},
            compiler_params=limit(8),
            cost_estimate=cost(width),
        )(plan, *[panels[m] for m in odd], held, early, gathered)
        parts = pl.pallas_call(
            functools.partial(late_kernel, masks),
            out_shape=[part, slab, part] if relay else [part] * len(masks),
            in_specs=smem(1) + vmem(3),
            out_specs=vmem(len(masks)),
            scratch_shapes=[part_acc],
            compiler_params=limit(8),
            cost_estimate=cost(width),
        )(plan, gathered, held, early)
        if relay:
            first = lax.ppermute(first, "row", [(0, 1), (3, 2), (1, 3), (2, 0)])
            joined = (parts[1] + first.astype(f32)).astype(bf16)
            received = [
                first,
                trade_rows(parts[0], [(0, 3), (3, 0)]),
                trade_rows(joined, [(1, 2), (2, 1)]),
                swap(parts[2], "row", 1),
            ]
        else:
            received = [swap(first, "row", first_mask)]
            received += [swap(part, "row", m) for m, part in zip(masks, parts)]
        base = pl.pallas_call(
            own_kernel,
            out_shape=slab,
            in_specs=smem(1) + vmem(7),
            out_specs=vmem(1)[0],
            scratch_shapes=[part_acc],
            compiler_params=limit(8),
            cost_estimate=cost(width),
        )(plan, gathered, held, early, current_block, previous_block, previous_coupling, diag)

    basis_rows = (stored_count + 1) * width
    half = (width // 8 * -(-basis_rows // 2 // LANES), 8, LANES)
    half = jax.ShapeDtypeStruct(half, f32)
    with jax.named_scope("coefficients"):
        recurrence, give = pl.pallas_call(
            functools.partial(give_kernel, cells, len(received), relay),
            out_shape=[slab, half],
            in_specs=smem(1) + vmem(len(received) + 4),
            out_specs=vmem(2),
            compiler_params=limit(16),
            cost_estimate=cost(width),
        )(plan, base, *received, mass, current_block, stored)
        keep = pl.pallas_call(
            functools.partial(keep_kernel, cells),
            out_shape=half,
            in_specs=smem(1) + vmem(4),
            out_specs=vmem(1)[0],
            compiler_params=limit(16),
            cost_estimate=cost(width),
        )(plan, recurrence, mass, current_block, stored)
        mine = keep + swap(give, "col", 1)
        mine = total_by_core(mine)
        other = swap(mine, "col", 1)

    with jax.named_scope("residual"):
        less = pl.pallas_call(
            less_kernel,
            out_shape=slab,
            in_specs=smem(1) + vmem(4),
            out_specs=vmem(1)[0],
            compiler_params=limit(16),
            cost_estimate=cost(width),
        )(plan, mine, recurrence, current_block, stored)
        residual, gram = pl.pallas_call(
            functools.partial(residual_kernel, cells),
            out_shape=[
                pltpu.VMEM((width, slab_len), f32),
                jax.ShapeDtypeStruct((width // 2, LANES), f32),
            ],
            in_specs=smem(1) + vmem(5),
            out_specs=vmem(2),
            compiler_params=limit(16),
            cost_estimate=cost(width),
        )(plan, other, less, mass, current_block, stored)
        residual_block = pl.pallas_call(
            store_kernel,
            out_shape=slab,
            in_specs=vmem(1),
            out_specs=anywhere[0],
            scratch_shapes=[pltpu.SemaphoreType.DMA((1,))],
            compiler_params=limit(1),
            cost_estimate=cost(width),
        )(residual)
        coef = pl.pallas_call(
            coefficient_kernel,
            out_shape=jax.ShapeDtypeStruct((basis_rows, width), f32),
            in_specs=smem(1) + vmem(2),
            out_specs=vmem(1)[0],
            compiler_params=limit(4),
            cost_estimate=cost(width),
        )(plan, mine, other)
        coefficients = coef.reshape(stored_count + 1, width, width)

    with jax.named_scope("gram"):
        gram = gram + swap(gram, "col", 1)
        gram = after(total(gram, "col", 2), in_hbm(residual_block), in_hbm(coef))
        gram = total(gram, "row", 1)
        gram = jnp.concatenate(
            [gram[:, :width], gram[:, LANES // 2 : LANES // 2 + width]], axis=0
        )
    return (residual_block, coefficients, gram)


def solution(mesh):
    return jax.shard_map(
        local,
        mesh=mesh,
        in_specs=(
            P(None, ("row", "col")),
            P(None, ("row", "col")),
            P(),
            P(None, None, ("row", "col")),
            P(("row", "col")),
            P(("row", "col")),
            P(("row", "col"), None, None),
            P(("row", "col")),
            P(("row", "col")),
            P(("row", "col")),
        ),
        out_specs=(P(None, ("row", "col")), P(), P()),
        check_vma=False,
    )
```

```python
import functools

import jax
import jax.numpy as jnp
from jax import lax
from jax.experimental import pallas as pl
from jax.experimental.pallas import tpu as pltpu
from jax.sharding import PartitionSpec as P

LANES = 128
CHUNK = 32
GROUP = 2
UNROLL = 8
TILE_BIT, SOURCE_BIT, ROW_BIT = 10, 15, 20
NT = (((1,), (1,)), ((), ()))
MIB = 1 << 20


def swap(value, axis, mask):
    count = lax.axis_size(axis)
    return lax.ppermute(value, axis, [(i, i ^ mask) for i in range(count)])


def trade_rows(value, pairs):
    row_devs, col_devs = lax.axis_size("row"), lax.axis_size("col")
    to = dict(pairs)
    trades = []
    for r in range(row_devs):
        for c in range(col_devs):
            partner = to[r] * col_devs + c if r in to else r * col_devs + (c ^ 1)
            trades.append((r * col_devs + c, partner))
    return lax.ppermute(value, ("row", "col"), trades)


def tree_sum(values):
    values = [values[m] for m in sorted(values)]
    while len(values) > 1:
        values = [values[i] + values[i + 1] for i in range(0, len(values), 2)]
    return values[0]


def total(value, axis, step):
    values = {0: value}
    for m in range(lax.axis_size(axis) - step, 0, -step):
        values[m] = swap(value, axis, m)
    return tree_sum(values)


def total_by_core(value):
    row_devs, col_devs = lax.axis_size("row"), lax.axis_size("col")
    if col_devs != 2 * row_devs:
        return total(total(value, "col", 2), "row", 1)
    places = [(r, c) for r in range(row_devs) for c in range(col_devs)]
    for turn in range(2):
        values = {0: value}
        for m in range(row_devs - 1, 0, -1):
            partners = [(r, c ^ (2 * m)) if c % 2 == turn else (r ^ m, c) for r, c in places]
            trades = [(i, r * col_devs + c) for i, (r, c) in enumerate(partners)]
            values[m] = lax.ppermute(value, ("row", "col"), trades)
        value = tree_sum(values)
    return value


def split(value):
    high = value.astype(jnp.bfloat16)
    low = (value - high.astype(jnp.float32)).astype(jnp.bfloat16)
    return high, low


def mm(a, b, dims=(((1,), (0,)), ((), ()))):
    return lax.dot_general(a, b, dims, preferred_element_type=jnp.float32)


def dot_split(a, b, dims=(((1,), (0,)), ((), ()))):
    rows = a.shape[0]
    a_high, a_low = split(a)
    b_high, b_low = split(b)
    both = mm(jnp.concatenate([a_high, a_low], axis=0), b_high, dims)
    return both[:rows] + both[rows:] + mm(a_high, b_low, dims)


def blocks(shape):
    return [(q, k) for q in range(0, shape[0], 8) for k in range(0, shape[1], LANES)]


def early_kernel(
    row_devs,
    col_devs,
    slab_tiles,
    place,
    counts,
    rows_hbm,
    cols_hbm,
    tiles,
    own_panel,
    near_panel,
    plan,
    held,
    acc,
    panel_buf,
    rows,
    cols,
    out,
    tile_sem,
    list_sem,
    panel_sem,
):
    chunks = (counts[0] + CHUNK - 1) // CHUNK
    row_copy = pltpu.make_async_copy(rows_hbm, rows, list_sem.at[0])
    col_copy = pltpu.make_async_copy(cols_hbm, cols, list_sem.at[1])
    row_copy.start()
    col_copy.start()

    def tile_copy(k):
        window = pl.ds(k * CHUNK, CHUNK)
        return pltpu.make_async_copy(tiles.at[window], held.at[window], tile_sem.at[k])

    @pl.loop(0, chunks)
    def _(k):
        tile_copy(k).start()

    copies = load_panels({0: own_panel, 1: near_panel}, panel_buf, panel_sem)
    zero_panel = panel_buf.shape[0] - 1
    panel_buf[zero_panel, :, :LANES] = jnp.zeros((panel_buf.shape[1], LANES), jnp.bfloat16)
    f32, bf16, i32 = jnp.float32, jnp.bfloat16, jnp.int32
    slots, places = rows.shape[1], out.shape[1] - LANES
    early_chunks = 3 * slots // CHUNK // 4
    targets = row_devs * slab_tiles
    bins = 2 * targets

    def iota(shape, dim):
        return lax.broadcasted_iota(i32, shape, dim)

    slot = iota((1, slots), 1)
    occupied = slot < counts[0]
    earlier = (iota((slots, slots), 0) < iota((slots, slots), 1)).astype(f32).astype(bf16)
    row_copy.wait()
    col_copy.wait()
    row = rows[...]
    row_owner = jnp.floor(row.astype(f32) * (1.0 / slab_tiles)).astype(i32)
    col_f = cols[...].astype(f32)
    source_f = jnp.floor(col_f * (1.0 / slab_tiles))
    source = source_f.astype(i32) ^ place[1]
    tile_f = col_f - slab_tiles * source_f
    far = row_devs - 1 - (row_owner ^ place[0])
    late_bin = targets + far * slab_tiles + row - row_owner * slab_tiles
    early = (source < 2) & (slot < early_chunks * CHUNK)
    bin_of = jnp.where(occupied, jnp.where(early, row, late_bin), -1)
    member = (iota((bins, slots), 0) == bin_of).astype(f32)
    member_bf = member.astype(bf16)
    rank = jnp.sum(member * mm(member_bf, earlier), axis=0, keepdims=True)
    sizes = mm(jnp.ones((8, slots), bf16), member_bf, NT)
    sizes = GROUP * jnp.floor((sizes + (GROUP - 1.0)) * (1.0 / GROUP))
    before = (iota((bins, bins), 1) < iota((bins, bins), 0)).astype(f32)
    begin = jnp.sum(before * sizes[:1], axis=1, keepdims=True)
    position = jnp.sum(member * begin, axis=0, keepdims=True) + rank
    position = jnp.where(occupied, position.astype(i32), -1)
    chosen = (iota((places, slots), 0) == position).astype(f32).astype(bf16)
    slot_f = slot.astype(f32)
    slot_high = jnp.floor(slot_f * (1.0 / 16.0))
    facts = [slot_high, slot_f - 16.0 * slot_high, source.astype(f32), tile_f, row.astype(f32), jnp.ones((1, slots), f32)]
    facts = jnp.concatenate(facts + [jnp.zeros((2, slots), f32)], axis=0).astype(bf16)
    found = mm(facts, chosen, NT).astype(i32)
    source = jnp.where(found[5:6] > 0, found[2:3], col_devs)
    words = (found[4:5] << ROW_BIT) + (source << SOURCE_BIT) + (found[3:4] << TILE_BIT)
    out[:, :places] = words + (found[0:1] << 4) + found[1:2]
    phase = iota((bins, LANES), 1)
    edge = jnp.where(phase > 0, targets + (phase - 1) * slab_tiles, 0)
    inside = (iota((bins, LANES), 0) < edge).astype(f32).astype(bf16)
    edges = mm(sizes.astype(bf16), inside)[:1].astype(i32)
    lane = iota((1, LANES), 1)
    edges = jnp.where(lane == LANES - 2, place[0], jnp.where(lane == LANES - 1, place[1], edges))
    out[:, places:] = edges
    plan_copy = pltpu.make_async_copy(out, plan, list_sem.at[2])
    plan_copy.start()
    acc[...] = jnp.zeros_like(acc)
    for copy in copies + [plan_copy]:
        copy.wait()

    @pl.loop(0, jnp.minimum(chunks, early_chunks))
    def _(k):
        tile_copy(k).wait()

    add_products(plan, 0, 0, targets, held, panel_buf, acc)

    @pl.loop(early_chunks, chunks)
    def _(k):
        tile_copy(k).wait()


def row_of(plan):
    return plan[0, plan.shape[1] - 2]


def core_of(plan):
    return plan[0, plan.shape[1] - 1] & 1


def field(word, low, high):
    return (word >> low) & ((1 << (high - low)) - 1)


def add_products(plan, phase, first_row, spare_row, tiles, panel_buf, acc):
    phases = plan.shape[1] - LANES
    begin, end = plan[0, phases + phase], plan[0, phases + phase + 1]

    def panel(word):
        where = pl.multiple_of(field(word, TILE_BIT, SOURCE_BIT) * LANES, LANES)
        return panel_buf[field(word, SOURCE_BIT, ROW_BIT), :, pl.ds(where, LANES)]

    @pl.loop(0, (end - begin + GROUP * UNROLL - 1) // (GROUP * UNROLL))
    def _(g):
        first = begin + g * GROUP * UNROLL
        parts = []
        for u in range(UNROLL):
            words = [plan[0, first + GROUP * u + i] for i in range(GROUP)]
            left = jnp.concatenate([panel(word) for word in words], axis=1)
            right = jnp.concatenate([tiles[field(word, 0, TILE_BIT)] for word in words], axis=1)
            parts.append(mm(left, right, NT))
        for u in range(UNROLL):
            p = first + GROUP * u
            a = jnp.where(p < end, (plan[0, p] >> ROW_BIT) - first_row, spare_row)
            acc[a] += parts[u]


def load_panels(panels, panel_buf, sem):
    copies = [pltpu.make_async_copy(ref, panel_buf.at[m], sem.at[i]) for i, (m, ref) in enumerate(panels.items())]
    for copy in copies:
        copy.start()
    return copies


def collect_kernel(masks, *refs):
    panels, (_, panel_buf, sem) = refs[: len(masks)], refs[len(masks) :]
    for copy in load_panels(dict(zip(masks, panels)), panel_buf, sem):
        copy.wait()


def first_late_kernel(masks, odd, plan, *refs):
    panels = dict(zip(odd, refs))
    tiles, early, _ = refs[len(odd) : len(odd) + 3]
    sends = refs[len(odd) + 3 : -3]
    panel_buf, acc, sem = refs[-3:]
    copies = load_panels(panels, panel_buf, sem)
    for mask, send in zip(masks, sends):
        late_part(mask, plan, tiles, early, panel_buf, acc, copies)
        put(send, acc)
        copies = ()


def late_kernel(masks, plan, panel_buf, tiles, early, *refs):
    sends, acc = refs[:-1], refs[-1]
    for i, (mask, send) in enumerate(zip(masks, sends)):
        if i == 0 or mask != masks[i - 1]:
            late_part(mask, plan, tiles, early, panel_buf, acc, ())
        put(send, acc)


def own_kernel(plan, panel_buf, tiles, early, current, previous, coupling, diag, base, acc):
    late_part(0, plan, tiles, early, panel_buf, acc, ())
    put(base, acc)
    base[...] += diag[...] * current[...] - jnp.dot(
        coupling[...],
        previous[...],
        precision=lax.Precision.HIGHEST,
        preferred_element_type=jnp.float32,
    )


def late_part(mask, plan, tiles, early, panel_buf, acc, copies):
    slab_tiles = acc.shape[0] - 1
    row_devs = (early.shape[0] - 1) // slab_tiles
    first_row = (row_of(plan) ^ mask) * slab_tiles
    for s in range(slab_tiles):
        acc[s] = early[first_row + s]
    for copy in copies:
        copy.wait()
    add_products(plan, row_devs - mask, first_row, slab_tiles, tiles, panel_buf, acc)


def put(out, acc):
    for s in range(acc.shape[0] - 1):
        out[:, s * LANES : (s + 1) * LANES] = acc[s].astype(out.dtype)


def half_basis(half, current, stored):
    rows = (current.shape[0] + stored.shape[0]) // 2
    cut = rows - current.shape[0]
    return jnp.where(half == 0, jnp.concatenate([current[...], stored[:cut]], axis=0), stored[cut:])


def pack(coef, out):
    spare = -coef.shape[1] % LANES
    coef = jnp.concatenate([coef, jnp.zeros((coef.shape[0], spare), jnp.float32)], axis=1)
    for p, (q, k) in enumerate(blocks(coef.shape)):
        out[p] = coef[q : q + 8, k : k + LANES]


def unpack(pieces, width, columns):
    groups = pieces.shape[0] * 8 // width
    rows = [jnp.concatenate([pieces[p + g] for g in range(groups)], axis=1) for p in range(0, pieces.shape[0], groups)]
    return jnp.concatenate(rows, axis=0)[:, :columns]


def give_kernel(cells, received_count, relay, plan, base, *refs):
    received = refs[:received_count]
    mass, current, stored, recurrence, give = refs[received_count:]
    total = base[...]
    for i, ref in enumerate(received):
        value = ref[...].astype(jnp.float32)
        if relay and i < 3:
            inner = (row_of(plan) == 1) | (row_of(plan) == 2)
            value = jnp.where(inner if i < 2 else jnp.logical_not(inner), 0.0, value)
        total = total + value
    recurrence[...] = total
    weighted = total * (mass[...] * (1.0 / cells))
    pack(dot_split(weighted, half_basis(1 - core_of(plan), current, stored), NT), give)


def keep_kernel(cells, plan, recurrence, mass, current, stored, keep):
    weighted = recurrence[...] * (mass[...] * (1.0 / cells))
    pack(dot_split(weighted, half_basis(core_of(plan), current, stored), NT), keep)


def less_kernel(plan, mine, recurrence, current, stored, less):
    basis = half_basis(core_of(plan), current, stored)
    less[...] = recurrence[...] - dot_split(unpack(mine, recurrence.shape[0], basis.shape[0]), basis)


def turned(pieces, width, rows):
    value = unpack(pieces, width, pieces.shape[0] * 8 // width * LANES)
    spare = jnp.zeros((LANES - width, value.shape[1]), jnp.float32)
    return jnp.concatenate([value, spare], axis=0).T[:rows, :width]


def coefficient_kernel(plan, mine, other, out):
    rows = out.shape[0] // 2
    core = core_of(plan)
    own_half, other_half = turned(mine, out.shape[1], rows), turned(other, out.shape[1], rows)
    out[:rows] = jnp.where(core == 0, own_half, other_half)
    out[rows:] = jnp.where(core == 0, other_half, own_half)


def store_kernel(value, out, sem):
    copy = pltpu.make_async_copy(value, out, sem.at[0])
    copy.start()
    copy.wait()


def residual_kernel(cells, plan, other, less, mass, current, stored, residual, gram):
    width = less.shape[0]
    basis = half_basis(1 - core_of(plan), current, stored)
    value = less[...] - dot_split(unpack(other, width, basis.shape[0]), basis)
    residual[...] = value
    local = dot_split(value * (mass[...] * (1.0 / cells)), value, NT)
    half = width // 2
    gram[...] = jnp.zeros_like(gram)
    gram[:, :width] = local[:half]
    gram[:, LANES // 2 : LANES // 2 + width] = local[half:]


def after_kernel(*refs):
    pass


def after(value, *earlier):
    anywhere = pl.BlockSpec(memory_space=pl.ANY)
    return pl.pallas_call(
        after_kernel,
        out_shape=jax.ShapeDtypeStruct(value.shape, value.dtype),
        in_specs=[anywhere] * (1 + len(earlier)),
        out_specs=anywhere,
        input_output_aliases={0: 0},
        compiler_params=limit(1),
    )(value, *earlier)


def in_hbm(value):
    return pltpu.with_memory_space_constraint(value, pltpu.HBM)


def limit(mib):
    return pltpu.CompilerParams(vmem_limit_bytes=mib * MIB)


def vmem(count):
    return [pl.BlockSpec(memory_space=pltpu.VMEM)] * count


def smem(count):
    return [pl.BlockSpec(memory_space=pltpu.SMEM)] * count


def local(
    current_block,
    previous_block,
    previous_coupling,
    stored_blocks,
    stiffness_diag,
    lumped_mass,
    tile_values,
    tile_rows,
    tile_cols,
    tile_counts,
):
    row_devs = lax.axis_size("row")
    col_devs = lax.axis_size("col")
    width, slab_len = current_block.shape
    stored_count = stored_blocks.shape[0]
    slots, tile_len, _ = tile_values.shape
    slab_tiles = slab_len // tile_len
    cells = slab_len * row_devs * col_devs
    f32, bf16 = jnp.float32, jnp.bfloat16
    place = jnp.stack([lax.axis_index("row"), lax.axis_index("col")]).astype(jnp.int32)
    stored = stored_blocks.reshape(stored_count * width, slab_len)
    mass = lumped_mass.reshape(1, slab_len)
    diag = stiffness_diag.reshape(1, slab_len)
    slab = jax.ShapeDtypeStruct((width, slab_len), f32)

    targets = row_devs * slab_tiles
    anywhere = [pl.BlockSpec(memory_space=pl.ANY)]
    panel_shape = (col_devs + 1, width, slab_len)
    early_shape = (targets + 1, width, tile_len)
    part_acc = pltpu.VMEM((slab_tiles + 1, width, tile_len), f32)

    def cost(flops):
        return pl.CostEstimate(flops=flops, bytes_accessed=flops // width, transcendentals=0)

    with jax.named_scope("gather"):
        rounded = current_block.astype(bf16)
        panels = [rounded] + [None] * (col_devs - 1)
        for m in range(2, col_devs, 2):
            panels[m] = swap(rounded, "col", m)
        panels[1] = swap(rounded, "col", 1)

    with jax.named_scope("early"):
        places = -(-(slots + (GROUP - 1) * 2 * targets + GROUP * UNROLL) // LANES) * LANES
        plan_shape = (1, places + LANES)
        plan, held, early, gathered = pl.pallas_call(
            functools.partial(early_kernel, row_devs, col_devs, slab_tiles),
            out_shape=[
                pltpu.SMEM(plan_shape, jnp.int32),
                pltpu.VMEM(tile_values.shape, bf16),
                pltpu.VMEM(early_shape, f32),
                pltpu.VMEM(panel_shape, bf16),
            ],
            in_specs=smem(2) + [pl.BlockSpec(memory_space=pltpu.HBM)] * 3 + anywhere * 2,
            out_specs=smem(1) + vmem(3),
            scratch_shapes=[
                pltpu.VMEM((1, slots), jnp.int32),
                pltpu.VMEM((1, slots), jnp.int32),
                pltpu.VMEM(plan_shape, jnp.int32),
                pltpu.SemaphoreType.DMA((slots // CHUNK,)),
                pltpu.SemaphoreType.DMA((3,)),
                pltpu.SemaphoreType.DMA((2,)),
            ],
            compiler_params=limit(12),
            cost_estimate=cost(2 * slots * width * tile_len * tile_len),
        )(
            place,
            tile_counts,
            in_hbm(tile_rows.reshape(1, slots)),
            in_hbm(tile_cols.reshape(1, slots)),
            in_hbm(tile_values),
            panels[0],
            panels[1],
        )

    with jax.named_scope("gather"):
        for m in range(2, col_devs, 2):
            panels[m] = after(panels[m], early)
            panels[m + 1] = swap(panels[m], "col", 1)
        even, odd = list(range(2, col_devs, 2)), list(range(3, col_devs, 2))
        gathered = pl.pallas_call(
            functools.partial(collect_kernel, even),
            out_shape=pltpu.VMEM(panel_shape, bf16),
            in_specs=anywhere * len(even) + vmem(1),
            out_specs=vmem(1)[0],
            scratch_shapes=[pltpu.SemaphoreType.DMA((len(even),))],
            input_output_aliases={len(even): 0},
            compiler_params=limit(1),
            cost_estimate=cost(width),
        )(*[panels[m] for m in even], gathered)

    with jax.named_scope("late"):
        relay = row_devs == 4
        first_mask = 2 if relay else row_devs - 1
        masks = [3, 3, 1] if relay else list(range(row_devs - 2, 0, -1))
        part = jax.ShapeDtypeStruct((width, slab_len), bf16)
        first, gathered = pl.pallas_call(
            functools.partial(first_late_kernel, [first_mask], odd),
            out_shape=[part, pltpu.VMEM(panel_shape, bf16)],
            in_specs=smem(1) + anywhere * len(odd) + vmem(3),
            out_specs=vmem(2),
            scratch_shapes=[part_acc, pltpu.SemaphoreType.DMA((len(odd),))],
            input_output_aliases={3 + len(odd): 1},
            compiler_params=limit(8),
            cost_estimate=cost(width),
        )(plan, *[panels[m] for m in odd], held, early, gathered)
        parts = pl.pallas_call(
            functools.partial(late_kernel, masks),
            out_shape=[part, slab, part] if relay else [part] * len(masks),
            in_specs=smem(1) + vmem(3),
            out_specs=vmem(len(masks)),
            scratch_shapes=[part_acc],
            compiler_params=limit(8),
            cost_estimate=cost(width),
        )(plan, gathered, held, early)
        if relay:
            first = lax.ppermute(first, "row", [(0, 1), (3, 2), (1, 3), (2, 0)])
            joined = (parts[1] + first.astype(f32)).astype(bf16)
            received = [
                first,
                trade_rows(parts[0], [(0, 3), (3, 0)]),
                trade_rows(joined, [(1, 2), (2, 1)]),
                swap(after(parts[2], joined), "row", 1),
            ]
        else:
            received = [swap(first, "row", first_mask)]
            received += [swap(part, "row", m) for m, part in zip(masks, parts)]
        base = pl.pallas_call(
            own_kernel,
            out_shape=slab,
            in_specs=smem(1) + vmem(7),
            out_specs=vmem(1)[0],
            scratch_shapes=[part_acc],
            compiler_params=limit(8),
            cost_estimate=cost(width),
        )(plan, gathered, held, early, current_block, previous_block, previous_coupling, diag)

    basis_rows = (stored_count + 1) * width
    half = (width // 8 * -(-basis_rows // 2 // LANES), 8, LANES)
    half = jax.ShapeDtypeStruct(half, f32)
    with jax.named_scope("coefficients"):
        recurrence, give = pl.pallas_call(
            functools.partial(give_kernel, cells, len(received), relay),
            out_shape=[slab, half],
            in_specs=smem(1) + vmem(len(received) + 4),
            out_specs=vmem(2),
            compiler_params=limit(16),
            cost_estimate=cost(width),
        )(plan, base, *received, mass, current_block, stored)
        keep = pl.pallas_call(
            functools.partial(keep_kernel, cells),
            out_shape=half,
            in_specs=smem(1) + vmem(4),
            out_specs=vmem(1)[0],
            compiler_params=limit(16),
            cost_estimate=cost(width),
        )(plan, recurrence, mass, current_block, stored)
        mine = keep + swap(give, "col", 1)
        mine = total_by_core(mine)
        other = swap(mine, "col", 1)

    with jax.named_scope("residual"):
        less = pl.pallas_call(
            less_kernel,
            out_shape=slab,
            in_specs=smem(1) + vmem(4),
            out_specs=vmem(1)[0],
            compiler_params=limit(16),
            cost_estimate=cost(width),
        )(plan, mine, recurrence, current_block, stored)
        residual, gram = pl.pallas_call(
            functools.partial(residual_kernel, cells),
            out_shape=[
                pltpu.VMEM((width, slab_len), f32),
                jax.ShapeDtypeStruct((width // 2, LANES), f32),
            ],
            in_specs=smem(1) + vmem(5),
            out_specs=vmem(2),
            compiler_params=limit(16),
            cost_estimate=cost(width),
        )(plan, other, less, mass, current_block, stored)
        residual_block = pl.pallas_call(
            store_kernel,
            out_shape=slab,
            in_specs=vmem(1),
            out_specs=anywhere[0],
            scratch_shapes=[pltpu.SemaphoreType.DMA((1,))],
            compiler_params=limit(1),
            cost_estimate=cost(width),
        )(residual)
        coef = pl.pallas_call(
            coefficient_kernel,
            out_shape=jax.ShapeDtypeStruct((basis_rows, width), f32),
            in_specs=smem(1) + vmem(2),
            out_specs=vmem(1)[0],
            compiler_params=limit(4),
            cost_estimate=cost(width),
        )(plan, mine, other)
        coefficients = coef.reshape(stored_count + 1, width, width)

    with jax.named_scope("gram"):
        gram = gram + swap(gram, "col", 1)
        gram = after(total(gram, "col", 2), in_hbm(residual_block), in_hbm(coef))
        gram = total(gram, "row", 1)
        gram = jnp.concatenate(
            [gram[:, :width], gram[:, LANES // 2 : LANES // 2 + width]], axis=0
        )
    return (residual_block, coefficients, gram)


def solution(mesh):
    return jax.shard_map(
        local,
        mesh=mesh,
        in_specs=(
            P(None, ("row", "col")),
            P(None, ("row", "col")),
            P(),
            P(None, None, ("row", "col")),
            P(("row", "col")),
            P(("row", "col")),
            P(("row", "col"), None, None),
            P(("row", "col")),
            P(("row", "col")),
            P(("row", "col")),
        ),
        out_specs=(P(None, ("row", "col")), P(), P()),
        check_vma=False,
    )
```

```python
import functools

import jax
import jax.numpy as jnp
from jax import lax
from jax.experimental import pallas as pl
from jax.experimental.pallas import tpu as pltpu
from jax.sharding import PartitionSpec as P

LANES = 128
CHUNK = 32
GROUP = 2
UNROLL = 8
TILE_BIT, SOURCE_BIT, ROW_BIT = 10, 15, 20
NT = (((1,), (1,)), ((), ()))
MIB = 1 << 20


def swap(value, axis, mask):
    count = lax.axis_size(axis)
    return lax.ppermute(value, axis, [(i, i ^ mask) for i in range(count)])


def trade_rows(value, pairs):
    row_devs, col_devs = lax.axis_size("row"), lax.axis_size("col")
    to = dict(pairs)
    trades = []
    for r in range(row_devs):
        for c in range(col_devs):
            partner = to[r] * col_devs + c if r in to else r * col_devs + (c ^ 1)
            trades.append((r * col_devs + c, partner))
    return lax.ppermute(value, ("row", "col"), trades)


def tree_sum(values):
    values = [values[m] for m in sorted(values)]
    while len(values) > 1:
        values = [values[i] + values[i + 1] for i in range(0, len(values), 2)]
    return values[0]


def total(value, axis, step):
    values = {0: value}
    for m in range(lax.axis_size(axis) - step, 0, -step):
        values[m] = swap(value, axis, m)
    return tree_sum(values)


def split(value):
    high = value.astype(jnp.bfloat16)
    low = (value - high.astype(jnp.float32)).astype(jnp.bfloat16)
    return high, low


def mm(a, b, dims=(((1,), (0,)), ((), ()))):
    return lax.dot_general(a, b, dims, preferred_element_type=jnp.float32)


def dot_split(a, b, dims=(((1,), (0,)), ((), ()))):
    rows = a.shape[0]
    a_high, a_low = split(a)
    b_high, b_low = split(b)
    both = mm(jnp.concatenate([a_high, a_low], axis=0), b_high, dims)
    return both[:rows] + both[rows:] + mm(a_high, b_low, dims)


def blocks(shape):
    return [(q, k) for q in range(0, shape[0], 8) for k in range(0, shape[1], LANES)]


def early_kernel(
    row_devs,
    col_devs,
    slab_tiles,
    place,
    counts,
    rows_hbm,
    cols_hbm,
    tiles,
    own_panel,
    near_panel,
    plan,
    held,
    acc,
    panel_buf,
    rows,
    cols,
    out,
    tile_sem,
    list_sem,
    panel_sem,
):
    chunks = (counts[0] + CHUNK - 1) // CHUNK
    row_copy = pltpu.make_async_copy(rows_hbm, rows, list_sem.at[0])
    col_copy = pltpu.make_async_copy(cols_hbm, cols, list_sem.at[1])
    row_copy.start()
    col_copy.start()

    def tile_copy(k):
        window = pl.ds(k * CHUNK, CHUNK)
        return pltpu.make_async_copy(tiles.at[window], held.at[window], tile_sem.at[k])

    @pl.loop(0, chunks)
    def _(k):
        tile_copy(k).start()

    copies = load_panels({0: own_panel, 1: near_panel}, panel_buf, panel_sem)
    zero_panel = panel_buf.shape[0] - 1
    panel_buf[zero_panel, :, :LANES] = jnp.zeros((panel_buf.shape[1], LANES), jnp.bfloat16)
    f32, bf16, i32 = jnp.float32, jnp.bfloat16, jnp.int32
    slots, places = rows.shape[1], out.shape[1] - LANES
    early_chunks = 3 * slots // CHUNK // 4
    targets = row_devs * slab_tiles
    bins = 2 * targets

    def iota(shape, dim):
        return lax.broadcasted_iota(i32, shape, dim)

    slot = iota((1, slots), 1)
    occupied = slot < counts[0]
    earlier = (iota((slots, slots), 0) < iota((slots, slots), 1)).astype(f32).astype(bf16)
    row_copy.wait()
    col_copy.wait()
    row = rows[...]
    row_owner = jnp.floor(row.astype(f32) * (1.0 / slab_tiles)).astype(i32)
    col_f = cols[...].astype(f32)
    source_f = jnp.floor(col_f * (1.0 / slab_tiles))
    source = source_f.astype(i32) ^ place[1]
    tile_f = col_f - slab_tiles * source_f
    far = row_devs - 1 - (row_owner ^ place[0])
    late_bin = targets + far * slab_tiles + row - row_owner * slab_tiles
    early = (source < 2) & (slot < early_chunks * CHUNK)
    bin_of = jnp.where(occupied, jnp.where(early, row, late_bin), -1)
    member = (iota((bins, slots), 0) == bin_of).astype(f32)
    member_bf = member.astype(bf16)
    rank = jnp.sum(member * mm(member_bf, earlier), axis=0, keepdims=True)
    sizes = mm(jnp.ones((8, slots), bf16), member_bf, NT)
    sizes = GROUP * jnp.floor((sizes + (GROUP - 1.0)) * (1.0 / GROUP))
    before = (iota((bins, bins), 1) < iota((bins, bins), 0)).astype(f32)
    begin = jnp.sum(before * sizes[:1], axis=1, keepdims=True)
    position = jnp.sum(member * begin, axis=0, keepdims=True) + rank
    position = jnp.where(occupied, position.astype(i32), -1)
    chosen = (iota((places, slots), 0) == position).astype(f32).astype(bf16)
    slot_f = slot.astype(f32)
    slot_high = jnp.floor(slot_f * (1.0 / 16.0))
    facts = [slot_high, slot_f - 16.0 * slot_high, source.astype(f32), tile_f, row.astype(f32), jnp.ones((1, slots), f32)]
    facts = jnp.concatenate(facts + [jnp.zeros((2, slots), f32)], axis=0).astype(bf16)
    found = mm(facts, chosen, NT).astype(i32)
    source = jnp.where(found[5:6] > 0, found[2:3], col_devs)
    words = (found[4:5] << ROW_BIT) + (source << SOURCE_BIT) + (found[3:4] << TILE_BIT)
    out[:, :places] = words + (found[0:1] << 4) + found[1:2]
    phase = iota((bins, LANES), 1)
    edge = jnp.where(phase > 0, targets + (phase - 1) * slab_tiles, 0)
    inside = (iota((bins, LANES), 0) < edge).astype(f32).astype(bf16)
    edges = mm(sizes.astype(bf16), inside)[:1].astype(i32)
    lane = iota((1, LANES), 1)
    edges = jnp.where(lane == LANES - 2, place[0], jnp.where(lane == LANES - 1, place[1], edges))
    out[:, places:] = edges
    plan_copy = pltpu.make_async_copy(out, plan, list_sem.at[2])
    plan_copy.start()
    acc[...] = jnp.zeros_like(acc)
    for copy in copies + [plan_copy]:
        copy.wait()

    @pl.loop(0, jnp.minimum(chunks, early_chunks))
    def _(k):
        tile_copy(k).wait()

    add_products(plan, 0, 0, targets, held, panel_buf, acc)

    @pl.loop(early_chunks, chunks)
    def _(k):
        tile_copy(k).wait()


def row_of(plan):
    return plan[0, plan.shape[1] - 2]


def core_of(plan):
    return plan[0, plan.shape[1] - 1] & 1


def field(word, low, high):
    return (word >> low) & ((1 << (high - low)) - 1)


def add_products(plan, phase, first_row, spare_row, tiles, panel_buf, acc):
    phases = plan.shape[1] - LANES
    begin, end = plan[0, phases + phase], plan[0, phases + phase + 1]

    def panel(word):
        where = pl.multiple_of(field(word, TILE_BIT, SOURCE_BIT) * LANES, LANES)
        return panel_buf[field(word, SOURCE_BIT, ROW_BIT), :, pl.ds(where, LANES)]

    @pl.loop(0, (end - begin + GROUP * UNROLL - 1) // (GROUP * UNROLL))
    def _(g):
        first = begin + g * GROUP * UNROLL
        parts = []
        for u in range(UNROLL):
            words = [plan[0, first + GROUP * u + i] for i in range(GROUP)]
            left = jnp.concatenate([panel(word) for word in words], axis=1)
            right = jnp.concatenate([tiles[field(word, 0, TILE_BIT)] for word in words], axis=1)
            parts.append(mm(left, right, NT))
        for u in range(UNROLL):
            p = first + GROUP * u
            a = jnp.where(p < end, (plan[0, p] >> ROW_BIT) - first_row, spare_row)
            acc[a] += parts[u]


def load_panels(panels, panel_buf, sem):
    copies = [pltpu.make_async_copy(ref, panel_buf.at[m], sem.at[i]) for i, (m, ref) in enumerate(panels.items())]
    for copy in copies:
        copy.start()
    return copies


def collect_kernel(masks, *refs):
    panels, (_, panel_buf, sem) = refs[: len(masks)], refs[len(masks) :]
    for copy in load_panels(dict(zip(masks, panels)), panel_buf, sem):
        copy.wait()


def first_late_kernel(masks, odd, plan, *refs):
    panels = dict(zip(odd, refs))
    tiles, early, _ = refs[len(odd) : len(odd) + 3]
    sends = refs[len(odd) + 3 : -3]
    panel_buf, acc, sem = refs[-3:]
    copies = load_panels(panels, panel_buf, sem)
    for mask, send in zip(masks, sends):
        late_part(mask, plan, tiles, early, panel_buf, acc, copies)
        put(send, acc)
        copies = ()


def late_kernel(masks, plan, panel_buf, tiles, early, *refs):
    sends, acc = refs[:-1], refs[-1]
    for i, (mask, send) in enumerate(zip(masks, sends)):
        if i == 0 or mask != masks[i - 1]:
            late_part(mask, plan, tiles, early, panel_buf, acc, ())
        put(send, acc)


def own_kernel(plan, panel_buf, tiles, early, current, previous, coupling, diag, base, acc):
    late_part(0, plan, tiles, early, panel_buf, acc, ())
    put(base, acc)
    base[...] += diag[...] * current[...] - jnp.dot(
        coupling[...],
        previous[...],
        precision=lax.Precision.HIGHEST,
        preferred_element_type=jnp.float32,
    )


def late_part(mask, plan, tiles, early, panel_buf, acc, copies):
    slab_tiles = acc.shape[0] - 1
    row_devs = (early.shape[0] - 1) // slab_tiles
    first_row = (row_of(plan) ^ mask) * slab_tiles
    for s in range(slab_tiles):
        acc[s] = early[first_row + s]
    for copy in copies:
        copy.wait()
    add_products(plan, row_devs - mask, first_row, slab_tiles, tiles, panel_buf, acc)


def put(out, acc):
    for s in range(acc.shape[0] - 1):
        out[:, s * LANES : (s + 1) * LANES] = acc[s].astype(out.dtype)


def half_basis(half, current, stored):
    rows = (current.shape[0] + stored.shape[0]) // 2
    cut = rows - current.shape[0]
    return jnp.where(half == 0, jnp.concatenate([current[...], stored[:cut]], axis=0), stored[cut:])


def pack(coef, out):
    spare = -coef.shape[1] % LANES
    coef = jnp.concatenate([coef, jnp.zeros((coef.shape[0], spare), jnp.float32)], axis=1)
    for p, (q, k) in enumerate(blocks(coef.shape)):
        out[p] = coef[q : q + 8, k : k + LANES]


def unpack(pieces, width, columns):
    groups = pieces.shape[0] * 8 // width
    rows = [jnp.concatenate([pieces[p + g] for g in range(groups)], axis=1) for p in range(0, pieces.shape[0], groups)]
    return jnp.concatenate(rows, axis=0)[:, :columns]


def give_kernel(cells, received_count, relay, plan, base, *refs):
    received = refs[:received_count]
    mass, current, stored, recurrence, give = refs[received_count:]
    total = base[...]
    for i, ref in enumerate(received):
        value = ref[...].astype(jnp.float32)
        if relay and i < 3:
            inner = (row_of(plan) == 1) | (row_of(plan) == 2)
            value = jnp.where(inner if i < 2 else jnp.logical_not(inner), 0.0, value)
        total = total + value
    recurrence[...] = total
    weighted = total * (mass[...] * (1.0 / cells))
    pack(dot_split(weighted, half_basis(1 - core_of(plan), current, stored), NT), give)


def keep_kernel(cells, plan, recurrence, mass, current, stored, keep):
    weighted = recurrence[...] * (mass[...] * (1.0 / cells))
    pack(dot_split(weighted, half_basis(core_of(plan), current, stored), NT), keep)


def less_kernel(plan, mine, recurrence, current, stored, less):
    basis = half_basis(core_of(plan), current, stored)
    less[...] = recurrence[...] - dot_split(unpack(mine, recurrence.shape[0], basis.shape[0]), basis)


def turned(pieces, width, rows):
    value = unpack(pieces, width, pieces.shape[0] * 8 // width * LANES)
    spare = jnp.zeros((LANES - width, value.shape[1]), jnp.float32)
    return jnp.concatenate([value, spare], axis=0).T[:rows, :width]


def coefficient_kernel(plan, mine, other, out):
    rows = out.shape[0] // 2
    core = core_of(plan)
    own_half, other_half = turned(mine, out.shape[1], rows), turned(other, out.shape[1], rows)
    out[:rows] = jnp.where(core == 0, own_half, other_half)
    out[rows:] = jnp.where(core == 0, other_half, own_half)


def store_kernel(value, out, sem):
    copy = pltpu.make_async_copy(value, out, sem.at[0])
    copy.start()
    copy.wait()


def residual_kernel(cells, plan, other, less, mass, current, stored, residual, gram):
    width = less.shape[0]
    basis = half_basis(1 - core_of(plan), current, stored)
    value = less[...] - dot_split(unpack(other, width, basis.shape[0]), basis)
    residual[...] = value
    local = dot_split(value * (mass[...] * (1.0 / cells)), value, NT)
    half = width // 2
    gram[...] = jnp.zeros_like(gram)
    gram[:, :width] = local[:half]
    gram[:, LANES // 2 : LANES // 2 + width] = local[half:]


def after_kernel(*refs):
    pass


def after(value, *earlier):
    anywhere = pl.BlockSpec(memory_space=pl.ANY)
    return pl.pallas_call(
        after_kernel,
        out_shape=jax.ShapeDtypeStruct(value.shape, value.dtype),
        in_specs=[anywhere] * (1 + len(earlier)),
        out_specs=anywhere,
        input_output_aliases={0: 0},
        compiler_params=limit(1),
    )(value, *earlier)


def in_hbm(value):
    return pltpu.with_memory_space_constraint(value, pltpu.HBM)


def limit(mib):
    return pltpu.CompilerParams(vmem_limit_bytes=mib * MIB)


def vmem(count):
    return [pl.BlockSpec(memory_space=pltpu.VMEM)] * count


def smem(count):
    return [pl.BlockSpec(memory_space=pltpu.SMEM)] * count


def local(
    current_block,
    previous_block,
    previous_coupling,
    stored_blocks,
    stiffness_diag,
    lumped_mass,
    tile_values,
    tile_rows,
    tile_cols,
    tile_counts,
):
    row_devs = lax.axis_size("row")
    col_devs = lax.axis_size("col")
    width, slab_len = current_block.shape
    stored_count = stored_blocks.shape[0]
    slots, tile_len, _ = tile_values.shape
    slab_tiles = slab_len // tile_len
    cells = slab_len * row_devs * col_devs
    f32, bf16 = jnp.float32, jnp.bfloat16
    place = jnp.stack([lax.axis_index("row"), lax.axis_index("col")]).astype(jnp.int32)
    stored = stored_blocks.reshape(stored_count * width, slab_len)
    mass = lumped_mass.reshape(1, slab_len)
    diag = stiffness_diag.reshape(1, slab_len)
    slab = jax.ShapeDtypeStruct((width, slab_len), f32)

    targets = row_devs * slab_tiles
    anywhere = [pl.BlockSpec(memory_space=pl.ANY)]
    panel_shape = (col_devs + 1, width, slab_len)
    early_shape = (targets + 1, width, tile_len)
    part_acc = pltpu.VMEM((slab_tiles + 1, width, tile_len), f32)

    def cost(flops):
        return pl.CostEstimate(flops=flops, bytes_accessed=flops // width, transcendentals=0)

    with jax.named_scope("gather"):
        rounded = current_block.astype(bf16)
        panels = [rounded] + [None] * (col_devs - 1)
        for m in range(2, col_devs, 2):
            panels[m] = swap(rounded, "col", m)
        panels[1] = swap(rounded, "col", 1)

    with jax.named_scope("early"):
        places = -(-(slots + (GROUP - 1) * 2 * targets + GROUP * UNROLL) // LANES) * LANES
        plan_shape = (1, places + LANES)
        plan, held, early, gathered = pl.pallas_call(
            functools.partial(early_kernel, row_devs, col_devs, slab_tiles),
            out_shape=[
                pltpu.SMEM(plan_shape, jnp.int32),
                pltpu.VMEM(tile_values.shape, bf16),
                pltpu.VMEM(early_shape, f32),
                pltpu.VMEM(panel_shape, bf16),
            ],
            in_specs=smem(2) + [pl.BlockSpec(memory_space=pltpu.HBM)] * 3 + anywhere * 2,
            out_specs=smem(1) + vmem(3),
            scratch_shapes=[
                pltpu.VMEM((1, slots), jnp.int32),
                pltpu.VMEM((1, slots), jnp.int32),
                pltpu.VMEM(plan_shape, jnp.int32),
                pltpu.SemaphoreType.DMA((slots // CHUNK,)),
                pltpu.SemaphoreType.DMA((3,)),
                pltpu.SemaphoreType.DMA((2,)),
            ],
            compiler_params=limit(12),
            cost_estimate=cost(2 * slots * width * tile_len * tile_len),
        )(
            place,
            tile_counts,
            in_hbm(tile_rows.reshape(1, slots)),
            in_hbm(tile_cols.reshape(1, slots)),
            in_hbm(tile_values),
            panels[0],
            panels[1],
        )

    with jax.named_scope("gather"):
        for m in range(2, col_devs, 2):
            panels[m] = after(panels[m], early)
            panels[m + 1] = swap(panels[m], "col", 1)
        even, odd = list(range(2, col_devs, 2)), list(range(3, col_devs, 2))
        gathered = pl.pallas_call(
            functools.partial(collect_kernel, even),
            out_shape=pltpu.VMEM(panel_shape, bf16),
            in_specs=anywhere * len(even) + vmem(1),
            out_specs=vmem(1)[0],
            scratch_shapes=[pltpu.SemaphoreType.DMA((len(even),))],
            input_output_aliases={len(even): 0},
            compiler_params=limit(1),
            cost_estimate=cost(width),
        )(*[panels[m] for m in even], gathered)

    with jax.named_scope("late"):
        relay = row_devs == 4
        first_mask = 2 if relay else row_devs - 1
        masks = [3, 3, 1] if relay else list(range(row_devs - 2, 0, -1))
        part = jax.ShapeDtypeStruct((width, slab_len), bf16)
        first, gathered = pl.pallas_call(
            functools.partial(first_late_kernel, [first_mask], odd),
            out_shape=[part, pltpu.VMEM(panel_shape, bf16)],
            in_specs=smem(1) + anywhere * len(odd) + vmem(3),
            out_specs=vmem(2),
            scratch_shapes=[part_acc, pltpu.SemaphoreType.DMA((len(odd),))],
            input_output_aliases={3 + len(odd): 1},
            compiler_params=limit(8),
            cost_estimate=cost(width),
        )(plan, *[panels[m] for m in odd], held, early, gathered)
        parts = pl.pallas_call(
            functools.partial(late_kernel, masks),
            out_shape=[part, slab, part] if relay else [part] * len(masks),
            in_specs=smem(1) + vmem(3),
            out_specs=vmem(len(masks)),
            scratch_shapes=[part_acc],
            compiler_params=limit(8),
            cost_estimate=cost(width),
        )(plan, gathered, held, early)
        if relay:
            first = lax.ppermute(first, "row", [(0, 1), (3, 2), (1, 3), (2, 0)])
            joined = (parts[1] + first.astype(f32)).astype(bf16)
            received = [
                first,
                trade_rows(parts[0], [(0, 3), (3, 0)]),
                trade_rows(joined, [(1, 2), (2, 1)]),
                swap(parts[2], "row", 1),
            ]
        else:
            received = [swap(first, "row", first_mask)]
            received += [swap(part, "row", m) for m, part in zip(masks, parts)]
        base = pl.pallas_call(
            own_kernel,
            out_shape=slab,
            in_specs=smem(1) + vmem(7),
            out_specs=vmem(1)[0],
            scratch_shapes=[part_acc],
            compiler_params=limit(8),
            cost_estimate=cost(width),
        )(plan, gathered, held, early, current_block, previous_block, previous_coupling, diag)

    basis_rows = (stored_count + 1) * width
    half = (width // 8 * -(-basis_rows // 2 // LANES), 8, LANES)
    half = jax.ShapeDtypeStruct(half, f32)
    with jax.named_scope("coefficients"):
        recurrence, give = pl.pallas_call(
            functools.partial(give_kernel, cells, len(received), relay),
            out_shape=[slab, half],
            in_specs=smem(1) + vmem(len(received) + 4),
            out_specs=vmem(2),
            compiler_params=limit(16),
            cost_estimate=cost(width),
        )(plan, base, *received, mass, current_block, stored)
        keep = pl.pallas_call(
            functools.partial(keep_kernel, cells),
            out_shape=half,
            in_specs=smem(1) + vmem(4),
            out_specs=vmem(1)[0],
            compiler_params=limit(16),
            cost_estimate=cost(width),
        )(plan, recurrence, mass, current_block, stored)
        mine = keep + swap(give, "col", 1)
        mine = total(total(mine, "col", 2), "row", 1)
        other = swap(mine, "col", 1)

    with jax.named_scope("residual"):
        less = pl.pallas_call(
            less_kernel,
            out_shape=slab,
            in_specs=smem(1) + vmem(4),
            out_specs=vmem(1)[0],
            compiler_params=limit(16),
            cost_estimate=cost(width),
        )(plan, mine, recurrence, current_block, stored)
        residual, gram = pl.pallas_call(
            functools.partial(residual_kernel, cells),
            out_shape=[
                pltpu.VMEM((width, slab_len), f32),
                jax.ShapeDtypeStruct((width // 2, LANES), f32),
            ],
            in_specs=smem(1) + vmem(5),
            out_specs=vmem(2),
            compiler_params=limit(16),
            cost_estimate=cost(width),
        )(plan, other, less, mass, current_block, stored)
        residual_block = pl.pallas_call(
            store_kernel,
            out_shape=slab,
            in_specs=vmem(1),
            out_specs=anywhere[0],
            scratch_shapes=[pltpu.SemaphoreType.DMA((1,))],
            compiler_params=limit(1),
            cost_estimate=cost(width),
        )(residual)
        coef = pl.pallas_call(
            coefficient_kernel,
            out_shape=jax.ShapeDtypeStruct((basis_rows, width), f32),
            in_specs=smem(1) + vmem(2),
            out_specs=vmem(1)[0],
            compiler_params=limit(4),
            cost_estimate=cost(width),
        )(plan, mine, other)
        coefficients = coef.reshape(stored_count + 1, width, width)

    with jax.named_scope("gram"):
        gram = gram + swap(gram, "col", 1)
        gram = after(total(gram, "col", 2), in_hbm(residual_block), in_hbm(coef))
        gram = total(gram, "row", 1)
        gram = jnp.concatenate(
            [gram[:, :width], gram[:, LANES // 2 : LANES // 2 + width]], axis=0
        )
    return (residual_block, coefficients, gram)


def solution(mesh):
    return jax.shard_map(
        local,
        mesh=mesh,
        in_specs=(
            P(None, ("row", "col")),
            P(None, ("row", "col")),
            P(),
            P(None, None, ("row", "col")),
            P(("row", "col")),
            P(("row", "col")),
            P(("row", "col"), None, None),
            P(("row", "col")),
            P(("row", "col")),
            P(("row", "col")),
        ),
        out_specs=(P(None, ("row", "col")), P(), P()),
        check_vma=False,
    )
```

```python
import functools

import jax
import jax.numpy as jnp
from jax import lax
from jax.experimental import pallas as pl
from jax.experimental.pallas import tpu as pltpu
from jax.sharding import PartitionSpec as P

LANES = 128
CHUNK = 32
GROUP = 2
UNROLL = 8
TILE_BIT, SOURCE_BIT, ROW_BIT = 10, 15, 20
NT = (((1,), (1,)), ((), ()))
MIB = 1 << 20


def swap(value, axis, mask):
    count = lax.axis_size(axis)
    return lax.ppermute(value, axis, [(i, i ^ mask) for i in range(count)])


def trade_rows(value, pairs):
    row_devs, col_devs = lax.axis_size("row"), lax.axis_size("col")
    to = dict(pairs)
    trades = []
    for r in range(row_devs):
        for c in range(col_devs):
            partner = to[r] * col_devs + c if r in to else r * col_devs + (c ^ 1)
            trades.append((r * col_devs + c, partner))
    return lax.ppermute(value, ("row", "col"), trades)


def tree_sum(values):
    values = [values[m] for m in sorted(values)]
    while len(values) > 1:
        values = [values[i] + values[i + 1] for i in range(0, len(values), 2)]
    return values[0]


def total(value, axis, step):
    values = {0: value}
    for m in range(lax.axis_size(axis) - step, 0, -step):
        values[m] = swap(value, axis, m)
    return tree_sum(values)


def split(value):
    high = value.astype(jnp.bfloat16)
    low = (value - high.astype(jnp.float32)).astype(jnp.bfloat16)
    return high, low


def mm(a, b, dims=(((1,), (0,)), ((), ()))):
    return lax.dot_general(a, b, dims, preferred_element_type=jnp.float32)


def dot_split(a, b, dims=(((1,), (0,)), ((), ()))):
    rows = a.shape[0]
    a_high, a_low = split(a)
    b_high, b_low = split(b)
    both = mm(jnp.concatenate([a_high, a_low], axis=0), b_high, dims)
    return both[:rows] + both[rows:] + mm(a_high, b_low, dims)


def blocks(shape):
    return [(q, k) for q in range(0, shape[0], 8) for k in range(0, shape[1], LANES)]


def early_kernel(
    row_devs,
    col_devs,
    slab_tiles,
    place,
    counts,
    rows_hbm,
    cols_hbm,
    tiles,
    own_panel,
    near_panel,
    plan,
    held,
    acc,
    panel_buf,
    rows,
    cols,
    out,
    tile_sem,
    list_sem,
    panel_sem,
):
    chunks = (counts[0] + CHUNK - 1) // CHUNK
    row_copy = pltpu.make_async_copy(rows_hbm, rows, list_sem.at[0])
    col_copy = pltpu.make_async_copy(cols_hbm, cols, list_sem.at[1])
    row_copy.start()
    col_copy.start()

    def tile_copy(k):
        window = pl.ds(k * CHUNK, CHUNK)
        return pltpu.make_async_copy(tiles.at[window], held.at[window], tile_sem.at[k])

    @pl.loop(0, chunks)
    def _(k):
        tile_copy(k).start()

    copies = load_panels({0: own_panel, 1: near_panel}, panel_buf, panel_sem)
    zero_panel = panel_buf.shape[0] - 1
    panel_buf[zero_panel, :, :LANES] = jnp.zeros((panel_buf.shape[1], LANES), jnp.bfloat16)
    f32, bf16, i32 = jnp.float32, jnp.bfloat16, jnp.int32
    slots, places = rows.shape[1], out.shape[1] - LANES
    early_chunks = 3 * slots // CHUNK // 4
    targets = row_devs * slab_tiles
    bins = 2 * targets

    def iota(shape, dim):
        return lax.broadcasted_iota(i32, shape, dim)

    slot = iota((1, slots), 1)
    occupied = slot < counts[0]
    earlier = (iota((slots, slots), 0) < iota((slots, slots), 1)).astype(f32).astype(bf16)
    row_copy.wait()
    col_copy.wait()
    row = rows[...]
    row_owner = jnp.floor(row.astype(f32) * (1.0 / slab_tiles)).astype(i32)
    col_f = cols[...].astype(f32)
    source_f = jnp.floor(col_f * (1.0 / slab_tiles))
    source = source_f.astype(i32) ^ place[1]
    tile_f = col_f - slab_tiles * source_f
    far = row_devs - 1 - (row_owner ^ place[0])
    late_bin = targets + far * slab_tiles + row - row_owner * slab_tiles
    early = (source < 2) & (slot < early_chunks * CHUNK)
    bin_of = jnp.where(occupied, jnp.where(early, row, late_bin), -1)
    member = (iota((bins, slots), 0) == bin_of).astype(f32)
    member_bf = member.astype(bf16)
    rank = jnp.sum(member * mm(member_bf, earlier), axis=0, keepdims=True)
    sizes = mm(jnp.ones((8, slots), bf16), member_bf, NT)
    sizes = GROUP * jnp.floor((sizes + (GROUP - 1.0)) * (1.0 / GROUP))
    before = (iota((bins, bins), 1) < iota((bins, bins), 0)).astype(f32)
    begin = jnp.sum(before * sizes[:1], axis=1, keepdims=True)
    position = jnp.sum(member * begin, axis=0, keepdims=True) + rank
    position = jnp.where(occupied, position.astype(i32), -1)
    chosen = (iota((places, slots), 0) == position).astype(f32).astype(bf16)
    slot_f = slot.astype(f32)
    slot_high = jnp.floor(slot_f * (1.0 / 16.0))
    facts = [slot_high, slot_f - 16.0 * slot_high, source.astype(f32), tile_f, row.astype(f32), jnp.ones((1, slots), f32)]
    facts = jnp.concatenate(facts + [jnp.zeros((2, slots), f32)], axis=0).astype(bf16)
    found = mm(facts, chosen, NT).astype(i32)
    source = jnp.where(found[5:6] > 0, found[2:3], col_devs)
    words = (found[4:5] << ROW_BIT) + (source << SOURCE_BIT) + (found[3:4] << TILE_BIT)
    out[:, :places] = words + (found[0:1] << 4) + found[1:2]
    phase = iota((bins, LANES), 1)
    edge = jnp.where(phase > 0, targets + (phase - 1) * slab_tiles, 0)
    inside = (iota((bins, LANES), 0) < edge).astype(f32).astype(bf16)
    edges = mm(sizes.astype(bf16), inside)[:1].astype(i32)
    lane = iota((1, LANES), 1)
    edges = jnp.where(lane == LANES - 2, place[0], jnp.where(lane == LANES - 1, place[1], edges))
    out[:, places:] = edges
    plan_copy = pltpu.make_async_copy(out, plan, list_sem.at[2])
    plan_copy.start()
    acc[...] = jnp.zeros_like(acc)
    for copy in copies + [plan_copy]:
        copy.wait()

    @pl.loop(0, jnp.minimum(chunks, early_chunks))
    def _(k):
        tile_copy(k).wait()

    add_products(plan, 0, 0, targets, held, panel_buf, acc)

    @pl.loop(early_chunks, chunks)
    def _(k):
        tile_copy(k).wait()


def row_of(plan):
    return plan[0, plan.shape[1] - 2]


def core_of(plan):
    return plan[0, plan.shape[1] - 1] & 1


def field(word, low, high):
    return (word >> low) & ((1 << (high - low)) - 1)


def add_products(plan, phase, first_row, spare_row, tiles, panel_buf, acc):
    phases = plan.shape[1] - LANES
    begin, end = plan[0, phases + phase], plan[0, phases + phase + 1]

    def panel(word):
        where = pl.multiple_of(field(word, TILE_BIT, SOURCE_BIT) * LANES, LANES)
        return panel_buf[field(word, SOURCE_BIT, ROW_BIT), :, pl.ds(where, LANES)]

    @pl.loop(0, (end - begin + GROUP * UNROLL - 1) // (GROUP * UNROLL))
    def _(g):
        first = begin + g * GROUP * UNROLL
        parts = []
        for u in range(UNROLL):
            words = [plan[0, first + GROUP * u + i] for i in range(GROUP)]
            left = jnp.concatenate([panel(word) for word in words], axis=1)
            right = jnp.concatenate([tiles[field(word, 0, TILE_BIT)] for word in words], axis=1)
            parts.append(mm(left, right, NT))
        for u in range(UNROLL):
            p = first + GROUP * u
            a = jnp.where(p < end, (plan[0, p] >> ROW_BIT) - first_row, spare_row)
            acc[a] += parts[u]


def load_panels(panels, panel_buf, sem):
    copies = [pltpu.make_async_copy(ref, panel_buf.at[m], sem.at[i]) for i, (m, ref) in enumerate(panels.items())]
    for copy in copies:
        copy.start()
    return copies


def collect_kernel(masks, *refs):
    panels, (_, panel_buf, sem) = refs[: len(masks)], refs[len(masks) :]
    for copy in load_panels(dict(zip(masks, panels)), panel_buf, sem):
        copy.wait()


def first_late_kernel(masks, odd, plan, *refs):
    panels = dict(zip(odd, refs))
    tiles, early, _ = refs[len(odd) : len(odd) + 3]
    sends = refs[len(odd) + 3 : -3]
    panel_buf, acc, sem = refs[-3:]
    copies = load_panels(panels, panel_buf, sem)
    for mask, send in zip(masks, sends):
        late_part(mask, plan, tiles, early, panel_buf, acc, copies)
        put(send, acc)
        copies = ()


def late_kernel(masks, plan, panel_buf, tiles, early, *refs):
    sends, acc = refs[:-1], refs[-1]
    for i, (mask, send) in enumerate(zip(masks, sends)):
        if i == 0 or mask != masks[i - 1]:
            late_part(mask, plan, tiles, early, panel_buf, acc, ())
        put(send, acc)


def own_kernel(plan, panel_buf, tiles, early, current, previous, coupling, diag, base, acc):
    late_part(0, plan, tiles, early, panel_buf, acc, ())
    put(base, acc)
    base[...] += diag[...] * current[...] - jnp.dot(
        coupling[...],
        previous[...],
        precision=lax.Precision.HIGHEST,
        preferred_element_type=jnp.float32,
    )


def late_part(mask, plan, tiles, early, panel_buf, acc, copies):
    slab_tiles = acc.shape[0] - 1
    row_devs = (early.shape[0] - 1) // slab_tiles
    first_row = (row_of(plan) ^ mask) * slab_tiles
    for s in range(slab_tiles):
        acc[s] = early[first_row + s]
    for copy in copies:
        copy.wait()
    add_products(plan, row_devs - mask, first_row, slab_tiles, tiles, panel_buf, acc)


def put(out, acc):
    for s in range(acc.shape[0] - 1):
        out[:, s * LANES : (s + 1) * LANES] = acc[s].astype(out.dtype)


def half_basis(half, current, stored):
    rows = (current.shape[0] + stored.shape[0]) // 2
    cut = rows - current.shape[0]
    return jnp.where(half == 0, jnp.concatenate([current[...], stored[:cut]], axis=0), stored[cut:])


def pack(coef, out):
    spare = -coef.shape[1] % LANES
    coef = jnp.concatenate([coef, jnp.zeros((coef.shape[0], spare), jnp.float32)], axis=1)
    for p, (q, k) in enumerate(blocks(coef.shape)):
        out[p] = coef[q : q + 8, k : k + LANES]


def unpack(pieces, width, columns):
    groups = pieces.shape[0] * 8 // width
    rows = [jnp.concatenate([pieces[p + g] for g in range(groups)], axis=1) for p in range(0, pieces.shape[0], groups)]
    return jnp.concatenate(rows, axis=0)[:, :columns]


def give_kernel(cells, received_count, relay, plan, base, *refs):
    received = refs[:received_count]
    mass, current, stored, recurrence, give = refs[received_count:]
    total = base[...]
    for i, ref in enumerate(received):
        value = ref[...].astype(jnp.float32)
        if relay and i != 1:
            inner = (row_of(plan) == 1) | (row_of(plan) == 2)
            value = jnp.where(jnp.logical_not(inner) if i == 2 else inner, 0.0, value)
        total = total + value
    recurrence[...] = total
    weighted = total * (mass[...] * (1.0 / cells))
    pack(dot_split(weighted, half_basis(1 - core_of(plan), current, stored), NT), give)


def keep_kernel(cells, plan, recurrence, mass, current, stored, keep):
    weighted = recurrence[...] * (mass[...] * (1.0 / cells))
    pack(dot_split(weighted, half_basis(core_of(plan), current, stored), NT), keep)


def less_kernel(plan, mine, recurrence, current, stored, less):
    basis = half_basis(core_of(plan), current, stored)
    less[...] = recurrence[...] - dot_split(unpack(mine, recurrence.shape[0], basis.shape[0]), basis)


def turned(pieces, width, rows):
    value = unpack(pieces, width, pieces.shape[0] * 8 // width * LANES)
    spare = jnp.zeros((LANES - width, value.shape[1]), jnp.float32)
    return jnp.concatenate([value, spare], axis=0).T[:rows, :width]


def coefficient_kernel(plan, mine, other, out):
    rows = out.shape[0] // 2
    core = core_of(plan)
    own_half, other_half = turned(mine, out.shape[1], rows), turned(other, out.shape[1], rows)
    out[:rows] = jnp.where(core == 0, own_half, other_half)
    out[rows:] = jnp.where(core == 0, other_half, own_half)


def store_kernel(value, out, sem):
    copy = pltpu.make_async_copy(value, out, sem.at[0])
    copy.start()
    copy.wait()


def residual_kernel(cells, plan, other, less, mass, current, stored, residual, gram):
    width = less.shape[0]
    basis = half_basis(1 - core_of(plan), current, stored)
    value = less[...] - dot_split(unpack(other, width, basis.shape[0]), basis)
    residual[...] = value
    local = dot_split(value * (mass[...] * (1.0 / cells)), value, NT)
    half = width // 2
    gram[...] = jnp.zeros_like(gram)
    gram[:, :width] = local[:half]
    gram[:, LANES // 2 : LANES // 2 + width] = local[half:]


def after_kernel(*refs):
    pass


def after(value, *earlier):
    anywhere = pl.BlockSpec(memory_space=pl.ANY)
    return pl.pallas_call(
        after_kernel,
        out_shape=jax.ShapeDtypeStruct(value.shape, value.dtype),
        in_specs=[anywhere] * (1 + len(earlier)),
        out_specs=anywhere,
        input_output_aliases={0: 0},
        compiler_params=limit(1),
    )(value, *earlier)


def in_hbm(value):
    return pltpu.with_memory_space_constraint(value, pltpu.HBM)


def limit(mib):
    return pltpu.CompilerParams(vmem_limit_bytes=mib * MIB)


def vmem(count):
    return [pl.BlockSpec(memory_space=pltpu.VMEM)] * count


def smem(count):
    return [pl.BlockSpec(memory_space=pltpu.SMEM)] * count


def local(
    current_block,
    previous_block,
    previous_coupling,
    stored_blocks,
    stiffness_diag,
    lumped_mass,
    tile_values,
    tile_rows,
    tile_cols,
    tile_counts,
):
    row_devs = lax.axis_size("row")
    col_devs = lax.axis_size("col")
    width, slab_len = current_block.shape
    stored_count = stored_blocks.shape[0]
    slots, tile_len, _ = tile_values.shape
    slab_tiles = slab_len // tile_len
    cells = slab_len * row_devs * col_devs
    f32, bf16 = jnp.float32, jnp.bfloat16
    place = jnp.stack([lax.axis_index("row"), lax.axis_index("col")]).astype(jnp.int32)
    stored = stored_blocks.reshape(stored_count * width, slab_len)
    mass = lumped_mass.reshape(1, slab_len)
    diag = stiffness_diag.reshape(1, slab_len)
    slab = jax.ShapeDtypeStruct((width, slab_len), f32)

    targets = row_devs * slab_tiles
    anywhere = [pl.BlockSpec(memory_space=pl.ANY)]
    panel_shape = (col_devs + 1, width, slab_len)
    early_shape = (targets + 1, width, tile_len)
    part_acc = pltpu.VMEM((slab_tiles + 1, width, tile_len), f32)

    def cost(flops):
        return pl.CostEstimate(flops=flops, bytes_accessed=flops // width, transcendentals=0)

    with jax.named_scope("gather"):
        rounded = current_block.astype(bf16)
        panels = [rounded] + [None] * (col_devs - 1)
        for m in range(2, col_devs, 2):
            panels[m] = swap(rounded, "col", m)
        panels[1] = swap(rounded, "col", 1)

    with jax.named_scope("early"):
        places = -(-(slots + (GROUP - 1) * 2 * targets + GROUP * UNROLL) // LANES) * LANES
        plan_shape = (1, places + LANES)
        plan, held, early, gathered = pl.pallas_call(
            functools.partial(early_kernel, row_devs, col_devs, slab_tiles),
            out_shape=[
                pltpu.SMEM(plan_shape, jnp.int32),
                pltpu.VMEM(tile_values.shape, bf16),
                pltpu.VMEM(early_shape, f32),
                pltpu.VMEM(panel_shape, bf16),
            ],
            in_specs=smem(2) + [pl.BlockSpec(memory_space=pltpu.HBM)] * 3 + anywhere * 2,
            out_specs=smem(1) + vmem(3),
            scratch_shapes=[
                pltpu.VMEM((1, slots), jnp.int32),
                pltpu.VMEM((1, slots), jnp.int32),
                pltpu.VMEM(plan_shape, jnp.int32),
                pltpu.SemaphoreType.DMA((slots // CHUNK,)),
                pltpu.SemaphoreType.DMA((3,)),
                pltpu.SemaphoreType.DMA((2,)),
            ],
            compiler_params=limit(12),
            cost_estimate=cost(2 * slots * width * tile_len * tile_len),
        )(
            place,
            tile_counts,
            in_hbm(tile_rows.reshape(1, slots)),
            in_hbm(tile_cols.reshape(1, slots)),
            in_hbm(tile_values),
            panels[0],
            panels[1],
        )

    with jax.named_scope("gather"):
        for m in range(2, col_devs, 2):
            panels[m] = after(panels[m], early)
            panels[m + 1] = swap(panels[m], "col", 1)
        even, odd = list(range(2, col_devs, 2)), list(range(3, col_devs, 2))
        gathered = pl.pallas_call(
            functools.partial(collect_kernel, even),
            out_shape=pltpu.VMEM(panel_shape, bf16),
            in_specs=anywhere * len(even) + vmem(1),
            out_specs=vmem(1)[0],
            scratch_shapes=[pltpu.SemaphoreType.DMA((len(even),))],
            input_output_aliases={len(even): 0},
            compiler_params=limit(1),
            cost_estimate=cost(width),
        )(*[panels[m] for m in even], gathered)

    with jax.named_scope("late"):
        relay = row_devs == 4
        first_mask = 2 if relay else row_devs - 1
        masks = [3, 3, 1] if relay else list(range(row_devs - 2, 0, -1))
        part = jax.ShapeDtypeStruct((width, slab_len), bf16)
        first, gathered = pl.pallas_call(
            functools.partial(first_late_kernel, [first_mask], odd),
            out_shape=[part, pltpu.VMEM(panel_shape, bf16)],
            in_specs=smem(1) + anywhere * len(odd) + vmem(3),
            out_specs=vmem(2),
            scratch_shapes=[part_acc, pltpu.SemaphoreType.DMA((len(odd),))],
            input_output_aliases={3 + len(odd): 1},
            compiler_params=limit(8),
            cost_estimate=cost(width),
        )(plan, *[panels[m] for m in odd], held, early, gathered)
        parts = pl.pallas_call(
            functools.partial(late_kernel, masks),
            out_shape=[part, slab, part] if relay else [part] * len(masks),
            in_specs=smem(1) + vmem(3),
            out_specs=vmem(len(masks)),
            scratch_shapes=[part_acc],
            compiler_params=limit(8),
            cost_estimate=cost(width),
        )(plan, gathered, held, early)
        if relay:
            first = lax.ppermute(first, "row", [(0, 1), (3, 2), (1, 3), (2, 0)])
            joined = (parts[1] + first.astype(f32)).astype(bf16)
            received = [
                first,
                swap(parts[2], "row", 1),
                trade_rows(joined, [(1, 2), (2, 1)]),
                trade_rows(parts[0], [(0, 3), (3, 0)]),
            ]
        else:
            received = [swap(first, "row", first_mask)]
            received += [swap(part, "row", m) for m, part in zip(masks, parts)]
        base = pl.pallas_call(
            own_kernel,
            out_shape=slab,
            in_specs=smem(1) + vmem(7),
            out_specs=vmem(1)[0],
            scratch_shapes=[part_acc],
            compiler_params=limit(8),
            cost_estimate=cost(width),
        )(plan, gathered, held, early, current_block, previous_block, previous_coupling, diag)

    basis_rows = (stored_count + 1) * width
    half = (width // 8 * -(-basis_rows // 2 // LANES), 8, LANES)
    half = jax.ShapeDtypeStruct(half, f32)
    with jax.named_scope("coefficients"):
        recurrence, give = pl.pallas_call(
            functools.partial(give_kernel, cells, len(received), relay),
            out_shape=[slab, half],
            in_specs=smem(1) + vmem(len(received) + 4),
            out_specs=vmem(2),
            compiler_params=limit(16),
            cost_estimate=cost(width),
        )(plan, base, *received, mass, current_block, stored)
        keep = pl.pallas_call(
            functools.partial(keep_kernel, cells),
            out_shape=half,
            in_specs=smem(1) + vmem(4),
            out_specs=vmem(1)[0],
            compiler_params=limit(16),
            cost_estimate=cost(width),
        )(plan, recurrence, mass, current_block, stored)
        mine = keep + swap(give, "col", 1)
        mine = total(total(mine, "col", 2), "row", 1)
        other = swap(mine, "col", 1)

    with jax.named_scope("residual"):
        less = pl.pallas_call(
            less_kernel,
            out_shape=slab,
            in_specs=smem(1) + vmem(4),
            out_specs=vmem(1)[0],
            compiler_params=limit(16),
            cost_estimate=cost(width),
        )(plan, mine, recurrence, current_block, stored)
        residual, gram = pl.pallas_call(
            functools.partial(residual_kernel, cells),
            out_shape=[
                pltpu.VMEM((width, slab_len), f32),
                jax.ShapeDtypeStruct((width // 2, LANES), f32),
            ],
            in_specs=smem(1) + vmem(5),
            out_specs=vmem(2),
            compiler_params=limit(16),
            cost_estimate=cost(width),
        )(plan, other, less, mass, current_block, stored)
        residual_block = pl.pallas_call(
            store_kernel,
            out_shape=slab,
            in_specs=vmem(1),
            out_specs=anywhere[0],
            scratch_shapes=[pltpu.SemaphoreType.DMA((1,))],
            compiler_params=limit(1),
            cost_estimate=cost(width),
        )(residual)
        coef = pl.pallas_call(
            coefficient_kernel,
            out_shape=jax.ShapeDtypeStruct((basis_rows, width), f32),
            in_specs=smem(1) + vmem(2),
            out_specs=vmem(1)[0],
            compiler_params=limit(4),
            cost_estimate=cost(width),
        )(plan, mine, other)
        coefficients = coef.reshape(stored_count + 1, width, width)

    with jax.named_scope("gram"):
        gram = gram + swap(gram, "col", 1)
        gram = after(total(gram, "col", 2), in_hbm(residual_block), in_hbm(coef))
        gram = total(gram, "row", 1)
        gram = jnp.concatenate(
            [gram[:, :width], gram[:, LANES // 2 : LANES // 2 + width]], axis=0
        )
    return (residual_block, coefficients, gram)


def solution(mesh):
    return jax.shard_map(
        local,
        mesh=mesh,
        in_specs=(
            P(None, ("row", "col")),
            P(None, ("row", "col")),
            P(),
            P(None, None, ("row", "col")),
            P(("row", "col")),
            P(("row", "col")),
            P(("row", "col"), None, None),
            P(("row", "col")),
            P(("row", "col")),
            P(("row", "col")),
        ),
        out_specs=(P(None, ("row", "col")), P(), P()),
        check_vma=False,
    )
```

```python
import functools

import jax
import jax.numpy as jnp
from jax import lax
from jax.experimental import pallas as pl
from jax.experimental.pallas import tpu as pltpu
from jax.sharding import PartitionSpec as P

LANES = 128
CHUNK = 32
GROUP = 2
UNROLL = 4
TILE_BIT, SOURCE_BIT, ROW_BIT = 10, 15, 20
NT = (((1,), (1,)), ((), ()))
MIB = 1 << 20


def swap(value, axis, mask):
    count = lax.axis_size(axis)
    return lax.ppermute(value, axis, [(i, i ^ mask) for i in range(count)])


def trade_rows(value, pairs):
    row_devs, col_devs = lax.axis_size("row"), lax.axis_size("col")
    to = dict(pairs)
    trades = []
    for r in range(row_devs):
        for c in range(col_devs):
            partner = to[r] * col_devs + c if r in to else r * col_devs + (c ^ 1)
            trades.append((r * col_devs + c, partner))
    return lax.ppermute(value, ("row", "col"), trades)


def tree_sum(values):
    values = [values[m] for m in sorted(values)]
    while len(values) > 1:
        values = [values[i] + values[i + 1] for i in range(0, len(values), 2)]
    return values[0]


def total(value, axis, step):
    values = {0: value}
    for m in range(lax.axis_size(axis) - step, 0, -step):
        values[m] = swap(value, axis, m)
    return tree_sum(values)


def total_by_core(value):
    row_devs, col_devs = lax.axis_size("row"), lax.axis_size("col")
    if col_devs != 2 * row_devs:
        return total(total(value, "col", 2), "row", 1)
    places = [(r, c) for r in range(row_devs) for c in range(col_devs)]
    for turn in range(2):
        values = {0: value}
        for m in range(row_devs - 1, 0, -1):
            partners = [(r, c ^ (2 * m)) if c % 2 == turn else (r ^ m, c) for r, c in places]
            trades = [(i, r * col_devs + c) for i, (r, c) in enumerate(partners)]
            values[m] = lax.ppermute(value, ("row", "col"), trades)
        value = tree_sum(values)
    return value


def split(value):
    high = value.astype(jnp.bfloat16)
    low = (value - high.astype(jnp.float32)).astype(jnp.bfloat16)
    return high, low


def mm(a, b, dims=(((1,), (0,)), ((), ()))):
    return lax.dot_general(a, b, dims, preferred_element_type=jnp.float32)


def dot_split(a, b, dims=(((1,), (0,)), ((), ()))):
    rows = a.shape[0]
    a_high, a_low = split(a)
    b_high, b_low = split(b)
    both = mm(jnp.concatenate([a_high, a_low], axis=0), b_high, dims)
    return both[:rows] + both[rows:] + mm(a_high, b_low, dims)


def blocks(shape):
    return [(q, k) for q in range(0, shape[0], 8) for k in range(0, shape[1], LANES)]


def early_kernel(
    row_devs,
    col_devs,
    slab_tiles,
    place,
    counts,
    rows_hbm,
    cols_hbm,
    tiles,
    own_panel,
    near_panel,
    plan,
    held,
    acc,
    panel_buf,
    rows,
    cols,
    out,
    tile_sem,
    list_sem,
    panel_sem,
):
    chunks = (counts[0] + CHUNK - 1) // CHUNK
    row_copy = pltpu.make_async_copy(rows_hbm, rows, list_sem.at[0])
    col_copy = pltpu.make_async_copy(cols_hbm, cols, list_sem.at[1])
    row_copy.start()
    col_copy.start()

    def tile_copy(k):
        window = pl.ds(k * CHUNK, CHUNK)
        return pltpu.make_async_copy(tiles.at[window], held.at[window], tile_sem.at[k])

    @pl.loop(0, chunks)
    def _(k):
        tile_copy(k).start()

    copies = load_panels({0: own_panel, 1: near_panel}, panel_buf, panel_sem)
    zero_panel = panel_buf.shape[0] - 1
    panel_buf[zero_panel, :, :LANES] = jnp.zeros((panel_buf.shape[1], LANES), jnp.bfloat16)
    f32, bf16, i32 = jnp.float32, jnp.bfloat16, jnp.int32
    slots, places = rows.shape[1], out.shape[1] - LANES
    early_chunks = 3 * slots // CHUNK // 4
    targets = row_devs * slab_tiles
    bins = 2 * targets

    def iota(shape, dim):
        return lax.broadcasted_iota(i32, shape, dim)

    slot = iota((1, slots), 1)
    occupied = slot < counts[0]
    earlier = (iota((slots, slots), 0) < iota((slots, slots), 1)).astype(f32).astype(bf16)
    row_copy.wait()
    col_copy.wait()
    row = rows[...]
    row_owner = jnp.floor(row.astype(f32) * (1.0 / slab_tiles)).astype(i32)
    col_f = cols[...].astype(f32)
    source_f = jnp.floor(col_f * (1.0 / slab_tiles))
    source = source_f.astype(i32) ^ place[1]
    tile_f = col_f - slab_tiles * source_f
    far = row_devs - 1 - (row_owner ^ place[0])
    late_bin = targets + far * slab_tiles + row - row_owner * slab_tiles
    early = (source < 2) & (slot < early_chunks * CHUNK)
    bin_of = jnp.where(occupied, jnp.where(early, row, late_bin), -1)
    member = (iota((bins, slots), 0) == bin_of).astype(f32)
    member_bf = member.astype(bf16)
    rank = jnp.sum(member * mm(member_bf, earlier), axis=0, keepdims=True)
    sizes = mm(jnp.ones((8, slots), bf16), member_bf, NT)
    sizes = GROUP * jnp.floor((sizes + (GROUP - 1.0)) * (1.0 / GROUP))
    before = (iota((bins, bins), 1) < iota((bins, bins), 0)).astype(f32)
    begin = jnp.sum(before * sizes[:1], axis=1, keepdims=True)
    position = jnp.sum(member * begin, axis=0, keepdims=True) + rank
    position = jnp.where(occupied, position.astype(i32), -1)
    chosen = (iota((places, slots), 0) == position).astype(f32).astype(bf16)
    slot_f = slot.astype(f32)
    slot_high = jnp.floor(slot_f * (1.0 / 16.0))
    facts = [slot_high, slot_f - 16.0 * slot_high, source.astype(f32), tile_f, row.astype(f32), jnp.ones((1, slots), f32)]
    facts = jnp.concatenate(facts + [jnp.zeros((2, slots), f32)], axis=0).astype(bf16)
    found = mm(facts, chosen, NT).astype(i32)
    source = jnp.where(found[5:6] > 0, found[2:3], col_devs)
    words = (found[4:5] << ROW_BIT) + (source << SOURCE_BIT) + (found[3:4] << TILE_BIT)
    out[:, :places] = words + (found[0:1] << 4) + found[1:2]
    phase = iota((bins, LANES), 1)
    edge = jnp.where(phase > 0, targets + (phase - 1) * slab_tiles, 0)
    inside = (iota((bins, LANES), 0) < edge).astype(f32).astype(bf16)
    edges = mm(sizes.astype(bf16), inside)[:1].astype(i32)
    lane = iota((1, LANES), 1)
    edges = jnp.where(lane == LANES - 2, place[0], jnp.where(lane == LANES - 1, place[1], edges))
    out[:, places:] = edges
    plan_copy = pltpu.make_async_copy(out, plan, list_sem.at[2])
    plan_copy.start()
    acc[...] = jnp.zeros_like(acc)
    for copy in copies + [plan_copy]:
        copy.wait()

    @pl.loop(0, jnp.minimum(chunks, early_chunks))
    def _(k):
        tile_copy(k).wait()

    add_products(plan, 0, 0, targets, held, panel_buf, acc)

    @pl.loop(early_chunks, chunks)
    def _(k):
        tile_copy(k).wait()


def row_of(plan):
    return plan[0, plan.shape[1] - 2]


def core_of(plan):
    return plan[0, plan.shape[1] - 1] & 1


def field(word, low, high):
    return (word >> low) & ((1 << (high - low)) - 1)


def add_products(plan, phase, first_row, spare_row, tiles, panel_buf, acc):
    phases = plan.shape[1] - LANES
    begin, end = plan[0, phases + phase], plan[0, phases + phase + 1]

    def panel(word):
        where = pl.multiple_of(field(word, TILE_BIT, SOURCE_BIT) * LANES, LANES)
        return panel_buf[field(word, SOURCE_BIT, ROW_BIT), :, pl.ds(where, LANES)]

    @pl.loop(0, (end - begin + GROUP * UNROLL - 1) // (GROUP * UNROLL))
    def _(g):
        first = begin + g * GROUP * UNROLL
        parts = []
        for u in range(UNROLL):
            words = [plan[0, first + GROUP * u + i] for i in range(GROUP)]
            left = jnp.concatenate([panel(word) for word in words], axis=1)
            right = jnp.concatenate([tiles[field(word, 0, TILE_BIT)] for word in words], axis=1)
            parts.append(mm(left, right, NT))
        for u in range(UNROLL):
            p = first + GROUP * u
            a = jnp.where(p < end, (plan[0, p] >> ROW_BIT) - first_row, spare_row)
            acc[a] += parts[u]


def load_panels(panels, panel_buf, sem):
    copies = [pltpu.make_async_copy(ref, panel_buf.at[m], sem.at[i]) for i, (m, ref) in enumerate(panels.items())]
    for copy in copies:
        copy.start()
    return copies


def collect_kernel(masks, *refs):
    panels, (_, panel_buf, sem) = refs[: len(masks)], refs[len(masks) :]
    for copy in load_panels(dict(zip(masks, panels)), panel_buf, sem):
        copy.wait()


def first_late_kernel(masks, odd, plan, *refs):
    panels = dict(zip(odd, refs))
    tiles, early, _ = refs[len(odd) : len(odd) + 3]
    sends = refs[len(odd) + 3 : -3]
    panel_buf, acc, sem = refs[-3:]
    copies = load_panels(panels, panel_buf, sem)
    for mask, send in zip(masks, sends):
        late_part(mask, plan, tiles, early, panel_buf, acc, copies)
        put(send, acc)
        copies = ()


def late_kernel(masks, plan, panel_buf, tiles, early, *refs):
    sends, acc = refs[:-1], refs[-1]
    for i, (mask, send) in enumerate(zip(masks, sends)):
        if i == 0 or mask != masks[i - 1]:
            late_part(mask, plan, tiles, early, panel_buf, acc, ())
        put(send, acc)


def own_kernel(plan, panel_buf, tiles, early, current, previous, coupling, diag, base, acc):
    late_part(0, plan, tiles, early, panel_buf, acc, ())
    put(base, acc)
    base[...] += diag[...] * current[...] - jnp.dot(
        coupling[...],
        previous[...],
        precision=lax.Precision.HIGHEST,
        preferred_element_type=jnp.float32,
    )


def late_part(mask, plan, tiles, early, panel_buf, acc, copies):
    slab_tiles = acc.shape[0] - 1
    row_devs = (early.shape[0] - 1) // slab_tiles
    first_row = (row_of(plan) ^ mask) * slab_tiles
    for s in range(slab_tiles):
        acc[s] = early[first_row + s]
    for copy in copies:
        copy.wait()
    add_products(plan, row_devs - mask, first_row, slab_tiles, tiles, panel_buf, acc)


def put(out, acc):
    for s in range(acc.shape[0] - 1):
        out[:, s * LANES : (s + 1) * LANES] = acc[s].astype(out.dtype)


def half_basis(half, current, stored):
    rows = (current.shape[0] + stored.shape[0]) // 2
    cut = rows - current.shape[0]
    return jnp.where(half == 0, jnp.concatenate([current[...], stored[:cut]], axis=0), stored[cut:])


def pack(coef, out):
    spare = -coef.shape[1] % LANES
    coef = jnp.concatenate([coef, jnp.zeros((coef.shape[0], spare), jnp.float32)], axis=1)
    for p, (q, k) in enumerate(blocks(coef.shape)):
        out[p] = coef[q : q + 8, k : k + LANES]


def unpack(pieces, width, columns):
    groups = pieces.shape[0] * 8 // width
    rows = [jnp.concatenate([pieces[p + g] for g in range(groups)], axis=1) for p in range(0, pieces.shape[0], groups)]
    return jnp.concatenate(rows, axis=0)[:, :columns]


def give_kernel(cells, received_count, relay, plan, base, *refs):
    received = refs[:received_count]
    mass, current, stored, recurrence, give = refs[received_count:]
    total = base[...]
    for i, ref in enumerate(received):
        value = ref[...].astype(jnp.float32)
        if relay and i < 3:
            inner = (row_of(plan) == 1) | (row_of(plan) == 2)
            value = jnp.where(inner if i < 2 else jnp.logical_not(inner), 0.0, value)
        total = total + value
    recurrence[...] = total
    weighted = total * (mass[...] * (1.0 / cells))
    pack(dot_split(weighted, half_basis(1 - core_of(plan), current, stored), NT), give)


def keep_kernel(cells, plan, recurrence, mass, current, stored, keep):
    weighted = recurrence[...] * (mass[...] * (1.0 / cells))
    pack(dot_split(weighted, half_basis(core_of(plan), current, stored), NT), keep)


def less_kernel(plan, mine, recurrence, current, stored, less):
    basis = half_basis(core_of(plan), current, stored)
    less[...] = recurrence[...] - dot_split(unpack(mine, recurrence.shape[0], basis.shape[0]), basis)


def turned(pieces, width, rows):
    value = unpack(pieces, width, pieces.shape[0] * 8 // width * LANES)
    spare = jnp.zeros((LANES - width, value.shape[1]), jnp.float32)
    return jnp.concatenate([value, spare], axis=0).T[:rows, :width]


def coefficient_kernel(plan, mine, other, out):
    rows = out.shape[0] // 2
    core = core_of(plan)
    own_half, other_half = turned(mine, out.shape[1], rows), turned(other, out.shape[1], rows)
    out[:rows] = jnp.where(core == 0, own_half, other_half)
    out[rows:] = jnp.where(core == 0, other_half, own_half)


def store_kernel(value, out, sem):
    copy = pltpu.make_async_copy(value, out, sem.at[0])
    copy.start()
    copy.wait()


def residual_kernel(cells, plan, other, less, mass, current, stored, residual, gram):
    width = less.shape[0]
    basis = half_basis(1 - core_of(plan), current, stored)
    value = less[...] - dot_split(unpack(other, width, basis.shape[0]), basis)
    residual[...] = value
    local = dot_split(value * (mass[...] * (1.0 / cells)), value, NT)
    half = width // 2
    gram[...] = jnp.zeros_like(gram)
    gram[:, :width] = local[:half]
    gram[:, LANES // 2 : LANES // 2 + width] = local[half:]


def after_kernel(*refs):
    pass


def after(value, *earlier):
    anywhere = pl.BlockSpec(memory_space=pl.ANY)
    return pl.pallas_call(
        after_kernel,
        out_shape=jax.ShapeDtypeStruct(value.shape, value.dtype),
        in_specs=[anywhere] * (1 + len(earlier)),
        out_specs=anywhere,
        input_output_aliases={0: 0},
        compiler_params=limit(1),
    )(value, *earlier)


def in_hbm(value):
    return pltpu.with_memory_space_constraint(value, pltpu.HBM)


def limit(mib):
    return pltpu.CompilerParams(vmem_limit_bytes=mib * MIB)


def vmem(count):
    return [pl.BlockSpec(memory_space=pltpu.VMEM)] * count


def smem(count):
    return [pl.BlockSpec(memory_space=pltpu.SMEM)] * count


def local(
    current_block,
    previous_block,
    previous_coupling,
    stored_blocks,
    stiffness_diag,
    lumped_mass,
    tile_values,
    tile_rows,
    tile_cols,
    tile_counts,
):
    row_devs = lax.axis_size("row")
    col_devs = lax.axis_size("col")
    width, slab_len = current_block.shape
    stored_count = stored_blocks.shape[0]
    slots, tile_len, _ = tile_values.shape
    slab_tiles = slab_len // tile_len
    cells = slab_len * row_devs * col_devs
    f32, bf16 = jnp.float32, jnp.bfloat16
    place = jnp.stack([lax.axis_index("row"), lax.axis_index("col")]).astype(jnp.int32)
    stored = stored_blocks.reshape(stored_count * width, slab_len)
    mass = lumped_mass.reshape(1, slab_len)
    diag = stiffness_diag.reshape(1, slab_len)
    slab = jax.ShapeDtypeStruct((width, slab_len), f32)

    targets = row_devs * slab_tiles
    anywhere = [pl.BlockSpec(memory_space=pl.ANY)]
    panel_shape = (col_devs + 1, width, slab_len)
    early_shape = (targets + 1, width, tile_len)
    part_acc = pltpu.VMEM((slab_tiles + 1, width, tile_len), f32)

    def cost(flops):
        return pl.CostEstimate(flops=flops, bytes_accessed=flops // width, transcendentals=0)

    with jax.named_scope("gather"):
        rounded = current_block.astype(bf16)
        panels = [rounded] + [None] * (col_devs - 1)
        for m in range(2, col_devs, 2):
            panels[m] = swap(rounded, "col", m)
        panels[1] = swap(rounded, "col", 1)

    with jax.named_scope("early"):
        places = -(-(slots + (GROUP - 1) * 2 * targets + GROUP * UNROLL) // LANES) * LANES
        plan_shape = (1, places + LANES)
        plan, held, early, gathered = pl.pallas_call(
            functools.partial(early_kernel, row_devs, col_devs, slab_tiles),
            out_shape=[
                pltpu.SMEM(plan_shape, jnp.int32),
                pltpu.VMEM(tile_values.shape, bf16),
                pltpu.VMEM(early_shape, f32),
                pltpu.VMEM(panel_shape, bf16),
            ],
            in_specs=smem(2) + [pl.BlockSpec(memory_space=pltpu.HBM)] * 3 + anywhere * 2,
            out_specs=smem(1) + vmem(3),
            scratch_shapes=[
                pltpu.VMEM((1, slots), jnp.int32),
                pltpu.VMEM((1, slots), jnp.int32),
                pltpu.VMEM(plan_shape, jnp.int32),
                pltpu.SemaphoreType.DMA((slots // CHUNK,)),
                pltpu.SemaphoreType.DMA((3,)),
                pltpu.SemaphoreType.DMA((2,)),
            ],
            compiler_params=limit(12),
            cost_estimate=cost(2 * slots * width * tile_len * tile_len),
        )(
            place,
            tile_counts,
            in_hbm(tile_rows.reshape(1, slots)),
            in_hbm(tile_cols.reshape(1, slots)),
            in_hbm(tile_values),
            panels[0],
            panels[1],
        )

    with jax.named_scope("gather"):
        for m in range(2, col_devs, 2):
            panels[m] = after(panels[m], early)
            panels[m + 1] = swap(panels[m], "col", 1)
        even, odd = list(range(2, col_devs, 2)), list(range(3, col_devs, 2))
        gathered = pl.pallas_call(
            functools.partial(collect_kernel, even),
            out_shape=pltpu.VMEM(panel_shape, bf16),
            in_specs=anywhere * len(even) + vmem(1),
            out_specs=vmem(1)[0],
            scratch_shapes=[pltpu.SemaphoreType.DMA((len(even),))],
            input_output_aliases={len(even): 0},
            compiler_params=limit(1),
            cost_estimate=cost(width),
        )(*[panels[m] for m in even], gathered)

    with jax.named_scope("late"):
        relay = row_devs == 4
        first_mask = 2 if relay else row_devs - 1
        masks = [3, 3, 1] if relay else list(range(row_devs - 2, 0, -1))
        part = jax.ShapeDtypeStruct((width, slab_len), bf16)
        first, gathered = pl.pallas_call(
            functools.partial(first_late_kernel, [first_mask], odd),
            out_shape=[part, pltpu.VMEM(panel_shape, bf16)],
            in_specs=smem(1) + anywhere * len(odd) + vmem(3),
            out_specs=vmem(2),
            scratch_shapes=[part_acc, pltpu.SemaphoreType.DMA((len(odd),))],
            input_output_aliases={3 + len(odd): 1},
            compiler_params=limit(8),
            cost_estimate=cost(width),
        )(plan, *[panels[m] for m in odd], held, early, gathered)
        parts = pl.pallas_call(
            functools.partial(late_kernel, masks),
            out_shape=[part, slab, part] if relay else [part] * len(masks),
            in_specs=smem(1) + vmem(3),
            out_specs=vmem(len(masks)),
            scratch_shapes=[part_acc],
            compiler_params=limit(8),
            cost_estimate=cost(width),
        )(plan, gathered, held, early)
        if relay:
            first = lax.ppermute(first, "row", [(0, 1), (3, 2), (1, 3), (2, 0)])
            joined = (parts[1] + first.astype(f32)).astype(bf16)
            received = [
                first,
                trade_rows(parts[0], [(0, 3), (3, 0)]),
                trade_rows(joined, [(1, 2), (2, 1)]),
                swap(parts[2], "row", 1),
            ]
        else:
            received = [swap(first, "row", first_mask)]
            received += [swap(part, "row", m) for m, part in zip(masks, parts)]
        base = pl.pallas_call(
            own_kernel,
            out_shape=slab,
            in_specs=smem(1) + vmem(7),
            out_specs=vmem(1)[0],
            scratch_shapes=[part_acc],
            compiler_params=limit(8),
            cost_estimate=cost(width),
        )(plan, gathered, held, early, current_block, previous_block, previous_coupling, diag)

    basis_rows = (stored_count + 1) * width
    half = (width // 8 * -(-basis_rows // 2 // LANES), 8, LANES)
    half = jax.ShapeDtypeStruct(half, f32)
    with jax.named_scope("coefficients"):
        recurrence, give = pl.pallas_call(
            functools.partial(give_kernel, cells, len(received), relay),
            out_shape=[slab, half],
            in_specs=smem(1) + vmem(len(received) + 4),
            out_specs=vmem(2),
            compiler_params=limit(16),
            cost_estimate=cost(width),
        )(plan, base, *received, mass, current_block, stored)
        keep = pl.pallas_call(
            functools.partial(keep_kernel, cells),
            out_shape=half,
            in_specs=smem(1) + vmem(4),
            out_specs=vmem(1)[0],
            compiler_params=limit(16),
            cost_estimate=cost(width),
        )(plan, recurrence, mass, current_block, stored)
        mine = keep + swap(give, "col", 1)
        mine = total_by_core(mine)
        other = swap(mine, "col", 1)

    with jax.named_scope("residual"):
        less = pl.pallas_call(
            less_kernel,
            out_shape=slab,
            in_specs=smem(1) + vmem(4),
            out_specs=vmem(1)[0],
            compiler_params=limit(16),
            cost_estimate=cost(width),
        )(plan, mine, recurrence, current_block, stored)
        residual, gram = pl.pallas_call(
            functools.partial(residual_kernel, cells),
            out_shape=[
                pltpu.VMEM((width, slab_len), f32),
                jax.ShapeDtypeStruct((width // 2, LANES), f32),
            ],
            in_specs=smem(1) + vmem(5),
            out_specs=vmem(2),
            compiler_params=limit(16),
            cost_estimate=cost(width),
        )(plan, other, less, mass, current_block, stored)
        residual_block = pl.pallas_call(
            store_kernel,
            out_shape=slab,
            in_specs=vmem(1),
            out_specs=anywhere[0],
            scratch_shapes=[pltpu.SemaphoreType.DMA((1,))],
            compiler_params=limit(1),
            cost_estimate=cost(width),
        )(residual)
        coef = pl.pallas_call(
            coefficient_kernel,
            out_shape=jax.ShapeDtypeStruct((basis_rows, width), f32),
            in_specs=smem(1) + vmem(2),
            out_specs=vmem(1)[0],
            compiler_params=limit(4),
            cost_estimate=cost(width),
        )(plan, mine, other)
        coefficients = coef.reshape(stored_count + 1, width, width)

    with jax.named_scope("gram"):
        gram = gram + swap(gram, "col", 1)
        gram = after(total(gram, "col", 2), in_hbm(residual_block), in_hbm(coef))
        gram = total(gram, "row", 1)
        gram = jnp.concatenate(
            [gram[:, :width], gram[:, LANES // 2 : LANES // 2 + width]], axis=0
        )
    return (residual_block, coefficients, gram)


def solution(mesh):
    return jax.shard_map(
        local,
        mesh=mesh,
        in_specs=(
            P(None, ("row", "col")),
            P(None, ("row", "col")),
            P(),
            P(None, None, ("row", "col")),
            P(("row", "col")),
            P(("row", "col")),
            P(("row", "col"), None, None),
            P(("row", "col")),
            P(("row", "col")),
            P(("row", "col")),
        ),
        out_specs=(P(None, ("row", "col")), P(), P()),
        check_vma=False,
    )
```
